32 devices in a mesh: az: 8 (over z, y), ax: 4 (over x, core).
Axes of the slice: x: 2, y: 2, z: 4, core: 2. Of those that a mesh axis runs over, the one named last changes fastest.
Arguments:
- velocity: float32 [3, 256, 512, 128], P(None, 'az', 'ax'), may hold values from -60 to 60
Outputs:
- increment: float32 [3, 256, 512, 128], P(None, 'az', 'ax')
- time_step: float32 [], replicated
The draws below stay inside these ranges and needn't reach their ends.
All inputs are finite; a program needn't handle non-finite values.
Results may differ from the reference program's by a relative error of at most 0.0003.
Values sent between devices are 32-bit elements; how exact they have to be, the bound alone decides.
No kernel may reach another device: no remote copies, remote signals or barrier semaphores. Data moves between devices by JAX's collectives and lax.ppermute only.
A program may use at most 192 MiB of HBM per device.

```python
import math
import jax
import jax.numpy as jnp
from jax import lax

TDEV = 32
ZDEV = 128
NR = 128
NT = 256
NZ = 512
N_AZ = 8
N_AX = 4


def radial_envelope(radius):
    return 1.05 * radius * radius / (radius * radius + 0.05)


def core_profile(radius, core_width):
    scaled = radius / core_width
    return scaled * jnp.exp(-scaled * scaled)


def wave_sheet(key, angles, axial_angles, strength):
    amp_key, phase_key = jax.random.split(key)
    amplitudes = jax.random.normal(amp_key, (4, 3), jnp.float32) * (strength / math.sqrt(6.0))
    phases = jax.random.uniform(phase_key, (4, 3), jnp.float32, 0.0, 2.0 * math.pi)
    pattern = jnp.zeros((angles.shape[0], axial_angles.shape[0]), jnp.float32)
    for azimuth_order in range(4):
        for axial_order in range(3):
            pattern = pattern + amplitudes[azimuth_order, axial_order] * jnp.cos((azimuth_order + 1.0) * angles[:, None] + axial_order * axial_angles[None, :] + phases[azimuth_order, axial_order])
    return pattern


def draw_velocity(key, part):
    key = jax.random.fold_in(key, 11)
    subkeys = jax.random.split(key, 5)
    theta_step = 2.0 * math.pi / NT
    azimuth_nodes = jnp.arange(NT, dtype=jnp.float32) * theta_step
    between = azimuth_nodes + 0.5 * theta_step
    axial_phase = jnp.arange(NZ, dtype=jnp.float32) * (2.0 * math.pi / NZ)
    axial_between = axial_phase + math.pi / NZ
    radial_index = jnp.arange(NR, dtype=jnp.float32)
    centre = (radial_index + 0.5) / NR
    facing = (radial_index + 1.0) / NR
    core_width = 2.0 / NR
    small_scale = jax.random.truncated_normal(subkeys[0], -4.0, 4.0, (3, NT, NZ, NR), jnp.float32)
    phases = jax.random.uniform(subkeys[1], (4,), jnp.float32, 0.0, 2.0 * math.pi)
    radial_drift = 0.38 * (0.7 + 0.3 * jnp.cos(axial_phase + phases[0]))
    radial_part = radial_envelope(facing)[None, None, :] * wave_sheet(subkeys[2], azimuth_nodes, axial_phase, 0.06)[:, :, None] + radial_drift[None, :, None] * core_profile(facing, core_width)[None, None, :] + 0.03 * radial_envelope(facing) * small_scale[0]
    azimuthal_part = radial_envelope(centre)[None, None, :] * wave_sheet(subkeys[3], between, axial_phase, 0.06)[:, :, None] + 0.03 * radial_envelope(centre) * small_scale[1]
    turning = phases[1] + axial_between
    streak = 0.43 * jnp.cos(azimuth_nodes[:, None] - turning[None, :])
    axial_part = 1.25 * (1.0 - jnp.power(centre, 10))[None, None, :] + radial_envelope(centre)[None, None, :] * wave_sheet(subkeys[4], azimuth_nodes, axial_between, 0.2)[:, :, None] + streak[:, :, None] * core_profile(centre, core_width)[None, None, :] + 0.03 * radial_envelope(centre) * small_scale[2]
    velocity = 20.0 * jnp.stack([radial_part, azimuthal_part, axial_part])
    return jnp.clip(velocity, -60.0, 60.0)


def setup_inputs(seed: int = 0) -> dict:
    splits = jax.random.split(jax.random.key(seed), 2)
    return {
        "velocity": draw_velocity(jax.random.fold_in(splits[1], 71), 0),
    }


AXIAL_STEP = 0.01
VISCOSITY = 1e-3
CFL_TARGET = 1.2
GAMMA = 8.0 / 15.0


def explicit_terms(padded, partner, theta_step):
    tangent_count = padded.shape[1] - 4
    axial_count = padded.shape[2] - 4
    radial_count = padded.shape[3]
    spacing_r = 1.0 / radial_count
    radial_index = jnp.arange(radial_count).astype(jnp.float32)
    centre = (radial_index + 0.5) * spacing_r
    facing = (radial_index + 1.0) * spacing_r
    wall_mask = jnp.where(radial_index < radial_count - 1.5, 1.0, 0.0).astype(jnp.float32)

    def values_at(component, theta_off, axial_off):
        piece = padded[component, 2 + theta_off:2 + theta_off + tangent_count, 2 + axial_off:2 + axial_off + axial_count, :]
        if component == 0:
            piece = piece * wall_mask
        return piece

    def inward(field, ghost):
        return jnp.concatenate([ghost[..., None], field[..., :-1]], axis=-1)

    def outward(field, ghost):
        return jnp.concatenate([field[..., 1:], ghost[..., None]], axis=-1)

    def below_axis(field):
        return inward(field, jnp.zeros_like(field[..., 0]))

    def beyond_wall(field):
        return outward(field, -field[..., -1])

    def periodic_parts(component, theta_flag):
        def sample(offset):
            return values_at(component, offset, 0) if theta_flag else values_at(component, 0, offset)
        spacing = theta_step if theta_flag else AXIAL_STEP
        first_der = (8.0 * (sample(1) - sample(-1)) - (sample(2) - sample(-2))) / (12.0 * spacing)
        second_der = (-sample(2) + 16.0 * sample(1) - 30.0 * sample(0) + 16.0 * sample(-1) - sample(-2)) / (12.0 * spacing * spacing)
        return first_der, second_der

    def radial_parts(field, inner_ghost, outer_ghost):
        lower_vals = inward(field, inner_ghost)
        upper_vals = outward(field, outer_ghost)
        return (upper_vals - lower_vals) / (2.0 * spacing_r), (upper_vals - 2.0 * field + lower_vals) / (spacing_r * spacing_r)

    radial_vel = values_at(0, 0, 0)
    azim_vel = values_at(1, 0, 0)
    axial_vel = values_at(2, 0, 0)
    vr_dr, vr_drr = radial_parts(radial_vel, -partner[0], jnp.zeros_like(radial_vel[..., 0]))
    vt_dr, vt_drr = radial_parts(azim_vel, -partner[1], -azim_vel[..., -1])
    vz_dr, vz_drr = radial_parts(axial_vel, partner[2], -axial_vel[..., -1])
    vr_dt, vr_dtt = periodic_parts(0, True)
    vr_dz, vr_dzz = periodic_parts(0, False)
    vt_dt, vt_dtt = periodic_parts(1, True)
    vt_dz, vt_dzz = periodic_parts(1, False)
    vz_dt, vz_dtt = periodic_parts(2, True)
    vz_dz, vz_dzz = periodic_parts(2, False)

    azim_on_axial = 0.25 * (values_at(1, -1, 0) + azim_vel + values_at(1, -1, 1) + values_at(1, 0, 1))
    radial_next = values_at(0, 0, 1)
    rad_on_axial = 0.25 * (radial_vel + below_axis(radial_vel) + radial_next + below_axis(radial_next))
    axial_adv = -(rad_on_axial * vz_dr + azim_on_axial / centre * vz_dt + axial_vel * vz_dz)
    axial_visc = VISCOSITY * (vz_drr + vz_dr / centre + vz_dtt / (centre * centre) + vz_dzz)

    axial_on_azim = 0.25 * (values_at(2, 0, -1) + axial_vel + values_at(2, 1, -1) + values_at(2, 1, 0))
    radial_side = values_at(0, 1, 0)
    rad_on_azim = 0.25 * (radial_vel + below_axis(radial_vel) + radial_side + below_axis(radial_side))
    azim_adv = -(rad_on_azim * vt_dr + azim_vel / centre * vt_dt + axial_on_azim * vt_dz + rad_on_azim * azim_vel / centre)
    radial_turn = ((radial_side + below_axis(radial_side)) - (radial_vel + below_axis(radial_vel))) / (2.0 * theta_step)
    azim_visc = VISCOSITY * (vt_drr + vt_dr / centre + vt_dtt / (centre * centre) + vt_dzz
                             - azim_vel / (centre * centre) + 2.0 * radial_turn / (centre * centre))

    azim_back = values_at(1, -1, 0)
    azim_on_radial = 0.25 * (azim_back + azim_vel + beyond_wall(azim_back) + beyond_wall(azim_vel))
    axial_back = values_at(2, 0, -1)
    axial_on_radial = 0.25 * (axial_back + axial_vel + beyond_wall(axial_back) + beyond_wall(axial_vel))
    radial_adv = -(radial_vel * vr_dr + azim_on_radial / facing * vr_dt + axial_on_radial * vr_dz) + azim_on_radial * azim_on_radial / facing
    azim_turn = ((azim_vel + beyond_wall(azim_vel)) - (azim_back + beyond_wall(azim_back))) / (2.0 * theta_step)
    radial_visc = VISCOSITY * (vr_drr + vr_dr / facing + vr_dtt / (facing * facing) + vr_dzz
                               - radial_vel / (facing * facing) - 2.0 * azim_turn / (facing * facing))

    explicit = jnp.stack([(radial_adv + radial_visc) * wall_mask, azim_adv + azim_visc, axial_adv + axial_visc])
    cfl_rate = jnp.abs(radial_vel) / spacing_r + jnp.abs(azim_vel) / (centre * theta_step) + jnp.abs(axial_vel) / AXIAL_STEP
    return explicit, cfl_rate


def reference(velocity):
    padded = jnp.pad(velocity, ((0, 0), (2, 2), (2, 2), (0, 0)), mode="wrap")
    partner = jnp.roll(velocity[:, :, :, 0], NT // 2, axis=1)
    theta_step = 2.0 * math.pi / NT

    def block(block_index):
        theta_start = ((block_index // N_AX) * TDEV).astype(jnp.int32)
        axial_start = ((block_index % N_AX) * ZDEV).astype(jnp.int32)
        anchor = jnp.zeros((), jnp.int32)
        window = lax.dynamic_slice(padded, (anchor, theta_start, axial_start, anchor), (3, TDEV + 4, ZDEV + 4, NR))
        partner_block = lax.dynamic_slice(partner, (anchor, theta_start, axial_start), (3, TDEV, ZDEV))
        explicit, cfl_rate = explicit_terms(window, partner_block, theta_step)
        return explicit, jnp.max(cfl_rate)

    blocks, largest_each = lax.map(block, jnp.arange(N_AZ * N_AX, dtype=jnp.int32))
    time_step = CFL_TARGET / (jnp.max(largest_each) + 1e-6)
    arranged = blocks.reshape(N_AZ, N_AX, 3, TDEV, ZDEV, NR).transpose(2, 0, 3, 1, 4, 5).reshape(3, NT, NZ, NR)
    return (GAMMA * time_step) * arranged, time_step
```

```python
import functools
import math

import jax
import jax.numpy as jnp
import numpy as np
from jax import lax
from jax.experimental import pallas as pl
from jax.experimental.pallas import tpu as pltpu
from jax.sharding import PartitionSpec as P

AXIAL_STEP = 0.01
VISCOSITY = 0.001
CFL_TARGET = 1.2
GAMMA = 8.0 / 15.0

PAD = 8
GROUP = 4
VMEM_LIMIT = 40 * 2**20

(
    WALL,
    RATE_R,
    RATE_T,
    RADIAL_C,
    THETA_C,
    SECOND_C,
    CENTRE_Z,
    CENTRE_T,
    CURVE_T,
    TURN_T,
    RADIAL_F,
    THETA_F,
    SECOND_F,
    CENTRE_R,
    CURVE_R,
    TURN_R,
    COUNT,
) = range(17)


def coefficients(radial, theta_step):
    dr = 1.0 / radial
    index = np.arange(radial, dtype=np.float64)
    centre = (index + 0.5) * dr
    face = (index + 1.0) * dr
    wall = np.where(index < radial - 1.5, 1.0, 0.0)
    h = theta_step
    nu = VISCOSITY
    rows = np.zeros((COUNT, radial))
    rows[WALL] = wall
    rows[RATE_R] = wall / dr
    rows[RATE_T] = 1.0 / (centre * h)
    common = -2.0 * nu / dr**2 - 30.0 * nu / (12.0 * AXIAL_STEP**2)
    rows[RADIAL_C] = nu / (2.0 * dr * centre)
    rows[THETA_C] = -1.0 / (12.0 * h * centre)
    rows[SECOND_C] = nu / (12.0 * h * h * centre**2)
    rows[CENTRE_Z] = common - 30.0 * rows[SECOND_C]
    rows[CENTRE_T] = rows[CENTRE_Z] - nu / centre**2
    rows[CURVE_T] = 0.25 / centre
    rows[TURN_T] = nu / (h * centre**2)
    rows[RADIAL_F] = nu / (2.0 * dr * face)
    rows[THETA_F] = -0.25 / (12.0 * h * face)
    rows[SECOND_F] = nu / (12.0 * h * h * face**2)
    rows[CENTRE_R] = common - 30.0 * rows[SECOND_F] - nu / face**2
    rows[CURVE_R] = 1.0 / (16.0 * face)
    rows[TURN_R] = -nu / (h * face**2)
    return np.broadcast_to(rows[:, None, :], (COUNT, 8, radial)).astype(np.float32)


def terms(vel, ghost, coef, j, k, dr):
    lane = lax.broadcasted_iota(jnp.int32, (8, 128), 1)
    first_lane = lane == 0
    last_lane = lane == 127

    def at(component, dj, dk):
        return vel[component, j + dj, pl.ds(k + PAD + dk, 8), :]

    def out(x):
        return pltpu.roll(x, 127, 1)

    def inn(x):
        return pltpu.roll(x, 1, 1)

    nu = VISCOSITY
    lap = nu / dr**2
    adv_z = -1.0 / (12.0 * AXIAL_STEP)
    vis_z = nu / (12.0 * AXIAL_STEP**2)

    def pieces(component):
        p1, m1, p2, m2 = (at(component, d, 0) for d in (1, -1, 2, -2))
        first_t = 8.0 * (p1 - m1) - (p2 - m2)
        second_t = 16.0 * (p1 + m1) - (p2 + m2)
        p1, m1, p2, m2 = (at(component, 0, d) for d in (1, -1, 2, -2))
        first_z = 8.0 * (p1 - m1) - (p2 - m2)
        second_z = 16.0 * (p1 + m1) - (p2 + m2)
        return first_t, second_t, first_z, second_z

    a, b, c = (at(i, 0, 0) for i in range(3))
    a_in = inn(a)
    pair_a = a + a_in
    a_side = at(0, 1, 0)
    pair_side = a_side + inn(a_side)
    a_next = at(0, 0, 1)
    pair_next = a_next + inn(a_next)

    first_t, second_t, first_z, second_z = pieces(2)
    c_out = out(c)
    up = jnp.where(last_lane, -c, c_out)
    low = jnp.where(first_lane, ghost(2), inn(c))
    u_r = pair_a + pair_next
    u_t = (at(1, -1, 0) + b) + (at(1, -1, 1) + at(1, 0, 1))
    h_z = (up - low) * (coef(RADIAL_C) - u_r * (0.125 / dr)) + (up + low) * lap
    h_z = h_z + first_t * (u_t * (0.25 * coef(THETA_C)))
    h_z = h_z + second_t * coef(SECOND_C) + second_z * vis_z
    h_z = h_z + c * (coef(CENTRE_Z) + first_z * adv_z)

    first_t, second_t, first_z, second_z = pieces(1)
    b_out = out(b)
    up = jnp.where(last_lane, -b, b_out)
    low = jnp.where(first_lane, ghost(1), inn(b))
    u_r = pair_a + pair_side
    c_back = at(2, 0, -1)
    u_z = (c_back + c) + (at(2, 1, -1) + at(2, 1, 0))
    h_t = (up - low) * (coef(RADIAL_C) - u_r * (0.125 / dr)) + (up + low) * lap
    h_t = h_t + b * (coef(CENTRE_T) + first_t * coef(THETA_C) - u_r * coef(CURVE_T))
    h_t = h_t + second_t * coef(SECOND_C) + second_z * vis_z
    h_t = h_t + first_z * (u_z * (0.25 * adv_z))
    h_t = h_t + (pair_side - pair_a) * coef(TURN_T)

    first_t, second_t, first_z, second_z = pieces(0)
    up = out(a)
    low = jnp.where(first_lane, ghost(0), a_in)
    b_back = at(1, -1, 0)
    pair_b = b + b_out
    pair_back = b_back + out(b_back)
    u_t = pair_b + pair_back
    u_z = (c + c_out) + (c_back + out(c_back))
    h_r = (up - low) * (coef(RADIAL_F) - a * (0.5 / dr)) + (up + low) * lap
    h_r = h_r + u_t * (u_t * coef(CURVE_R) + first_t * coef(THETA_F))
    h_r = h_r + second_t * coef(SECOND_F) + second_z * vis_z
    h_r = h_r + first_z * (u_z * (0.25 * adv_z)) + a * coef(CENTRE_R)
    h_r = h_r + (pair_b - pair_back) * coef(TURN_R)
    return h_r, h_t, h_z


def theta_edges(v_ref, head_ref, tail_ref, sems):
    count = v_ref.shape[1]
    copies = [
        pltpu.make_async_copy(v_ref.at[:, 0:2], head_ref, sems.at[0]),
        pltpu.make_async_copy(v_ref.at[:, count - 2 : count], tail_ref, sems.at[1]),
    ]
    for copy in copies:
        copy.start()
    for copy in copies:
        copy.wait()


def first_pass(v_ref, coef_ref, low_ref, high_ref, inner_ref, pay_ref, vel, sems):
    _, planes, axial, radial = v_ref.shape
    groups = planes // GROUP

    def fetch(g):
        part = pl.ds(g * GROUP, GROUP)
        return pltpu.make_async_copy(v_ref.at[:, part], vel.at[:, part], sems.at[g])

    for g in range(groups):
        fetch(g).start()
    inner_ref[...] = jnp.zeros_like(inner_ref)
    lane = lax.broadcasted_iota(jnp.int32, (8, radial), 1)

    def step(g, largest):
        fetch(g).wait()
        for q in range(GROUP):
            j = g * GROUP + q
            for n in range(3):
                mask = coef_ref[WALL, 0:2] if n == 0 else 1.0
                low_ref[n, j] = vel[n, j, 0:2, :] * mask
                high_ref[n, j] = vel[n, j, axial - 2 : axial, :] * mask

        def rows(i, largest):
            k = pl.ds(pl.multiple_of(i * 8, 8), 8)
            inner = inner_ref[k, :]
            for q in range(GROUP):
                j = g * GROUP + q
                a, b, c = (vel[n, j, k, :] for n in range(3))
                rate = (
                    jnp.abs(a) * coef_ref[RATE_R]
                    + jnp.abs(b) * coef_ref[RATE_T]
                    + jnp.abs(c) * (1.0 / AXIAL_STEP)
                )
                largest = jnp.maximum(largest, rate)
                for n, x in enumerate((a, b, c)):
                    place = n * planes + j
                    inner = jnp.where(lane == place, pltpu.roll(x, place, 1), inner)
            inner_ref[k, :] = inner
            return largest

        return lax.fori_loop(0, axial // 8, rows, largest)

    largest = lax.fori_loop(0, groups, step, jnp.zeros((8, radial), jnp.float32))
    sign = jnp.where(lane < 2 * planes, -1.0, 1.0).astype(jnp.float32)

    def turn(i, carry):
        k = pl.ds(pl.multiple_of(i * 8, 8), 8)
        inner_ref[k, :] = inner_ref[k, :] * sign
        return carry

    lax.fori_loop(0, axial // 8, turn, 0)
    top = jnp.max(largest, axis=(0, 1), keepdims=True)
    pay_ref[...] = jnp.broadcast_to(top, pay_ref.shape)
    pay_ref[1:2, :] = vel[1, planes - 1, 0:1, :]
    pay_ref[2:3, :] = vel[2, 0, axial - 1 : axial, :]


def interior(
    scale_ref, v_ref, low_ref, high_ref, inner_ref, coef_ref, out_ref, vel, res, in_sems, out_sems
):
    _, planes, axial, radial = v_ref.shape
    dr = 1.0 / radial

    def fetch(j):
        return pltpu.make_async_copy(
            v_ref.at[:, j], vel.at[:, j, pl.ds(PAD, axial)], in_sems.at[j]
        )

    def store(j):
        slot = j % 2
        return pltpu.make_async_copy(res.at[slot], out_ref.at[:, j], out_sems.at[slot])

    def ready(j):
        fetch(j).wait()
        vel[:, j, PAD - 2 : PAD, :] = low_ref[:, j]
        vel[:, j, PAD + axial : PAD + axial + 2, :] = high_ref[:, j]
        for i in range(axial // 8):
            k = pl.ds(PAD + 8 * i, 8)
            vel[0, j, k, :] = vel[0, j, k, :] * coef_ref[WALL]

    def launch(j, carry):
        fetch(j).start()
        return carry

    lax.fori_loop(0, planes, launch, 0)
    for j in range(4):
        ready(j)
    scale = scale_ref[0]

    def plane(j, carry):
        ready(j + 2)

        @pl.when(j >= 4)
        def _():
            store(j - 2).wait()

        slot = j % 2

        def rows(i, carry):
            k = pl.multiple_of(i * 8, 8)
            inner = inner_ref[pl.ds(k, 8), :]

            def ghost(component):
                return pltpu.roll(inner, radial - (component * planes + j), 1)

            h_r, h_t, h_z = terms(vel, ghost, lambda n: coef_ref[n], j, k, dr)
            k = pl.ds(k, 8)
            res[slot, 0, k, :] = h_r * (scale * coef_ref[WALL])
            res[slot, 1, k, :] = h_t * scale
            res[slot, 2, k, :] = h_z * scale
            return carry

        lax.fori_loop(0, axial // 8, rows, 0)
        store(j).start()
        return carry

    lax.fori_loop(2, planes - 2, plane, 0)
    store(planes - 4).wait()
    store(planes - 3).wait()


def edges(
    scale_ref,
    v_ref,
    below_ref,
    above_ref,
    low_ref,
    high_ref,
    corner_ref,
    inner_ref,
    coef_ref,
    part_ref,
    out_ref,
    vel,
    res,
    in_sems,
    out_sems,
):
    del part_ref
    _, planes, axial, radial = v_ref.shape
    dr = 1.0 / radial
    cells = pl.ds(PAD, axial)
    fetches = [
        pltpu.make_async_copy(below_ref, vel.at[:, 0:2, cells], in_sems.at[0]),
        pltpu.make_async_copy(v_ref.at[:, 0:4], vel.at[:, 2:6, cells], in_sems.at[1]),
        pltpu.make_async_copy(
            v_ref.at[:, planes - 4 : planes], vel.at[:, 6:10, cells], in_sems.at[2]
        ),
        pltpu.make_async_copy(above_ref, vel.at[:, 10:12, cells], in_sems.at[3]),
    ]
    for fetch in fetches:
        fetch.start()
    for fetch in fetches:
        fetch.wait()
    own = {2: 0, 3: 1, 4: 2, 7: planes - 3, 8: planes - 2, 9: planes - 1}
    for q in own:
        vel[:, q, PAD - 2 : PAD, :] = low_ref[:, own[q]]
        vel[:, q, PAD + axial : PAD + axial + 2, :] = high_ref[:, own[q]]
    vel[1, 1, PAD + axial : PAD + axial + 1, :] = corner_ref[0:1, :]
    vel[2, 10, PAD - 1 : PAD, :] = corner_ref[1:2, :]
    for q in range(12):
        for i in range(axial // 8):
            k = pl.ds(PAD + 8 * i, 8)
            vel[0, q, k, :] = vel[0, q, k, :] * coef_ref[WALL]
    scale = scale_ref[0]
    copies = []
    for side, (start, first) in enumerate(((2, 0), (8, planes - 2))):
        for q in range(2):

            def rows(i, carry, side=side, start=start, first=first, q=q):
                k = pl.multiple_of(i * 8, 8)
                inner = inner_ref[pl.ds(k, 8), :]

                def ghost(component):
                    place = component * planes + first + q
                    return pltpu.roll(inner, (radial - place) % radial, 1)

                h_r, h_t, h_z = terms(vel, ghost, lambda n: coef_ref[n], start + q, k, dr)
                k = pl.ds(k, 8)
                res[side, 0, q, k, :] = h_r * (scale * coef_ref[WALL])
                res[side, 1, q, k, :] = h_t * scale
                res[side, 2, q, k, :] = h_z * scale
                return carry

            lax.fori_loop(0, axial // 8, rows, 0)
        copy = pltpu.make_async_copy(
            res.at[side], out_ref.at[:, first : first + 2], out_sems.at[side]
        )
        copy.start()
        copies.append(copy)
    for copy in copies:
        copy.wait()


def shifted(block, axis, distance):
    count = lax.axis_size(axis)
    return lax.ppermute(block, axis, [((i - distance) % count, i) for i in range(count)])


def per_device(velocity):
    _, planes, axial, radial = velocity.shape
    az, ax = lax.axis_size("az"), lax.axis_size("ax")
    theta_step = 2.0 * math.pi / (az * planes)
    coef = jnp.asarray(coefficients(radial, theta_step))
    f32 = jnp.float32
    anywhere = pl.BlockSpec(memory_space=pl.ANY)
    vmem = pl.BlockSpec(memory_space=pltpu.VMEM)
    smem = pl.BlockSpec(memory_space=pltpu.SMEM)
    params = pltpu.CompilerParams(vmem_limit_bytes=VMEM_LIMIT)
    shape = jax.ShapeDtypeStruct

    pair = shape((3, 2, axial, radial), f32)
    head, tail = pl.pallas_call(
        theta_edges,
        out_shape=(pair, pair),
        in_specs=[anywhere],
        out_specs=(anywhere, anywhere),
        scratch_shapes=[pltpu.SemaphoreType.DMA((2,))],
        name="theta_edges",
    )(velocity)
    below = shifted(tail, "az", 1)
    above = shifted(head, "az", -1)

    edge = shape((3, planes, 2, radial), f32)
    first, last, inner, pay = pl.pallas_call(
        first_pass,
        out_shape=(edge, edge, shape((axial, radial), f32), shape((8, radial), f32)),
        in_specs=[anywhere, vmem],
        out_specs=(vmem,) * 4,
        scratch_shapes=[
            pltpu.VMEM(velocity.shape, f32),
            pltpu.SemaphoreType.DMA((planes // GROUP,)),
        ],
        compiler_params=params,
        name="first_pass",
    )(velocity, coef)
    low = shifted(last, "ax", 1)
    high = shifted(first, "ax", -1)
    inner = shifted(inner, "az", az // 2)
    everyone = lax.all_gather(pay, ("az", "ax"))
    largest = jnp.max(everyone[:, 0, 0])
    time_step = CFL_TARGET / (largest + 1e-06)
    scale = (GAMMA * time_step).reshape(1)
    i, k = lax.axis_index("az"), lax.axis_index("ax")
    source_t = ((i - 1) % az) * ax + (k + 1) % ax
    source_z = ((i + 1) % az) * ax + (k - 1) % ax
    corner = jnp.stack([everyone[source_t, 1], everyone[source_z, 2]])

    rows = axial + 2 * PAD
    part = pl.pallas_call(
        interior,
        out_shape=shape(velocity.shape, f32),
        in_specs=[smem, anywhere, vmem, vmem, vmem, vmem],
        out_specs=anywhere,
        scratch_shapes=[
            pltpu.VMEM((3, planes, rows, radial), f32),
            pltpu.VMEM((2, 3, axial, radial), f32),
            pltpu.SemaphoreType.DMA((planes,)),
            pltpu.SemaphoreType.DMA((2,)),
        ],
        compiler_params=params,
        name="interior",
    )(scale, velocity, low, high, inner, coef)
    increment = pl.pallas_call(
        edges,
        out_shape=shape(velocity.shape, f32),
        in_specs=[smem, anywhere, anywhere, anywhere, vmem, vmem, vmem, vmem, vmem, anywhere],
        out_specs=anywhere,
        scratch_shapes=[
            pltpu.VMEM((3, 12, rows, radial), f32),
            pltpu.VMEM((2, 3, 2, axial, radial), f32),
            pltpu.SemaphoreType.DMA((4,)),
            pltpu.SemaphoreType.DMA((2,)),
        ],
        input_output_aliases={9: 0},
        compiler_params=params,
        name="edges",
    )(scale, velocity, below, above, low, high, corner, inner, coef, part)
    return increment, time_step


def solution(mesh):
    return jax.shard_map(
        per_device,
        mesh=mesh,
        in_specs=(P(None, "az", "ax", None),),
        out_specs=(P(None, "az", "ax", None), P()),
        check_vma=False,
    )
```

```python
import functools
import math

import jax
import jax.numpy as jnp
import numpy as np
from jax import lax
from jax.experimental import pallas as pl
from jax.experimental.pallas import tpu as pltpu
from jax.sharding import PartitionSpec as P

AXIAL_STEP = 0.01
VISCOSITY = 0.001
CFL_TARGET = 1.2
GAMMA = 8.0 / 15.0

PAD = 8
HALO = 2
GROUP = 4
UNROLL = 4

(
    WALL,
    RATE_R,
    RATE_T,
    RADIAL_C,
    THETA_C,
    SECOND_C,
    CENTRE_Z,
    CENTRE_T,
    CURVE_T,
    TURN_T,
    RADIAL_F,
    THETA_F,
    SECOND_F,
    CENTRE_R,
    CURVE_R,
    TURN_R,
    COUNT,
) = range(17)


def coefficients(radial, theta_step):
    dr = 1.0 / radial
    index = np.arange(radial, dtype=np.float64)
    centre = (index + 0.5) * dr
    face = (index + 1.0) * dr
    wall = np.where(index < radial - 1.5, 1.0, 0.0)
    h = theta_step
    nu = VISCOSITY
    rows = np.zeros((COUNT, radial))
    rows[WALL] = wall
    rows[RATE_R] = wall / dr
    rows[RATE_T] = 1.0 / (centre * h)
    common = -2.0 * nu / dr**2 - 30.0 * nu / (12.0 * AXIAL_STEP**2)
    rows[RADIAL_C] = nu / (2.0 * dr * centre)
    rows[THETA_C] = -1.0 / (12.0 * h * centre)
    rows[SECOND_C] = nu / (12.0 * h * h * centre**2)
    rows[CENTRE_Z] = common - 30.0 * rows[SECOND_C]
    rows[CENTRE_T] = rows[CENTRE_Z] - nu / centre**2
    rows[CURVE_T] = 0.25 / centre
    rows[TURN_T] = nu / (h * centre**2)
    rows[RADIAL_F] = nu / (2.0 * dr * face)
    rows[THETA_F] = -0.25 / (12.0 * h * face)
    rows[SECOND_F] = nu / (12.0 * h * h * face**2)
    rows[CENTRE_R] = common - 30.0 * rows[SECOND_F] - nu / face**2
    rows[CURVE_R] = 1.0 / (16.0 * face)
    rows[TURN_R] = -nu / (h * face**2)
    return np.broadcast_to(rows[:, None, :], (COUNT, 8, radial)).astype(np.float32)


def terms(vel, ghost, coef, j, k, dr):
    lane = lax.broadcasted_iota(jnp.int32, (8, 128), 1)
    first_lane = lane == 0
    last_lane = lane == 127

    def at(component, dj, dk):
        return vel[component, j + HALO + dj, pl.ds(k + PAD + dk, 8), :]

    def out(x):
        return pltpu.roll(x, 127, 1)

    def inn(x):
        return pltpu.roll(x, 1, 1)

    nu = VISCOSITY
    lap = nu / dr**2
    adv_z = -1.0 / (12.0 * AXIAL_STEP)
    vis_z = nu / (12.0 * AXIAL_STEP**2)

    def pieces(component):
        p1, m1, p2, m2 = (at(component, d, 0) for d in (1, -1, 2, -2))
        first_t = 8.0 * (p1 - m1) - (p2 - m2)
        second_t = 16.0 * (p1 + m1) - (p2 + m2)
        p1, m1, p2, m2 = (at(component, 0, d) for d in (1, -1, 2, -2))
        first_z = 8.0 * (p1 - m1) - (p2 - m2)
        second_z = 16.0 * (p1 + m1) - (p2 + m2)
        return first_t, second_t, first_z, second_z

    a, b, c = (at(i, 0, 0) for i in range(3))
    a_in = inn(a)
    pair_a = a + a_in
    a_side = at(0, 1, 0)
    pair_side = a_side + inn(a_side)
    a_next = at(0, 0, 1)
    pair_next = a_next + inn(a_next)

    first_t, second_t, first_z, second_z = pieces(2)
    c_out = out(c)
    up = jnp.where(last_lane, -c, c_out)
    low = jnp.where(first_lane, ghost(2), inn(c))
    u_r = pair_a + pair_next
    u_t = (at(1, -1, 0) + b) + (at(1, -1, 1) + at(1, 0, 1))
    h_z = (up - low) * (coef(RADIAL_C) - u_r * (0.125 / dr)) + (up + low) * lap
    h_z = h_z + first_t * (u_t * (0.25 * coef(THETA_C)))
    h_z = h_z + second_t * coef(SECOND_C) + second_z * vis_z
    h_z = h_z + c * (coef(CENTRE_Z) + first_z * adv_z)

    first_t, second_t, first_z, second_z = pieces(1)
    b_out = out(b)
    up = jnp.where(last_lane, -b, b_out)
    low = jnp.where(first_lane, ghost(1), inn(b))
    u_r = pair_a + pair_side
    c_back = at(2, 0, -1)
    u_z = (c_back + c) + (at(2, 1, -1) + at(2, 1, 0))
    h_t = (up - low) * (coef(RADIAL_C) - u_r * (0.125 / dr)) + (up + low) * lap
    h_t = h_t + b * (coef(CENTRE_T) + first_t * coef(THETA_C) - u_r * coef(CURVE_T))
    h_t = h_t + second_t * coef(SECOND_C) + second_z * vis_z
    h_t = h_t + first_z * (u_z * (0.25 * adv_z))
    h_t = h_t + (pair_side - pair_a) * coef(TURN_T)

    first_t, second_t, first_z, second_z = pieces(0)
    up = out(a)
    low = jnp.where(first_lane, ghost(0), a_in)
    b_back = at(1, -1, 0)
    pair_b = b + b_out
    pair_back = b_back + out(b_back)
    u_t = pair_b + pair_back
    u_z = (c + c_out) + (c_back + out(c_back))
    h_r = (up - low) * (coef(RADIAL_F) - a * (0.5 / dr)) + (up + low) * lap
    h_r = h_r + u_t * (u_t * coef(CURVE_R) + first_t * coef(THETA_F))
    h_r = h_r + second_t * coef(SECOND_F) + second_z * vis_z
    h_r = h_r + first_z * (u_z * (0.25 * adv_z)) + a * coef(CENTRE_R)
    h_r = h_r + (pair_b - pair_back) * coef(TURN_R)
    return h_r, h_t, h_z


def theta_edges(v_ref, head_ref, tail_ref):
    count = v_ref.shape[1]
    for n in range(3):
        for q in range(HALO):
            head_ref[n, q] = v_ref[n, q]
            tail_ref[n, q] = v_ref[n, count - HALO + q]


def first_pass(v_ref, coef_ref, vel_ref, low_ref, high_ref, inner_ref, pay_ref):
    _, planes, axial, radial = v_ref.shape
    lane = lax.broadcasted_iota(jnp.int32, (8, radial), 1)
    sign = jnp.where(lane < 2 * planes, -1.0, 1.0).astype(jnp.float32)

    def rows(i, largest):
        k = pl.ds(pl.multiple_of(i * 8, 8), 8)
        padded = pl.ds(pl.multiple_of(i * 8 + PAD, 8), 8)

        def group(g, carry):
            largest, inner = carry
            for q in range(GROUP):
                j = g * GROUP + q
                a, b, c = (v_ref[n, j, k, :] for n in range(3))
                a = a * coef_ref[WALL]
                rate = (
                    jnp.abs(a) * float(radial)
                    + jnp.abs(b) * coef_ref[RATE_T]
                    + jnp.abs(c) * (1.0 / AXIAL_STEP)
                )
                largest = jnp.maximum(largest, rate)
                for n, x in enumerate((a, b, c)):
                    vel_ref[n, j + HALO, padded, :] = x
                    place = n * planes + j
                    inner = jnp.where(lane == place, pltpu.roll(x, place, 1), inner)
            return largest, inner

        zero = jnp.zeros((8, radial), jnp.float32)
        largest, inner = lax.fori_loop(0, planes // GROUP, group, (largest, zero))
        inner_ref[k, :] = inner * sign
        return largest

    largest = lax.fori_loop(0, axial // 8, rows, jnp.zeros((8, radial), jnp.float32))
    top = jnp.max(largest, axis=(0, 1), keepdims=True)
    pay_ref[...] = jnp.broadcast_to(top, pay_ref.shape)
    inner_ref[0:8, :] = jnp.where(lane == radial - 1, top, inner_ref[0:8, :])

    def ends(j, carry):
        for n in range(3):
            low_ref[n, j] = v_ref[n, j, 0:2, :]
            high_ref[n, j] = v_ref[n, j, axial - 2 : axial, :]
        return carry

    lax.fori_loop(0, planes, ends, 0)
    last = lax.broadcasted_iota(jnp.int32, (2, radial), 1) == radial - 1
    for ref in (low_ref, high_ref):
        ref[0, 0] = jnp.where(last, top, ref[0, 0])


def fold(low_ref, high_ref, inner_ref, pay_ref, coef_ref, vel_in, out_ref, vel_ref):
    del vel_in
    planes, radial = low_ref.shape[1], low_ref.shape[3]
    axial = inner_ref.shape[0]
    top = jnp.maximum(
        jnp.maximum(low_ref[0, 0, 0:1, :], high_ref[0, 0, 0:1, :]), inner_ref[0:1, :]
    )
    lane = lax.broadcasted_iota(jnp.int32, (1, radial), 1)
    top = jnp.max(jnp.where(lane == radial - 1, top, 0.0), axis=(0, 1), keepdims=True)
    out_ref[...] = jnp.maximum(pay_ref[...], top)
    out_ref[1:2, :] = high_ref[1, planes - 1, 0:1, :]
    out_ref[2:3, :] = low_ref[2, 0, 1:2, :]
    wall = coef_ref[WALL, 0:2, :]

    def plane(j, carry):
        for n in range(3):
            mask = wall if n == 0 else 1.0
            vel_ref[n, j + HALO, PAD - 2 : PAD, :] = low_ref[n, j] * mask
            vel_ref[n, j + HALO, PAD + axial : PAD + axial + 2, :] = high_ref[n, j] * mask
        return carry

    lax.fori_loop(0, planes, plane, 0)


def sweep(vel_ref, inner_ref, coef_ref, first, last, write):
    axial, radial = inner_ref.shape
    planes = vel_ref.shape[1] - 2 * HALO

    def plane(j, carry):
        def rows(i, carry):
            k = pl.multiple_of(i * 8, 8)
            inner = inner_ref[pl.ds(k, 8), :]

            def ghost(component):
                turn = lax.rem(2 * radial - component * planes - j, radial)
                return pltpu.roll(inner, turn, 1)

            found = terms(vel_ref, ghost, lambda n: coef_ref[n], j, k, 1.0 / radial)
            for n, value in enumerate(found):
                write(n, j, pl.ds(k, 8), value)
            return carry

        return lax.fori_loop(0, axial // 8, rows, carry, unroll=UNROLL)

    lax.fori_loop(first, last, plane, 0)


def interior(first, last, vel_ref, inner_ref, coef_ref, _, out_ref):
    def write(n, j, k, value):
        out_ref[n, j - first, k, :] = value

    sweep(vel_ref, inner_ref, coef_ref, first, last, write)


def finish(
    spans,
    below_ref,
    above_ref,
    up_ref,
    down_ref,
    pay_ref,
    far_ref,
    inner_ref,
    coef_ref,
    *refs,
):
    parts, (vel_in, out_ref, step_ref, vel_ref, res, sems) = refs[: len(spans)], refs[len(spans) :]
    del vel_in
    axial, radial = inner_ref.shape
    planes = res.shape[1]
    largest = jnp.max(jnp.maximum(pay_ref[0:1, :], far_ref[0:1, :]))
    time_step = CFL_TARGET / (largest + 1e-06)
    step_ref[0] = time_step
    scale = GAMMA * time_step

    def store(first, last, n):
        part = pl.ds(first, last - first)
        return pltpu.make_async_copy(res.at[:, part], out_ref.at[:, part], sems.at[n])

    def write(n, j, k, value):
        factor = scale * coef_ref[WALL] if n == 0 else scale
        res[n, j, k, :] = value * factor

    pending = []
    for part, (first, last) in zip(parts, spans):

        def plane(j, carry, part=part, first=first):
            def rows(i, carry):
                k = pl.ds(pl.multiple_of(i * 8, 8), 8)
                for n in range(3):
                    write(n, j, k, part[n, j - first, k, :])
                return carry

            return lax.fori_loop(0, axial // 8, rows, carry, unroll=UNROLL)

        lax.fori_loop(first, last, plane, 0)
        pending.append(store(first, last, len(pending)))
        pending[-1].start()

    cells = pl.ds(PAD, axial)
    for q in range(HALO):
        for ref, place in ((below_ref, q), (above_ref, HALO + planes + q)):
            vel_ref[0, place, cells, :] = ref[0, q] * coef_ref[WALL, 0:1, :]
            vel_ref[1, place, cells, :] = ref[1, q]
            vel_ref[2, place, cells, :] = ref[2, q]
    vel_ref[1, HALO - 1, PAD + axial : PAD + axial + 1, :] = up_ref[1:2, :]
    vel_ref[2, HALO + planes, PAD - 1 : PAD, :] = down_ref[2:3, :]
    for first in (0, planes - HALO):
        sweep(vel_ref, inner_ref, coef_ref, first, first + HALO, write)
        pending.append(store(first, first + HALO, len(pending)))
        pending[-1].start()
    for copy in pending:
        copy.wait()


def shifted(block, distance):
    sizes = lax.axis_size("az"), lax.axis_size("ax")
    route = []
    for i in range(sizes[0]):
        for k in range(sizes[1]):
            source = (i - distance[0]) % sizes[0], (k - distance[1]) % sizes[1]
            route.append((source[0] * sizes[1] + source[1], i * sizes[1] + k))
    return lax.ppermute(block, ("az", "ax"), route)


def rounds(sizes, covered):
    plan = []
    shifts = [(i, k) for i in range(sizes[0]) for k in range(sizes[1])]

    def moved(cells, by):
        return {((i + by[0]) % sizes[0], (k + by[1]) % sizes[1]) for i, k in cells}

    def hops(by):
        return min(by[0], sizes[0] - by[0]) + min(by[1], sizes[1] - by[1])

    while len(covered) < sizes[0] * sizes[1]:
        best = max(shifts, key=lambda by: (len(covered | moved(covered, by)), -hops(by)))
        covered = covered | moved(covered, best)
        plan.append(best)
    return plan


def per_device(velocity):
    _, planes, axial, radial = velocity.shape
    sizes = lax.axis_size("az"), lax.axis_size("ax")
    theta_step = 2.0 * math.pi / (sizes[0] * planes)
    coef = jnp.asarray(coefficients(radial, theta_step))
    f32 = jnp.float32
    anywhere = pl.BlockSpec(memory_space=pl.ANY)
    vmem = pl.BlockSpec(memory_space=pltpu.VMEM)
    smem = pl.BlockSpec(memory_space=pltpu.SMEM)

    def shape(*sizes):
        return jax.ShapeDtypeStruct(sizes, f32)

    def call(kernel, name, work, scratch=0, **kwargs):
        return pl.pallas_call(
            kernel,
            name=name,
            compiler_params=pltpu.CompilerParams(vmem_limit_bytes=(4 + scratch) * 2**20),
            cost_estimate=pl.CostEstimate(
                flops=work, bytes_accessed=velocity.size * 4, transcendentals=0
            ),
            **kwargs,
        )

    pair = shape(3, HALO, axial, radial)
    head, tail = call(
        theta_edges,
        "theta_edges",
        0,
        out_shape=(pair, pair),
        in_specs=[vmem],
        out_specs=(vmem, vmem),
    )(velocity)
    below = shifted(tail, (1, 0))
    above = shifted(head, (-1, 0))

    edge = shape(3, planes, 2, radial)
    padded = shape(3, planes + 2 * HALO, axial + 2 * PAD, radial)
    vel, first, last, inner, pay = call(
        first_pass,
        "first_pass",
        10 * velocity.size,
        out_shape=(padded, edge, edge, shape(axial, radial), shape(8, radial)),
        in_specs=[vmem, vmem],
        out_specs=(vmem,) * 5,
    )(velocity, coef)
    low = shifted(last, (0, 1))
    high = shifted(first, (0, -1))
    inner = shifted(inner, (sizes[0] // 2, 0))
    pay, vel = call(
        fold,
        "fold",
        velocity.size // planes,
        out_shape=(shape(8, radial), padded),
        in_specs=[vmem] * 6,
        out_specs=(vmem, vmem),
        input_output_aliases={5: 1},
    )(low, high, inner, pay, coef, vel)
    up = shifted(pay, (1, 0))
    down = shifted(pay, (-1, 0))

    known = {(0, 0), (0, 1), (0, sizes[1] - 1), (sizes[0] // 2, 0)}
    known = {((i + d) % sizes[0], k) for i, k in known for d in (-1, 0, 1)}
    plan = rounds(sizes, known)
    count = len(plan) + 1
    bounds = [
        HALO + (planes - 2 * HALO) * n // count for n in range(count + 1)
    ]
    spans = list(zip(bounds[:-1], bounds[1:]))
    parts = []
    token = pay
    for n, (first, last) in enumerate(spans):
        parts.append(
            call(
                functools.partial(interior, first, last),
                f"interior_{n}",
                400 * (last - first) * axial * radial,
                out_shape=shape(3, last - first, axial, radial),
                in_specs=[vmem] * 4,
                out_specs=vmem,
            )(vel, inner, coef, token)
        )
        if n == 0:
            pay = jnp.maximum(pay, jnp.maximum(up, down))
            token = up
        else:
            pay = jnp.maximum(pay, far)
            token = far
        if n < len(plan):
            far = shifted(pay, plan[n])
    increment, time_step, _ = call(
        functools.partial(finish, spans),
        "finish",
        160 * velocity.size,
        scratch=8,
        out_shape=(shape(*velocity.shape), shape(1), padded),
        in_specs=[vmem] * (9 + len(parts)),
        out_specs=(anywhere, smem, vmem),
        scratch_shapes=[
            pltpu.VMEM(velocity.shape, f32),
            pltpu.SemaphoreType.DMA((len(parts) + 2,)),
        ],
        input_output_aliases={8 + len(parts): 2},
    )(below, above, up, down, pay, far, inner, coef, *parts, vel)
    return increment, time_step.reshape(())


def solution(mesh):
    return jax.shard_map(
        per_device,
        mesh=mesh,
        in_specs=(P(None, "az", "ax", None),),
        out_specs=(P(None, "az", "ax", None), P()),
        check_vma=False,
    )
```

```python
import functools
import math

import jax
import jax.numpy as jnp
import numpy as np
from jax import lax
from jax.experimental import pallas as pl
from jax.experimental.pallas import tpu as pltpu
from jax.sharding import PartitionSpec as P

AXIAL_STEP = 0.01
VISCOSITY = 0.001
CFL_TARGET = 1.2
GAMMA = 8.0 / 15.0

PAD = 8
HALO = 2
UNROLL = 4

(
    WALL,
    RATE_T,
    RADIAL_C,
    THETA_C,
    CROSS_Z,
    SECOND_C,
    CENTRE_Z,
    CENTRE_T,
    CURVE_T,
    TURN_T,
    RADIAL_F,
    THETA_F,
    SECOND_F,
    CENTRE_R,
    CURVE_R,
    TURN_R,
    COUNT,
) = range(17)


def coefficients(radial, theta_step):
    dr = 1.0 / radial
    index = np.arange(radial, dtype=np.float64)
    centre = (index + 0.5) * dr
    face = (index + 1.0) * dr
    wall = np.where(index < radial - 1.5, 1.0, 0.0)
    h = theta_step
    nu = VISCOSITY
    rows = np.zeros((COUNT, radial))
    rows[WALL] = wall
    rows[RATE_T] = 1.0 / (centre * h)
    common = -2.0 * nu / dr**2 - 30.0 * nu / (12.0 * AXIAL_STEP**2)
    rows[RADIAL_C] = nu / (2.0 * dr * centre)
    rows[THETA_C] = -1.0 / (12.0 * h * centre)
    rows[CROSS_Z] = 0.25 * rows[THETA_C]
    rows[SECOND_C] = nu / (12.0 * h * h * centre**2)
    rows[CENTRE_Z] = common - 30.0 * rows[SECOND_C]
    rows[CENTRE_T] = rows[CENTRE_Z] - nu / centre**2
    rows[CURVE_T] = 0.25 / centre
    rows[TURN_T] = nu / (h * centre**2)
    rows[RADIAL_F] = nu / (2.0 * dr * face)
    rows[THETA_F] = -0.25 / (12.0 * h * face)
    rows[SECOND_F] = nu / (12.0 * h * h * face**2)
    rows[CENTRE_R] = common - 30.0 * rows[SECOND_F] - nu / face**2
    rows[CURVE_R] = 1.0 / (16.0 * face)
    rows[TURN_R] = -nu / (h * face**2)
    return np.broadcast_to(rows[:, None, :], (COUNT, 8, radial)).astype(np.float32)


def terms(vel, ghost, coef, j, k, dr):
    lane = lax.broadcasted_iota(jnp.int32, (8, 128), 1)
    first_lane = lane == 0
    last_lane = lane == 127

    def at(component, dj, dk):
        return vel[component, j + HALO + dj, pl.ds(k + PAD + dk, 8), :]

    def out(x):
        return pltpu.roll(x, 127, 1)

    def inn(x):
        return pltpu.roll(x, 1, 1)

    nu = VISCOSITY
    lap = nu / dr**2
    adv_z = -1.0 / (12.0 * AXIAL_STEP)
    vis_z = nu / (12.0 * AXIAL_STEP**2)

    def differences(p1, m1, p2, m2):
        return 8.0 * (p1 - m1) - (p2 - m2), 16.0 * (p1 + m1) - (p2 + m2)

    def pieces(n):
        over = [at(n, d, 0) for d in (1, -1, 2, -2)]
        along = [at(n, 0, d) for d in (1, -1, 2, -2)]
        return over, along, differences(*over), differences(*along)

    a, b, c = (at(n, 0, 0) for n in range(3))
    (a_side, *_), (a_next, *_), a_theta, a_axial = pieces(0)
    (_, b_back, *_), (b_next, *_), b_theta, b_axial = pieces(1)
    (c_side, *_), (_, c_back, *_), c_theta, c_axial = pieces(2)
    a_in = inn(a)
    pair_a = a + a_in
    pair_side = a_side + inn(a_side)
    pair_next = a_next + inn(a_next)

    c_out = out(c)
    up = jnp.where(last_lane, -c, c_out)
    low = jnp.where(first_lane, ghost(2), inn(c))
    u_r = pair_a + pair_next
    u_t = (b_back + b) + (at(1, -1, 1) + b_next)
    h_z = (up - low) * (coef[RADIAL_C] - u_r * (0.125 / dr)) + (up + low) * lap
    h_z = h_z + c_theta[0] * (u_t * coef[CROSS_Z])
    h_z = h_z + (c_theta[1] * coef[SECOND_C] + c_axial[1] * vis_z)
    h_z = h_z + c * (coef[CENTRE_Z] + c_axial[0] * adv_z)

    b_out = out(b)
    up = jnp.where(last_lane, -b, b_out)
    low = jnp.where(first_lane, ghost(1), inn(b))
    u_r = pair_a + pair_side
    u_z = (c_back + c) + (at(2, 1, -1) + c_side)
    h_t = (up - low) * (coef[RADIAL_C] - u_r * (0.125 / dr)) + (up + low) * lap
    h_t = h_t + b * (coef[CENTRE_T] + b_theta[0] * coef[THETA_C] - u_r * coef[CURVE_T])
    h_t = h_t + (b_theta[1] * coef[SECOND_C] + b_axial[1] * vis_z)
    h_t = h_t + b_axial[0] * (u_z * (0.25 * adv_z))
    h_t = h_t + (pair_side - pair_a) * coef[TURN_T]

    up = out(a)
    low = jnp.where(first_lane, ghost(0), a_in)
    pair_b = b + b_out
    pair_back = b_back + out(b_back)
    u_t = pair_b + pair_back
    u_z = (c + c_out) + (c_back + out(c_back))
    h_r = (up - low) * (coef[RADIAL_F] - a * (0.5 / dr)) + (up + low) * lap
    h_r = h_r + u_t * (u_t * coef[CURVE_R] + a_theta[0] * coef[THETA_F])
    h_r = h_r + (a_theta[1] * coef[SECOND_F] + a_axial[1] * vis_z)
    h_r = h_r + (a_axial[0] * (u_z * (0.25 * adv_z)) + a * coef[CENTRE_R])
    h_r = h_r + (pair_b - pair_back) * coef[TURN_R]
    return h_r, h_t, h_z


def first_pass(
    v_ref, coef_ref, vel_ref, head_ref, tail_ref, low_ref, high_ref, inner_ref, pay_ref
):
    _, planes, axial, radial = v_ref.shape
    lane = lax.broadcasted_iota(jnp.int32, (8, radial), 1)
    sign = jnp.where(lane < 2 * planes, -1.0, 1.0).astype(jnp.float32)

    def rows(i, largest):
        k = pl.ds(pl.multiple_of(i * 8, 8), 8)
        padded = pl.ds(pl.multiple_of(i * 8 + PAD, 8), 8)
        wall, rate_t = coef_ref[WALL], coef_ref[RATE_T]
        inner = [jnp.zeros((8, radial), jnp.float32)] * 3
        for j in range(planes):
            a, b, c = cells = [v_ref[n, j, k, :] for n in range(3)]
            a = a * wall
            rate = jnp.abs(a) * float(radial) + jnp.abs(b) * rate_t
            largest = jnp.maximum(largest, rate + jnp.abs(c) * (1.0 / AXIAL_STEP))
            for n, x in enumerate(cells):
                vel_ref[n, j + HALO, padded, :] = a if n == 0 else x
                place = n * planes + j
                inner[n] = jnp.where(lane == place, pltpu.roll(x, place, 1), inner[n])
                if j < HALO:
                    head_ref[n, j, k, :] = x
                if j >= planes - HALO:
                    tail_ref[n, j - planes + HALO, k, :] = x
        inner_ref[k, :] = (inner[0] + inner[1] + inner[2]) * sign
        return largest

    largest = lax.fori_loop(0, axial // 8, rows, jnp.zeros((8, radial), jnp.float32))
    top = jnp.max(largest, axis=(0, 1), keepdims=True)
    pay_ref[...] = jnp.broadcast_to(top, pay_ref.shape)
    inner_ref[0:8, :] = jnp.where(lane == radial - 1, top, inner_ref[0:8, :])

    def ends(j, carry):
        for n in range(3):
            low_ref[n, j] = v_ref[n, j, 0:2, :]
            high_ref[n, j] = v_ref[n, j, axial - 2 : axial, :]
        return carry

    lax.fori_loop(0, planes, ends, 0, unroll=8)
    last = lax.broadcasted_iota(jnp.int32, (2, radial), 1) == radial - 1
    for ref in (low_ref, high_ref):
        ref[0, 0] = jnp.where(last, top, ref[0, 0])


def fold(low_ref, high_ref, inner_ref, pay_ref, coef_ref, vel_in, out_ref, vel_ref):
    del vel_in
    planes, radial = low_ref.shape[1], low_ref.shape[3]
    axial = inner_ref.shape[0]
    top = jnp.maximum(
        jnp.maximum(low_ref[0, 0, 0:1, :], high_ref[0, 0, 0:1, :]), inner_ref[0:1, :]
    )
    lane = lax.broadcasted_iota(jnp.int32, (1, radial), 1)
    top = jnp.max(jnp.where(lane == radial - 1, top, 0.0), axis=(0, 1), keepdims=True)
    out_ref[...] = jnp.maximum(pay_ref[...], top)
    out_ref[1:2, :] = high_ref[1, planes - 1, 0:1, :]
    out_ref[2:3, :] = low_ref[2, 0, 1:2, :]
    wall = coef_ref[WALL, 0:2, :]

    def plane(j, carry):
        for n in range(3):
            mask = wall if n == 0 else 1.0
            vel_ref[n, j + HALO, PAD - 2 : PAD, :] = low_ref[n, j] * mask
            vel_ref[n, j + HALO, PAD + axial : PAD + axial + 2, :] = high_ref[n, j] * mask
        return carry

    lax.fori_loop(0, planes, plane, 0)


def sweep(vel_ref, inner_ref, coef_ref, first, last, write, beside=None, after=None):
    axial, radial = inner_ref.shape
    planes = vel_ref.shape[1] - 2 * HALO

    def plane(j, carry):
        def rows(i, carry):
            coef = [coef_ref[n] for n in range(COUNT)]
            found = []
            for u in range(UNROLL):
                k = pl.multiple_of((i * UNROLL + u) * 8, 8)
                inner = inner_ref[pl.ds(k, 8), :]

                def ghost(component):
                    turn = lax.rem(2 * radial - component * planes - j, radial)
                    return pltpu.roll(inner, turn, 1)

                found.append((k, terms(vel_ref, ghost, coef, j, k, 1.0 / radial)))
            for k, values in found:
                for n, value in enumerate(values):
                    write(n, j, pl.ds(k, 8), value)
                if beside is not None:
                    beside(j, pl.ds(k, 8))
            return carry

        lax.fori_loop(0, axial // (8 * UNROLL), rows, 0)
        if after is not None:
            after(j)
        return carry

    lax.fori_loop(first, last, plane, 0)


def interior(first, last, vel_ref, inner_ref, coef_ref, _, out_ref):
    def write(n, j, k, value):
        out_ref[n, j - first, k, :] = value

    sweep(vel_ref, inner_ref, coef_ref, first, last, write)


def finish(
    spans,
    below_ref,
    above_ref,
    up_ref,
    down_ref,
    pay_ref,
    far_ref,
    inner_ref,
    coef_ref,
    *refs,
):
    parts, (vel_in, out_ref, step_ref, vel_ref, res, sems) = refs[:-6], refs[-6:]
    del vel_in
    axial, radial = inner_ref.shape
    planes = res.shape[1]
    largest = jnp.max(jnp.maximum(pay_ref[0:1, :], far_ref[0:1, :]))
    time_step = CFL_TARGET / (largest + 1e-06)
    step_ref[0] = time_step
    scale = GAMMA * time_step

    def store(j):
        return pltpu.make_async_copy(res.at[:, j], out_ref.at[:, j], sems.at[j])

    def write(n, j, k, value):
        factor = scale * coef_ref[WALL] if n == 0 else scale
        res[n, j, k, :] = value * factor

    (start, stop), others = spans[-1], spans[:-1]

    def beside(j, k):
        for part, (first, _) in zip(parts, others):
            for n in range(3):
                write(n, first + j - start, k, part[n, j - start, k, :])

    def after(j):
        store(j).start()
        for first, _ in others:
            store(first + j - start).start()

    sweep(vel_ref, inner_ref, coef_ref, start, stop, write, beside, after)

    cells = pl.ds(PAD, axial)
    for q in range(HALO):
        for ref, place in ((below_ref, q), (above_ref, HALO + planes + q)):
            vel_ref[0, place, cells, :] = ref[0, q] * coef_ref[WALL, 0:1, :]
            vel_ref[1, place, cells, :] = ref[1, q]
            vel_ref[2, place, cells, :] = ref[2, q]
    vel_ref[1, HALO - 1, PAD + axial : PAD + axial + 1, :] = up_ref[1:2, :]
    vel_ref[2, HALO + planes, PAD - 1 : PAD, :] = down_ref[2:3, :]
    for first in (0, planes - HALO):
        sweep(
            vel_ref,
            inner_ref,
            coef_ref,
            first,
            first + HALO,
            write,
            after=lambda j: store(j).start(),
        )

    def wait(j, carry):
        store(j).wait()
        return carry

    lax.fori_loop(0, planes, wait, 0)


def shifted(block, distance):
    sizes = lax.axis_size("az"), lax.axis_size("ax")
    route = []
    for i in range(sizes[0]):
        for k in range(sizes[1]):
            source = (i - distance[0]) % sizes[0], (k - distance[1]) % sizes[1]
            route.append((source[0] * sizes[1] + source[1], i * sizes[1] + k))
    return lax.ppermute(block, ("az", "ax"), route)


def rounds(sizes, covered):
    plan = []
    shifts = [(i, k) for i in range(sizes[0]) for k in range(sizes[1])]

    def moved(cells, by):
        return {((i + by[0]) % sizes[0], (k + by[1]) % sizes[1]) for i, k in cells}

    def hops(by):
        return min(by[0], sizes[0] - by[0]) + min(by[1], sizes[1] - by[1])

    while len(covered) < sizes[0] * sizes[1]:
        best = max(shifts, key=lambda by: (len(covered | moved(covered, by)), -hops(by)))
        covered = covered | moved(covered, best)
        plan.append(best)
    return plan


def per_device(velocity):
    _, planes, axial, radial = velocity.shape
    sizes = lax.axis_size("az"), lax.axis_size("ax")
    theta_step = 2.0 * math.pi / (sizes[0] * planes)
    coef = jnp.asarray(coefficients(radial, theta_step))
    f32 = jnp.float32
    anywhere = pl.BlockSpec(memory_space=pl.ANY)
    vmem = pl.BlockSpec(memory_space=pltpu.VMEM)
    smem = pl.BlockSpec(memory_space=pltpu.SMEM)

    def shape(*sizes):
        return jax.ShapeDtypeStruct(sizes, f32)

    def call(kernel, name, work, scratch=0, **kwargs):
        return pl.pallas_call(
            kernel,
            name=name,
            compiler_params=pltpu.CompilerParams(vmem_limit_bytes=(4 + scratch) * 2**20),
            cost_estimate=pl.CostEstimate(
                flops=work, bytes_accessed=velocity.size * 4, transcendentals=0
            ),
            **kwargs,
        )

    pair = shape(3, HALO, axial, radial)
    edge = shape(3, planes, 2, radial)
    padded = shape(3, planes + 2 * HALO, axial + 2 * PAD, radial)
    vel, head, tail, first, last, inner, pay = call(
        first_pass,
        "first_pass",
        10 * velocity.size,
        out_shape=(padded, pair, pair, edge, edge, shape(axial, radial), shape(8, radial)),
        in_specs=[vmem, vmem],
        out_specs=(vmem,) * 7,
    )(velocity, coef)
    low = shifted(last, (0, 1))
    high = shifted(first, (0, -1))
    inner = shifted(inner, (sizes[0] // 2, 0))
    below = shifted(tail, (1, 0))
    above = shifted(head, (-1, 0))
    pay, vel = call(
        fold,
        "fold",
        velocity.size // planes,
        out_shape=(shape(8, radial), padded),
        in_specs=[vmem] * 6,
        out_specs=(vmem, vmem),
        input_output_aliases={5: 1},
    )(low, high, inner, pay, coef, vel)
    up = shifted(pay, (1, 0))
    down = shifted(pay, (-1, 0))

    known = {(0, 0), (0, 1), (0, sizes[1] - 1), (sizes[0] // 2, 0)}
    known = {((i + d) % sizes[0], k) for i, k in known for d in (-1, 0, 1)}
    plan = rounds(sizes, known)
    inside = planes - 2 * HALO
    count = len(plan) + 2
    while inside % count:
        count += 1
    bounds = range(HALO, planes - HALO + 1, inside // count)
    spans = list(zip(bounds[:-1], bounds[1:]))
    parts = []
    token = pay
    for n, (first, last) in enumerate(spans[:-1]):
        parts.append(
            call(
                functools.partial(interior, first, last),
                f"interior_{n}",
                400 * (last - first) * axial * radial,
                out_shape=shape(3, last - first, axial, radial),
                in_specs=[vmem] * 4,
                out_specs=vmem,
            )(vel, inner, coef, token)
        )
        if n == 0:
            pay = jnp.maximum(pay, jnp.maximum(up, down))
            token = up
        elif n <= len(plan):
            token = far
        if n < len(plan):
            pay = pay if n == 0 else jnp.maximum(pay, far)
            far = shifted(pay, plan[n])
    increment, time_step, _ = call(
        functools.partial(finish, spans),
        "finish",
        160 * velocity.size,
        scratch=8,
        out_shape=(shape(*velocity.shape), shape(1), padded),
        in_specs=[vmem] * (9 + len(parts)),
        out_specs=(anywhere, smem, vmem),
        scratch_shapes=[
            pltpu.VMEM(velocity.shape, f32),
            pltpu.SemaphoreType.DMA((planes,)),
        ],
        input_output_aliases={8 + len(parts): 2},
    )(below, above, up, down, pay, far, inner, coef, *parts, vel)
    return increment, time_step.reshape(())


def solution(mesh):
    return jax.shard_map(
        per_device,
        mesh=mesh,
        in_specs=(P(None, "az", "ax", None),),
        out_specs=(P(None, "az", "ax", None), P()),
        check_vma=False,
    )
```

```python
import functools
import math

import jax
import jax.numpy as jnp
import numpy as np
from jax import lax
from jax.experimental import pallas as pl
from jax.experimental.pallas import tpu as pltpu
from jax.sharding import PartitionSpec as P

AXIAL_STEP = 0.01
VISCOSITY = 0.001
CFL_TARGET = 1.2
GAMMA = 8.0 / 15.0

PAD = 8
HALO = 2
UNROLL = 4

(
    WALL,
    RADIAL_C,
    THETA_C,
    CROSS_Z,
    SECOND_C,
    CENTRE_Z,
    CENTRE_T,
    CURVE_T,
    TURN_T,
    RADIAL_F,
    THETA_F,
    SECOND_F,
    CENTRE_R,
    CURVE_R,
    TURN_R,
    COUNT,
) = range(16)


def coefficients(radial, theta_step):
    dr = 1.0 / radial
    index = np.arange(radial, dtype=np.float64)
    centre = (index + 0.5) * dr
    face = (index + 1.0) * dr
    wall = np.where(index < radial - 1.5, 1.0, 0.0)
    h = theta_step
    nu = VISCOSITY
    rows = np.zeros((COUNT, radial))
    rows[WALL] = wall
    common = -2.0 * nu / dr**2 - 30.0 * nu / (12.0 * AXIAL_STEP**2)
    rows[RADIAL_C] = nu / (2.0 * dr * centre)
    rows[THETA_C] = -1.0 / (12.0 * h * centre)
    rows[CROSS_Z] = 0.25 * rows[THETA_C]
    rows[SECOND_C] = nu / (12.0 * h * h * centre**2)
    rows[CENTRE_Z] = common - 30.0 * rows[SECOND_C]
    rows[CENTRE_T] = rows[CENTRE_Z] - nu / centre**2
    rows[CURVE_T] = 0.25 / centre
    rows[TURN_T] = nu / (h * centre**2)
    rows[RADIAL_F] = nu / (2.0 * dr * face)
    rows[THETA_F] = -0.25 / (12.0 * h * face)
    rows[SECOND_F] = nu / (12.0 * h * h * face**2)
    rows[CENTRE_R] = common - 30.0 * rows[SECOND_F] - nu / face**2
    rows[CURVE_R] = 1.0 / (16.0 * face)
    rows[TURN_R] = -nu / (h * face**2)
    return np.broadcast_to(rows[:, None, :], (COUNT, 8, radial)).astype(np.float32)


def turned_in(x):
    return pltpu.roll(x, 1, 1)


def turned_out(x):
    return pltpu.roll(x, x.shape[1] - 1, 1)


def terms(vel, kept, ghost, coef, j, k, dr):
    a_in, a_in_side, a_in_next, b_out, b_out_back, c_out, c_out_back = kept
    lane = lax.broadcasted_iota(jnp.int32, a_in.shape, 1)
    first_lane = lane == 0
    last_lane = lane == a_in.shape[1] - 1

    def at(component, dj, dk):
        return vel[component, j + HALO + dj, pl.ds(k + PAD + dk, 8), :]

    nu = VISCOSITY
    lap = nu / dr**2
    adv_z = -1.0 / (12.0 * AXIAL_STEP)
    vis_z = nu / (12.0 * AXIAL_STEP**2)

    def differences(p1, m1, p2, m2):
        return 8.0 * (p1 - m1) - (p2 - m2), 16.0 * (p1 + m1) - (p2 + m2)

    def pieces(n):
        over = [at(n, d, 0) for d in (1, -1, 2, -2)]
        along = [at(n, 0, d) for d in (1, -1, 2, -2)]
        return over, along, differences(*over), differences(*along)

    def below(n, x):
        if ghost is not None:
            return jnp.where(first_lane, ghost(n), x)
        return x if n == 0 else jnp.where(first_lane, 0.0, x)

    a, b, c = (at(n, 0, 0) for n in range(3))
    (a_side, *_), (a_next, *_), a_theta, a_axial = pieces(0)
    (_, b_back, *_), (b_next, *_), b_theta, b_axial = pieces(1)
    (c_side, *_), (_, c_back, *_), c_theta, c_axial = pieces(2)
    pair_a = a + a_in
    pair_side = a_side + a_in_side
    pair_next = a_next + a_in_next

    up = jnp.where(last_lane, -c, c_out)
    low = below(2, turned_in(c))
    u_r = pair_a + pair_next
    u_t = (b_back + b) + (at(1, -1, 1) + b_next)
    h_z = (up - low) * (coef[RADIAL_C] - u_r * (0.125 / dr)) + (up + low) * lap
    h_z = h_z + c_theta[0] * (u_t * coef[CROSS_Z])
    h_z = h_z + (c_theta[1] * coef[SECOND_C] + c_axial[1] * vis_z)
    h_z = h_z + c * (coef[CENTRE_Z] + c_axial[0] * adv_z)

    up = jnp.where(last_lane, -b, b_out)
    low = below(1, turned_in(b))
    u_r = pair_a + pair_side
    u_z = (c_back + c) + (at(2, 1, -1) + c_side)
    h_t = (up - low) * (coef[RADIAL_C] - u_r * (0.125 / dr)) + (up + low) * lap
    h_t = h_t + b * (coef[CENTRE_T] + b_theta[0] * coef[THETA_C] - u_r * coef[CURVE_T])
    h_t = h_t + (b_theta[1] * coef[SECOND_C] + b_axial[1] * vis_z)
    h_t = h_t + b_axial[0] * (u_z * (0.25 * adv_z))
    h_t = h_t + (pair_side - pair_a) * coef[TURN_T]

    up = turned_out(a)
    low = below(0, a_in)
    pair_b = b + b_out
    pair_back = b_back + b_out_back
    u_t = pair_b + pair_back
    u_z = (c + c_out) + (c_back + c_out_back)
    h_r = (up - low) * (coef[RADIAL_F] - a * (0.5 / dr)) + (up + low) * lap
    h_r = h_r + u_t * (u_t * coef[CURVE_R] + a_theta[0] * coef[THETA_F])
    h_r = h_r + (a_theta[1] * coef[SECOND_F] + a_axial[1] * vis_z)
    h_r = h_r + (a_axial[0] * (u_z * (0.25 * adv_z)) + a * coef[CENTRE_R])
    h_r = h_r + (pair_b - pair_back) * coef[TURN_R]
    return h_r, h_t, h_z


def lane_zero_terms(vel, ghost, coef, j, k, dr):
    def at(dj, dk):
        return vel[0, j + HALO + dj, pl.ds(k + PAD + dk, 8), :]

    lap = VISCOSITY / dr**2
    a = at(0, 0)
    first_lane = lax.broadcasted_iota(jnp.int32, a.shape, 1) == 0
    add_r = ghost(0) * (lap - coef[RADIAL_F] + a * (0.5 / dr))
    add_t = ghost(1) * (lap - coef[RADIAL_C] + (a + at(1, 0)) * (0.125 / dr))
    add_z = ghost(2) * (lap - coef[RADIAL_C] + (a + at(0, 1)) * (0.125 / dr))
    return tuple(jnp.where(first_lane, x, 0.0) for x in (add_r, add_t, add_z))


def theta_edges(v_ref, head_ref, tail_ref):
    count = v_ref.shape[1]
    for n in range(3):
        for q in range(HALO):
            head_ref[n, q] = v_ref[n, q]
            tail_ref[n, q] = v_ref[n, count - HALO + q]


def wall_mask(rows, radial):
    lane = lax.broadcasted_iota(jnp.int32, (rows, radial), 1)
    return jnp.where(lane == radial - 1, 0.0, 1.0).astype(jnp.float32)


def first_pass(theta_step, v_ref, _, vel_ref, low_ref, high_ref, inner_ref, pay_ref):
    _, planes, axial, radial = v_ref.shape
    lane = lax.broadcasted_iota(jnp.int32, (8, radial), 1)
    sign = jnp.where(lane < 2 * planes, -1.0, 1.0).astype(jnp.float32)
    wall = wall_mask(8, radial)
    rate_t = (radial / theta_step) / (lane.astype(jnp.float32) + 0.5)

    def rows(i, largest):
        k = pl.ds(pl.multiple_of(i * 8, 8), 8)
        padded = pl.ds(pl.multiple_of(i * 8 + PAD, 8), 8)
        inner = [jnp.zeros((8, radial), jnp.float32)] * 3
        for j in range(planes):
            a, b, c = cells = [v_ref[n, j, k, :] for n in range(3)]
            a = a * wall
            rate = jnp.abs(a) * float(radial) + jnp.abs(b) * rate_t
            largest = jnp.maximum(largest, rate + jnp.abs(c) * (1.0 / AXIAL_STEP))
            for n, x in enumerate(cells):
                vel_ref[n, j + HALO, padded, :] = a if n == 0 else x
                place = n * planes + j
                inner[n] = jnp.where(lane == place, pltpu.roll(x, place, 1), inner[n])
        inner_ref[k, :] = (inner[0] + inner[1] + inner[2]) * sign
        return largest

    largest = lax.fori_loop(0, axial // 8, rows, jnp.zeros((8, radial), jnp.float32))
    top = jnp.max(largest, axis=(0, 1), keepdims=True)
    pay_ref[...] = jnp.broadcast_to(top, pay_ref.shape)
    pay_ref[1:2, :] = v_ref[1, planes - 1, 0:1, :]
    pay_ref[2:3, :] = v_ref[2, 0, axial - 1 : axial, :]

    def ends(j, carry):
        for n in range(3):
            low_ref[n, j] = v_ref[n, j, 0:2, :]
            high_ref[n, j] = v_ref[n, j, axial - 2 : axial, :]
        return carry

    lax.fori_loop(0, planes, ends, 0, unroll=8)
    last = lax.broadcasted_iota(jnp.int32, (2, radial), 1) == radial - 1
    for ref in (low_ref, high_ref):
        ref[0, 0] = jnp.where(last, top, ref[0, 0])


def fold(low_ref, high_ref, up_ref, down_ref, pay_ref, vel_in, out_ref, vel_ref):
    del vel_in
    planes, radial = low_ref.shape[1], low_ref.shape[3]
    axial = vel_ref.shape[2] - 2 * PAD
    lane = lax.broadcasted_iota(jnp.int32, (1, radial), 1)
    top = jnp.maximum(low_ref[0, 0, 0:1, :], high_ref[0, 0, 0:1, :])
    top = jnp.max(jnp.where(lane == radial - 1, top, 0.0), axis=(0, 1), keepdims=True)
    top = jnp.maximum(top, jnp.maximum(up_ref[0:1, :], down_ref[0:1, :]))
    out_ref[...] = jnp.broadcast_to(jnp.maximum(top, pay_ref[0:1, :]), out_ref.shape)
    wall = wall_mask(2, radial)

    def plane(j, carry):
        for n in range(3):
            mask = wall if n == 0 else 1.0
            vel_ref[n, j + HALO, PAD - 2 : PAD, :] = low_ref[n, j] * mask
            vel_ref[n, j + HALO, PAD + axial : PAD + axial + 2, :] = high_ref[n, j] * mask
        return carry

    lax.fori_loop(0, planes, plane, 0, unroll=4)


def ghosts(inner, planes, j):
    radial = inner.shape[1]

    def ghost(component):
        turn = lax.rem(2 * radial - component * planes - j, radial)
        return pltpu.roll(inner, turn, 1)

    return ghost


def sweep(vel_ref, inner_ref, coef_ref, kept_refs, first, last, write, beside=None, after=None):
    a_kept, b_kept, c_kept = kept_refs
    planes = vel_ref.shape[1] - 2 * HALO
    axial, radial = vel_ref.shape[2] - 2 * PAD, vel_ref.shape[3]

    def padded(n, j, k):
        return vel_ref[n, j + HALO, pl.ds(k + PAD, 8), :]

    def fill(i, carry):
        k = pl.multiple_of(i * 8, 8)
        a_kept[pl.ds(k, 8), :] = turned_in(padded(0, first, k))
        b_kept[pl.ds(k, 8), :] = turned_out(padded(1, first - 1, k))
        return carry

    lax.fori_loop(0, axial // 8, fill, 0, unroll=4)
    a_kept[pl.ds(axial, 8), :] = turned_in(padded(0, first, axial))

    def plane(j, carry):
        c_kept[0:PAD, :] = turned_out(padded(2, j, -PAD))

        def rows(i, carry):
            coef = [coef_ref[n] for n in range(COUNT)]
            ks = [pl.multiple_of((i * UNROLL + u) * 8, 8) for u in range(UNROLL)]
            a_in = [a_kept[pl.ds(k, 8), :] for k in ks]
            a_in_next = [a_kept[pl.ds(k + 1, 8), :] for k in ks]
            b_out_back = [b_kept[pl.ds(k, 8), :] for k in ks]
            a_in_side = [turned_in(padded(0, j + 1, k)) for k in ks]
            b_out = [turned_out(padded(1, j, k)) for k in ks]
            c_out = [turned_out(padded(2, j, k)) for k in ks]
            for u, k in enumerate(ks):
                a_kept[pl.ds(k, 8), :] = a_in_side[u]
                b_kept[pl.ds(k, 8), :] = b_out[u]
                c_kept[pl.ds(k + PAD, 8), :] = c_out[u]
            c_out_back = [c_kept[pl.ds(k + PAD - 1, 8), :] for k in ks]
            kept = zip(a_in, a_in_side, a_in_next, b_out, b_out_back, c_out, c_out_back)
            found = []
            for k, turned in zip(ks, kept):
                ghost = None
                if inner_ref is not None:
                    ghost = ghosts(inner_ref[pl.ds(k, 8), :], planes, j)
                found.append(terms(vel_ref, turned, ghost, coef, j, k, 1.0 / radial))
            for k, values in zip(ks, found):
                for n, value in enumerate(values):
                    write(n, j, pl.ds(k, 8), value)
                if beside is not None:
                    beside(j, k, coef)
            return carry

        lax.fori_loop(0, axial // (8 * UNROLL), rows, 0)
        a_kept[pl.ds(axial, 8), :] = turned_in(padded(0, j + 1, axial))
        if after is not None:
            after(j)
        return carry

    lax.fori_loop(first, last, plane, 0)


def interior(first, last, vel_ref, coef_ref, _, out_ref, zero_ref, *kept_refs):
    zero_ref[...] = jnp.zeros_like(zero_ref)

    def write(n, j, k, value):
        out_ref[n, j - first, k, :] = value

    sweep(vel_ref, None, coef_ref, kept_refs, first, last, write)


def finish(
    spans,
    below_ref,
    above_ref,
    up_ref,
    down_ref,
    pay_ref,
    far_ref,
    inner_ref,
    coef_ref,
    *refs,
):
    parts, refs = refs[: len(spans) - 1], refs[len(spans) - 1 :]
    vel_in, out_ref, step_ref, vel_ref, res, sems, *kept_refs = refs
    del vel_in
    axial, radial = inner_ref.shape
    planes = res.shape[1]
    largest = jnp.max(jnp.maximum(pay_ref[0:1, :], far_ref[0:1, :]))
    time_step = CFL_TARGET / (largest + 1e-06)
    step_ref[0] = time_step
    scale = GAMMA * time_step

    def store(j):
        return pltpu.make_async_copy(res.at[:, j], out_ref.at[:, j], sems.at[j])

    def write(n, j, k, value):
        factor = scale * coef_ref[WALL] if n == 0 else scale
        res[n, j, k, :] = value * factor

    (start, stop), others = spans[-1], spans[:-1]

    def beside(j, k, coef):
        inner = inner_ref[pl.ds(k, 8), :]
        for part, (first, _) in zip(parts, others):
            place = first + j - start
            ghost = ghosts(inner, planes, place)
            added = lane_zero_terms(vel_ref, ghost, coef, place, k, 1.0 / radial)
            for n, value in enumerate(added):
                write(n, place, pl.ds(k, 8), part[n, j - start, pl.ds(k, 8), :] + value)

    def after(j):
        store(j).start()
        for first, _ in others:
            store(first + j - start).start()

    sweep(vel_ref, inner_ref, coef_ref, kept_refs, start, stop, write, beside, after)

    cells = pl.ds(PAD, axial)
    for q in range(HALO):
        for ref, place in ((below_ref, q), (above_ref, HALO + planes + q)):
            vel_ref[0, place, cells, :] = ref[0, q] * coef_ref[WALL, 0:1, :]
            vel_ref[1, place, cells, :] = ref[1, q]
            vel_ref[2, place, cells, :] = ref[2, q]
    vel_ref[1, HALO - 1, PAD + axial : PAD + axial + 1, :] = up_ref[1:2, :]
    vel_ref[2, HALO + planes, PAD - 1 : PAD, :] = down_ref[2:3, :]
    for first in (0, planes - HALO):
        sweep(
            vel_ref,
            inner_ref,
            coef_ref,
            kept_refs,
            first,
            first + HALO,
            write,
            after=lambda j: store(j).start(),
        )

    def wait(j, carry):
        store(j).wait()
        return carry

    lax.fori_loop(0, planes, wait, 0)


def shifted(block, distance):
    sizes = lax.axis_size("az"), lax.axis_size("ax")
    route = []
    for i in range(sizes[0]):
        for k in range(sizes[1]):
            source = (i - distance[0]) % sizes[0], (k - distance[1]) % sizes[1]
            route.append((source[0] * sizes[1] + source[1], i * sizes[1] + k))
    return lax.ppermute(block, ("az", "ax"), route)


def rounds(sizes, covered, beam=16):
    shifts = [(i, k) for i in range(sizes[0]) for k in range(sizes[1])]

    def moved(cells, by):
        return {((i + by[0]) % sizes[0], (k + by[1]) % sizes[1]) for i, k in cells}

    def hops(plan):
        return sum(min(i, sizes[0] - i) + min(k, sizes[1] - k) for i, k in plan)

    found = [(frozenset(covered), ())]
    while len(found[0][0]) < len(shifts):
        grown = {}
        for cells, plan in found:
            for by in shifts:
                cover = cells | moved(cells, by)
                longer = plan + (by,)
                if cover not in grown or hops(longer) < hops(grown[cover]):
                    grown[cover] = longer
        ranked = sorted(grown.items(), key=lambda item: (-len(item[0]), hops(item[1]), item[1]))
        found = ranked[:beam]
    return found[0][1]


def per_device(velocity):
    _, planes, axial, radial = velocity.shape
    sizes = lax.axis_size("az"), lax.axis_size("ax")
    theta_step = 2.0 * math.pi / (sizes[0] * planes)
    coef = jnp.asarray(coefficients(radial, theta_step))
    f32 = jnp.float32
    anywhere = pl.BlockSpec(memory_space=pl.ANY)
    vmem = pl.BlockSpec(memory_space=pltpu.VMEM)
    smem = pl.BlockSpec(memory_space=pltpu.SMEM)

    def shape(*sizes):
        return jax.ShapeDtypeStruct(sizes, f32)

    def call(kernel, name, work, scratch=0, **kwargs):
        return pl.pallas_call(
            kernel,
            name=name,
            compiler_params=pltpu.CompilerParams(vmem_limit_bytes=(4 + scratch) * 2**20),
            cost_estimate=pl.CostEstimate(
                flops=work, bytes_accessed=velocity.size * 4, transcendentals=0
            ),
            **kwargs,
        )

    pair = shape(3, HALO, axial, radial)
    head, tail = call(
        theta_edges,
        "theta_edges",
        0,
        out_shape=(pair, pair),
        in_specs=[vmem],
        out_specs=(vmem, vmem),
    )(velocity)
    below = shifted(tail, (1, 0))
    above = shifted(head, (-1, 0))

    edge = shape(3, planes, 2, radial)
    padded = shape(3, planes + 2 * HALO, axial + 2 * PAD, radial)
    vel, first, last, inner, pay = call(
        functools.partial(first_pass, theta_step),
        "first_pass",
        10 * velocity.size,
        out_shape=(padded, edge, edge, shape(axial, radial), shape(8, radial)),
        in_specs=[vmem, vmem],
        out_specs=(vmem,) * 5,
    )(velocity, head)
    low = shifted(last, (0, 1))
    high = shifted(first, (0, -1))
    up = shifted(pay, (1, -1))
    down = shifted(pay, (-1, 1))
    inner = shifted(inner, (sizes[0] // 2, 0))
    pay, vel = call(
        fold,
        "fold",
        velocity.size // planes,
        out_shape=(shape(8, radial), padded),
        in_specs=[vmem] * 6,
        out_specs=(vmem, vmem),
        input_output_aliases={5: 1},
    )(low, high, up, down, pay, vel)

    known = {(0, 0)}
    for i, k in ((0, 1), (0, -1), (1, -1), (-1, 1)):
        known.add((i % sizes[0], k % sizes[1]))
    plan = rounds(sizes, known)
    inside = planes - 2 * HALO
    count = len(plan) + 1
    while inside % count:
        count += 1
    bounds = range(HALO, planes - HALO + 1, inside // count)
    spans = list(zip(bounds[:-1], bounds[1:]))
    kept = [
        pltpu.VMEM((axial + 8, radial), f32),
        pltpu.VMEM((axial, radial), f32),
        pltpu.VMEM((axial + PAD, radial), f32),
    ]
    parts = []
    far = zero = pay
    for n, (first, last) in enumerate(spans[:-1]):
        before = far
        if n < len(plan):
            pay = jnp.maximum(pay, jnp.maximum(far, zero)) if n else pay
            far = shifted(pay, plan[n])
        part, zero = call(
            functools.partial(interior, first, last),
            f"interior_{n}",
            400 * (last - first) * axial * radial,
            out_shape=(shape(3, last - first, axial, radial), shape(8, radial)),
            in_specs=[vmem] * 3,
            out_specs=(vmem, vmem),
            scratch_shapes=kept,
        )(vel, coef, before)
        parts.append(part)
    increment, time_step, _ = call(
        functools.partial(finish, spans),
        "finish",
        160 * velocity.size,
        scratch=8,
        out_shape=(shape(*velocity.shape), shape(1), padded),
        in_specs=[vmem] * (9 + len(parts)),
        out_specs=(anywhere, smem, vmem),
        scratch_shapes=[
            pltpu.VMEM(velocity.shape, f32),
            pltpu.SemaphoreType.DMA((planes,)),
            *kept,
        ],
        input_output_aliases={8 + len(parts): 2},
    )(below, above, up, down, pay, far, inner, coef, *parts, vel)
    return increment, time_step.reshape(())


def solution(mesh):
    return jax.shard_map(
        per_device,
        mesh=mesh,
        in_specs=(P(None, "az", "ax", None),),
        out_specs=(P(None, "az", "ax", None), P()),
        check_vma=False,
    )
```

```python
import functools
import math

import jax
import jax.numpy as jnp
import numpy as np
from jax import lax
from jax.experimental import pallas as pl
from jax.experimental.pallas import tpu as pltpu
from jax.sharding import PartitionSpec as P

AXIAL_STEP = 0.01
VISCOSITY = 0.001
CFL_TARGET = 1.2
GAMMA = 8.0 / 15.0

PAD = 8
HALO = 2
UNROLL = 4

(
    WALL,
    RADIAL_C,
    THETA_C,
    CROSS_Z,
    SECOND_C,
    CENTRE_Z,
    CENTRE_T,
    CURVE_T,
    TURN_T,
    RADIAL_F,
    THETA_F,
    SECOND_F,
    CENTRE_R,
    CURVE_R,
    TURN_R,
    COUNT,
) = range(16)


def coefficients(radial, theta_step):
    dr = 1.0 / radial
    index = np.arange(radial, dtype=np.float64)
    centre = (index + 0.5) * dr
    face = (index + 1.0) * dr
    wall = np.where(index < radial - 1.5, 1.0, 0.0)
    h = theta_step
    nu = VISCOSITY
    rows = np.zeros((COUNT, radial))
    rows[WALL] = wall
    common = -2.0 * nu / dr**2 - 30.0 * nu / (12.0 * AXIAL_STEP**2)
    rows[RADIAL_C] = nu / (2.0 * dr * centre)
    rows[THETA_C] = -1.0 / (12.0 * h * centre)
    rows[CROSS_Z] = 0.25 * rows[THETA_C]
    rows[SECOND_C] = nu / (12.0 * h * h * centre**2)
    rows[CENTRE_Z] = common - 30.0 * rows[SECOND_C]
    rows[CENTRE_T] = rows[CENTRE_Z] - nu / centre**2
    rows[CURVE_T] = 0.25 / centre
    rows[TURN_T] = nu / (h * centre**2)
    rows[RADIAL_F] = nu / (2.0 * dr * face)
    rows[THETA_F] = -0.25 / (12.0 * h * face)
    rows[SECOND_F] = nu / (12.0 * h * h * face**2)
    rows[CENTRE_R] = common - 30.0 * rows[SECOND_F] - nu / face**2
    rows[CURVE_R] = 1.0 / (16.0 * face)
    rows[TURN_R] = -nu / (h * face**2)
    return np.broadcast_to(rows[:, None, :], (COUNT, 8, radial)).astype(np.float32)


def terms(vel, ghost, coef, j, k, dr):
    lane = lax.broadcasted_iota(jnp.int32, (8, 128), 1)
    first_lane = lane == 0
    last_lane = lane == 127

    def at(component, dj, dk):
        return vel[component, j + HALO + dj, pl.ds(k + PAD + dk, 8), :]

    def out(x):
        return pltpu.roll(x, 127, 1)

    def inn(x):
        return pltpu.roll(x, 1, 1)

    nu = VISCOSITY
    lap = nu / dr**2
    adv_z = -1.0 / (12.0 * AXIAL_STEP)
    vis_z = nu / (12.0 * AXIAL_STEP**2)

    def differences(p1, m1, p2, m2):
        return 8.0 * (p1 - m1) - (p2 - m2), 16.0 * (p1 + m1) - (p2 + m2)

    def pieces(n):
        over = [at(n, d, 0) for d in (1, -1, 2, -2)]
        along = [at(n, 0, d) for d in (1, -1, 2, -2)]
        return over, along, differences(*over), differences(*along)

    def below(n, x):
        if ghost is not None:
            return jnp.where(first_lane, ghost(n), x)
        return x if n == 0 else jnp.where(first_lane, 0.0, x)

    a, b, c = (at(n, 0, 0) for n in range(3))
    (a_side, *_), (a_next, *_), a_theta, a_axial = pieces(0)
    (_, b_back, *_), (b_next, *_), b_theta, b_axial = pieces(1)
    (c_side, *_), (_, c_back, *_), c_theta, c_axial = pieces(2)
    a_in = inn(a)
    pair_a = a + a_in
    pair_side = a_side + inn(a_side)
    pair_next = a_next + inn(a_next)

    c_out = out(c)
    up = jnp.where(last_lane, -c, c_out)
    low = below(2, inn(c))
    u_r = pair_a + pair_next
    u_t = (b_back + b) + (at(1, -1, 1) + b_next)
    h_z = (up - low) * (coef[RADIAL_C] - u_r * (0.125 / dr)) + (up + low) * lap
    h_z = h_z + c_theta[0] * (u_t * coef[CROSS_Z])
    h_z = h_z + (c_theta[1] * coef[SECOND_C] + c_axial[1] * vis_z)
    h_z = h_z + c * (coef[CENTRE_Z] + c_axial[0] * adv_z)

    b_out = out(b)
    up = jnp.where(last_lane, -b, b_out)
    low = below(1, inn(b))
    u_r = pair_a + pair_side
    u_z = (c_back + c) + (at(2, 1, -1) + c_side)
    h_t = (up - low) * (coef[RADIAL_C] - u_r * (0.125 / dr)) + (up + low) * lap
    h_t = h_t + b * (coef[CENTRE_T] + b_theta[0] * coef[THETA_C] - u_r * coef[CURVE_T])
    h_t = h_t + (b_theta[1] * coef[SECOND_C] + b_axial[1] * vis_z)
    h_t = h_t + b_axial[0] * (u_z * (0.25 * adv_z))
    h_t = h_t + (pair_side - pair_a) * coef[TURN_T]

    up = out(a)
    low = below(0, a_in)
    pair_b = b + b_out
    pair_back = b_back + out(b_back)
    u_t = pair_b + pair_back
    u_z = (c + c_out) + (c_back + out(c_back))
    h_r = (up - low) * (coef[RADIAL_F] - a * (0.5 / dr)) + (up + low) * lap
    h_r = h_r + u_t * (u_t * coef[CURVE_R] + a_theta[0] * coef[THETA_F])
    h_r = h_r + (a_theta[1] * coef[SECOND_F] + a_axial[1] * vis_z)
    h_r = h_r + (a_axial[0] * (u_z * (0.25 * adv_z)) + a * coef[CENTRE_R])
    h_r = h_r + (pair_b - pair_back) * coef[TURN_R]
    return h_r, h_t, h_z


def lane_zero_terms(vel, ghost, coef, j, k, dr):
    def at(dj, dk):
        return vel[0, j + HALO + dj, pl.ds(k + PAD + dk, 8), :]

    lap = VISCOSITY / dr**2
    a = at(0, 0)
    first_lane = lax.broadcasted_iota(jnp.int32, a.shape, 1) == 0
    add_r = ghost(0) * (lap - coef[RADIAL_F] + a * (0.5 / dr))
    add_t = ghost(1) * (lap - coef[RADIAL_C] + (a + at(1, 0)) * (0.125 / dr))
    add_z = ghost(2) * (lap - coef[RADIAL_C] + (a + at(0, 1)) * (0.125 / dr))
    return tuple(jnp.where(first_lane, x, 0.0) for x in (add_r, add_t, add_z))


def theta_edges(v_ref, head_ref, tail_ref):
    count = v_ref.shape[1]
    for n in range(3):
        for q in range(HALO):
            head_ref[n, q] = v_ref[n, q]
            tail_ref[n, q] = v_ref[n, count - HALO + q]


def wall_mask(rows, radial):
    lane = lax.broadcasted_iota(jnp.int32, (rows, radial), 1)
    return jnp.where(lane == radial - 1, 0.0, 1.0).astype(jnp.float32)


def first_pass(theta_step, v_ref, _, vel_ref, low_ref, high_ref, inner_ref, pay_ref):
    _, planes, axial, radial = v_ref.shape
    lane = lax.broadcasted_iota(jnp.int32, (8, radial), 1)
    sign = jnp.where(lane < 2 * planes, -1.0, 1.0).astype(jnp.float32)
    wall = wall_mask(8, radial)
    rate_t = (radial / theta_step) / (lane.astype(jnp.float32) + 0.5)

    def rows(i, largest):
        k = pl.ds(pl.multiple_of(i * 8, 8), 8)
        padded = pl.ds(pl.multiple_of(i * 8 + PAD, 8), 8)
        inner = [jnp.zeros((8, radial), jnp.float32)] * 3
        for j in range(planes):
            a, b, c = cells = [v_ref[n, j, k, :] for n in range(3)]
            a = a * wall
            rate = jnp.abs(a) * float(radial) + jnp.abs(b) * rate_t
            largest = jnp.maximum(largest, rate + jnp.abs(c) * (1.0 / AXIAL_STEP))
            for n, x in enumerate(cells):
                vel_ref[n, j + HALO, padded, :] = a if n == 0 else x
                place = n * planes + j
                inner[n] = jnp.where(lane == place, pltpu.roll(x, place, 1), inner[n])
        inner_ref[k, :] = (inner[0] + inner[1] + inner[2]) * sign
        return largest

    largest = lax.fori_loop(0, axial // 8, rows, jnp.zeros((8, radial), jnp.float32))
    top = jnp.max(largest, axis=(0, 1), keepdims=True)
    pay_ref[...] = jnp.broadcast_to(top, pay_ref.shape)
    pay_ref[1:2, :] = v_ref[1, planes - 1, 0:1, :]
    pay_ref[2:3, :] = v_ref[2, 0, axial - 1 : axial, :]

    def ends(j, carry):
        for n in range(3):
            low_ref[n, j] = v_ref[n, j, 0:2, :]
            high_ref[n, j] = v_ref[n, j, axial - 2 : axial, :]
        return carry

    lax.fori_loop(0, planes, ends, 0, unroll=8)
    last = lax.broadcasted_iota(jnp.int32, (2, radial), 1) == radial - 1
    for ref in (low_ref, high_ref):
        ref[0, 0] = jnp.where(last, top, ref[0, 0])


def fold(low_ref, high_ref, pay_ref, vel_in, out_ref, vel_ref):
    del vel_in
    planes, radial = low_ref.shape[1], low_ref.shape[3]
    axial = vel_ref.shape[2] - 2 * PAD
    lane = lax.broadcasted_iota(jnp.int32, (1, radial), 1)
    top = jnp.maximum(low_ref[0, 0, 0:1, :], high_ref[0, 0, 0:1, :])
    top = jnp.max(jnp.where(lane == radial - 1, top, 0.0), axis=(0, 1), keepdims=True)
    out_ref[...] = jnp.maximum(pay_ref[...], top)
    out_ref[1:2, :] = high_ref[1, planes - 1, 0:1, :]
    out_ref[2:3, :] = low_ref[2, 0, 1:2, :]
    wall = wall_mask(2, radial)

    def plane(j, carry):
        for n in range(3):
            mask = wall if n == 0 else 1.0
            vel_ref[n, j + HALO, PAD - 2 : PAD, :] = low_ref[n, j] * mask
            vel_ref[n, j + HALO, PAD + axial : PAD + axial + 2, :] = high_ref[n, j] * mask
        return carry

    lax.fori_loop(0, planes, plane, 0, unroll=4)


def late(pay_ref, *refs):
    fars, (inner_in, tiles_ref, inner_ref) = refs[:-7], (refs[-7], *refs[-2:])
    tile = pay_ref[...]
    top = tile[0:1, :]
    for far in fars:
        top = jnp.maximum(top, far[0:1, :])
    row = lax.broadcasted_iota(jnp.int32, tile.shape, 0)
    tile = jnp.where(row == 0, top, tile)
    for i in range(tiles_ref.shape[0]):
        tiles_ref[i] = tile
    inner_ref[...] = inner_in[...]


def ghosts(inner, planes, j):
    radial = inner.shape[1]

    def ghost(component):
        turn = lax.rem(2 * radial - component * planes - j, radial)
        return pltpu.roll(inner, turn, 1)

    return ghost


def sweep(vel_ref, inner_ref, coef_ref, first, last, write, beside=None, after=None):
    planes = vel_ref.shape[1] - 2 * HALO
    axial, radial = vel_ref.shape[2] - 2 * PAD, vel_ref.shape[3]

    def plane(j, carry):
        def rows(i, carry):
            coef = [coef_ref[n] for n in range(COUNT)]
            ks = [pl.multiple_of((i * UNROLL + u) * 8, 8) for u in range(UNROLL)]
            found = []
            for k in ks:
                ghost = None
                if inner_ref is not None:
                    ghost = ghosts(inner_ref[pl.ds(k, 8), :], planes, j)
                found.append(terms(vel_ref, ghost, coef, j, k, 1.0 / radial))
            for k, values in zip(ks, found):
                for n, value in enumerate(values):
                    write(n, j, pl.ds(k, 8), value)
                if beside is not None:
                    beside(j, k, coef)
            return carry

        lax.fori_loop(0, axial // (8 * UNROLL), rows, 0)
        if after is not None:
            after(j)
        return carry

    lax.fori_loop(first, last, plane, 0)


def interior(first, last, vel_ref, coef_ref, _, out_ref):
    def write(n, j, k, value):
        out_ref[n, j - first, k, :] = value

    sweep(vel_ref, None, coef_ref, first, last, write)


def finish(
    spans,
    below_ref,
    above_ref,
    tiles_ref,
    inner_ref,
    coef_ref,
    *refs,
):
    parts, refs = refs[: len(spans) - 1], refs[len(spans) - 1 :]
    vel_in, out_ref, step_ref, vel_ref, res, sems = refs
    del vel_in
    axial, radial = inner_ref.shape
    planes = res.shape[1]
    count = tiles_ref.shape[0]
    top = tiles_ref[0, 0:1, :]
    for i in range(1, count):
        top = jnp.maximum(top, tiles_ref[i, 0:1, :])
    largest = jnp.max(top)
    time_step = CFL_TARGET / (largest + 1e-06)
    step_ref[0] = time_step
    scale = GAMMA * time_step

    def store(j):
        return pltpu.make_async_copy(res.at[:, j], out_ref.at[:, j], sems.at[j])

    def write(n, j, k, value):
        factor = scale * coef_ref[WALL] if n == 0 else scale
        res[n, j, k, :] = value * factor

    (start, stop), others = spans[-1], spans[:-1]

    def beside(j, k, coef):
        inner = inner_ref[pl.ds(k, 8), :]
        for part, (first, _) in zip(parts, others):
            place = first + j - start
            ghost = ghosts(inner, planes, place)
            added = lane_zero_terms(vel_ref, ghost, coef, place, k, 1.0 / radial)
            for n, value in enumerate(added):
                write(n, place, pl.ds(k, 8), part[n, j - start, pl.ds(k, 8), :] + value)

    def after(j):
        store(j).start()
        for first, _ in others:
            store(first + j - start).start()

    sweep(vel_ref, inner_ref, coef_ref, start, stop, write, beside, after)

    cells = pl.ds(PAD, axial)
    for q in range(HALO):
        for ref, place in ((below_ref, q), (above_ref, HALO + planes + q)):
            vel_ref[0, place, cells, :] = ref[0, q] * coef_ref[WALL, 0:1, :]
            vel_ref[1, place, cells, :] = ref[1, q]
            vel_ref[2, place, cells, :] = ref[2, q]
    place = lax.axis_index("az")
    lower, upper = lax.rem(place + count - 1, count), lax.rem(place + 1, count)
    vel_ref[1, HALO - 1, PAD + axial : PAD + axial + 1, :] = tiles_ref[lower, 1:2, :]
    vel_ref[2, HALO + planes, PAD - 1 : PAD, :] = tiles_ref[upper, 2:3, :]
    for first in (0, planes - HALO):
        sweep(
            vel_ref,
            inner_ref,
            coef_ref,
            first,
            first + HALO,
            write,
            after=lambda j: store(j).start(),
        )

    def wait(j, carry):
        store(j).wait()
        return carry

    lax.fori_loop(0, planes, wait, 0)


def shifted(block, distance):
    sizes = lax.axis_size("az"), lax.axis_size("ax")
    route = []
    for i in range(sizes[0]):
        for k in range(sizes[1]):
            source = (i - distance[0]) % sizes[0], (k - distance[1]) % sizes[1]
            route.append((source[0] * sizes[1] + source[1], i * sizes[1] + k))
    return lax.ppermute(block, ("az", "ax"), route)


def quarters(planes):
    step = (planes - 2 * HALO) // 4
    return [(HALO + n * step, HALO + (n + 1) * step) for n in range(4)]


def per_device(velocity):
    _, planes, axial, radial = velocity.shape
    sizes = lax.axis_size("az"), lax.axis_size("ax")
    theta_step = 2.0 * math.pi / (sizes[0] * planes)
    coef = jnp.asarray(coefficients(radial, theta_step))
    f32 = jnp.float32
    anywhere = pl.BlockSpec(memory_space=pl.ANY)
    vmem = pl.BlockSpec(memory_space=pltpu.VMEM)
    smem = pl.BlockSpec(memory_space=pltpu.SMEM)

    def shape(*sizes):
        return jax.ShapeDtypeStruct(sizes, f32)

    def call(kernel, name, work, scratch=0, **kwargs):
        return pl.pallas_call(
            kernel,
            name=name,
            compiler_params=pltpu.CompilerParams(vmem_limit_bytes=(4 + scratch) * 2**20),
            cost_estimate=pl.CostEstimate(flops=work, bytes_accessed=work, transcendentals=0),
            **kwargs,
        )

    pair = shape(3, HALO, axial, radial)
    head, tail = call(
        theta_edges,
        "theta_edges",
        0,
        out_shape=(pair, pair),
        in_specs=[vmem],
        out_specs=(vmem, vmem),
    )(velocity)
    below = shifted(tail, (1, 0))
    above = shifted(head, (-1, 0))

    edge = shape(3, planes, 2, radial)
    padded = shape(3, planes + 2 * HALO, axial + 2 * PAD, radial)
    vel, first, last, inner, pay = call(
        functools.partial(first_pass, theta_step),
        "first_pass",
        0,
        out_shape=(padded, edge, edge, shape(axial, radial), shape(8, radial)),
        in_specs=[vmem, vmem],
        out_specs=(vmem,) * 5,
    )(velocity, head)
    low = shifted(last, (0, 1))
    high = shifted(first, (0, -1))
    pay, vel = call(
        fold,
        "fold",
        0,
        out_shape=(shape(8, radial), padded),
        in_specs=[vmem] * 4,
        out_specs=(vmem, vmem),
        input_output_aliases={3: 1},
    )(low, high, pay, vel)
    top, fars, known = pay, [], 3
    while known < sizes[1]:
        step = min(known, sizes[1] - known)
        fars.append(shifted(top, (0, step)))
        top = jnp.maximum(top, fars[-1])
        known += step

    spans = quarters(planes)
    parts = []

    def inside(n, token):
        first, last = spans[n]
        part = call(
            functools.partial(interior, first, last),
            f"interior_{n}",
            velocity.size,
            out_shape=shape(3, last - first, axial, radial),
            in_specs=[vmem] * 3,
            out_specs=vmem,
        )(vel, coef, token)
        parts.append(part)

    inside(0, pay)
    inside(1, pay)
    tiles, inner = call(
        late,
        "late",
        0,
        out_shape=(shape(sizes[0], 8, radial), shape(axial, radial)),
        in_specs=[vmem] * (6 + len(fars)),
        out_specs=(vmem, vmem),
    )(pay, *fars, inner, below, above, *parts)
    inner = shifted(inner, (sizes[0] // 2, 0))
    moved = lax.all_to_all(tiles, "az", 0, 0)
    inside(2, tiles)
    increment, time_step, _ = call(
        functools.partial(finish, spans),
        "finish",
        0,
        scratch=8,
        out_shape=(shape(*velocity.shape), shape(1), padded),
        in_specs=[vmem] * (6 + len(parts)),
        out_specs=(anywhere, smem, vmem),
        scratch_shapes=[
            pltpu.VMEM(velocity.shape, f32),
            pltpu.SemaphoreType.DMA((planes,)),
        ],
        input_output_aliases={5 + len(parts): 2},
    )(below, above, moved, inner, coef, *parts, vel)
    return increment, time_step.reshape(())


def solution(mesh):
    return jax.shard_map(
        per_device,
        mesh=mesh,
        in_specs=(P(None, "az", "ax", None),),
        out_specs=(P(None, "az", "ax", None), P()),
        check_vma=False,
    )
```

```python
import functools
import math

import jax
import jax.numpy as jnp
import numpy as np
from jax import lax
from jax.experimental import pallas as pl
from jax.experimental.pallas import tpu as pltpu
from jax.sharding import PartitionSpec as P

AXIAL_STEP = 0.01
VISCOSITY = 0.001
CFL_TARGET = 1.2
GAMMA = 8.0 / 15.0

PAD = 8
HALO = 2
BLOCK = 4
GROUP = 4
UNROLL = 4

(
    WALL,
    RADIAL_C,
    THETA_C,
    CROSS_Z,
    SECOND_C,
    CENTRE_Z,
    CENTRE_T,
    CURVE_T,
    TURN_T,
    RADIAL_F,
    THETA_F,
    SECOND_F,
    CENTRE_R,
    CURVE_R,
    TURN_R,
    COUNT,
) = range(16)


def coefficients(radial, theta_step):
    dr = 1.0 / radial
    index = np.arange(radial, dtype=np.float64)
    centre = (index + 0.5) * dr
    face = (index + 1.0) * dr
    wall = np.where(index < radial - 1.5, 1.0, 0.0)
    h = theta_step
    nu = VISCOSITY
    rows = np.zeros((COUNT, radial))
    rows[WALL] = wall
    common = -2.0 * nu / dr**2 - 30.0 * nu / (12.0 * AXIAL_STEP**2)
    rows[RADIAL_C] = nu / (2.0 * dr * centre)
    rows[THETA_C] = -1.0 / (12.0 * h * centre)
    rows[CROSS_Z] = 0.25 * rows[THETA_C]
    rows[SECOND_C] = nu / (12.0 * h * h * centre**2)
    rows[CENTRE_Z] = common - 30.0 * rows[SECOND_C]
    rows[CENTRE_T] = rows[CENTRE_Z] - nu / centre**2
    rows[CURVE_T] = 0.25 / centre
    rows[TURN_T] = nu / (h * centre**2)
    rows[RADIAL_F] = nu / (2.0 * dr * face)
    rows[THETA_F] = -0.25 / (12.0 * h * face)
    rows[SECOND_F] = nu / (12.0 * h * h * face**2)
    rows[CENTRE_R] = common - 30.0 * rows[SECOND_F] - nu / face**2
    rows[CURVE_R] = 1.0 / (16.0 * face)
    rows[TURN_R] = -nu / (h * face**2)
    return np.broadcast_to(rows[:, None, :], (COUNT, 8, radial)).astype(np.float32)


class Cells:
    def __init__(self, vel, j, k):
        self.vel, self.j, self.k, self.known = vel, j, k, {}

    def once(self, key, make):
        if key not in self.known:
            self.known[key] = make()
        return self.known[key]

    def at(self, n, dj, dk=0):
        rows = pl.ds(self.k + PAD + dk, 8)
        return self.once((n, dj, dk), lambda: self.vel[n, self.j + HALO + dj, rows, :])

    def turned(self, by, n, dj, dk=0):
        return self.once(
            (by, n, dj, dk), lambda: pltpu.roll(self.at(n, dj, dk), by % self.vel.shape[3], 1)
        )

    def pair(self, by, n, dj, dk=0):
        return self.once(
            ("pair", n, dj, dk), lambda: self.at(n, dj, dk) + self.turned(by, n, dj, dk)
        )

    def beside(self, dj, dk):
        n = 1 if dk >= 0 else 2
        other = (1, dj - 1, dk) if n == 1 else (2, dj, dk)
        here = (1, dj, dk) if n == 1 else (2, dj, dk + 1)
        return self.once(("sum", n, dj, dk), lambda: self.at(*other) + self.at(*here))


def terms(cells, ghost, coef, q, dr):
    at, turned, pair = cells.at, cells.turned, cells.pair
    a, b, c = (at(n, q) for n in range(3))
    lane = lax.broadcasted_iota(jnp.int32, a.shape, 1)
    first_lane = lane == 0
    last_lane = lane == a.shape[1] - 1

    nu = VISCOSITY
    lap = nu / dr**2
    adv_z = -1.0 / (12.0 * AXIAL_STEP)
    vis_z = nu / (12.0 * AXIAL_STEP**2)

    def differences(p1, m1, p2, m2):
        return 8.0 * (p1 - m1) - (p2 - m2), 16.0 * (p1 + m1) - (p2 + m2)

    def pieces(n):
        over = differences(*(at(n, q + d) for d in (1, -1, 2, -2)))
        along = differences(*(at(n, q, d) for d in (1, -1, 2, -2)))
        return over, along

    def below(n):
        x = turned(1, n, q)
        if ghost is not None:
            return jnp.where(first_lane, ghost(n), x)
        return x if n == 0 else jnp.where(first_lane, 0.0, x)

    def above(n):
        return jnp.where(last_lane, -at(n, q), turned(-1, n, q))

    pair_a, pair_side, pair_next = pair(1, 0, q), pair(1, 0, q + 1), pair(1, 0, q, 1)
    pair_b, pair_back = pair(-1, 1, q), pair(-1, 1, q - 1)

    theta, axial = pieces(2)
    up, low = above(2), below(2)
    u_r = pair_a + pair_next
    u_t = cells.beside(q, 0) + cells.beside(q, 1)
    h_z = (up - low) * (coef[RADIAL_C] - u_r * (0.125 / dr)) + (up + low) * lap
    h_z = h_z + theta[0] * (u_t * coef[CROSS_Z])
    h_z = h_z + (theta[1] * coef[SECOND_C] + axial[1] * vis_z)
    h_z = h_z + c * (coef[CENTRE_Z] + axial[0] * adv_z)

    theta, axial = pieces(1)
    up, low = above(1), below(1)
    u_r = pair_a + pair_side
    u_z = cells.beside(q, -1) + cells.beside(q + 1, -1)
    h_t = (up - low) * (coef[RADIAL_C] - u_r * (0.125 / dr)) + (up + low) * lap
    h_t = h_t + b * (coef[CENTRE_T] + theta[0] * coef[THETA_C] - u_r * coef[CURVE_T])
    h_t = h_t + (theta[1] * coef[SECOND_C] + axial[1] * vis_z)
    h_t = h_t + axial[0] * (u_z * (0.25 * adv_z))
    h_t = h_t + (pair_side - pair_a) * coef[TURN_T]

    theta, axial = pieces(0)
    up, low = turned(-1, 0, q), below(0)
    u_t = pair_b + pair_back
    u_z = pair(-1, 2, q) + pair(-1, 2, q, -1)
    h_r = (up - low) * (coef[RADIAL_F] - a * (0.5 / dr)) + (up + low) * lap
    h_r = h_r + u_t * (u_t * coef[CURVE_R] + theta[0] * coef[THETA_F])
    h_r = h_r + (theta[1] * coef[SECOND_F] + axial[1] * vis_z)
    h_r = h_r + (axial[0] * (u_z * (0.25 * adv_z)) + a * coef[CENTRE_R])
    h_r = h_r + (pair_b - pair_back) * coef[TURN_R]
    return h_r, h_t, h_z


def lane_zero_terms(vel, ghost, coef, j, k, dr):
    def at(dj, dk):
        return vel[0, j + HALO + dj, pl.ds(k + PAD + dk, 8), :]

    lap = VISCOSITY / dr**2
    a = at(0, 0)
    first_lane = lax.broadcasted_iota(jnp.int32, a.shape, 1) == 0
    add_r = ghost(0) * (lap - coef[RADIAL_F] + a * (0.5 / dr))
    add_t = ghost(1) * (lap - coef[RADIAL_C] + (a + at(1, 0)) * (0.125 / dr))
    add_z = ghost(2) * (lap - coef[RADIAL_C] + (a + at(0, 1)) * (0.125 / dr))
    return tuple(jnp.where(first_lane, x, 0.0) for x in (add_r, add_t, add_z))


def wall_mask(rows, radial):
    lane = lax.broadcasted_iota(jnp.int32, (rows, radial), 1)
    return jnp.where(lane == radial - 1, 0.0, 1.0).astype(jnp.float32)


def first_pass(theta_step, v_ref, vel_ref, low_ref, high_ref, pay_ref, sems):
    _, planes, axial, radial = v_ref.shape
    lane = lax.broadcasted_iota(jnp.int32, (8, radial), 1)
    wall = wall_mask(8, radial)
    rate_t = (radial / theta_step) / (lane.astype(jnp.float32) + 0.5)

    def fetch(g):
        part = pl.ds(g * GROUP, GROUP)
        target = vel_ref.at[:, pl.ds(g * GROUP + HALO, GROUP), pl.ds(PAD, axial)]
        return pltpu.make_async_copy(v_ref.at[:, part], target, sems.at[g])

    for g in range(planes // GROUP):
        fetch(g).start()

    def group(g, largest):
        fetch(g).wait()

        def rows(i, largest):
            k = pl.ds(pl.multiple_of(i * 8, 8) + PAD, 8)
            largest = list(largest)
            for q in range(GROUP):
                j = g * GROUP + HALO + q
                a, b, c = (vel_ref[n, j, k, :] for n in range(3))
                a = a * wall
                vel_ref[0, j, k, :] = a
                rate = jnp.abs(a) * float(radial) + jnp.abs(b) * rate_t
                rate = rate + jnp.abs(c) * (1.0 / AXIAL_STEP)
                largest[q % 4] = jnp.maximum(largest[q % 4], rate)
            return tuple(largest)

        largest = lax.fori_loop(0, axial // 8, rows, largest, unroll=4)
        for q in range(GROUP):
            for n in range(3):
                j = g * GROUP + q
                low_ref[n, j] = vel_ref[n, j + HALO, PAD : PAD + 2, :]
                high_ref[n, j] = vel_ref[n, j + HALO, PAD + axial - 2 : PAD + axial, :]
        return largest

    zero = jnp.zeros((8, radial), jnp.float32)
    m = lax.fori_loop(0, planes // GROUP, group, (zero,) * 4)
    largest = jnp.maximum(jnp.maximum(m[0], m[1]), jnp.maximum(m[2], m[3]))
    top = jnp.max(largest, axis=(0, 1), keepdims=True)
    pay_ref[...] = jnp.broadcast_to(top, pay_ref.shape)
    last = lax.broadcasted_iota(jnp.int32, (2, radial), 1) == radial - 1
    for ref in (low_ref, high_ref):
        ref[0, 0] = jnp.where(last, top, ref[0, 0])


def pack(vel_ref, inner_ref):
    planes, (axial, radial) = vel_ref.shape[1] - 2 * HALO, inner_ref.shape
    lane = lax.broadcasted_iota(jnp.int32, (8, radial), 1)
    sign = jnp.where(lane < 2 * planes, -1.0, 1.0).astype(jnp.float32)

    def rows(i, carry):
        k = pl.multiple_of(i * 8, 8)
        inner = [jnp.zeros((8, radial), jnp.float32)] * 3
        for j in range(planes):
            for n in range(3):
                place = n * planes + j
                x = vel_ref[n, j + HALO, pl.ds(k + PAD, 8), :]
                x = pltpu.roll(x, place, 1)
                inner[n] = jnp.where(lane == place, x, inner[n])
        inner_ref[pl.ds(k, 8), :] = (inner[0] + inner[1] + inner[2]) * sign
        return carry

    lax.fori_loop(0, axial // 8, rows, 0)


def fold(low_ref, high_ref, pay_ref, vel_in, _, out_ref, vel_ref):
    del vel_in
    planes, radial = low_ref.shape[1], low_ref.shape[3]
    axial = vel_ref.shape[2] - 2 * PAD
    lane = lax.broadcasted_iota(jnp.int32, (1, radial), 1)
    top = jnp.maximum(low_ref[0, 0, 0:1, :], high_ref[0, 0, 0:1, :])
    top = jnp.max(jnp.where(lane == radial - 1, top, 0.0), axis=(0, 1), keepdims=True)
    out_ref[...] = jnp.maximum(pay_ref[...], top)
    out_ref[1:2, :] = high_ref[1, planes - 1, 0:1, :]
    out_ref[2:3, :] = low_ref[2, 0, 1:2, :]
    wall = wall_mask(2, radial)

    def plane(j, carry):
        for n in range(3):
            mask = wall if n == 0 else 1.0
            vel_ref[n, j + HALO, PAD - 2 : PAD, :] = low_ref[n, j] * mask
            vel_ref[n, j + HALO, PAD + axial : PAD + axial + 2, :] = high_ref[n, j] * mask
        return carry

    lax.fori_loop(0, planes, plane, 0, unroll=4)


def largest_along_ax(pay_ref, *refs):
    (inner_in, inner_ref), fars = (refs[-6], refs[-1]), refs[:-6]
    top = pay_ref[0:1, :]
    for far in fars:
        top = jnp.maximum(top, far[0:1, :])
    inner_ref[...] = inner_in[...]
    lane = lax.broadcasted_iota(jnp.int32, top.shape, 1)
    inner_ref[0:1, :] = jnp.where(lane == top.shape[1] - 1, top, inner_ref[0:1, :])


def largest_with_partner(pay_ref, mine_ref, inner_ref, _, out_ref):
    top = jnp.maximum(mine_ref[0:1, :], inner_ref[0:1, :])
    lane = lax.broadcasted_iota(jnp.int32, top.shape, 1)
    top = jnp.max(jnp.where(lane == top.shape[1] - 1, top, 0.0), axis=(0, 1), keepdims=True)
    row = lax.broadcasted_iota(jnp.int32, out_ref.shape, 0)
    out_ref[...] = jnp.where(row == 0, top, pay_ref[...])


def ghosts(inner, planes, j):
    radial = inner.shape[1]

    def ghost(component):
        turn = lax.rem(2 * radial - component * planes - j, radial)
        return pltpu.roll(inner, turn, 1)

    return ghost


def sweep(vel_ref, inner_ref, coef_ref, first, last, write):
    planes = vel_ref.shape[1] - 2 * HALO
    axial, radial = vel_ref.shape[2] - 2 * PAD, vel_ref.shape[3]
    size = math.gcd(BLOCK, last - first)

    def block(m, carry):
        j = first + m * size

        def rows(i, carry):
            k = pl.multiple_of(i * 8, 8)
            coef = [coef_ref[n] for n in range(COUNT)]
            cells = Cells(vel_ref, j, k)
            inner = None if inner_ref is None else inner_ref[pl.ds(k, 8), :]
            found = []
            for q in range(size):
                ghost = None if inner is None else ghosts(inner, planes, j + q)
                found.append(terms(cells, ghost, coef, q, 1.0 / radial))
            for q, values in enumerate(found):
                for n, value in enumerate(values):
                    write(n, j + q, pl.ds(k, 8), value)
            return carry

        return lax.fori_loop(0, axial // 8, rows, carry)

    lax.fori_loop(0, (last - first) // size, block, 0)


def interior(first, last, vel_ref, coef_ref, _, out_ref):
    def write(n, j, k, value):
        out_ref[n, j - first, k, :] = value

    sweep(vel_ref, None, coef_ref, first, last, write)


def finish(
    spans,
    below_ref,
    above_ref,
    up_ref,
    down_ref,
    pay_ref,
    far_refs,
    inner_ref,
    coef_ref,
    parts,
    out_ref,
    step_ref,
    vel_ref,
    res,
    sems,
):
    axial, radial = inner_ref.shape
    planes = res.shape[1]
    top = pay_ref[0:1, :]
    for ref in (up_ref, down_ref, *far_refs):
        top = jnp.maximum(top, ref[0:1, :])
    time_step = CFL_TARGET / (jnp.max(top) + 1e-06)
    step_ref[0] = time_step
    scale = GAMMA * time_step

    def store(j):
        return pltpu.make_async_copy(res.at[:, j], out_ref.at[:, j], sems.at[j])

    def send(first, last):
        def start(j, carry):
            store(j).start()
            return carry

        lax.fori_loop(first, last, start, 0)

    def write(n, j, k, value):
        factor = scale * coef_ref[WALL] if n == 0 else scale
        res[n, j, k, :] = value * factor

    for part, (first, last) in zip(parts, spans):

        def plane(j, carry, part=part, first=first):
            def rows(i, carry):
                k = pl.multiple_of(i * 8, 8)
                ghost = ghosts(inner_ref[pl.ds(k, 8), :], planes, j)
                added = lane_zero_terms(vel_ref, ghost, coef_ref, j, k, 1.0 / radial)
                for n, value in enumerate(added):
                    write(n, j, pl.ds(k, 8), part[n, j - first, pl.ds(k, 8), :] + value)
                return carry

            lax.fori_loop(0, axial // 8, rows, carry, unroll=UNROLL)
            store(j).start()
            return carry

        lax.fori_loop(first, last, plane, 0)

    sweep(vel_ref, inner_ref, coef_ref, *spans[-1], write)
    send(*spans[-1])

    cells = pl.ds(PAD, axial)
    for q in range(HALO):
        for ref, place in ((below_ref, q), (above_ref, HALO + planes + q)):
            vel_ref[0, place, cells, :] = ref[0, q] * coef_ref[WALL, 0:1, :]
            vel_ref[1, place, cells, :] = ref[1, q]
            vel_ref[2, place, cells, :] = ref[2, q]
    vel_ref[1, HALO - 1, PAD + axial : PAD + axial + 1, :] = up_ref[1:2, :]
    vel_ref[2, HALO + planes, PAD - 1 : PAD, :] = down_ref[2:3, :]
    for first in (0, planes - HALO):
        sweep(vel_ref, inner_ref, coef_ref, first, first + HALO, write)
        send(first, first + HALO)

    def wait(j, carry):
        store(j).wait()
        return carry

    lax.fori_loop(0, planes, wait, 0)


def shifted(block, distance):
    sizes = lax.axis_size("az"), lax.axis_size("ax")
    route = []
    for i in range(sizes[0]):
        for k in range(sizes[1]):
            source = (i - distance[0]) % sizes[0], (k - distance[1]) % sizes[1]
            route.append((source[0] * sizes[1] + source[1], i * sizes[1] + k))
    return lax.ppermute(block, ("az", "ax"), route)


def cuts(planes):
    blocks = (planes - 2 * HALO) // BLOCK
    ends = [blocks * n // 7 for n in (0, 2, 4, 5, 6)] + [blocks]
    return [(HALO + BLOCK * m, HALO + BLOCK * n) for m, n in zip(ends[:-1], ends[1:])]


def doublings(count, known):
    covered = {i % count for i in known}
    plan = []
    while len(covered) < count:
        best = max(range(1, count), key=lambda s: len(covered | {(i + s) % count for i in covered}))
        covered |= {(i + best) % count for i in covered}
        plan.append(best)
    return plan


def per_device(velocity):
    _, planes, axial, radial = velocity.shape
    sizes = lax.axis_size("az"), lax.axis_size("ax")
    theta_step = 2.0 * math.pi / (sizes[0] * planes)
    coef = jnp.asarray(coefficients(radial, theta_step))
    f32 = jnp.float32
    anywhere = pl.BlockSpec(memory_space=pl.ANY)
    vmem = pl.BlockSpec(memory_space=pltpu.VMEM)
    smem = pl.BlockSpec(memory_space=pltpu.SMEM)

    def shape(*sizes):
        return jax.ShapeDtypeStruct(sizes, f32)

    def call(kernel, name, work, scratch=0, **kwargs):
        return pl.pallas_call(
            kernel,
            name=name,
            compiler_params=pltpu.CompilerParams(vmem_limit_bytes=(4 + scratch) * 2**20),
            cost_estimate=pl.CostEstimate(flops=work, bytes_accessed=work, transcendentals=0),
            **kwargs,
        )

    below = shifted(velocity[:, planes - HALO :], (1, 0))
    above = shifted(velocity[:, :HALO], (-1, 0))

    edge = shape(3, planes, 2, radial)
    padded = shape(3, planes + 2 * HALO, axial + 2 * PAD, radial)
    tile = shape(8, radial)
    vel, first, last, pay = call(
        functools.partial(first_pass, theta_step),
        "first_pass",
        0,
        out_shape=(padded, edge, edge, tile),
        in_specs=[anywhere],
        out_specs=(vmem,) * 4,
        scratch_shapes=[pltpu.SemaphoreType.DMA((planes // GROUP,))],
    )(pltpu.with_memory_space_constraint(velocity, pltpu.HBM))
    low = shifted(last, (0, 1))
    high = shifted(first, (0, -1))
    inner = call(
        pack,
        "pack",
        velocity.size,
        out_shape=shape(axial, radial),
        in_specs=[vmem],
        out_specs=vmem,
    )(vel)
    pay, vel = call(
        fold,
        "fold",
        0,
        out_shape=(tile, padded),
        in_specs=[vmem] * 5,
        out_specs=(vmem, vmem),
        input_output_aliases={3: 1},
    )(low, high, pay, vel, inner)
    top, fars = pay, []
    for step in doublings(sizes[1], (0, 1, -1)):
        fars.append(shifted(top, (0, step)))
        top = jnp.maximum(top, fars[-1])

    spans = cuts(planes)
    parts = []

    def inside(n, token):
        first, last = spans[n]
        part = call(
            functools.partial(interior, first, last),
            f"interior_{n}",
            velocity.size,
            out_shape=shape(3, last - first, axial, radial),
            in_specs=[vmem] * 3,
            out_specs=vmem,
        )(vel, coef, token)
        parts.append(part)

    inside(0, pay)
    inside(1, pay)
    mine = call(
        largest_along_ax,
        "largest_along_ax",
        0,
        out_shape=shape(axial, radial),
        in_specs=[vmem] * (6 + len(fars)),
        out_specs=vmem,
    )(pay, *fars, inner, below, above, *parts)
    inner = shifted(mine, (sizes[0] // 2, 0))
    inside(2, mine)
    pay = call(
        largest_with_partner,
        "largest_with_partner",
        0,
        out_shape=tile,
        in_specs=[vmem] * 4,
        out_specs=vmem,
    )(pay, mine, inner, parts[2])
    up = shifted(pay, (1, 0))
    down = shifted(pay, (-1, 0))
    around = [(i, 0) for i in (0, sizes[0] // 2)]
    near = {(i + s) % sizes[0] for i, _ in around for s in (-1, 0, 1)}
    others = []
    while len(near) < sizes[0]:
        step = min(set(range(sizes[0])) - near)
        others.append(shifted(pay, (step, 0)))
        near |= {(i + step) % sizes[0] for i, _ in around}
    inside(3, pay)

    def last_kernel(*refs):
        ins, parts_in, rest = refs[:5], refs[5 : 5 + len(others)], refs[5 + len(others) :]
        inner_ref, coef_ref, *rest = rest
        parts_refs, rest = rest[: len(parts)], rest[len(parts) :]
        _, out_ref, step_ref, vel_ref, res, sems = rest
        finish(
            spans, *ins, parts_in, inner_ref, coef_ref, parts_refs, out_ref, step_ref, vel_ref,
            res, sems,
        )

    count = 7 + len(others) + len(parts)
    increment, time_step, _ = call(
        last_kernel,
        "finish",
        0,
        scratch=8,
        out_shape=(shape(*velocity.shape), shape(1), padded),
        in_specs=[vmem] * (count + 1),
        out_specs=(anywhere, smem, vmem),
        scratch_shapes=[
            pltpu.VMEM(velocity.shape, f32),
            pltpu.SemaphoreType.DMA((planes,)),
        ],
        input_output_aliases={count: 2},
    )(below, above, up, down, pay, *others, inner, coef, *parts, vel)
    return increment, time_step.reshape(())


def solution(mesh):
    return jax.shard_map(
        per_device,
        mesh=mesh,
        in_specs=(P(None, "az", "ax", None),),
        out_specs=(P(None, "az", "ax", None), P()),
        check_vma=False,
    )
```

```python
import functools
import math

import jax
import jax.numpy as jnp
import numpy as np
from jax import lax
from jax.experimental import pallas as pl
from jax.experimental.pallas import tpu as pltpu
from jax.sharding import PartitionSpec as P

AXIAL_STEP = 0.01
VISCOSITY = 0.001
CFL_TARGET = 1.2
GAMMA = 8.0 / 15.0

PAD = 8
HALO = 2
BLOCK = 4
GROUP = 4
UNROLL = 4

(
    WALL,
    RADIAL_C,
    THETA_C,
    CROSS_Z,
    SECOND_C,
    CENTRE_Z,
    CENTRE_T,
    CURVE_T,
    TURN_T,
    RADIAL_F,
    THETA_F,
    SECOND_F,
    CENTRE_R,
    CURVE_R,
    TURN_R,
    COUNT,
) = range(16)


def coefficients(radial, theta_step):
    dr = 1.0 / radial
    index = np.arange(radial, dtype=np.float64)
    centre = (index + 0.5) * dr
    face = (index + 1.0) * dr
    wall = np.where(index < radial - 1.5, 1.0, 0.0)
    h = theta_step
    nu = VISCOSITY
    rows = np.zeros((COUNT, radial))
    rows[WALL] = wall
    common = -2.0 * nu / dr**2 - 30.0 * nu / (12.0 * AXIAL_STEP**2)
    rows[RADIAL_C] = nu / (2.0 * dr * centre)
    rows[THETA_C] = -1.0 / (12.0 * h * centre)
    rows[CROSS_Z] = 0.25 * rows[THETA_C]
    rows[SECOND_C] = nu / (12.0 * h * h * centre**2)
    rows[CENTRE_Z] = common - 30.0 * rows[SECOND_C]
    rows[CENTRE_T] = rows[CENTRE_Z] - nu / centre**2
    rows[CURVE_T] = 0.25 / centre
    rows[TURN_T] = nu / (h * centre**2)
    rows[RADIAL_F] = nu / (2.0 * dr * face)
    rows[THETA_F] = -0.25 / (12.0 * h * face)
    rows[SECOND_F] = nu / (12.0 * h * h * face**2)
    rows[CENTRE_R] = common - 30.0 * rows[SECOND_F] - nu / face**2
    rows[CURVE_R] = 1.0 / (16.0 * face)
    rows[TURN_R] = -nu / (h * face**2)
    return np.broadcast_to(rows[:, None, :], (COUNT, 8, radial)).astype(np.float32)


class Cells:
    def __init__(self, vel, j, k):
        self.vel, self.j, self.k, self.known = vel, j, k, {}

    def once(self, key, make):
        if key not in self.known:
            self.known[key] = make()
        return self.known[key]

    def at(self, n, dj, dk=0):
        rows = pl.ds(self.k + PAD + dk, 8)
        return self.once((n, dj, dk), lambda: self.vel[n, self.j + HALO + dj, rows, :])

    def turned(self, by, n, dj, dk=0):
        return self.once(
            (by, n, dj, dk), lambda: pltpu.roll(self.at(n, dj, dk), by % self.vel.shape[3], 1)
        )

    def pair(self, by, n, dj, dk=0):
        return self.once(
            ("pair", n, dj, dk), lambda: self.at(n, dj, dk) + self.turned(by, n, dj, dk)
        )

    def beside(self, dj, dk):
        n = 1 if dk >= 0 else 2
        other = (1, dj - 1, dk) if n == 1 else (2, dj, dk)
        here = (1, dj, dk) if n == 1 else (2, dj, dk + 1)
        return self.once(("sum", n, dj, dk), lambda: self.at(*other) + self.at(*here))


def terms(cells, ghost, coef, q, dr):
    at, turned, pair = cells.at, cells.turned, cells.pair
    a, b, c = (at(n, q) for n in range(3))
    lane = lax.broadcasted_iota(jnp.int32, a.shape, 1)
    first_lane = lane == 0
    last_lane = lane == a.shape[1] - 1

    nu = VISCOSITY
    lap = nu / dr**2
    adv_z = -1.0 / (12.0 * AXIAL_STEP)
    vis_z = nu / (12.0 * AXIAL_STEP**2)

    def differences(p1, m1, p2, m2):
        return 8.0 * (p1 - m1) - (p2 - m2), 16.0 * (p1 + m1) - (p2 + m2)

    def pieces(n):
        over = differences(*(at(n, q + d) for d in (1, -1, 2, -2)))
        along = differences(*(at(n, q, d) for d in (1, -1, 2, -2)))
        return over, along

    def below(n):
        if ghost is not None and n > 0 and q % 2 == 0:
            x = jnp.where(last_lane, ghost(n, q + 1), at(n, q))
            return pltpu.roll(x, 1, 1)
        x = turned(1, n, q)
        if ghost is not None:
            return jnp.where(first_lane, ghost(n, q), x)
        return x if n == 0 else jnp.where(first_lane, 0.0, x)

    def above(n):
        return jnp.where(last_lane, -at(n, q), turned(-1, n, q))

    pair_a, pair_side, pair_next = pair(1, 0, q), pair(1, 0, q + 1), pair(1, 0, q, 1)
    pair_b, pair_back = pair(-1, 1, q), pair(-1, 1, q - 1)

    theta, axial = pieces(2)
    up, low = above(2), below(2)
    u_r = pair_a + pair_next
    u_t = cells.beside(q, 0) + cells.beside(q, 1)
    h_z = (up - low) * (coef[RADIAL_C] - u_r * (0.125 / dr)) + (up + low) * lap
    h_z = h_z + theta[0] * (u_t * coef[CROSS_Z])
    h_z = h_z + (theta[1] * coef[SECOND_C] + axial[1] * vis_z)
    h_z = h_z + c * (coef[CENTRE_Z] + axial[0] * adv_z)

    theta, axial = pieces(1)
    up, low = above(1), below(1)
    u_r = pair_a + pair_side
    u_z = cells.beside(q, -1) + cells.beside(q + 1, -1)
    h_t = (up - low) * (coef[RADIAL_C] - u_r * (0.125 / dr)) + (up + low) * lap
    h_t = h_t + b * (coef[CENTRE_T] + theta[0] * coef[THETA_C] - u_r * coef[CURVE_T])
    h_t = h_t + (theta[1] * coef[SECOND_C] + axial[1] * vis_z)
    h_t = h_t + axial[0] * (u_z * (0.25 * adv_z))
    h_t = h_t + (pair_side - pair_a) * coef[TURN_T]

    theta, axial = pieces(0)
    up, low = turned(-1, 0, q), below(0)
    u_t = pair_b + pair_back
    u_z = pair(-1, 2, q) + pair(-1, 2, q, -1)
    h_r = (up - low) * (coef[RADIAL_F] - a * (0.5 / dr)) + (up + low) * lap
    h_r = h_r + u_t * (u_t * coef[CURVE_R] + theta[0] * coef[THETA_F])
    h_r = h_r + (theta[1] * coef[SECOND_F] + axial[1] * vis_z)
    h_r = h_r + (axial[0] * (u_z * (0.25 * adv_z)) + a * coef[CENTRE_R])
    h_r = h_r + (pair_b - pair_back) * coef[TURN_R]
    return h_r, h_t, h_z


def lane_zero_terms(cells, ghost, coef, q, dr):
    lap = VISCOSITY / dr**2
    a = cells.at(0, q)
    first_lane = lax.broadcasted_iota(jnp.int32, a.shape, 1) == 0
    add_r = ghost(0, q) * (lap - coef[RADIAL_F] + a * (0.5 / dr))
    add_t = ghost(1, q) * (lap - coef[RADIAL_C] + (a + cells.at(0, q + 1)) * (0.125 / dr))
    add_z = ghost(2, q) * (lap - coef[RADIAL_C] + (a + cells.at(0, q, 1)) * (0.125 / dr))
    return tuple(jnp.where(first_lane, x, 0.0) for x in (add_r, add_t, add_z))


def wall_mask(rows, radial):
    lane = lax.broadcasted_iota(jnp.int32, (rows, radial), 1)
    return jnp.where(lane == radial - 1, 0.0, 1.0).astype(jnp.float32)


def first_pass(theta_step, v_ref, vel_ref, low_ref, high_ref, inner_ref, pay_ref, sems):
    _, planes, axial, radial = v_ref.shape
    lane = lax.broadcasted_iota(jnp.int32, (8, radial), 1)
    sign = jnp.where(lane < 2 * planes, -1.0, 1.0).astype(jnp.float32)
    wall = wall_mask(8, radial)
    rate_t = (radial / theta_step) / (lane.astype(jnp.float32) + 0.5)

    def fetch(g):
        part = pl.ds(g * GROUP, GROUP)
        target = vel_ref.at[:, pl.ds(g * GROUP + HALO, GROUP), pl.ds(PAD, axial)]
        return pltpu.make_async_copy(v_ref.at[:, part], target, sems.at[g])

    for g in range(planes // GROUP):
        fetch(g).start()

    zero = jnp.zeros((8, radial), jnp.float32)
    largest = (zero,) * 4
    for g in range(planes // GROUP):
        fetch(g).wait()

        def rows(i, largest, g=g):
            k = pl.multiple_of(i * 8, 8)
            largest = list(largest)
            inner = [zero] * 3
            for q in range(GROUP):
                j = g * GROUP + q
                cells = [vel_ref[n, j + HALO, pl.ds(k + PAD, 8), :] for n in range(3)]
                for n, x in enumerate(cells):
                    place = n * planes + j
                    x = pltpu.roll(x, place, 1) if place else x
                    inner[n] = jnp.where(lane == place, x, inner[n])
                a, b, c = cells
                a = a * wall
                vel_ref[0, j + HALO, pl.ds(k + PAD, 8), :] = a
                rate = jnp.abs(a) * float(radial) + jnp.abs(b) * rate_t
                rate = rate + jnp.abs(c) * (1.0 / AXIAL_STEP)
                largest[q % 4] = jnp.maximum(largest[q % 4], rate)
            inner = (inner[0] + inner[1] + inner[2]) * sign
            if g > 0:
                inner = inner_ref[pl.ds(k, 8), :] + inner
            inner_ref[pl.ds(k, 8), :] = inner
            return tuple(largest)

        largest = lax.fori_loop(0, axial // 8, rows, largest, unroll=UNROLL)
        for q in range(GROUP):
            for n in range(3):
                j = g * GROUP + q
                low_ref[n, j] = vel_ref[n, j + HALO, PAD : PAD + 2, :]
                high_ref[n, j] = vel_ref[n, j + HALO, PAD + axial - 2 : PAD + axial, :]

    largest = jnp.maximum(
        jnp.maximum(largest[0], largest[1]), jnp.maximum(largest[2], largest[3])
    )
    top = jnp.max(largest, axis=(0, 1), keepdims=True)
    pay_ref[...] = jnp.broadcast_to(top, pay_ref.shape)
    last = lax.broadcasted_iota(jnp.int32, (2, radial), 1) == radial - 1
    for ref in (low_ref, high_ref):
        ref[0, 0] = jnp.where(last, top, ref[0, 0])


def fold(low_ref, high_ref, pay_ref, inner_in, vel_in, *refs):
    del vel_in
    fars, (out_ref, inner_ref, vel_ref) = refs[2:-3], refs[-3:]
    planes = low_ref.shape[1]
    axial, radial = inner_in.shape
    lane = lax.broadcasted_iota(jnp.int32, (1, radial), 1)
    top = jnp.maximum(low_ref[0, 0, 0:1, :], high_ref[0, 0, 0:1, :])
    top = jnp.max(jnp.where(lane == radial - 1, top, 0.0), axis=(0, 1), keepdims=True)
    top = jnp.maximum(pay_ref[...], top)
    for far in fars:
        top = jnp.maximum(top, far[...])
    out_ref[...] = top
    out_ref[1:2, :] = high_ref[1, planes - 1, 0:1, :]
    out_ref[2:3, :] = low_ref[2, 0, 1:2, :]
    lane = lax.broadcasted_iota(jnp.int32, top.shape, 1)
    inner_ref[...] = inner_in[...]
    inner_ref[0:8, :] = jnp.where(lane == radial - 1, top, inner_in[0:8, :])
    wall = wall_mask(2, radial)

    def plane(j, carry):
        for n in range(3):
            mask = wall if n == 0 else 1.0
            vel_ref[n, j + HALO, PAD - 2 : PAD, :] = low_ref[n, j] * mask
            vel_ref[n, j + HALO, PAD + axial : PAD + axial + 2, :] = high_ref[n, j] * mask
        return carry

    lax.fori_loop(0, planes, plane, 0, unroll=4)


def with_partner(pay_ref, inner_ref, _, out_ref):
    lane = lax.broadcasted_iota(jnp.int32, (1, inner_ref.shape[1]), 1)
    top = jnp.where(lane == inner_ref.shape[1] - 1, inner_ref[0:1, :], 0.0)
    top = jnp.maximum(jnp.max(top, axis=(0, 1), keepdims=True), pay_ref[0:1, :])
    row = lax.broadcasted_iota(jnp.int32, out_ref.shape, 0)
    out_ref[...] = jnp.where(row == 0, top, pay_ref[...])


def theta_rest(vel_ref, *refs):
    head_ref, tail_ref = refs[-2:]
    planes, axial = vel_ref.shape[1] - 2 * HALO, head_ref.shape[2]
    for n in (1, 2):
        for q in range(HALO):
            head_ref[n - 1, q] = vel_ref[n, HALO + q, pl.ds(PAD, axial), :]
            tail_ref[n - 1, q] = vel_ref[n, planes + q, pl.ds(PAD, axial), :]


def ghosts(cells, inner, planes):
    radial = inner.shape[1]

    def ghost(n, q):
        turn = lax.rem(2 * radial - n * planes - q - cells.j, radial)
        return cells.once(("ghost", n, q), lambda: pltpu.roll(inner, turn, 1))

    return ghost


def sweep(vel_ref, inner_ref, coef_ref, first, last, write, after=None):
    planes = vel_ref.shape[1] - 2 * HALO
    axial, radial = vel_ref.shape[2] - 2 * PAD, vel_ref.shape[3]
    size = math.gcd(BLOCK, last - first)

    def block(m, carry):
        j = first + m * size

        def rows(i, carry):
            k = pl.multiple_of(i * 8, 8)
            coef = [coef_ref[n] for n in range(COUNT)]
            cells = Cells(vel_ref, j, k)
            ghost = None
            if inner_ref is not None:
                ghost = ghosts(cells, inner_ref[pl.ds(k, 8), :], planes)
            found = [terms(cells, ghost, coef, q, 1.0 / radial) for q in range(size)]
            for q, values in enumerate(found):
                for n, value in enumerate(values):
                    write(n, j + q, pl.ds(k, 8), value)
            return carry

        lax.fori_loop(0, axial // 8, rows, 0)
        if after is not None:
            after(j, size)
        return carry

    lax.fori_loop(0, (last - first) // size, block, 0)


def ahead(first, last, vel_ref, coef_ref, _, out_ref):
    def write(n, j, k, value):
        out_ref[n, j - first, k, :] = value

    sweep(vel_ref, None, coef_ref, first, last, write)


def ahead_with_ghosts(first, last, vel_ref, inner_ref, coef_ref, _, out_ref):
    def write(n, j, k, value):
        out_ref[n, j - first, k, :] = value

    sweep(vel_ref, inner_ref, coef_ref, first, last, write)


def stores(res, base, out_ref, sems):
    def copy(j):
        return pltpu.make_async_copy(res.at[:, j - base], out_ref.at[:, j], sems.at[j - base])

    def start(j, size):
        for q in range(size):
            copy(j + q).start()

    def wait(first, last):
        def one(j, carry):
            copy(j).wait()
            return carry

        lax.fori_loop(first, last, one, 0)

    return start, wait


def interior(
    spans, count, vel_ref, inner_ref, coef_ref, part_a, part_b, *refs
):
    tops, (out_ref, step_ref, res, sems) = refs[:count], refs[count:]
    axial, radial = inner_ref.shape
    planes = vel_ref.shape[1] - 2 * HALO
    top = tops[0][0:1, :]
    for ref in tops[1:]:
        top = jnp.maximum(top, ref[0:1, :])
    time_step = CFL_TARGET / (jnp.max(top) + 1e-06)
    step_ref[0] = time_step
    scale = GAMMA * time_step
    base = spans[0][0]
    start, wait = stores(res, base, out_ref, sems)

    def write(n, j, k, value):
        factor = scale * coef_ref[WALL] if n == 0 else scale
        res[n, j - base, k, :] = value * factor

    for part, (first, last), add in ((part_a, spans[0], True), (part_b, spans[1], False)):

        def block(m, carry, part=part, first=first, add=add):
            j = first + m * BLOCK

            def rows(i, carry):
                k = pl.multiple_of(i * 8, 8)
                cells = Cells(vel_ref, j, k)
                ghost = ghosts(cells, inner_ref[pl.ds(k, 8), :], planes)
                found = []
                for q in range(BLOCK):
                    values = [part[n, j + q - first, pl.ds(k, 8), :] for n in range(3)]
                    if add:
                        added = lane_zero_terms(cells, ghost, coef_ref, q, 1.0 / radial)
                        values = [x + y for x, y in zip(values, added)]
                    found.append(values)
                for q, values in enumerate(found):
                    for n, value in enumerate(values):
                        write(n, j + q, pl.ds(k, 8), value)
                return carry

            lax.fori_loop(0, axial // 8, rows, 0, unroll=2)
            start(j, BLOCK)
            return carry

        lax.fori_loop(0, (last - first) // BLOCK, block, 0)

    sweep(vel_ref, inner_ref, coef_ref, *spans[2], write, start)
    wait(spans[0][0], spans[2][1])


def edges(
    step_ref, below_r, above_r, below, above, up_ref, down_ref, inner_ref, coef_ref, vel_in, part,
    out_ref, vel_ref, res, sems,
):
    del vel_in, part
    axial, radial = inner_ref.shape
    planes = vel_ref.shape[1] - 2 * HALO
    scale = GAMMA * step_ref[0]
    cells = pl.ds(PAD, axial)
    for q in range(HALO):
        for first, rest, place in (
            (below_r, below, q),
            (above_r, above, HALO + planes + q),
        ):
            vel_ref[0, place, cells, :] = first[q] * coef_ref[WALL, 0:1, :]
            vel_ref[1, place, cells, :] = rest[0, q]
            vel_ref[2, place, cells, :] = rest[1, q]
    vel_ref[1, HALO - 1, PAD + axial : PAD + axial + 1, :] = up_ref[1:2, :]
    vel_ref[2, HALO + planes, PAD - 1 : PAD, :] = down_ref[2:3, :]
    for side, first in enumerate((0, planes - HALO)):
        base = first - side * HALO
        start, _ = stores(res, base, out_ref, sems)

        def write(n, j, k, value, base=base):
            factor = scale * coef_ref[WALL] if n == 0 else scale
            res[n, j - base, k, :] = value * factor

        sweep(vel_ref, inner_ref, coef_ref, first, first + HALO, write, start)
    for side, first in enumerate((0, planes - HALO)):
        stores(res, first - side * HALO, out_ref, sems)[1](first, first + HALO)


def shifted(block, distance):
    sizes = lax.axis_size("az"), lax.axis_size("ax")
    route = []
    for i in range(sizes[0]):
        for k in range(sizes[1]):
            source = (i - distance[0]) % sizes[0], (k - distance[1]) % sizes[1]
            route.append((source[0] * sizes[1] + source[1], i * sizes[1] + k))
    return lax.ppermute(block, ("az", "ax"), route)


def cuts(planes):
    ends = (HALO, HALO + BLOCK, HALO + 2 * BLOCK, planes - HALO)
    return list(zip(ends[:-1], ends[1:]))


def per_device(velocity):
    _, planes, axial, radial = velocity.shape
    sizes = lax.axis_size("az"), lax.axis_size("ax")
    theta_step = 2.0 * math.pi / (sizes[0] * planes)
    coef = jnp.asarray(coefficients(radial, theta_step))
    f32 = jnp.float32
    anywhere = pl.BlockSpec(memory_space=pl.ANY)
    vmem = pl.BlockSpec(memory_space=pltpu.VMEM)
    smem = pl.BlockSpec(memory_space=pltpu.SMEM)

    def shape(*sizes):
        return jax.ShapeDtypeStruct(sizes, f32)

    def call(kernel, name, work, scratch=0, **kwargs):
        return pl.pallas_call(
            kernel,
            name=name,
            compiler_params=pltpu.CompilerParams(vmem_limit_bytes=(4 + scratch) * 2**20),
            cost_estimate=pl.CostEstimate(flops=work, bytes_accessed=work, transcendentals=0),
            **kwargs,
        )

    below_r = shifted(velocity[0, planes - HALO :], (1, 0))
    above_r = shifted(velocity[0, :HALO], (-1, 0))

    edge = shape(3, planes, 2, radial)
    padded = shape(3, planes + 2 * HALO, axial + 2 * PAD, radial)
    row = shape(axial, radial)
    tile = shape(8, radial)
    vel, first, last, inner, pay = call(
        functools.partial(first_pass, theta_step),
        "first_pass",
        0,
        out_shape=(padded, edge, edge, row, tile),
        in_specs=[anywhere],
        out_specs=(vmem,) * 5,
        scratch_shapes=[pltpu.SemaphoreType.DMA((planes // GROUP,))],
    )(pltpu.with_memory_space_constraint(velocity, pltpu.HBM))
    low = shifted(last, (0, 1))
    high = shifted(first, (0, -1))
    fars = [shifted(pay, (0, step)) for step in range(2, sizes[1] - 1)]
    pay, inner, vel = call(
        fold,
        "fold",
        0,
        out_shape=(tile, row, padded),
        in_specs=[vmem] * (7 + len(fars)),
        out_specs=(vmem,) * 3,
        input_output_aliases={4: 2},
    )(low, high, pay, inner, vel, below_r, above_r, *fars)
    inner = shifted(inner, (sizes[0] // 2, 0))

    spans = cuts(planes)
    part_shape = shape(3, BLOCK, axial, radial)
    part_a = call(
        functools.partial(ahead, *spans[0]),
        "ahead",
        velocity.size,
        out_shape=part_shape,
        in_specs=[vmem] * 3,
        out_specs=vmem,
    )(vel, coef, pay)
    pay = call(
        with_partner,
        "with_partner",
        0,
        out_shape=tile,
        in_specs=[vmem] * 3,
        out_specs=vmem,
    )(pay, inner, part_a)
    up = shifted(pay, (1, 0))
    down = shifted(pay, (-1, 0))
    others, near = [], {(i + s) % sizes[0] for i in (0, sizes[0] // 2) for s in (-1, 0, 1)}
    while len(near) < sizes[0]:
        step = min(set(range(sizes[0])) - near)
        others.append(shifted(pay, (step, 0)))
        near |= {step, (step + sizes[0] // 2) % sizes[0]}
    part_b = call(
        functools.partial(ahead_with_ghosts, *spans[1]),
        "ahead_with_ghosts",
        velocity.size,
        out_shape=part_shape,
        in_specs=[vmem] * 4,
        out_specs=vmem,
    )(vel, inner, coef, pay)
    pair = shape(2, HALO, axial, radial)
    head, tail = call(
        theta_rest,
        "theta_rest",
        0,
        out_shape=(pair, pair),
        in_specs=[vmem] * (4 + len(others)),
        out_specs=(vmem, vmem),
    )(vel, up, down, *others, part_b)
    below = shifted(tail, (1, 0))
    above = shifted(head, (-1, 0))
    tops = (pay, up, down, *others)
    part, time_step = call(
        functools.partial(interior, spans, len(tops)),
        "interior",
        4 * velocity.size,
        scratch=6,
        out_shape=(shape(*velocity.shape), shape(1)),
        in_specs=[vmem] * (5 + len(tops)),
        out_specs=(anywhere, smem),
        scratch_shapes=[
            pltpu.VMEM((3, planes - 2 * HALO, axial, radial), f32),
            pltpu.SemaphoreType.DMA((planes - 2 * HALO,)),
        ],
    )(vel, inner, coef, part_a, part_b, *tops)
    increment, _ = call(
        edges,
        "edges",
        0,
        scratch=2,
        out_shape=(shape(*velocity.shape), padded),
        in_specs=[smem] + [vmem] * 9 + [anywhere],
        out_specs=(anywhere, vmem),
        scratch_shapes=[
            pltpu.VMEM((3, 2 * HALO, axial, radial), f32),
            pltpu.SemaphoreType.DMA((2 * HALO,)),
        ],
        input_output_aliases={9: 1, 10: 0},
    )(time_step, below_r, above_r, below, above, up, down, inner, coef, vel, part)
    return increment, time_step.reshape(())


def solution(mesh):
    return jax.shard_map(
        per_device,
        mesh=mesh,
        in_specs=(P(None, "az", "ax", None),),
        out_specs=(P(None, "az", "ax", None), P()),
        check_vma=False,
    )
```

```python
import functools
import math

import jax
import jax.numpy as jnp
import numpy as np
from jax import lax
from jax.experimental import pallas as pl
from jax.experimental.pallas import tpu as pltpu
from jax.sharding import PartitionSpec as P

AXIAL_STEP = 0.01
VISCOSITY = 0.001
CFL_TARGET = 1.2
GAMMA = 8.0 / 15.0

PAD = 8
HALO = 2
BLOCK = 4
GROUP = 4
UNROLL = 4

(
    WALL,
    RADIAL_C,
    THETA_C,
    CROSS_Z,
    SECOND_C,
    CENTRE_Z,
    CENTRE_T,
    CURVE_T,
    TURN_T,
    RADIAL_F,
    THETA_F,
    SECOND_F,
    CENTRE_R,
    CURVE_R,
    TURN_R,
    COUNT,
) = range(16)


def coefficients(radial, theta_step):
    dr = 1.0 / radial
    index = np.arange(radial, dtype=np.float64)
    centre = (index + 0.5) * dr
    face = (index + 1.0) * dr
    wall = np.where(index < radial - 1.5, 1.0, 0.0)
    h = theta_step
    nu = VISCOSITY
    rows = np.zeros((COUNT, radial))
    rows[WALL] = wall
    common = -2.0 * nu / dr**2 - 30.0 * nu / (12.0 * AXIAL_STEP**2)
    rows[RADIAL_C] = nu / (2.0 * dr * centre)
    rows[THETA_C] = -1.0 / (12.0 * h * centre)
    rows[CROSS_Z] = 0.25 * rows[THETA_C]
    rows[SECOND_C] = nu / (12.0 * h * h * centre**2)
    rows[CENTRE_Z] = common - 30.0 * rows[SECOND_C]
    rows[CENTRE_T] = rows[CENTRE_Z] - nu / centre**2
    rows[CURVE_T] = 0.25 / centre
    rows[TURN_T] = nu / (h * centre**2)
    rows[RADIAL_F] = nu / (2.0 * dr * face)
    rows[THETA_F] = -0.25 / (12.0 * h * face)
    rows[SECOND_F] = nu / (12.0 * h * h * face**2)
    rows[CENTRE_R] = common - 30.0 * rows[SECOND_F] - nu / face**2
    rows[CURVE_R] = 1.0 / (16.0 * face)
    rows[TURN_R] = -nu / (h * face**2)
    return np.broadcast_to(rows[:, None, :], (COUNT, 8, radial)).astype(np.float32)


class Cells:
    def __init__(self, vel, j, k):
        self.vel, self.j, self.k, self.known = vel, j, k, {}

    def once(self, key, make):
        if key not in self.known:
            self.known[key] = make()
        return self.known[key]

    def at(self, n, dj, dk=0):
        rows = pl.ds(self.k + PAD + dk, 8)
        return self.once((n, dj, dk), lambda: self.vel[n, self.j + HALO + dj, rows, :])

    def turned(self, by, n, dj, dk=0):
        return self.once(
            (by, n, dj, dk), lambda: pltpu.roll(self.at(n, dj, dk), by % self.vel.shape[3], 1)
        )

    def pair(self, by, n, dj, dk=0):
        return self.once(
            ("pair", n, dj, dk), lambda: self.at(n, dj, dk) + self.turned(by, n, dj, dk)
        )

    def beside(self, dj, dk):
        n = 1 if dk >= 0 else 2
        other = (1, dj - 1, dk) if n == 1 else (2, dj, dk)
        here = (1, dj, dk) if n == 1 else (2, dj, dk + 1)
        return self.once(("sum", n, dj, dk), lambda: self.at(*other) + self.at(*here))


def terms(cells, ghost, coef, q, dr):
    at, turned, pair = cells.at, cells.turned, cells.pair
    a, b, c = (at(n, q) for n in range(3))
    lane = lax.broadcasted_iota(jnp.int32, a.shape, 1)
    first_lane = lane == 0
    last_lane = lane == a.shape[1] - 1

    nu = VISCOSITY
    lap = nu / dr**2
    adv_z = -1.0 / (12.0 * AXIAL_STEP)
    vis_z = nu / (12.0 * AXIAL_STEP**2)

    def differences(p1, m1, p2, m2):
        return 8.0 * (p1 - m1) - (p2 - m2), 16.0 * (p1 + m1) - (p2 + m2)

    def pieces(n):
        over = differences(*(at(n, q + d) for d in (1, -1, 2, -2)))
        along = differences(*(at(n, q, d) for d in (1, -1, 2, -2)))
        return over, along

    def below(n):
        if ghost is not None and n > 0 and q % 2 == 0:
            x = jnp.where(last_lane, ghost(n, q + 1), at(n, q))
            return pltpu.roll(x, 1, 1)
        x = turned(1, n, q)
        if ghost is not None:
            return jnp.where(first_lane, ghost(n, q), x)
        return x if n == 0 else jnp.where(first_lane, 0.0, x)

    def above(n):
        return jnp.where(last_lane, -at(n, q), turned(-1, n, q))

    pair_a, pair_side, pair_next = pair(1, 0, q), pair(1, 0, q + 1), pair(1, 0, q, 1)
    pair_b, pair_back = pair(-1, 1, q), pair(-1, 1, q - 1)

    theta, axial = pieces(2)
    up, low = above(2), below(2)
    u_r = pair_a + pair_next
    u_t = cells.beside(q, 0) + cells.beside(q, 1)
    h_z = (up - low) * (coef[RADIAL_C] - u_r * (0.125 / dr)) + (up + low) * lap
    h_z = h_z + theta[0] * (u_t * coef[CROSS_Z])
    h_z = h_z + (theta[1] * coef[SECOND_C] + axial[1] * vis_z)
    h_z = h_z + c * (coef[CENTRE_Z] + axial[0] * adv_z)

    theta, axial = pieces(1)
    up, low = above(1), below(1)
    u_r = pair_a + pair_side
    u_z = cells.beside(q, -1) + cells.beside(q + 1, -1)
    h_t = (up - low) * (coef[RADIAL_C] - u_r * (0.125 / dr)) + (up + low) * lap
    h_t = h_t + b * (coef[CENTRE_T] + theta[0] * coef[THETA_C] - u_r * coef[CURVE_T])
    h_t = h_t + (theta[1] * coef[SECOND_C] + axial[1] * vis_z)
    h_t = h_t + axial[0] * (u_z * (0.25 * adv_z))
    h_t = h_t + (pair_side - pair_a) * coef[TURN_T]

    theta, axial = pieces(0)
    up, low = turned(-1, 0, q), below(0)
    u_t = pair_b + pair_back
    u_z = pair(-1, 2, q) + pair(-1, 2, q, -1)
    h_r = (up - low) * (coef[RADIAL_F] - a * (0.5 / dr)) + (up + low) * lap
    h_r = h_r + u_t * (u_t * coef[CURVE_R] + theta[0] * coef[THETA_F])
    h_r = h_r + (theta[1] * coef[SECOND_F] + axial[1] * vis_z)
    h_r = h_r + (axial[0] * (u_z * (0.25 * adv_z)) + a * coef[CENTRE_R])
    h_r = h_r + (pair_b - pair_back) * coef[TURN_R]
    return h_r, h_t, h_z


def lane_zero_terms(cells, ghost, coef, q, dr):
    lap = VISCOSITY / dr**2
    a = cells.at(0, q)
    first_lane = lax.broadcasted_iota(jnp.int32, a.shape, 1) == 0
    add_r = ghost(0, q) * (lap - coef[RADIAL_F] + a * (0.5 / dr))
    add_t = ghost(1, q) * (lap - coef[RADIAL_C] + (a + cells.at(0, q + 1)) * (0.125 / dr))
    add_z = ghost(2, q) * (lap - coef[RADIAL_C] + (a + cells.at(0, q, 1)) * (0.125 / dr))
    return tuple(jnp.where(first_lane, x, 0.0) for x in (add_r, add_t, add_z))


def wall_mask(rows, radial):
    lane = lax.broadcasted_iota(jnp.int32, (rows, radial), 1)
    return jnp.where(lane == radial - 1, 0.0, 1.0).astype(jnp.float32)


def first_pass(theta_step, v_ref, vel_ref, low_ref, high_ref, pay_ref, sems):
    _, planes, axial, radial = v_ref.shape
    lane = lax.broadcasted_iota(jnp.int32, (8, radial), 1)
    wall = wall_mask(8, radial)
    rate_t = (radial / theta_step) / (lane.astype(jnp.float32) + 0.5)

    def fetch(g):
        part = pl.ds(g * GROUP, GROUP)
        target = vel_ref.at[:, pl.ds(g * GROUP + HALO, GROUP), pl.ds(PAD, axial)]
        return pltpu.make_async_copy(v_ref.at[:, part], target, sems.at[g])

    for g in range(planes // GROUP):
        fetch(g).start()

    def group(g, largest):
        fetch(g).wait()

        def rows(i, largest):
            k = pl.ds(pl.multiple_of(i * 8, 8) + PAD, 8)
            largest = list(largest)
            for q in range(GROUP):
                j = g * GROUP + HALO + q
                a, b, c = (vel_ref[n, j, k, :] for n in range(3))
                a = a * wall
                vel_ref[0, j, k, :] = a
                rate = jnp.abs(a) * float(radial) + jnp.abs(b) * rate_t
                rate = rate + jnp.abs(c) * (1.0 / AXIAL_STEP)
                largest[q % 4] = jnp.maximum(largest[q % 4], rate)
            return tuple(largest)

        largest = lax.fori_loop(0, axial // 8, rows, largest, unroll=4)
        for q in range(GROUP):
            for n in range(3):
                j = g * GROUP + q
                low_ref[n, j] = vel_ref[n, j + HALO, PAD : PAD + 2, :]
                high_ref[n, j] = vel_ref[n, j + HALO, PAD + axial - 2 : PAD + axial, :]
        return largest

    zero = jnp.zeros((8, radial), jnp.float32)
    m = lax.fori_loop(0, planes // GROUP, group, (zero,) * 4)
    largest = jnp.maximum(jnp.maximum(m[0], m[1]), jnp.maximum(m[2], m[3]))
    top = jnp.max(largest, axis=(0, 1), keepdims=True)
    pay_ref[...] = jnp.broadcast_to(top, pay_ref.shape)
    last = lax.broadcasted_iota(jnp.int32, (2, radial), 1) == radial - 1
    for ref in (low_ref, high_ref):
        ref[0, 0] = jnp.where(last, top, ref[0, 0])


def pack(vel_ref, inner_ref):
    planes, (axial, radial) = vel_ref.shape[1] - 2 * HALO, inner_ref.shape
    lane = lax.broadcasted_iota(jnp.int32, (8, radial), 1)
    sign = jnp.where(lane < 2 * planes, -1.0, 1.0).astype(jnp.float32)

    def rows(i, carry):
        k = pl.multiple_of(i * 8, 8)
        inner = [jnp.zeros((8, radial), jnp.float32)] * 3
        for j in range(planes):
            for n in range(3):
                place = n * planes + j
                x = vel_ref[n, j + HALO, pl.ds(k + PAD, 8), :]
                x = pltpu.roll(x, place, 1)
                inner[n] = jnp.where(lane == place, x, inner[n])
        inner_ref[pl.ds(k, 8), :] = (inner[0] + inner[1] + inner[2]) * sign
        return carry

    lax.fori_loop(0, axial // 8, rows, 0)


def fold(low_ref, high_ref, pay_ref, inner_in, vel_in, *refs):
    del vel_in
    fars, (inner_ref, vel_ref) = refs[:-2], refs[-2:]
    planes = low_ref.shape[1]
    axial, radial = inner_in.shape
    lane = lax.broadcasted_iota(jnp.int32, (1, radial), 1)
    top = jnp.maximum(low_ref[0, 0, 0:1, :], high_ref[0, 0, 0:1, :])
    top = jnp.max(jnp.where(lane == radial - 1, top, 0.0), axis=(0, 1), keepdims=True)
    top = jnp.maximum(pay_ref[...], top)
    for far in fars:
        top = jnp.maximum(top, far[...])
    lane = lax.broadcasted_iota(jnp.int32, top.shape, 1)
    inner_ref[...] = inner_in[...]
    inner_ref[0:8, :] = jnp.where(lane == radial - 1, top, inner_in[0:8, :])
    wall = wall_mask(2, radial)

    def plane(j, carry):
        for n in range(3):
            mask = wall if n == 0 else 1.0
            vel_ref[n, j + HALO, PAD - 2 : PAD, :] = low_ref[n, j] * mask
            vel_ref[n, j + HALO, PAD + axial : PAD + axial + 2, :] = high_ref[n, j] * mask
        return carry

    lax.fori_loop(0, planes, plane, 0, unroll=4)


def theta_in(below_ref, above_ref, inner_in, vel_in, _, tile_ref, inner_ref, vel_ref):
    del vel_in
    planes = vel_ref.shape[1] - 2 * HALO
    axial, radial = inner_in.shape
    cells = pl.ds(PAD, axial)
    wall = wall_mask(1, radial)
    for q in range(HALO):
        for ref, place in ((below_ref, q), (above_ref, HALO + planes + q)):
            vel_ref[0, place, cells, :] = ref[0, q] * wall
            vel_ref[1, place, cells, :] = ref[1, q]
            vel_ref[2, place, cells, :] = ref[2, q]
    tile_ref[...] = jnp.zeros_like(tile_ref)
    tile_ref[1:2, :] = below_ref[1, HALO - 1, 0:1, :]
    tile_ref[2:3, :] = above_ref[2, 0, axial - 1 : axial, :]
    inner_ref[...] = inner_in[...]


def corners_in(mine_ref, inner_ref, next_ref, back_ref, vel_in, _, top_ref, vel_ref):
    del vel_in
    planes = vel_ref.shape[1] - 2 * HALO
    axial, radial = inner_ref.shape
    vel_ref[1, HALO - 1, PAD + axial : PAD + axial + 1, :] = next_ref[1:2, :]
    vel_ref[2, HALO + planes, PAD - 1 : PAD, :] = back_ref[2:3, :]
    lane = lax.broadcasted_iota(jnp.int32, (1, radial), 1)
    top = jnp.maximum(mine_ref[0:1, :], inner_ref[0:1, :])
    top = jnp.max(jnp.where(lane == radial - 1, top, 0.0), axis=(0, 1), keepdims=True)
    top_ref[...] = jnp.broadcast_to(top, top_ref.shape)


def ghosts(cells, inner, planes):
    radial = inner.shape[1]

    def ghost(n, q):
        turn = -(n * planes + q + cells.j) % radial
        return cells.once(("ghost", n, q), lambda: pltpu.roll(inner, turn, 1) if turn else inner)

    return ghost


def block_terms(vel_ref, inner_ref, coef_ref, j, size, write):
    planes = vel_ref.shape[1] - 2 * HALO
    axial, radial = vel_ref.shape[2] - 2 * PAD, vel_ref.shape[3]
    groups = 2 * BLOCK // size

    def rows(i, carry):
        coef = [coef_ref[n] for n in range(COUNT)]
        found = []
        for u in range(groups):
            k = pl.multiple_of((i * groups + u) * 8, 8)
            cells = Cells(vel_ref, j, k)
            ghost = None
            if inner_ref is not None:
                ghost = ghosts(cells, inner_ref[pl.ds(k, 8), :], planes)
            for q in range(size):
                found.append((q, k, terms(cells, ghost, coef, q, 1.0 / radial)))
        for q, k, values in found:
            for n, value in enumerate(values):
                write(n, j + q, pl.ds(k, 8), value)
        return carry

    lax.fori_loop(0, axial // (8 * groups), rows, 0)


def ahead(first, last, vel_ref, coef_ref, _, out_ref):
    def write(n, j, k, value):
        out_ref[n, j - first, k, :] = value

    def block(m, carry):
        block_terms(vel_ref, None, coef_ref, first + m * BLOCK, BLOCK, write)
        return carry

    lax.fori_loop(0, (last - first) // BLOCK, block, 0)


def rest(first, last, vel_ref, inner_ref, coef_ref, _, out_ref):
    planes = vel_ref.shape[1] - 2 * HALO
    runs = [(j, BLOCK, j - first) for j in range(first, last, BLOCK)]
    runs += [(0, HALO, last - first), (planes - HALO, HALO, last - first + HALO)]
    for j, size, place in runs:

        def write(n, plane, k, value, shift=place - j):
            out_ref[n, plane + shift, k, :] = value

        block_terms(vel_ref, inner_ref, coef_ref, j, size, write)


def finish(spans, count, vel_ref, inner_ref, coef_ref, part_a, part_b, part_c, *refs):
    tops, (out_ref, step_ref, res, sems) = refs[:count], refs[count:]
    axial, radial = inner_ref.shape
    planes = vel_ref.shape[1] - 2 * HALO
    top = tops[0][0:1, :]
    for ref in tops[1:]:
        top = jnp.maximum(top, ref[0:1, :])
    time_step = CFL_TARGET / (jnp.max(top) + 1e-06)
    step_ref[0] = time_step
    scale = GAMMA * time_step
    factors = (scale * coef_ref[WALL], scale, scale)
    pending = []

    def complete(part, j, size, place, add):
        groups = 2 * BLOCK // size

        def rows(i, carry):
            found = []
            for u in range(groups):
                k = pl.multiple_of((i * groups + u) * 8, 8)
                cells = Cells(vel_ref, j, k)
                ghost = ghosts(cells, inner_ref[pl.ds(k, 8), :], planes) if add else None
                for q in range(size):
                    values = [part[n, place + q, pl.ds(k, 8), :] for n in range(3)]
                    if add:
                        added = lane_zero_terms(cells, ghost, coef_ref, q, 1.0 / radial)
                        values = [x + y for x, y in zip(values, added)]
                    found.append((q, k, values))
            for q, k, values in found:
                for n, value in enumerate(values):
                    res[n, j + q, pl.ds(k, 8), :] = value * factors[n]
            return carry

        lax.fori_loop(0, axial // (8 * groups), rows, 0)
        part_of = pl.ds(j, size)
        copy = pltpu.make_async_copy(
            res.at[:, part_of], out_ref.at[:, part_of], sems.at[len(pending)]
        )
        copy.start()
        pending.append(copy)

    first, last = spans[2]
    for j in range(first, last, BLOCK):
        complete(part_c, j, BLOCK, j - first, False)
    complete(part_c, 0, HALO, last - first, False)
    complete(part_c, planes - HALO, HALO, last - first + HALO, False)
    for part, (first, last) in ((part_a, spans[0]), (part_b, spans[1])):
        for j in range(first, last, BLOCK):
            complete(part, j, BLOCK, j - first, True)
    for copy in pending:
        copy.wait()


def shifted(block, distance):
    sizes = lax.axis_size("az"), lax.axis_size("ax")
    route = []
    for i in range(sizes[0]):
        for k in range(sizes[1]):
            source = (i - distance[0]) % sizes[0], (k - distance[1]) % sizes[1]
            route.append((source[0] * sizes[1] + source[1], i * sizes[1] + k))
    return lax.ppermute(block, ("az", "ax"), route)


def cuts(planes):
    ends = (HALO, planes - HALO - 2 * BLOCK, planes - HALO - BLOCK, planes - HALO)
    return list(zip(ends[:-1], ends[1:]))


def exchanged(block, step):
    sizes = lax.axis_size("az"), lax.axis_size("ax")
    route = []
    for i in range(sizes[0]):
        for k in range(sizes[1]):
            route.append(((i ^ step) * sizes[1] + k, i * sizes[1] + k))
    return lax.ppermute(block, ("az", "ax"), route)


def per_device(velocity):
    _, planes, axial, radial = velocity.shape
    sizes = lax.axis_size("az"), lax.axis_size("ax")
    theta_step = 2.0 * math.pi / (sizes[0] * planes)
    coef = jnp.asarray(coefficients(radial, theta_step))
    f32 = jnp.float32
    anywhere = pl.BlockSpec(memory_space=pl.ANY)
    vmem = pl.BlockSpec(memory_space=pltpu.VMEM)
    smem = pl.BlockSpec(memory_space=pltpu.SMEM)

    def shape(*sizes):
        return jax.ShapeDtypeStruct(sizes, f32)

    def call(kernel, name, work, scratch=0, **kwargs):
        return pl.pallas_call(
            kernel,
            name=name,
            compiler_params=pltpu.CompilerParams(vmem_limit_bytes=(4 + scratch) * 2**20),
            cost_estimate=pl.CostEstimate(flops=work, bytes_accessed=work, transcendentals=0),
            **kwargs,
        )

    below = shifted(velocity[:, planes - HALO :], (1, 0))
    above = shifted(velocity[:, :HALO], (-1, 0))

    edge = shape(3, planes, 2, radial)
    padded = shape(3, planes + 2 * HALO, axial + 2 * PAD, radial)
    row = shape(axial, radial)
    tile = shape(8, radial)
    vel, first, last, pay = call(
        functools.partial(first_pass, theta_step),
        "first_pass",
        0,
        out_shape=(padded, edge, edge, tile),
        in_specs=[anywhere],
        out_specs=(vmem,) * 4,
        scratch_shapes=[pltpu.SemaphoreType.DMA((planes // GROUP,))],
    )(pltpu.with_memory_space_constraint(velocity, pltpu.HBM))
    low = shifted(last, (0, 1))
    high = shifted(first, (0, -1))
    fars = [shifted(pay, (0, step)) for step in range(2, sizes[1] - 1)]
    inner = call(
        pack,
        "pack",
        velocity.size,
        out_shape=row,
        in_specs=[vmem],
        out_specs=vmem,
    )(vel)
    mine, vel = call(
        fold,
        "fold",
        0,
        out_shape=(row, padded),
        in_specs=[vmem] * (5 + len(fars)),
        out_specs=(vmem,) * 2,
        input_output_aliases={4: 1},
    )(low, high, pay, inner, vel, *fars)

    spans = cuts(planes)

    def in_advance(n, vel, token):
        first, last = spans[n]
        return call(
            functools.partial(ahead, first, last),
            f"ahead_{n}",
            velocity.size * (2 - n),
            out_shape=shape(3, last - first, axial, radial),
            in_specs=[vmem] * 3,
            out_specs=vmem,
        )(vel, coef, token)

    part_a = in_advance(0, vel, mine)
    tile_out, mine, vel = call(
        theta_in,
        "theta_in",
        0,
        out_shape=(tile, row, padded),
        in_specs=[vmem] * 5,
        out_specs=(vmem,) * 3,
        input_output_aliases={3: 2},
    )(below, above, mine, vel, part_a)
    inner = exchanged(mine, sizes[0] // 2)
    following = shifted(tile_out, (0, -1))
    preceding = shifted(tile_out, (0, 1))
    part_b = in_advance(1, vel, tile_out)
    top, vel = call(
        corners_in,
        "corners_in",
        0,
        out_shape=(tile, padded),
        in_specs=[vmem] * 6,
        out_specs=(vmem,) * 2,
        input_output_aliases={4: 1},
    )(mine, inner, following, preceding, vel, part_b)
    tops = (top, *(exchanged(top, step) for step in range(1, sizes[0] // 2)))
    first, last = spans[2]
    part_c = call(
        functools.partial(rest, first, last),
        "rest",
        velocity.size,
        out_shape=shape(3, last - first + 2 * HALO, axial, radial),
        in_specs=[vmem] * 4,
        out_specs=vmem,
    )(vel, inner, coef, top)
    return_shape = shape(*velocity.shape)
    increment, time_step = call(
        functools.partial(finish, spans, len(tops)),
        "finish",
        0,
        scratch=8,
        out_shape=(return_shape, shape(1)),
        in_specs=[vmem] * (6 + len(tops)),
        out_specs=(anywhere, smem),
        scratch_shapes=[
            pltpu.VMEM(velocity.shape, f32),
            pltpu.SemaphoreType.DMA(((planes - 2 * HALO) // BLOCK + 2,)),
        ],
    )(vel, inner, coef, part_a, part_b, part_c, *tops)
    return increment, time_step.reshape(())


def solution(mesh):
    return jax.shard_map(
        per_device,
        mesh=mesh,
        in_specs=(P(None, "az", "ax", None),),
        out_specs=(P(None, "az", "ax", None), P()),
        check_vma=False,
    )
```

```python
import functools
import math

import jax
import jax.numpy as jnp
import numpy as np
from jax import lax
from jax.experimental import pallas as pl
from jax.experimental.pallas import tpu as pltpu
from jax.sharding import PartitionSpec as P

AXIAL_STEP = 0.01
VISCOSITY = 0.001
CFL_TARGET = 1.2
GAMMA = 8.0 / 15.0

PAD = 8
HALO = 2
BLOCK = 4
GROUP = 4
UNROLL = 4

(
    WALL,
    RADIAL_C,
    THETA_C,
    CROSS_Z,
    SECOND_C,
    CENTRE_Z,
    CENTRE_T,
    CURVE_T,
    TURN_T,
    RADIAL_F,
    THETA_F,
    SECOND_F,
    CENTRE_R,
    CURVE_R,
    TURN_R,
    COUNT,
) = range(16)


def coefficients(radial, theta_step):
    dr = 1.0 / radial
    index = np.arange(radial, dtype=np.float64)
    centre = (index + 0.5) * dr
    face = (index + 1.0) * dr
    wall = np.where(index < radial - 1.5, 1.0, 0.0)
    h = theta_step
    nu = VISCOSITY
    rows = np.zeros((COUNT, radial))
    rows[WALL] = wall
    common = -2.0 * nu / dr**2 - 30.0 * nu / (12.0 * AXIAL_STEP**2)
    rows[RADIAL_C] = nu / (2.0 * dr * centre)
    rows[THETA_C] = -1.0 / (12.0 * h * centre)
    rows[CROSS_Z] = 0.25 * rows[THETA_C]
    rows[SECOND_C] = nu / (12.0 * h * h * centre**2)
    rows[CENTRE_Z] = common - 30.0 * rows[SECOND_C]
    rows[CENTRE_T] = rows[CENTRE_Z] - nu / centre**2
    rows[CURVE_T] = 0.25 / centre
    rows[TURN_T] = nu / (h * centre**2)
    rows[RADIAL_F] = nu / (2.0 * dr * face)
    rows[THETA_F] = -0.25 / (12.0 * h * face)
    rows[SECOND_F] = nu / (12.0 * h * h * face**2)
    rows[CENTRE_R] = common - 30.0 * rows[SECOND_F] - nu / face**2
    rows[CURVE_R] = 1.0 / (16.0 * face)
    rows[TURN_R] = -nu / (h * face**2)
    return np.broadcast_to(rows[:, None, :], (COUNT, 8, radial)).astype(np.float32)


class Cells:
    def __init__(self, vel, j, k):
        self.vel, self.j, self.k, self.known = vel, j, k, {}

    def once(self, key, make):
        if key not in self.known:
            self.known[key] = make()
        return self.known[key]

    def at(self, n, dj, dk=0):
        rows = pl.ds(self.k + PAD + dk, 8)
        return self.once((n, dj, dk), lambda: self.vel[n, self.j + HALO + dj, rows, :])

    def turned(self, by, n, dj, dk=0):
        return self.once(
            (by, n, dj, dk), lambda: pltpu.roll(self.at(n, dj, dk), by % self.vel.shape[3], 1)
        )

    def pair(self, by, n, dj, dk=0):
        return self.once(
            ("pair", n, dj, dk), lambda: self.at(n, dj, dk) + self.turned(by, n, dj, dk)
        )

    def beside(self, dj, dk):
        n = 1 if dk >= 0 else 2
        other = (1, dj - 1, dk) if n == 1 else (2, dj, dk)
        here = (1, dj, dk) if n == 1 else (2, dj, dk + 1)
        return self.once(("sum", n, dj, dk), lambda: self.at(*other) + self.at(*here))


def terms(cells, ghost, coef, q, dr):
    at, turned, pair = cells.at, cells.turned, cells.pair
    a, b, c = (at(n, q) for n in range(3))
    lane = lax.broadcasted_iota(jnp.int32, a.shape, 1)
    first_lane = lane == 0
    last_lane = lane == a.shape[1] - 1

    nu = VISCOSITY
    lap = nu / dr**2
    adv_z = -1.0 / (12.0 * AXIAL_STEP)
    vis_z = nu / (12.0 * AXIAL_STEP**2)

    def differences(p1, m1, p2, m2):
        return 8.0 * (p1 - m1) - (p2 - m2), 16.0 * (p1 + m1) - (p2 + m2)

    def pieces(n):
        over = differences(*(at(n, q + d) for d in (1, -1, 2, -2)))
        along = differences(*(at(n, q, d) for d in (1, -1, 2, -2)))
        return over, along

    def below(n):
        if ghost is not None and n > 0 and q % 2 == 0:
            x = jnp.where(last_lane, ghost(n, q + 1), at(n, q))
            return pltpu.roll(x, 1, 1)
        x = turned(1, n, q)
        if ghost is not None:
            return jnp.where(first_lane, ghost(n, q), x)
        return x if n == 0 else jnp.where(first_lane, 0.0, x)

    def above(n):
        return jnp.where(last_lane, -at(n, q), turned(-1, n, q))

    pair_a, pair_side, pair_next = pair(1, 0, q), pair(1, 0, q + 1), pair(1, 0, q, 1)
    pair_b, pair_back = pair(-1, 1, q), pair(-1, 1, q - 1)

    theta, axial = pieces(2)
    up, low = above(2), below(2)
    u_r = pair_a + pair_next
    u_t = cells.beside(q, 0) + cells.beside(q, 1)
    h_z = (up - low) * (coef[RADIAL_C] - u_r * (0.125 / dr)) + (up + low) * lap
    h_z = h_z + theta[0] * (u_t * coef[CROSS_Z])
    h_z = h_z + (theta[1] * coef[SECOND_C] + axial[1] * vis_z)
    h_z = h_z + c * (coef[CENTRE_Z] + axial[0] * adv_z)

    theta, axial = pieces(1)
    up, low = above(1), below(1)
    u_r = pair_a + pair_side
    u_z = cells.beside(q, -1) + cells.beside(q + 1, -1)
    h_t = (up - low) * (coef[RADIAL_C] - u_r * (0.125 / dr)) + (up + low) * lap
    h_t = h_t + b * (coef[CENTRE_T] + theta[0] * coef[THETA_C] - u_r * coef[CURVE_T])
    h_t = h_t + (theta[1] * coef[SECOND_C] + axial[1] * vis_z)
    h_t = h_t + axial[0] * (u_z * (0.25 * adv_z))
    h_t = h_t + (pair_side - pair_a) * coef[TURN_T]

    theta, axial = pieces(0)
    up, low = turned(-1, 0, q), below(0)
    u_t = pair_b + pair_back
    u_z = pair(-1, 2, q) + pair(-1, 2, q, -1)
    h_r = (up - low) * (coef[RADIAL_F] - a * (0.5 / dr)) + (up + low) * lap
    h_r = h_r + u_t * (u_t * coef[CURVE_R] + theta[0] * coef[THETA_F])
    h_r = h_r + (theta[1] * coef[SECOND_F] + axial[1] * vis_z)
    h_r = h_r + (axial[0] * (u_z * (0.25 * adv_z)) + a * coef[CENTRE_R])
    h_r = h_r + (pair_b - pair_back) * coef[TURN_R]
    return h_r, h_t, h_z


def lane_zero_terms(cells, ghost, coef, q, dr):
    lap = VISCOSITY / dr**2
    a = cells.at(0, q)
    first_lane = lax.broadcasted_iota(jnp.int32, a.shape, 1) == 0
    add_r = ghost(0, q) * (lap - coef[RADIAL_F] + a * (0.5 / dr))
    add_t = ghost(1, q) * (lap - coef[RADIAL_C] + (a + cells.at(0, q + 1)) * (0.125 / dr))
    add_z = ghost(2, q) * (lap - coef[RADIAL_C] + (a + cells.at(0, q, 1)) * (0.125 / dr))
    return tuple(jnp.where(first_lane, x, 0.0) for x in (add_r, add_t, add_z))


def wall_mask(rows, radial):
    lane = lax.broadcasted_iota(jnp.int32, (rows, radial), 1)
    return jnp.where(lane == radial - 1, 0.0, 1.0).astype(jnp.float32)


def first_pass(theta_step, v_ref, vel_ref, low_ref, high_ref, pay_ref, sems):
    _, planes, axial, radial = v_ref.shape
    lane = lax.broadcasted_iota(jnp.int32, (8, radial), 1)
    wall = wall_mask(8, radial)
    rate_t = (radial / theta_step) / (lane.astype(jnp.float32) + 0.5)

    def fetch(g):
        part = pl.ds(g * GROUP, GROUP)
        target = vel_ref.at[:, pl.ds(g * GROUP + HALO, GROUP), pl.ds(PAD, axial)]
        return pltpu.make_async_copy(v_ref.at[:, part], target, sems.at[g])

    for g in range(planes // GROUP):
        fetch(g).start()

    def group(g, largest):
        fetch(g).wait()

        def rows(i, largest):
            k = pl.ds(pl.multiple_of(i * 8, 8) + PAD, 8)
            largest = list(largest)
            for q in range(GROUP):
                j = g * GROUP + HALO + q
                a, b, c = (vel_ref[n, j, k, :] for n in range(3))
                a = a * wall
                vel_ref[0, j, k, :] = a
                rate = jnp.abs(a) * float(radial) + jnp.abs(b) * rate_t
                rate = rate + jnp.abs(c) * (1.0 / AXIAL_STEP)
                largest[q % 4] = jnp.maximum(largest[q % 4], rate)
            return tuple(largest)

        largest = lax.fori_loop(0, axial // 8, rows, largest, unroll=4)
        for q in range(GROUP):
            for n in range(3):
                j = g * GROUP + q
                low_ref[n, j] = vel_ref[n, j + HALO, PAD : PAD + 2, :]
                high_ref[n, j] = vel_ref[n, j + HALO, PAD + axial - 2 : PAD + axial, :]
        return largest

    zero = jnp.zeros((8, radial), jnp.float32)
    m = lax.fori_loop(0, planes // GROUP, group, (zero,) * 4)
    largest = jnp.maximum(jnp.maximum(m[0], m[1]), jnp.maximum(m[2], m[3]))
    top = jnp.max(largest, axis=(0, 1), keepdims=True)
    pay_ref[...] = jnp.broadcast_to(top, pay_ref.shape)


def pack(vel_ref, inner_ref):
    planes, (axial, radial) = vel_ref.shape[1] - 2 * HALO, inner_ref.shape
    lane = lax.broadcasted_iota(jnp.int32, (8, radial), 1)
    sign = jnp.where(lane < 2 * planes, -1.0, 1.0).astype(jnp.float32)

    def rows(i, carry):
        k = pl.multiple_of(i * 8, 8)
        inner = [jnp.zeros((8, radial), jnp.float32)] * 3
        for j in range(planes):
            for n in range(3):
                place = n * planes + j
                x = vel_ref[n, j + HALO, pl.ds(k + PAD, 8), :]
                x = pltpu.roll(x, place, 1)
                inner[n] = jnp.where(lane == place, x, inner[n])
        inner_ref[pl.ds(k, 8), :] = (inner[0] + inner[1] + inner[2]) * sign
        return carry

    lax.fori_loop(0, axial // 8, rows, 0)


def fold(low_ref, high_ref, vel_in, _, vel_ref):
    del vel_in
    planes, radial = low_ref.shape[1], low_ref.shape[3]
    axial = vel_ref.shape[2] - 2 * PAD
    wall = wall_mask(2, radial)

    def plane(j, carry):
        for n in range(3):
            mask = wall if n == 0 else 1.0
            vel_ref[n, j + HALO, PAD - 2 : PAD, :] = low_ref[n, j] * mask
            vel_ref[n, j + HALO, PAD + axial : PAD + axial + 2, :] = high_ref[n, j] * mask
        return carry

    lax.fori_loop(0, planes, plane, 0, unroll=4)


def theta_in(below_ref, above_ref, inner_in, vel_in, *refs):
    del vel_in
    tile_ref, inner_ref, vel_ref = refs[-3:]
    planes = vel_ref.shape[1] - 2 * HALO
    axial, radial = inner_in.shape
    cells = pl.ds(PAD, axial)
    wall = wall_mask(1, radial)
    for q in range(HALO):
        for ref, place in ((below_ref, q), (above_ref, HALO + planes + q)):
            vel_ref[0, place, cells, :] = ref[0, q] * wall
            vel_ref[1, place, cells, :] = ref[1, q]
            vel_ref[2, place, cells, :] = ref[2, q]
    tile_ref[...] = jnp.zeros_like(tile_ref)
    tile_ref[1:2, :] = below_ref[1, HALO - 1, 0:1, :]
    tile_ref[2:3, :] = above_ref[2, 0, axial - 1 : axial, :]
    inner_ref[...] = inner_in[...]


def corners_in(next_ref, back_ref, vel_in, _, vel_ref):
    del vel_in
    planes, axial = vel_ref.shape[1] - 2 * HALO, vel_ref.shape[2] - 2 * PAD
    vel_ref[1, HALO - 1, PAD + axial : PAD + axial + 1, :] = next_ref[1:2, :]
    vel_ref[2, HALO + planes, PAD - 1 : PAD, :] = back_ref[2:3, :]


def ghosts(cells, inner, planes):
    radial = inner.shape[1]

    def ghost(n, q):
        turn = -(n * planes + q + cells.j) % radial
        return cells.once(("ghost", n, q), lambda: pltpu.roll(inner, turn, 1) if turn else inner)

    return ghost


def block_terms(vel_ref, inner_ref, coef_ref, j, size, write):
    planes = vel_ref.shape[1] - 2 * HALO
    axial, radial = vel_ref.shape[2] - 2 * PAD, vel_ref.shape[3]
    groups = 2 * BLOCK // size

    def rows(i, carry):
        coef = [coef_ref[n] for n in range(COUNT)]
        found = []
        for u in range(groups):
            k = pl.multiple_of((i * groups + u) * 8, 8)
            cells = Cells(vel_ref, j, k)
            ghost = None
            if inner_ref is not None:
                ghost = ghosts(cells, inner_ref[pl.ds(k, 8), :], planes)
            for q in range(size):
                found.append((q, k, terms(cells, ghost, coef, q, 1.0 / radial)))
        for q, k, values in found:
            for n, value in enumerate(values):
                write(n, j + q, pl.ds(k, 8), value)
        return carry

    lax.fori_loop(0, axial // (8 * groups), rows, 0)


def ahead(first, last, vel_ref, coef_ref, _, out_ref):
    def write(n, j, k, value):
        out_ref[n, j - first, k, :] = value

    def block(m, carry):
        block_terms(vel_ref, None, coef_ref, first + m * BLOCK, BLOCK, write)
        return carry

    lax.fori_loop(0, (last - first) // BLOCK, block, 0)


def rest(first, last, vel_ref, inner_ref, coef_ref, _, out_ref):
    planes = vel_ref.shape[1] - 2 * HALO
    runs = [(j, BLOCK, j - first) for j in range(first, last, BLOCK)]
    runs += [(0, HALO, last - first), (planes - HALO, HALO, last - first + HALO)]
    for j, size, place in runs:

        def write(n, plane, k, value, shift=place - j):
            out_ref[n, plane + shift, k, :] = value

        block_terms(vel_ref, inner_ref, coef_ref, j, size, write)


def finish(
    spans, vel_ref, inner_ref, coef_ref, part_a, part_b, part_c, top_ref, out_ref, step_ref, res,
    sems,
):
    axial, radial = inner_ref.shape
    planes = vel_ref.shape[1] - 2 * HALO
    time_step = CFL_TARGET / (jnp.max(top_ref[0:8, :]) + 1e-06)
    step_ref[0] = time_step
    scale = GAMMA * time_step
    factors = (scale * coef_ref[WALL], scale, scale)
    pending = []

    def complete(part, j, size, place, add):
        groups = 4 * BLOCK // size

        def rows(i, carry):
            found = []
            for u in range(groups):
                k = pl.multiple_of((i * groups + u) * 8, 8)
                cells = Cells(vel_ref, j, k)
                ghost = ghosts(cells, inner_ref[pl.ds(k, 8), :], planes) if add else None
                for q in range(size):
                    values = [part[n, place + q, pl.ds(k, 8), :] for n in range(3)]
                    if add:
                        added = lane_zero_terms(cells, ghost, coef_ref, q, 1.0 / radial)
                        values = [x + y for x, y in zip(values, added)]
                    found.append((q, k, values))
            for q, k, values in found:
                for n, value in enumerate(values):
                    res[n, j + q, pl.ds(k, 8), :] = value * factors[n]
            return carry

        lax.fori_loop(0, axial // (8 * groups), rows, 0)
        part_of = pl.ds(j, size)
        copy = pltpu.make_async_copy(
            res.at[:, part_of], out_ref.at[:, part_of], sems.at[len(pending)]
        )
        copy.start()
        pending.append(copy)

    first, last = spans[2]
    for j in range(first, last, BLOCK):
        complete(part_c, j, BLOCK, j - first, False)
    complete(part_c, 0, HALO, last - first, False)
    complete(part_c, planes - HALO, HALO, last - first + HALO, False)
    for part, (first, last) in ((part_a, spans[0]), (part_b, spans[1])):
        for j in range(first, last, BLOCK):
            complete(part, j, BLOCK, j - first, True)
    for copy in pending:
        copy.wait()


def shifted(block, distance):
    sizes = lax.axis_size("az"), lax.axis_size("ax")
    route = []
    for i in range(sizes[0]):
        for k in range(sizes[1]):
            source = (i - distance[0]) % sizes[0], (k - distance[1]) % sizes[1]
            route.append((source[0] * sizes[1] + source[1], i * sizes[1] + k))
    return lax.ppermute(block, ("az", "ax"), route)


def cuts(planes):
    ends = (HALO, planes - HALO - 3 * BLOCK, planes - HALO - BLOCK, planes - HALO)
    return list(zip(ends[:-1], ends[1:]))


def per_device(velocity):
    _, planes, axial, radial = velocity.shape
    sizes = lax.axis_size("az"), lax.axis_size("ax")
    theta_step = 2.0 * math.pi / (sizes[0] * planes)
    coef = jnp.asarray(coefficients(radial, theta_step))
    f32 = jnp.float32
    anywhere = pl.BlockSpec(memory_space=pl.ANY)
    vmem = pl.BlockSpec(memory_space=pltpu.VMEM)
    smem = pl.BlockSpec(memory_space=pltpu.SMEM)

    def shape(*sizes):
        return jax.ShapeDtypeStruct(sizes, f32)

    def call(kernel, name, work, scratch=0, **kwargs):
        return pl.pallas_call(
            kernel,
            name=name,
            compiler_params=pltpu.CompilerParams(vmem_limit_bytes=(4 + scratch) * 2**20),
            cost_estimate=pl.CostEstimate(flops=work, bytes_accessed=work, transcendentals=0),
            **kwargs,
        )

    below = shifted(velocity[:, planes - HALO :], (1, 0))
    above = shifted(velocity[:, :HALO], (-1, 0))

    edge = shape(3, planes, 2, radial)
    padded = shape(3, planes + 2 * HALO, axial + 2 * PAD, radial)
    row = shape(axial, radial)
    tile = shape(8, radial)
    vel, first, last, pay = call(
        functools.partial(first_pass, theta_step),
        "first_pass",
        0,
        out_shape=(padded, edge, edge, row),
        in_specs=[anywhere],
        out_specs=(vmem,) * 4,
        scratch_shapes=[pltpu.SemaphoreType.DMA((planes // GROUP,))],
    )(pltpu.with_memory_space_constraint(velocity, pltpu.HBM))
    low = shifted(last, (0, 1))
    high = shifted(first, (0, -1))
    largest = lax.pmax(pay, ("az", "ax"))
    inner = call(
        pack,
        "pack",
        velocity.size,
        out_shape=row,
        in_specs=[vmem],
        out_specs=vmem,
    )(vel)
    vel = call(
        fold,
        "fold",
        0,
        out_shape=padded,
        in_specs=[vmem] * 4,
        out_specs=vmem,
        input_output_aliases={2: 0},
    )(low, high, vel, inner)

    spans = cuts(planes)

    def in_advance(n, vel, token):
        first, last = spans[n]
        return call(
            functools.partial(ahead, first, last),
            f"ahead_{n}",
            8 * velocity.size,
            out_shape=shape(3, last - first, axial, radial),
            in_specs=[vmem] * 3,
            out_specs=vmem,
        )(vel, coef, token)

    part_a = in_advance(0, vel, inner)
    tile_out, mine, vel = call(
        theta_in,
        "theta_in",
        0,
        out_shape=(tile, row, padded),
        in_specs=[vmem] * 6,
        out_specs=(vmem,) * 3,
        input_output_aliases={3: 2},
    )(below, above, inner, vel, part_a, largest)
    inner = shifted(mine, (sizes[0] // 2, 0))
    following = shifted(tile_out, (0, -1))
    preceding = shifted(tile_out, (0, 1))
    part_b = in_advance(1, vel, tile_out)
    vel = call(
        corners_in,
        "corners_in",
        0,
        out_shape=padded,
        in_specs=[vmem] * 4,
        out_specs=vmem,
        input_output_aliases={2: 0},
    )(following, preceding, vel, part_b)
    first, last = spans[2]
    part_c = call(
        functools.partial(rest, first, last),
        "rest",
        0,
        out_shape=shape(3, last - first + 2 * HALO, axial, radial),
        in_specs=[vmem] * 4,
        out_specs=vmem,
    )(vel, inner, coef, part_b)
    return_shape = shape(*velocity.shape)
    increment, time_step = call(
        functools.partial(finish, spans),
        "finish",
        0,
        scratch=8,
        out_shape=(return_shape, shape(1)),
        in_specs=[vmem] * 7,
        out_specs=(anywhere, smem),
        scratch_shapes=[
            pltpu.VMEM(velocity.shape, f32),
            pltpu.SemaphoreType.DMA(((planes - 2 * HALO) // BLOCK + 2,)),
        ],
    )(vel, inner, coef, part_a, part_b, part_c, largest)
    return increment, time_step.reshape(())


def solution(mesh):
    return jax.shard_map(
        per_device,
        mesh=mesh,
        in_specs=(P(None, "az", "ax", None),),
        out_specs=(P(None, "az", "ax", None), P()),
        check_vma=False,
    )
```

```python
import functools
import math

import jax
import jax.numpy as jnp
import numpy as np
from jax import lax
from jax.experimental import pallas as pl
from jax.experimental.pallas import tpu as pltpu
from jax.sharding import PartitionSpec as P

AXIAL_STEP = 0.01
VISCOSITY = 0.001
CFL_TARGET = 1.2
GAMMA = 8.0 / 15.0

PAD = 8
HALO = 2
BLOCK = 4
GROUP = 4
UNROLL = 4

(
    WALL,
    RADIAL_C,
    THETA_C,
    CROSS_Z,
    SECOND_C,
    CENTRE_Z,
    CENTRE_T,
    CURVE_T,
    TURN_T,
    RADIAL_F,
    THETA_F,
    SECOND_F,
    CENTRE_R,
    CURVE_R,
    TURN_R,
    COUNT,
) = range(16)


def coefficients(radial, theta_step):
    dr = 1.0 / radial
    index = np.arange(radial, dtype=np.float64)
    centre = (index + 0.5) * dr
    face = (index + 1.0) * dr
    wall = np.where(index < radial - 1.5, 1.0, 0.0)
    h = theta_step
    nu = VISCOSITY
    rows = np.zeros((COUNT, radial))
    rows[WALL] = wall
    common = -2.0 * nu / dr**2 - 30.0 * nu / (12.0 * AXIAL_STEP**2)
    rows[RADIAL_C] = nu / (2.0 * dr * centre)
    rows[THETA_C] = -1.0 / (12.0 * h * centre)
    rows[CROSS_Z] = 0.25 * rows[THETA_C]
    rows[SECOND_C] = nu / (12.0 * h * h * centre**2)
    rows[CENTRE_Z] = common - 30.0 * rows[SECOND_C]
    rows[CENTRE_T] = rows[CENTRE_Z] - nu / centre**2
    rows[CURVE_T] = 0.25 / centre
    rows[TURN_T] = nu / (h * centre**2)
    rows[RADIAL_F] = nu / (2.0 * dr * face)
    rows[THETA_F] = -0.25 / (12.0 * h * face)
    rows[SECOND_F] = nu / (12.0 * h * h * face**2)
    rows[CENTRE_R] = common - 30.0 * rows[SECOND_F] - nu / face**2
    rows[CURVE_R] = 1.0 / (16.0 * face)
    rows[TURN_R] = -nu / (h * face**2)
    return np.broadcast_to(rows[:, None, :], (COUNT, 8, radial)).astype(np.float32)


class Cells:
    def __init__(self, vel, j, k):
        self.vel, self.j, self.k, self.known = vel, j, k, {}

    def once(self, key, make):
        if key not in self.known:
            self.known[key] = make()
        return self.known[key]

    def at(self, n, dj, dk=0):
        rows = pl.ds(self.k + PAD + dk, 8)
        return self.once((n, dj, dk), lambda: self.vel[n, self.j + HALO + dj, rows, :])

    def turned(self, by, n, dj, dk=0):
        return self.once(
            (by, n, dj, dk), lambda: pltpu.roll(self.at(n, dj, dk), by % self.vel.shape[3], 1)
        )

    def pair(self, by, n, dj, dk=0):
        return self.once(
            ("pair", n, dj, dk), lambda: self.at(n, dj, dk) + self.turned(by, n, dj, dk)
        )

    def beside(self, dj, dk):
        n = 1 if dk >= 0 else 2
        other = (1, dj - 1, dk) if n == 1 else (2, dj, dk)
        here = (1, dj, dk) if n == 1 else (2, dj, dk + 1)
        return self.once(("sum", n, dj, dk), lambda: self.at(*other) + self.at(*here))


def terms(cells, ghost, coef, q, dr):
    at, turned, pair = cells.at, cells.turned, cells.pair
    a, b, c = (at(n, q) for n in range(3))
    lane = lax.broadcasted_iota(jnp.int32, a.shape, 1)
    first_lane = lane == 0
    last_lane = lane == a.shape[1] - 1

    nu = VISCOSITY
    lap = nu / dr**2
    adv_z = -1.0 / (12.0 * AXIAL_STEP)
    vis_z = nu / (12.0 * AXIAL_STEP**2)

    def differences(p1, m1, p2, m2):
        return 8.0 * (p1 - m1) - (p2 - m2), 16.0 * (p1 + m1) - (p2 + m2)

    def pieces(n):
        over = differences(*(at(n, q + d) for d in (1, -1, 2, -2)))
        along = differences(*(at(n, q, d) for d in (1, -1, 2, -2)))
        return over, along

    def below(n):
        if ghost is not None and n > 0 and q % 2 == 0:
            x = jnp.where(last_lane, ghost(n, q + 1), at(n, q))
            return pltpu.roll(x, 1, 1)
        x = turned(1, n, q)
        if ghost is not None:
            return jnp.where(first_lane, ghost(n, q), x)
        return x if n == 0 else jnp.where(first_lane, 0.0, x)

    def above(n):
        return jnp.where(last_lane, -at(n, q), turned(-1, n, q))

    pair_a, pair_side, pair_next = pair(1, 0, q), pair(1, 0, q + 1), pair(1, 0, q, 1)
    pair_b, pair_back = pair(-1, 1, q), pair(-1, 1, q - 1)

    theta, axial = pieces(2)
    up, low = above(2), below(2)
    u_r = pair_a + pair_next
    u_t = cells.beside(q, 0) + cells.beside(q, 1)
    h_z = (up - low) * (coef[RADIAL_C] - u_r * (0.125 / dr)) + (up + low) * lap
    h_z = h_z + theta[0] * (u_t * coef[CROSS_Z])
    h_z = h_z + (theta[1] * coef[SECOND_C] + axial[1] * vis_z)
    h_z = h_z + c * (coef[CENTRE_Z] + axial[0] * adv_z)

    theta, axial = pieces(1)
    up, low = above(1), below(1)
    u_r = pair_a + pair_side
    u_z = cells.beside(q, -1) + cells.beside(q + 1, -1)
    h_t = (up - low) * (coef[RADIAL_C] - u_r * (0.125 / dr)) + (up + low) * lap
    h_t = h_t + b * (coef[CENTRE_T] + theta[0] * coef[THETA_C] - u_r * coef[CURVE_T])
    h_t = h_t + (theta[1] * coef[SECOND_C] + axial[1] * vis_z)
    h_t = h_t + axial[0] * (u_z * (0.25 * adv_z))
    h_t = h_t + (pair_side - pair_a) * coef[TURN_T]

    theta, axial = pieces(0)
    up, low = turned(-1, 0, q), below(0)
    u_t = pair_b + pair_back
    u_z = pair(-1, 2, q) + pair(-1, 2, q, -1)
    h_r = (up - low) * (coef[RADIAL_F] - a * (0.5 / dr)) + (up + low) * lap
    h_r = h_r + u_t * (u_t * coef[CURVE_R] + theta[0] * coef[THETA_F])
    h_r = h_r + (theta[1] * coef[SECOND_F] + axial[1] * vis_z)
    h_r = h_r + (axial[0] * (u_z * (0.25 * adv_z)) + a * coef[CENTRE_R])
    h_r = h_r + (pair_b - pair_back) * coef[TURN_R]
    return h_r, h_t, h_z


def lane_zero_terms(cells, ghost, coef, q, dr):
    lap = VISCOSITY / dr**2
    a = cells.at(0, q)
    first_lane = lax.broadcasted_iota(jnp.int32, a.shape, 1) == 0
    add_r = ghost(0, q) * (lap - coef[RADIAL_F] + a * (0.5 / dr))
    add_t = ghost(1, q) * (lap - coef[RADIAL_C] + (a + cells.at(0, q + 1)) * (0.125 / dr))
    add_z = ghost(2, q) * (lap - coef[RADIAL_C] + (a + cells.at(0, q, 1)) * (0.125 / dr))
    return tuple(jnp.where(first_lane, x, 0.0) for x in (add_r, add_t, add_z))


def wall_mask(rows, radial):
    lane = lax.broadcasted_iota(jnp.int32, (rows, radial), 1)
    return jnp.where(lane == radial - 1, 0.0, 1.0).astype(jnp.float32)


def first_pass(theta_step, v_ref, vel_ref, even_ref, odd_ref, pay_ref, sems):
    _, planes, axial, radial = v_ref.shape
    lane = lax.broadcasted_iota(jnp.int32, (8, radial), 1)
    wall = wall_mask(8, radial)
    rate_t = (radial / theta_step) / (lane.astype(jnp.float32) + 0.5)

    odd = lax.rem(lax.axis_index("ax"), 2) == 1

    def fetch(g):
        part = pl.ds(g * GROUP, GROUP)
        target = vel_ref.at[:, pl.ds(g * GROUP + HALO, GROUP), pl.ds(PAD, axial)]
        return pltpu.make_async_copy(v_ref.at[:, part], target, sems.at[g])

    for g in range(planes // GROUP):
        fetch(g).start()

    def group(g, largest):
        fetch(g).wait()

        def rows(i, largest):
            k = pl.ds(pl.multiple_of(i * 8, 8) + PAD, 8)
            largest = list(largest)
            for q in range(GROUP):
                j = g * GROUP + HALO + q
                a, b, c = (vel_ref[n, j, k, :] for n in range(3))
                a = a * wall
                vel_ref[0, j, k, :] = a
                rate = jnp.abs(a) * float(radial) + jnp.abs(b) * rate_t
                rate = rate + jnp.abs(c) * (1.0 / AXIAL_STEP)
                largest[q % 4] = jnp.maximum(largest[q % 4], rate)
            return tuple(largest)

        largest = lax.fori_loop(0, axial // 8, rows, largest, unroll=4)
        for q in range(GROUP):
            for n in range(3):
                j = g * GROUP + q
                first = vel_ref[n, j + HALO, PAD : PAD + 2, :]
                last = vel_ref[n, j + HALO, PAD + axial - 2 : PAD + axial, :]
                even_ref[n, j] = jnp.where(odd, first, last)
                odd_ref[n, j] = jnp.where(odd, last, first)
        return largest

    zero = jnp.zeros((8, radial), jnp.float32)
    m = lax.fori_loop(0, planes // GROUP, group, (zero,) * 4)
    largest = jnp.maximum(jnp.maximum(m[0], m[1]), jnp.maximum(m[2], m[3]))
    top = jnp.max(largest, axis=(0, 1), keepdims=True)
    pay_ref[...] = jnp.broadcast_to(top, pay_ref.shape)
    last = lax.broadcasted_iota(jnp.int32, (2, radial), 1) == radial - 1
    for ref in (even_ref, odd_ref):
        ref[0, 0] = jnp.where(last, top, ref[0, 0])


def pack(vel_ref, inner_ref):
    planes, (axial, radial) = vel_ref.shape[1] - 2 * HALO, inner_ref.shape
    lane = lax.broadcasted_iota(jnp.int32, (8, radial), 1)
    sign = jnp.where(lane < 2 * planes, -1.0, 1.0).astype(jnp.float32)

    def rows(i, carry):
        k = pl.multiple_of(i * 8, 8)
        inner = [jnp.zeros((8, radial), jnp.float32)] * 3
        for j in range(planes):
            for n in range(3):
                place = n * planes + j
                x = vel_ref[n, j + HALO, pl.ds(k + PAD, 8), :]
                x = pltpu.roll(x, place, 1)
                inner[n] = jnp.where(lane == place, x, inner[n])
        inner_ref[pl.ds(k, 8), :] = (inner[0] + inner[1] + inner[2]) * sign
        return carry

    lax.fori_loop(0, axial // 8, rows, 0)


def fold(even_ref, odd_ref, pay_ref, inner_in, vel_in, *refs):
    del vel_in
    fars, (inner_ref, vel_ref) = refs[:-2], refs[-2:]
    planes = even_ref.shape[1]
    axial, radial = inner_in.shape
    lane = lax.broadcasted_iota(jnp.int32, (1, radial), 1)
    top = jnp.maximum(even_ref[0, 0, 0:1, :], odd_ref[0, 0, 0:1, :])
    top = jnp.max(jnp.where(lane == radial - 1, top, 0.0), axis=(0, 1), keepdims=True)
    top = jnp.maximum(pay_ref[...], top)
    for far in fars:
        top = jnp.maximum(top, far[...])
    lane = lax.broadcasted_iota(jnp.int32, top.shape, 1)
    inner_ref[...] = inner_in[...]
    inner_ref[0:8, :] = jnp.where(lane == radial - 1, top, inner_in[0:8, :])
    wall = wall_mask(2, radial)
    odd = lax.rem(lax.axis_index("ax"), 2) == 1

    def plane(j, carry):
        for n in range(3):
            mask = wall if n == 0 else 1.0
            even, other = even_ref[n, j] * mask, odd_ref[n, j] * mask
            low, high = jnp.where(odd, even, other), jnp.where(odd, other, even)
            vel_ref[n, j + HALO, PAD - 2 : PAD, :] = low
            vel_ref[n, j + HALO, PAD + axial : PAD + axial + 2, :] = high
        return carry

    lax.fori_loop(0, planes, plane, 0, unroll=4)


def with_partner(mine_ref, inner_ref, _, top_ref):
    radial = inner_ref.shape[1]
    lane = lax.broadcasted_iota(jnp.int32, (1, radial), 1)
    top = jnp.maximum(mine_ref[0:1, :], inner_ref[0:1, :])
    top = jnp.max(jnp.where(lane == radial - 1, top, 0.0), axis=(0, 1), keepdims=True)
    top_ref[...] = jnp.broadcast_to(top, top_ref.shape)


def theta_in(even_ref, odd_ref, vel_in, _, even_tile, odd_tile, vel_ref):
    del vel_in
    planes, axial = vel_ref.shape[1] - 2 * HALO, vel_ref.shape[2] - 2 * PAD
    cells = pl.ds(PAD, axial)
    wall = wall_mask(1, vel_ref.shape[3])
    odd = lax.rem(lax.axis_index("az"), 2)
    below, above = 0, HALO + planes
    for ref, place in (
        (even_ref, jnp.where(odd == 1, below, above)),
        (odd_ref, jnp.where(odd == 1, above, below)),
    ):
        for q in range(HALO):
            vel_ref[0, place + q, cells, :] = ref[0, q] * wall
            vel_ref[1, place + q, cells, :] = ref[1, q]
            vel_ref[2, place + q, cells, :] = ref[2, q]
    first = vel_ref[1, below + HALO - 1, PAD : PAD + 1, :]
    last = vel_ref[2, above, PAD + axial - 1 : PAD + axial, :]
    odd = lax.rem(lax.axis_index("ax"), 2) == 1
    shape = even_tile.shape
    even_tile[...] = jnp.broadcast_to(jnp.where(odd, first, last), shape)
    odd_tile[...] = jnp.broadcast_to(jnp.where(odd, last, first), shape)


def ghosts(cells, inner, planes):
    radial = inner.shape[1]

    def ghost(n, q):
        turn = -(n * planes + q + cells.j) % radial
        return cells.once(("ghost", n, q), lambda: pltpu.roll(inner, turn, 1) if turn else inner)

    return ghost


def block_terms(vel_ref, inner_ref, coef_ref, j, size, write):
    planes = vel_ref.shape[1] - 2 * HALO
    axial, radial = vel_ref.shape[2] - 2 * PAD, vel_ref.shape[3]
    groups = 2 * BLOCK // size

    def rows(i, carry):
        coef = [coef_ref[n] for n in range(COUNT)]
        found = []
        for u in range(groups):
            k = pl.multiple_of((i * groups + u) * 8, 8)
            cells = Cells(vel_ref, j, k)
            ghost = None
            if inner_ref is not None:
                ghost = ghosts(cells, inner_ref[pl.ds(k, 8), :], planes)
            for q in range(size):
                found.append((q, k, terms(cells, ghost, coef, q, 1.0 / radial)))
        for q, k, values in found:
            for n, value in enumerate(values):
                write(n, j + q, pl.ds(k, 8), value)
        return carry

    lax.fori_loop(0, axial // (8 * groups), rows, 0)


def ahead(first, last, vel_ref, coef_ref, _, out_ref):
    def write(n, j, k, value):
        out_ref[n, j - first, k, :] = value

    def block(m, carry):
        block_terms(vel_ref, None, coef_ref, first + m * BLOCK, BLOCK, write)
        return carry

    lax.fori_loop(0, (last - first) // BLOCK, block, 0)


def ahead_with_ghosts(first, last, vel_ref, inner_ref, coef_ref, _, out_ref):
    def write(n, j, k, value):
        out_ref[n, j - first, k, :] = value

    for j in range(first, last, BLOCK):
        block_terms(vel_ref, inner_ref, coef_ref, j, BLOCK, write)


def interior(spans, count, vel_ref, inner_ref, coef_ref, part_a, part_b, *refs):
    tops, (out_ref, step_ref, res, sems) = refs[:count], refs[-4:]
    axial, radial = inner_ref.shape
    planes = vel_ref.shape[1] - 2 * HALO
    top = tops[0][0:1, :]
    for ref in tops[1:]:
        top = jnp.maximum(top, ref[0:1, :])
    time_step = CFL_TARGET / (jnp.max(top) + 1e-06)
    step_ref[0] = time_step
    scale = GAMMA * time_step
    factors = (scale * coef_ref[WALL], scale, scale)
    pending = []

    def send(j):
        part_of = pl.ds(j, BLOCK)
        copy = pltpu.make_async_copy(
            res.at[:, pl.ds(j - HALO, BLOCK)], out_ref.at[:, part_of], sems.at[len(pending)]
        )
        copy.start()
        pending.append(copy)

    def write(n, j, k, value):
        res[n, j - HALO, k, :] = value * factors[n]

    def complete(part, j, place, add):
        groups = 4

        def rows(i, carry):
            found = []
            for u in range(groups):
                k = pl.multiple_of((i * groups + u) * 8, 8)
                cells = Cells(vel_ref, j, k)
                ghost = ghosts(cells, inner_ref[pl.ds(k, 8), :], planes) if add else None
                for q in range(BLOCK):
                    values = [part[n, place + q, pl.ds(k, 8), :] for n in range(3)]
                    if add:
                        added = lane_zero_terms(cells, ghost, coef_ref, q, 1.0 / radial)
                        values = [x + y for x, y in zip(values, added)]
                    found.append((q, k, values))
            for q, k, values in found:
                for n, value in enumerate(values):
                    write(n, j + q, pl.ds(k, 8), value)
            return carry

        lax.fori_loop(0, axial // (8 * groups), rows, 0)
        send(j)

    for part, (first, last), add in ((part_a, spans[0], True), (part_b, spans[1], False)):
        for j in range(first, last, BLOCK):
            complete(part, j, j - first, add)
    for j in range(*spans[2], BLOCK):
        block_terms(vel_ref, inner_ref, coef_ref, j, BLOCK, write)
        send(j)
    for copy in pending:
        copy.wait()


def edges(
    step_ref, even_ref, odd_ref, inner_ref, coef_ref, vel_in, part, out_ref, vel_ref, res, sems
):
    del vel_in, part
    axial = inner_ref.shape[0]
    planes = vel_ref.shape[1] - 2 * HALO
    scale = GAMMA * step_ref[0]
    factors = (scale * coef_ref[WALL], scale, scale)
    odd = lax.rem(lax.axis_index("ax"), 2) == 1
    even, other = even_ref[0:1, :], odd_ref[0:1, :]
    following, preceding = jnp.where(odd, other, even), jnp.where(odd, even, other)
    vel_ref[1, HALO - 1, PAD + axial : PAD + axial + 1, :] = following
    vel_ref[2, HALO + planes, PAD - 1 : PAD, :] = preceding
    pending = []
    for side, first in enumerate((0, planes - HALO)):

        def write(n, j, k, value, shift=side * HALO - first):
            res[n, j + shift, k, :] = value * factors[n]

        block_terms(vel_ref, inner_ref, coef_ref, first, HALO, write)
        copy = pltpu.make_async_copy(
            res.at[:, pl.ds(side * HALO, HALO)],
            out_ref.at[:, pl.ds(first, HALO)],
            sems.at[side],
        )
        copy.start()
        pending.append(copy)
    for copy in pending:
        copy.wait()


def routed(block, axis, source):
    count = lax.axis_size(axis)
    return lax.ppermute(block, axis, [(source(i), i) for i in range(count)])


def exchanged(block, axis, step):
    return routed(block, axis, lambda i: i ^ step)


def across_edges(even, odd, axis):
    count = lax.axis_size(axis)

    def source(i):
        return (i + (1 if i % 2 else -1)) % count

    return exchanged(even, axis, 1), routed(odd, axis, source)


def cuts(planes):
    ends = (HALO, HALO + 2 * BLOCK, HALO + 3 * BLOCK, planes - HALO)
    return list(zip(ends[:-1], ends[1:]))


def per_device(velocity):
    _, planes, axial, radial = velocity.shape
    sizes = lax.axis_size("az"), lax.axis_size("ax")
    theta_step = 2.0 * math.pi / (sizes[0] * planes)
    coef = jnp.asarray(coefficients(radial, theta_step))
    f32 = jnp.float32
    anywhere = pl.BlockSpec(memory_space=pl.ANY)
    vmem = pl.BlockSpec(memory_space=pltpu.VMEM)
    smem = pl.BlockSpec(memory_space=pltpu.SMEM)

    def shape(*sizes):
        return jax.ShapeDtypeStruct(sizes, f32)

    def call(kernel, name, work, scratch=0, **kwargs):
        return pl.pallas_call(
            kernel,
            name=name,
            compiler_params=pltpu.CompilerParams(vmem_limit_bytes=(4 + scratch) * 2**20),
            cost_estimate=pl.CostEstimate(flops=work, bytes_accessed=work, transcendentals=0),
            **kwargs,
        )

    odd = lax.axis_index("az") % 2
    ends = (planes - HALO, 0)
    even_end = jnp.where(odd == 1, ends[1], ends[0])
    odd_end = jnp.where(odd == 1, ends[0], ends[1])
    theta_even, theta_odd = across_edges(
        lax.dynamic_slice_in_dim(velocity, even_end, HALO, 1),
        lax.dynamic_slice_in_dim(velocity, odd_end, HALO, 1),
        "az",
    )

    edge = shape(3, planes, 2, radial)
    padded = shape(3, planes + 2 * HALO, axial + 2 * PAD, radial)
    row = shape(axial, radial)
    tile = shape(8, radial)
    vel, edge_even, edge_odd, pay = call(
        functools.partial(first_pass, theta_step),
        "first_pass",
        0,
        out_shape=(padded, edge, edge, tile),
        in_specs=[anywhere],
        out_specs=(vmem,) * 4,
        scratch_shapes=[pltpu.SemaphoreType.DMA((planes // GROUP,))],
    )(pltpu.with_memory_space_constraint(velocity, pltpu.HBM))
    z_even, z_odd = across_edges(edge_even, edge_odd, "ax")
    fars = [
        routed(pay, "ax", lambda i, step=step: (i + step) % sizes[1])
        for step in range(2, sizes[1] - 1)
    ]
    inner = call(
        pack,
        "pack",
        velocity.size,
        out_shape=row,
        in_specs=[vmem],
        out_specs=vmem,
    )(vel)
    mine, vel = call(
        fold,
        "fold",
        0,
        out_shape=(row, padded),
        in_specs=[vmem] * (5 + len(fars)),
        out_specs=(vmem,) * 2,
        input_output_aliases={4: 1},
    )(z_even, z_odd, pay, inner, vel, *fars)
    inner = exchanged(mine, "az", sizes[0] // 2)

    spans = cuts(planes)

    def part_shape(n):
        return shape(3, spans[n][1] - spans[n][0], axial, radial)

    part_a = call(
        functools.partial(ahead, *spans[0]),
        "ahead",
        velocity.size,
        out_shape=part_shape(0),
        in_specs=[vmem] * 3,
        out_specs=vmem,
    )(vel, coef, mine)
    top = call(
        with_partner,
        "with_partner",
        0,
        out_shape=tile,
        in_specs=[vmem] * 3,
        out_specs=vmem,
    )(mine, inner, part_a)
    tops = (top, *(exchanged(top, "az", step) for step in range(1, sizes[0] // 2)))
    part_b = call(
        functools.partial(ahead_with_ghosts, *spans[1]),
        "ahead_with_ghosts",
        velocity.size,
        out_shape=part_shape(1),
        in_specs=[vmem] * 4,
        out_specs=vmem,
    )(vel, inner, coef, top)
    tile_even, tile_odd, vel = call(
        theta_in,
        "theta_in",
        0,
        out_shape=(tile, tile, padded),
        in_specs=[vmem] * 4,
        out_specs=(vmem,) * 3,
        input_output_aliases={2: 2},
    )(theta_even, theta_odd, vel, part_b)
    corner_even, corner_odd = across_edges(tile_even, tile_odd, "ax")
    part, time_step = call(
        functools.partial(interior, spans, len(tops)),
        "interior",
        4 * velocity.size,
        scratch=6,
        out_shape=(shape(*velocity.shape), shape(1)),
        in_specs=[vmem] * (5 + len(tops)),
        out_specs=(anywhere, smem),
        scratch_shapes=[
            pltpu.VMEM((3, planes - 2 * HALO, axial, radial), f32),
            pltpu.SemaphoreType.DMA(((planes - 2 * HALO) // BLOCK,)),
        ],
    )(vel, inner, coef, part_a, part_b, *tops)
    increment, _ = call(
        edges,
        "edges",
        0,
        scratch=2,
        out_shape=(shape(*velocity.shape), padded),
        in_specs=[smem] + [vmem] * 5 + [anywhere],
        out_specs=(anywhere, vmem),
        scratch_shapes=[
            pltpu.VMEM((3, 2 * HALO, axial, radial), f32),
            pltpu.SemaphoreType.DMA((2,)),
        ],
        input_output_aliases={5: 1, 6: 0},
    )(time_step, corner_even, corner_odd, inner, coef, vel, part)
    return increment, time_step.reshape(())


def solution(mesh):
    return jax.shard_map(
        per_device,
        mesh=mesh,
        in_specs=(P(None, "az", "ax", None),),
        out_specs=(P(None, "az", "ax", None), P()),
        check_vma=False,
    )
```

```python
import functools
import math

import jax
import jax.numpy as jnp
import numpy as np
from jax import lax
from jax.experimental import pallas as pl
from jax.experimental.pallas import tpu as pltpu
from jax.sharding import PartitionSpec as P

AXIAL_STEP = 0.01
VISCOSITY = 0.001
CFL_TARGET = 1.2
GAMMA = 8.0 / 15.0

PAD = 8
HALO = 2
BLOCK = 4
GROUP = 4
UNROLL = 4

(
    WALL,
    RADIAL_C,
    THETA_C,
    CROSS_Z,
    SECOND_C,
    CENTRE_Z,
    CENTRE_T,
    CURVE_T,
    TURN_T,
    RADIAL_F,
    THETA_F,
    SECOND_F,
    CENTRE_R,
    CURVE_R,
    TURN_R,
    COUNT,
) = range(16)


UNIT = VISCOSITY / (12.0 * AXIAL_STEP**2)


def coefficients(radial, theta_step):
    dr = 1.0 / radial
    index = np.arange(radial, dtype=np.float64)
    centre = (index + 0.5) * dr
    face = (index + 1.0) * dr
    wall = np.where(index < radial - 1.5, 1.0, 0.0)
    h = theta_step
    nu = VISCOSITY
    rows = np.zeros((COUNT, radial))
    rows[WALL] = wall
    common = -2.0 * nu / dr**2 - 30.0 * nu / (12.0 * AXIAL_STEP**2)
    rows[RADIAL_C] = nu / (2.0 * dr * centre)
    rows[THETA_C] = -1.0 / (12.0 * h * centre)
    rows[CROSS_Z] = 0.25 * rows[THETA_C]
    rows[SECOND_C] = nu / (12.0 * h * h * centre**2)
    rows[CENTRE_Z] = common - 30.0 * rows[SECOND_C]
    rows[CENTRE_T] = rows[CENTRE_Z] - nu / centre**2
    rows[CURVE_T] = 0.25 / centre
    rows[TURN_T] = nu / (h * centre**2)
    rows[RADIAL_F] = nu / (2.0 * dr * face)
    rows[THETA_F] = -0.25 / (12.0 * h * face)
    rows[SECOND_F] = nu / (12.0 * h * h * face**2)
    rows[CENTRE_R] = common - 30.0 * rows[SECOND_F] - nu / face**2
    rows[CURVE_R] = 1.0 / (16.0 * face)
    rows[TURN_R] = -nu / (h * face**2)
    rows[RADIAL_C:] /= UNIT
    return np.broadcast_to(rows[:, None, :], (COUNT, 8, radial)).astype(np.float32)


class Cells:
    def __init__(self, vel, j, k):
        self.vel, self.j, self.k, self.known = vel, j, k, {}

    def once(self, key, make):
        if key not in self.known:
            self.known[key] = make()
        return self.known[key]

    def at(self, n, dj, dk=0):
        rows = pl.ds(self.k + PAD + dk, 8)
        return self.once((n, dj, dk), lambda: self.vel[n, self.j + HALO + dj, rows, :])

    def turned(self, by, n, dj, dk=0):
        return self.once(
            (by, n, dj, dk), lambda: pltpu.roll(self.at(n, dj, dk), by % self.vel.shape[3], 1)
        )

    def pair(self, by, n, dj, dk=0):
        return self.once(
            ("pair", n, dj, dk), lambda: self.at(n, dj, dk) + self.turned(by, n, dj, dk)
        )

    def beside(self, dj, dk):
        n = 1 if dk >= 0 else 2
        other = (1, dj - 1, dk) if n == 1 else (2, dj, dk)
        here = (1, dj, dk) if n == 1 else (2, dj, dk + 1)
        return self.once(("sum", n, dj, dk), lambda: self.at(*other) + self.at(*here))


def terms(cells, ghost, coef, q, dr):
    at, turned, pair = cells.at, cells.turned, cells.pair
    a, b, c = (at(n, q) for n in range(3))
    lane = lax.broadcasted_iota(jnp.int32, a.shape, 1)
    first_lane = lane == 0
    last_lane = lane == a.shape[1] - 1

    lap = VISCOSITY / dr**2 / UNIT
    adv_z = -1.0 / (12.0 * AXIAL_STEP) / UNIT
    by_dr = 1.0 / dr / UNIT

    def differences(p1, m1, p2, m2):
        return 8.0 * (p1 - m1) - (p2 - m2), 16.0 * (p1 + m1) - (p2 + m2)

    def pieces(n):
        over = differences(*(at(n, q + d) for d in (1, -1, 2, -2)))
        along = differences(*(at(n, q, d) for d in (1, -1, 2, -2)))
        return over, along

    def below(n):
        if ghost is not None and n > 0 and q % 2 == 0:
            x = jnp.where(last_lane, ghost(n, q + 1), at(n, q))
            return pltpu.roll(x, 1, 1)
        x = turned(1, n, q)
        if ghost is not None:
            return jnp.where(first_lane, ghost(n, q), x)
        return x if n == 0 else jnp.where(first_lane, 0.0, x)

    def above(n):
        return jnp.where(last_lane, -at(n, q), turned(-1, n, q))

    pair_a, pair_side, pair_next = pair(1, 0, q), pair(1, 0, q + 1), pair(1, 0, q, 1)
    pair_b, pair_back = pair(-1, 1, q), pair(-1, 1, q - 1)

    theta, axial = pieces(2)
    up, low = above(2), below(2)
    u_r = pair_a + pair_next
    u_t = cells.beside(q, 0) + cells.beside(q, 1)
    h_z = (up - low) * (coef[RADIAL_C] - u_r * (0.125 * by_dr)) + (up + low) * lap
    h_z = h_z + theta[0] * (u_t * coef[CROSS_Z])
    h_z = h_z + (theta[1] * coef[SECOND_C] + axial[1])
    h_z = h_z + c * (coef[CENTRE_Z] + axial[0] * adv_z)

    theta, axial = pieces(1)
    up, low = above(1), below(1)
    u_r = pair_a + pair_side
    u_z = cells.beside(q, -1) + cells.beside(q + 1, -1)
    h_t = (up - low) * (coef[RADIAL_C] - u_r * (0.125 * by_dr)) + (up + low) * lap
    h_t = h_t + b * (coef[CENTRE_T] + theta[0] * coef[THETA_C] - u_r * coef[CURVE_T])
    h_t = h_t + (theta[1] * coef[SECOND_C] + axial[1])
    h_t = h_t + axial[0] * (u_z * (0.25 * adv_z))
    h_t = h_t + (pair_side - pair_a) * coef[TURN_T]

    theta, axial = pieces(0)
    up, low = turned(-1, 0, q), below(0)
    u_t = pair_b + pair_back
    u_z = pair(-1, 2, q) + pair(-1, 2, q, -1)
    h_r = (up - low) * (coef[RADIAL_F] - a * (0.5 * by_dr)) + (up + low) * lap
    h_r = h_r + u_t * (u_t * coef[CURVE_R] + theta[0] * coef[THETA_F])
    h_r = h_r + (theta[1] * coef[SECOND_F] + axial[1])
    h_r = h_r + (axial[0] * (u_z * (0.25 * adv_z)) + a * coef[CENTRE_R])
    h_r = h_r + (pair_b - pair_back) * coef[TURN_R]
    return h_r, h_t, h_z


def lane_zero_terms(cells, ghost, coef, q, dr):
    lap = VISCOSITY / dr**2 / UNIT
    by_dr = 1.0 / dr / UNIT
    a = cells.at(0, q)
    first_lane = lax.broadcasted_iota(jnp.int32, a.shape, 1) == 0
    add_r = ghost(0, q) * (lap - coef[RADIAL_F] + a * (0.5 * by_dr))
    add_t = ghost(1, q) * (lap - coef[RADIAL_C] + (a + cells.at(0, q + 1)) * (0.125 * by_dr))
    add_z = ghost(2, q) * (lap - coef[RADIAL_C] + (a + cells.at(0, q, 1)) * (0.125 * by_dr))
    return tuple(jnp.where(first_lane, x, 0.0) for x in (add_r, add_t, add_z))


def wall_mask(rows, radial):
    lane = lax.broadcasted_iota(jnp.int32, (rows, radial), 1)
    return jnp.where(lane == radial - 1, 0.0, 1.0).astype(jnp.float32)


def first_pass(theta_step, v_ref, vel_ref, even_ref, odd_ref, pay_ref, sems):
    _, planes, axial, radial = v_ref.shape
    lane = lax.broadcasted_iota(jnp.int32, (8, radial), 1)
    wall = wall_mask(8, radial)
    rate_t = (radial / theta_step) / (lane.astype(jnp.float32) + 0.5)

    odd = lax.rem(lax.axis_index("ax"), 2) == 1

    def fetch(g):
        part = pl.ds(g * GROUP, GROUP)
        target = vel_ref.at[:, pl.ds(g * GROUP + HALO, GROUP), pl.ds(PAD, axial)]
        return pltpu.make_async_copy(v_ref.at[:, part], target, sems.at[g])

    for g in range(planes // GROUP):
        fetch(g).start()

    def group(g, largest):
        fetch(g).wait()

        def rows(i, largest):
            k = pl.ds(pl.multiple_of(i * 8, 8) + PAD, 8)
            largest = list(largest)
            for q in range(GROUP):
                j = g * GROUP + HALO + q
                a, b, c = (vel_ref[n, j, k, :] for n in range(3))
                a = a * wall
                vel_ref[0, j, k, :] = a
                rate = jnp.abs(a) * float(radial) + jnp.abs(b) * rate_t
                rate = rate + jnp.abs(c) * (1.0 / AXIAL_STEP)
                largest[q % 4] = jnp.maximum(largest[q % 4], rate)
            return tuple(largest)

        largest = lax.fori_loop(0, axial // 8, rows, largest, unroll=4)
        for q in range(GROUP):
            for n in range(3):
                j = g * GROUP + q
                first = vel_ref[n, j + HALO, PAD : PAD + 2, :]
                last = vel_ref[n, j + HALO, PAD + axial - 2 : PAD + axial, :]
                even_ref[n, j] = jnp.where(odd, first, last)
                odd_ref[n, j] = jnp.where(odd, last, first)
        return largest

    zero = jnp.zeros((8, radial), jnp.float32)
    m = lax.fori_loop(0, planes // GROUP, group, (zero,) * 4)
    largest = jnp.maximum(jnp.maximum(m[0], m[1]), jnp.maximum(m[2], m[3]))
    top = jnp.max(largest, axis=(0, 1), keepdims=True)
    pay_ref[...] = jnp.broadcast_to(top, pay_ref.shape)
    last = lax.broadcasted_iota(jnp.int32, (2, radial), 1) == radial - 1
    for ref in (even_ref, odd_ref):
        ref[0, 0] = jnp.where(last, top, ref[0, 0])


def pack(vel_ref, inner_ref):
    planes, (axial, radial) = vel_ref.shape[1] - 2 * HALO, inner_ref.shape
    lane = lax.broadcasted_iota(jnp.int32, (8, radial), 1)
    sign = jnp.where(lane < 2 * planes, -1.0, 1.0).astype(jnp.float32)

    def rows(i, carry):
        k = pl.multiple_of(i * 8, 8)
        inner = [jnp.zeros((8, radial), jnp.float32)] * 3
        for j in range(planes):
            for n in range(3):
                place = n * planes + j
                x = vel_ref[n, j + HALO, pl.ds(k + PAD, 8), :]
                x = pltpu.roll(x, place, 1)
                inner[n] = jnp.where(lane == place, x, inner[n])
        inner_ref[pl.ds(k, 8), :] = (inner[0] + inner[1] + inner[2]) * sign
        return carry

    lax.fori_loop(0, axial // 8, rows, 0)


def fold(even_ref, odd_ref, pay_ref, inner_in, vel_in, *refs):
    del vel_in
    fars, (inner_ref, vel_ref) = refs[:-2], refs[-2:]
    planes = even_ref.shape[1]
    axial, radial = inner_in.shape
    lane = lax.broadcasted_iota(jnp.int32, (1, radial), 1)
    top = jnp.maximum(even_ref[0, 0, 0:1, :], odd_ref[0, 0, 0:1, :])
    top = jnp.max(jnp.where(lane == radial - 1, top, 0.0), axis=(0, 1), keepdims=True)
    top = jnp.maximum(pay_ref[...], top)
    for far in fars:
        top = jnp.maximum(top, far[...])
    lane = lax.broadcasted_iota(jnp.int32, top.shape, 1)
    inner_ref[...] = inner_in[...]
    inner_ref[0:8, :] = jnp.where(lane == radial - 1, top, inner_in[0:8, :])
    wall = wall_mask(2, radial)
    odd = lax.rem(lax.axis_index("ax"), 2) == 1

    def plane(j, carry):
        for n in range(3):
            mask = wall if n == 0 else 1.0
            even, other = even_ref[n, j] * mask, odd_ref[n, j] * mask
            low, high = jnp.where(odd, even, other), jnp.where(odd, other, even)
            vel_ref[n, j + HALO, PAD - 2 : PAD, :] = low
            vel_ref[n, j + HALO, PAD + axial : PAD + axial + 2, :] = high
        return carry

    lax.fori_loop(0, planes, plane, 0, unroll=4)


def with_partner(mine_ref, inner_ref, _, top_ref):
    radial = inner_ref.shape[1]
    lane = lax.broadcasted_iota(jnp.int32, (1, radial), 1)
    top = jnp.maximum(mine_ref[0:1, :], inner_ref[0:1, :])
    top = jnp.max(jnp.where(lane == radial - 1, top, 0.0), axis=(0, 1), keepdims=True)
    top_ref[...] = jnp.broadcast_to(top, top_ref.shape)


def merged(mine_ref, far_ref, _, top_ref):
    top_ref[...] = jnp.maximum(mine_ref[...], far_ref[...])


def theta_in(even_ref, odd_ref, vel_in, _, even_tile, odd_tile, vel_ref):
    del vel_in
    planes, axial = vel_ref.shape[1] - 2 * HALO, vel_ref.shape[2] - 2 * PAD
    cells = pl.ds(PAD, axial)
    wall = wall_mask(1, vel_ref.shape[3])
    odd = lax.rem(lax.axis_index("az"), 2)
    below, above = 0, HALO + planes
    for ref, place in (
        (even_ref, jnp.where(odd == 1, below, above)),
        (odd_ref, jnp.where(odd == 1, above, below)),
    ):
        for q in range(HALO):
            vel_ref[0, place + q, cells, :] = ref[0, q] * wall
            vel_ref[1, place + q, cells, :] = ref[1, q]
            vel_ref[2, place + q, cells, :] = ref[2, q]
    first = vel_ref[1, below + HALO - 1, PAD : PAD + 1, :]
    last = vel_ref[2, above, PAD + axial - 1 : PAD + axial, :]
    odd = lax.rem(lax.axis_index("ax"), 2) == 1
    shape = even_tile.shape
    even_tile[...] = jnp.broadcast_to(jnp.where(odd, first, last), shape)
    odd_tile[...] = jnp.broadcast_to(jnp.where(odd, last, first), shape)


def ghosts(cells, inner, planes):
    radial = inner.shape[1]

    def ghost(n, q):
        turn = -(n * planes + q + cells.j) % radial
        return cells.once(("ghost", n, q), lambda: pltpu.roll(inner, turn, 1) if turn else inner)

    return ghost


def block_terms(vel_ref, inner_ref, coef_ref, j, size, write):
    planes = vel_ref.shape[1] - 2 * HALO
    axial, radial = vel_ref.shape[2] - 2 * PAD, vel_ref.shape[3]
    groups = 2 * BLOCK // size

    def rows(i, carry):
        coef = [coef_ref[n] for n in range(COUNT)]
        found = []
        for u in range(groups):
            k = pl.multiple_of((i * groups + u) * 8, 8)
            cells = Cells(vel_ref, j, k)
            ghost = None
            if inner_ref is not None:
                ghost = ghosts(cells, inner_ref[pl.ds(k, 8), :], planes)
            for q in range(size):
                found.append((q, k, terms(cells, ghost, coef, q, 1.0 / radial)))
        for q, k, values in found:
            for n, value in enumerate(values):
                write(n, j + q, pl.ds(k, 8), value)
        return carry

    lax.fori_loop(0, axial // (8 * groups), rows, 0)


def ahead(first, last, vel_ref, coef_ref, _, out_ref):
    def write(n, j, k, value):
        out_ref[n, j - first, k, :] = value

    def block(m, carry):
        block_terms(vel_ref, None, coef_ref, first + m * BLOCK, BLOCK, write)
        return carry

    lax.fori_loop(0, (last - first) // BLOCK, block, 0)


def ahead_with_ghosts(first, last, vel_ref, inner_ref, coef_ref, _, out_ref):
    def write(n, j, k, value):
        out_ref[n, j - first, k, :] = value

    for j in range(first, last, BLOCK):
        block_terms(vel_ref, inner_ref, coef_ref, j, BLOCK, write)


def finish(spans, vel_in, inner_ref, coef_ref, part_a, part_b, part_c, top, far, even, odd, *refs):
    del vel_in
    out_ref, step_ref, vel_ref, res, sems = refs
    axial, radial = inner_ref.shape
    planes = vel_ref.shape[1] - 2 * HALO
    largest = jnp.maximum(top[0:1, :], far[0:1, :])
    time_step = CFL_TARGET / (jnp.max(largest) + 1e-06)
    step_ref[0] = time_step
    scale = GAMMA * UNIT * time_step
    factors = (scale * coef_ref[WALL], scale, scale)
    pending = []

    def send(j, size):
        part_of = pl.ds(j, size)
        copy = pltpu.make_async_copy(
            res.at[:, part_of], out_ref.at[:, part_of], sems.at[len(pending)]
        )
        copy.start()
        pending.append(copy)

    def write(n, j, k, value):
        res[n, j, k, :] = value * factors[n]

    def complete(part, j, place, add):
        groups = 4

        def rows(i, carry):
            found = []
            for u in range(groups):
                k = pl.multiple_of((i * groups + u) * 8, 8)
                cells = Cells(vel_ref, j, k)
                ghost = ghosts(cells, inner_ref[pl.ds(k, 8), :], planes) if add else None
                for q in range(BLOCK):
                    values = [part[n, place + q, pl.ds(k, 8), :] for n in range(3)]
                    if add:
                        added = lane_zero_terms(cells, ghost, coef_ref, q, 1.0 / radial)
                        values = [x + y for x, y in zip(values, added)]
                    found.append((q, k, values))
            for q, k, values in found:
                for n, value in enumerate(values):
                    write(n, j + q, pl.ds(k, 8), value)
            return carry

        lax.fori_loop(0, axial // (8 * groups), rows, 0)
        send(j, BLOCK)

    for part, (first, last), add in zip((part_a, part_b, part_c), spans, (True, False, False)):
        for j in range(first, last, BLOCK):
            complete(part, j, j - first, add)
    for j in range(*spans[3], BLOCK):
        block_terms(vel_ref, inner_ref, coef_ref, j, BLOCK, write)
        send(j, BLOCK)

    second = lax.rem(lax.axis_index("ax"), 2) == 1
    even, odd = even[0:1, :], odd[0:1, :]
    following, preceding = jnp.where(second, odd, even), jnp.where(second, even, odd)
    vel_ref[1, HALO - 1, PAD + axial : PAD + axial + 1, :] = following
    vel_ref[2, HALO + planes, PAD - 1 : PAD, :] = preceding
    for j in (0, planes - HALO):
        block_terms(vel_ref, inner_ref, coef_ref, j, HALO, write)
        send(j, HALO)
    for copy in pending:
        copy.wait()


def routed(block, axis, source):
    count = lax.axis_size(axis)
    return lax.ppermute(block, axis, [(source(i), i) for i in range(count)])


def exchanged(block, axis, step):
    return routed(block, axis, lambda i: i ^ step)


def across_edges(even, odd, axis):
    count = lax.axis_size(axis)

    def source(i):
        return (i + (1 if i % 2 else -1)) % count

    return exchanged(even, axis, 1), routed(odd, axis, source)


def cuts(planes):
    last = planes - HALO
    ends = (HALO, last - 3 * BLOCK, last - 2 * BLOCK, last - BLOCK, last)
    return list(zip(ends[:-1], ends[1:]))


def per_device(velocity):
    _, planes, axial, radial = velocity.shape
    sizes = lax.axis_size("az"), lax.axis_size("ax")
    theta_step = 2.0 * math.pi / (sizes[0] * planes)
    coef = jnp.asarray(coefficients(radial, theta_step))
    f32 = jnp.float32
    anywhere = pl.BlockSpec(memory_space=pl.ANY)
    vmem = pl.BlockSpec(memory_space=pltpu.VMEM)
    smem = pl.BlockSpec(memory_space=pltpu.SMEM)

    def shape(*sizes):
        return jax.ShapeDtypeStruct(sizes, f32)

    def call(kernel, name, work, scratch=0, **kwargs):
        return pl.pallas_call(
            kernel,
            name=name,
            compiler_params=pltpu.CompilerParams(vmem_limit_bytes=(4 + scratch) * 2**20),
            cost_estimate=pl.CostEstimate(flops=work, bytes_accessed=work, transcendentals=0),
            **kwargs,
        )

    odd = lax.axis_index("az") % 2
    ends = (planes - HALO, 0)
    even_end = jnp.where(odd == 1, ends[1], ends[0])
    odd_end = jnp.where(odd == 1, ends[0], ends[1])
    theta_even, theta_odd = across_edges(
        lax.dynamic_slice_in_dim(velocity, even_end, HALO, 1),
        lax.dynamic_slice_in_dim(velocity, odd_end, HALO, 1),
        "az",
    )

    edge = shape(3, planes, 2, radial)
    padded = shape(3, planes + 2 * HALO, axial + 2 * PAD, radial)
    row = shape(axial, radial)
    tile = shape(8, radial)
    vel, edge_even, edge_odd, pay = call(
        functools.partial(first_pass, theta_step),
        "first_pass",
        0,
        out_shape=(padded, edge, edge, tile),
        in_specs=[anywhere],
        out_specs=(vmem,) * 4,
        scratch_shapes=[pltpu.SemaphoreType.DMA((planes // GROUP,))],
    )(pltpu.with_memory_space_constraint(velocity, pltpu.HBM))
    z_even, z_odd = across_edges(edge_even, edge_odd, "ax")
    fars = [
        routed(pay, "ax", lambda i, step=step: (i + step) % sizes[1])
        for step in range(2, sizes[1] - 1)
    ]
    inner = call(
        pack,
        "pack",
        velocity.size,
        out_shape=row,
        in_specs=[vmem],
        out_specs=vmem,
    )(vel)
    mine, vel = call(
        fold,
        "fold",
        0,
        out_shape=(row, padded),
        in_specs=[vmem] * (5 + len(fars)),
        out_specs=(vmem,) * 2,
        input_output_aliases={4: 1},
    )(z_even, z_odd, pay, inner, vel, *fars)
    inner = exchanged(mine, "az", sizes[0] // 2)

    spans = cuts(planes)

    def part_shape(n):
        return shape(3, spans[n][1] - spans[n][0], axial, radial)

    part_a = call(
        functools.partial(ahead, *spans[0]),
        "ahead",
        velocity.size,
        out_shape=part_shape(0),
        in_specs=[vmem] * 3,
        out_specs=vmem,
    )(vel, coef, mine)
    top = call(
        with_partner,
        "with_partner",
        0,
        out_shape=tile,
        in_specs=[vmem] * 3,
        out_specs=vmem,
    )(mine, inner, part_a)
    steps = [1 << n for n in range((sizes[0] // 2).bit_length() - 1)]
    far = exchanged(top, "az", steps[0])

    def with_ghosts(n, token):
        return call(
            functools.partial(ahead_with_ghosts, *spans[n]),
            f"ahead_with_ghosts_{n}",
            velocity.size,
            out_shape=part_shape(n),
            in_specs=[vmem] * 4,
            out_specs=vmem,
        )(vel, inner, coef, token)

    part_b = with_ghosts(1, top)
    for step in steps[1:]:
        top = call(
            merged,
            "merged",
            0,
            out_shape=tile,
            in_specs=[vmem] * 3,
            out_specs=vmem,
        )(top, far, part_b)
        far = exchanged(top, "az", step)
    tile_even, tile_odd, vel = call(
        theta_in,
        "theta_in",
        0,
        out_shape=(tile, tile, padded),
        in_specs=[vmem] * 4,
        out_specs=(vmem,) * 3,
        input_output_aliases={2: 2},
    )(theta_even, theta_odd, vel, top)
    corner_even, corner_odd = across_edges(tile_even, tile_odd, "ax")
    part_c = with_ghosts(2, tile_even)
    increment, time_step, _ = call(
        functools.partial(finish, spans),
        "finish",
        0,
        scratch=8,
        out_shape=(shape(*velocity.shape), shape(1), padded),
        in_specs=[vmem] * 10,
        out_specs=(anywhere, smem, vmem),
        scratch_shapes=[
            pltpu.VMEM(velocity.shape, f32),
            pltpu.SemaphoreType.DMA(((planes - 2 * HALO) // BLOCK + 2,)),
        ],
        input_output_aliases={0: 2},
    )(vel, inner, coef, part_a, part_b, part_c, top, far, corner_even, corner_odd)
    return increment, time_step.reshape(())


def solution(mesh):
    return jax.shard_map(
        per_device,
        mesh=mesh,
        in_specs=(P(None, "az", "ax", None),),
        out_specs=(P(None, "az", "ax", None), P()),
        check_vma=False,
    )
```

```python
import functools
import math

import jax
import jax.numpy as jnp
import numpy as np
from jax import lax
from jax.experimental import pallas as pl
from jax.experimental.pallas import tpu as pltpu
from jax.sharding import PartitionSpec as P

AXIAL_STEP = 0.01
VISCOSITY = 0.001
CFL_TARGET = 1.2
GAMMA = 8.0 / 15.0

PAD = 8
HALO = 2
BLOCK = 4
GROUP = 4
UNROLL = 4

(
    WALL,
    RADIAL_C,
    THETA_C,
    CROSS_Z,
    SECOND_C,
    CENTRE_Z,
    CENTRE_T,
    CURVE_T,
    TURN_T,
    RADIAL_F,
    THETA_F,
    SECOND_F,
    CENTRE_R,
    CURVE_R,
    TURN_R,
    COUNT,
) = range(16)


UNIT = VISCOSITY / (12.0 * AXIAL_STEP**2)


def coefficients(radial, theta_step):
    dr = 1.0 / radial
    index = np.arange(radial, dtype=np.float64)
    centre = (index + 0.5) * dr
    face = (index + 1.0) * dr
    wall = np.where(index < radial - 1.5, 1.0, 0.0)
    h = theta_step
    nu = VISCOSITY
    rows = np.zeros((COUNT, radial))
    rows[WALL] = wall
    common = -2.0 * nu / dr**2 - 30.0 * nu / (12.0 * AXIAL_STEP**2)
    rows[RADIAL_C] = nu / (2.0 * dr * centre)
    rows[THETA_C] = -1.0 / (12.0 * h * centre)
    rows[CROSS_Z] = 0.25 * rows[THETA_C]
    rows[SECOND_C] = nu / (12.0 * h * h * centre**2)
    rows[CENTRE_Z] = common - 30.0 * rows[SECOND_C]
    rows[CENTRE_T] = rows[CENTRE_Z] - nu / centre**2
    rows[CURVE_T] = 0.25 / centre
    rows[TURN_T] = nu / (h * centre**2)
    rows[RADIAL_F] = nu / (2.0 * dr * face)
    rows[THETA_F] = -0.25 / (12.0 * h * face)
    rows[SECOND_F] = nu / (12.0 * h * h * face**2)
    rows[CENTRE_R] = common - 30.0 * rows[SECOND_F] - nu / face**2
    rows[CURVE_R] = 1.0 / (16.0 * face)
    rows[TURN_R] = -nu / (h * face**2)
    rows[RADIAL_C:] /= UNIT
    return np.broadcast_to(rows[:, None, :], (COUNT, 8, radial)).astype(np.float32)


class Cells:
    def __init__(self, vel, j, k):
        self.vel, self.j, self.k, self.known = vel, j, k, {}

    def once(self, key, make):
        if key not in self.known:
            self.known[key] = make()
        return self.known[key]

    def at(self, n, dj, dk=0):
        rows = pl.ds(self.k + PAD + dk, 8)
        return self.once((n, dj, dk), lambda: self.vel[n, self.j + HALO + dj, rows, :])

    def turned(self, by, n, dj, dk=0):
        return self.once(
            (by, n, dj, dk), lambda: pltpu.roll(self.at(n, dj, dk), by % self.vel.shape[3], 1)
        )

    def pair(self, by, n, dj, dk=0):
        return self.once(
            ("pair", n, dj, dk), lambda: self.at(n, dj, dk) + self.turned(by, n, dj, dk)
        )

    def beside(self, dj, dk):
        n = 1 if dk >= 0 else 2
        other = (1, dj - 1, dk) if n == 1 else (2, dj, dk)
        here = (1, dj, dk) if n == 1 else (2, dj, dk + 1)
        return self.once(("sum", n, dj, dk), lambda: self.at(*other) + self.at(*here))


def terms(cells, ghost, coef, q, dr):
    at, turned, pair = cells.at, cells.turned, cells.pair
    a, b, c = (at(n, q) for n in range(3))
    lane = lax.broadcasted_iota(jnp.int32, a.shape, 1)
    first_lane = lane == 0
    last_lane = lane == a.shape[1] - 1

    lap = VISCOSITY / dr**2 / UNIT
    adv_z = -1.0 / (12.0 * AXIAL_STEP) / UNIT
    by_dr = 1.0 / dr / UNIT

    def differences(p1, m1, p2, m2):
        return 8.0 * (p1 - m1) - (p2 - m2), 16.0 * (p1 + m1) - (p2 + m2)

    def pieces(n):
        over = differences(*(at(n, q + d) for d in (1, -1, 2, -2)))
        along = differences(*(at(n, q, d) for d in (1, -1, 2, -2)))
        return over, along

    def below(n):
        if ghost is not None and n > 0 and q % 2 == 0:
            x = jnp.where(last_lane, ghost(n, q + 1), at(n, q))
            return pltpu.roll(x, 1, 1)
        x = turned(1, n, q)
        if ghost is not None:
            return jnp.where(first_lane, ghost(n, q), x)
        return x if n == 0 else jnp.where(first_lane, 0.0, x)

    def above(n):
        return jnp.where(last_lane, -at(n, q), turned(-1, n, q))

    pair_a, pair_side, pair_next = pair(1, 0, q), pair(1, 0, q + 1), pair(1, 0, q, 1)
    pair_b, pair_back = pair(-1, 1, q), pair(-1, 1, q - 1)

    theta, axial = pieces(2)
    up, low = above(2), below(2)
    u_r = pair_a + pair_next
    u_t = cells.beside(q, 0) + cells.beside(q, 1)
    h_z = (up - low) * (coef[RADIAL_C] - u_r * (0.125 * by_dr)) + (up + low) * lap
    h_z = h_z + theta[0] * (u_t * coef[CROSS_Z])
    h_z = h_z + (theta[1] * coef[SECOND_C] + axial[1])
    h_z = h_z + c * (coef[CENTRE_Z] + axial[0] * adv_z)

    theta, axial = pieces(1)
    up, low = above(1), below(1)
    u_r = pair_a + pair_side
    u_z = cells.beside(q, -1) + cells.beside(q + 1, -1)
    h_t = (up - low) * (coef[RADIAL_C] - u_r * (0.125 * by_dr)) + (up + low) * lap
    h_t = h_t + b * (coef[CENTRE_T] + theta[0] * coef[THETA_C] - u_r * coef[CURVE_T])
    h_t = h_t + (theta[1] * coef[SECOND_C] + axial[1])
    h_t = h_t + axial[0] * (u_z * (0.25 * adv_z))
    h_t = h_t + (pair_side - pair_a) * coef[TURN_T]

    theta, axial = pieces(0)
    up, low = turned(-1, 0, q), below(0)
    u_t = pair_b + pair_back
    u_z = pair(-1, 2, q) + pair(-1, 2, q, -1)
    h_r = (up - low) * (coef[RADIAL_F] - a * (0.5 * by_dr)) + (up + low) * lap
    h_r = h_r + u_t * (u_t * coef[CURVE_R] + theta[0] * coef[THETA_F])
    h_r = h_r + (theta[1] * coef[SECOND_F] + axial[1])
    h_r = h_r + (axial[0] * (u_z * (0.25 * adv_z)) + a * coef[CENTRE_R])
    h_r = h_r + (pair_b - pair_back) * coef[TURN_R]
    return h_r, h_t, h_z


def lane_zero_terms(cells, ghost, coef, q, dr):
    lap = VISCOSITY / dr**2 / UNIT
    by_dr = 1.0 / dr / UNIT
    a = cells.at(0, q)
    first_lane = lax.broadcasted_iota(jnp.int32, a.shape, 1) == 0
    add_r = ghost(0, q) * (lap - coef[RADIAL_F] + a * (0.5 * by_dr))
    add_t = ghost(1, q) * (lap - coef[RADIAL_C] + (a + cells.at(0, q + 1)) * (0.125 * by_dr))
    add_z = ghost(2, q) * (lap - coef[RADIAL_C] + (a + cells.at(0, q, 1)) * (0.125 * by_dr))
    return tuple(jnp.where(first_lane, x, 0.0) for x in (add_r, add_t, add_z))


def wall_mask(rows, radial):
    lane = lax.broadcasted_iota(jnp.int32, (rows, radial), 1)
    return jnp.where(lane == radial - 1, 0.0, 1.0).astype(jnp.float32)


def first_pass(theta_step, v_ref, vel_ref, even_ref, odd_ref, inner_ref, pay_ref, sems):
    _, planes, axial, radial = v_ref.shape
    lane = lax.broadcasted_iota(jnp.int32, (8, radial), 1)
    wall = wall_mask(8, radial)
    rate_t = (radial / theta_step) / (lane.astype(jnp.float32) + 0.5)
    odd = lax.rem(lax.axis_index("ax"), 2) == 1

    def fetch(g):
        part = pl.ds(g * GROUP, GROUP)
        target = vel_ref.at[:, pl.ds(g * GROUP + HALO, GROUP), pl.ds(PAD, axial)]
        return pltpu.make_async_copy(v_ref.at[:, part], target, sems.at[g])

    for g in range(planes // GROUP):
        fetch(g).start()

    zero = jnp.zeros((8, radial), jnp.float32)
    largest = [zero] * 4
    for g in range(planes // GROUP):
        fetch(g).wait()
        for i in range(axial // 8):
            k = pl.ds(8 * i, 8)
            padded = pl.ds(8 * i + PAD, 8)
            inner = zero if g == 0 else inner_ref[k, :]
            for q in range(GROUP):
                j = g * GROUP + q
                cells = [vel_ref[n, j + HALO, padded, :] for n in range(3)]
                for n, x in enumerate(cells):
                    place = n * planes + j
                    x = pltpu.roll(x, place, 1) if place else x
                    inner = jnp.where(lane == place, x if n == 2 else -x, inner)
                a, b, c = cells
                a = a * wall
                vel_ref[0, j + HALO, padded, :] = a
                rate = jnp.abs(a) * float(radial) + jnp.abs(b) * rate_t
                rate = rate + jnp.abs(c) * (1.0 / AXIAL_STEP)
                largest[q % 4] = jnp.maximum(largest[q % 4], rate)
            inner_ref[k, :] = inner
        for q in range(GROUP):
            for n in range(3):
                j = g * GROUP + q
                first = vel_ref[n, j + HALO, PAD : PAD + 2, :]
                last = vel_ref[n, j + HALO, PAD + axial - 2 : PAD + axial, :]
                even_ref[n, j] = jnp.where(odd, first, last)
                odd_ref[n, j] = jnp.where(odd, last, first)

    largest = jnp.maximum(
        jnp.maximum(largest[0], largest[1]), jnp.maximum(largest[2], largest[3])
    )
    top = jnp.max(largest, axis=(0, 1), keepdims=True)
    pay_ref[...] = jnp.broadcast_to(top, pay_ref.shape)
    end = lax.broadcasted_iota(jnp.int32, (2, radial), 1) == radial - 1
    for ref in (even_ref, odd_ref):
        ref[0, 0] = jnp.where(end, top, ref[0, 0])


def fold(even_ref, odd_ref, pay_ref, vel_in, *refs):
    del vel_in
    fars, (top_ref, vel_ref) = refs[:-2], refs[-2:]
    planes, radial = even_ref.shape[1], even_ref.shape[3]
    axial = vel_ref.shape[2] - 2 * PAD
    lane = lax.broadcasted_iota(jnp.int32, (1, radial), 1)
    top = jnp.maximum(even_ref[0, 0, 0:1, :], odd_ref[0, 0, 0:1, :])
    top = jnp.max(jnp.where(lane == radial - 1, top, 0.0), axis=(0, 1), keepdims=True)
    top = jnp.maximum(pay_ref[...], top)
    for far in fars:
        top = jnp.maximum(top, far[...])
    top_ref[...] = top
    wall = wall_mask(2, radial)
    odd = lax.rem(lax.axis_index("ax"), 2) == 1

    def plane(j, carry):
        for n in range(3):
            mask = wall if n == 0 else 1.0
            even, other = even_ref[n, j] * mask, odd_ref[n, j] * mask
            low, high = jnp.where(odd, even, other), jnp.where(odd, other, even)
            vel_ref[n, j + HALO, PAD - 2 : PAD, :] = low
            vel_ref[n, j + HALO, PAD + axial : PAD + axial + 2, :] = high
        return carry

    lax.fori_loop(0, planes, plane, 0, unroll=4)


def merged(mine_ref, far_ref, _, top_ref):
    top_ref[...] = jnp.maximum(mine_ref[...], far_ref[...])


def theta_in(even_ref, odd_ref, vel_in, _, even_tile, odd_tile, vel_ref):
    del vel_in
    planes, axial = vel_ref.shape[1] - 2 * HALO, vel_ref.shape[2] - 2 * PAD
    cells = pl.ds(PAD, axial)
    wall = wall_mask(1, vel_ref.shape[3])
    odd = lax.rem(lax.axis_index("az"), 2)
    below, above = 0, HALO + planes
    for ref, place in (
        (even_ref, jnp.where(odd == 1, below, above)),
        (odd_ref, jnp.where(odd == 1, above, below)),
    ):
        for q in range(HALO):
            vel_ref[0, place + q, cells, :] = ref[0, q] * wall
            vel_ref[1, place + q, cells, :] = ref[1, q]
            vel_ref[2, place + q, cells, :] = ref[2, q]
    first = vel_ref[1, below + HALO - 1, PAD : PAD + 1, :]
    last = vel_ref[2, above, PAD + axial - 1 : PAD + axial, :]
    odd = lax.rem(lax.axis_index("ax"), 2) == 1
    shape = even_tile.shape
    even_tile[...] = jnp.broadcast_to(jnp.where(odd, first, last), shape)
    odd_tile[...] = jnp.broadcast_to(jnp.where(odd, last, first), shape)


def ghosts(cells, inner, planes):
    radial = inner.shape[1]

    def ghost(n, q):
        turn = -(n * planes + q + cells.j) % radial
        return cells.once(("ghost", n, q), lambda: pltpu.roll(inner, turn, 1) if turn else inner)

    return ghost


def block_terms(vel_ref, inner_ref, coef_ref, j, size, write):
    planes = vel_ref.shape[1] - 2 * HALO
    axial, radial = vel_ref.shape[2] - 2 * PAD, vel_ref.shape[3]
    groups = 2 * BLOCK // size

    def rows(i, carry):
        coef = [coef_ref[n] for n in range(COUNT)]
        found = []
        for u in range(groups):
            k = pl.multiple_of((i * groups + u) * 8, 8)
            cells = Cells(vel_ref, j, k)
            ghost = None
            if inner_ref is not None:
                ghost = ghosts(cells, inner_ref[pl.ds(k, 8), :], planes)
            for q in range(size):
                found.append((q, k, terms(cells, ghost, coef, q, 1.0 / radial)))
        for q, k, values in found:
            for n, value in enumerate(values):
                write(n, j + q, pl.ds(k, 8), value)
        return carry

    lax.fori_loop(0, axial // (8 * groups), rows, 0)


def ahead(first, last, vel_ref, coef_ref, _, out_ref):
    def write(n, j, k, value):
        out_ref[n, j - first, k, :] = value

    def block(m, carry):
        block_terms(vel_ref, None, coef_ref, first + m * BLOCK, BLOCK, write)
        return carry

    lax.fori_loop(0, (last - first) // BLOCK, block, 0)


def ahead_with_ghosts(first, last, vel_ref, inner_ref, coef_ref, _, out_ref):
    def write(n, j, k, value):
        out_ref[n, j - first, k, :] = value

    for j in range(first, last, BLOCK):
        block_terms(vel_ref, inner_ref, coef_ref, j, BLOCK, write)


def finish(spans, vel_in, inner_ref, coef_ref, top, far, even, odd, *refs):
    parts, refs = refs[: len(spans)], refs[len(spans) :]
    del vel_in
    out_ref, step_ref, vel_ref, res, sems = refs
    axial, radial = inner_ref.shape
    planes = vel_ref.shape[1] - 2 * HALO
    largest = jnp.maximum(top[0:1, :], far[0:1, :])
    time_step = CFL_TARGET / (jnp.max(largest) + 1e-06)
    step_ref[0] = time_step
    scale = GAMMA * UNIT * time_step
    factors = (scale * coef_ref[WALL], scale, scale)
    pending = []

    def send(j, size):
        part_of = pl.ds(j, size)
        copy = pltpu.make_async_copy(
            res.at[:, part_of], out_ref.at[:, part_of], sems.at[len(pending)]
        )
        copy.start()
        pending.append(copy)

    def write(n, j, k, value):
        res[n, j, k, :] = value * factors[n]

    def complete(part, j, place, add):
        groups = 4

        def rows(i, carry):
            found = []
            for u in range(groups):
                k = pl.multiple_of((i * groups + u) * 8, 8)
                cells = Cells(vel_ref, j, k)
                ghost = ghosts(cells, inner_ref[pl.ds(k, 8), :], planes) if add else None
                for q in range(BLOCK):
                    values = [part[n, place + q, pl.ds(k, 8), :] for n in range(3)]
                    if add:
                        added = lane_zero_terms(cells, ghost, coef_ref, q, 1.0 / radial)
                        values = [x + y for x, y in zip(values, added)]
                    found.append((q, k, values))
            for q, k, values in found:
                for n, value in enumerate(values):
                    write(n, j + q, pl.ds(k, 8), value)
            return carry

        lax.fori_loop(0, axial // (8 * groups), rows, 0)
        send(j, BLOCK)

    for n, (part, (first, last)) in enumerate(zip(parts, spans)):
        for j in range(first, last, BLOCK):
            complete(part, j, j - first, n == 0)

    second = lax.rem(lax.axis_index("ax"), 2) == 1
    even, odd = even[0:1, :], odd[0:1, :]
    following, preceding = jnp.where(second, odd, even), jnp.where(second, even, odd)
    vel_ref[1, HALO - 1, PAD + axial : PAD + axial + 1, :] = following
    vel_ref[2, HALO + planes, PAD - 1 : PAD, :] = preceding
    for j in (0, planes - HALO):
        block_terms(vel_ref, inner_ref, coef_ref, j, HALO, write)
        send(j, HALO)
    for copy in pending:
        copy.wait()


def routed(block, axis, source):
    count = lax.axis_size(axis)
    return lax.ppermute(block, axis, [(source(i), i) for i in range(count)])


def exchanged(block, axis, step):
    return routed(block, axis, lambda i: i ^ step)


def across_edges(even, odd, axis):
    count = lax.axis_size(axis)

    def source(i):
        return (i + (1 if i % 2 else -1)) % count

    return exchanged(even, axis, 1), routed(odd, axis, source)


def cuts(planes):
    last = planes - HALO
    ends = (HALO, last - 5 * BLOCK, last - 3 * BLOCK, last - BLOCK, last)
    return list(zip(ends[:-1], ends[1:]))


def per_device(velocity):
    _, planes, axial, radial = velocity.shape
    sizes = lax.axis_size("az"), lax.axis_size("ax")
    theta_step = 2.0 * math.pi / (sizes[0] * planes)
    coef = jnp.asarray(coefficients(radial, theta_step))
    f32 = jnp.float32
    anywhere = pl.BlockSpec(memory_space=pl.ANY)
    vmem = pl.BlockSpec(memory_space=pltpu.VMEM)
    smem = pl.BlockSpec(memory_space=pltpu.SMEM)

    def shape(*sizes):
        return jax.ShapeDtypeStruct(sizes, f32)

    def call(kernel, name, work, scratch=0, **kwargs):
        return pl.pallas_call(
            kernel,
            name=name,
            compiler_params=pltpu.CompilerParams(vmem_limit_bytes=(4 + scratch) * 2**20),
            cost_estimate=pl.CostEstimate(flops=work, bytes_accessed=work, transcendentals=0),
            **kwargs,
        )

    odd = lax.axis_index("az") % 2
    ends = (planes - HALO, 0)
    even_end = jnp.where(odd == 1, ends[1], ends[0])
    odd_end = jnp.where(odd == 1, ends[0], ends[1])
    theta_even, theta_odd = across_edges(
        lax.dynamic_slice_in_dim(velocity, even_end, HALO, 1),
        lax.dynamic_slice_in_dim(velocity, odd_end, HALO, 1),
        "az",
    )

    edge = shape(3, planes, 2, radial)
    padded = shape(3, planes + 2 * HALO, axial + 2 * PAD, radial)
    row = shape(axial, radial)
    tile = shape(8, radial)
    vel, edge_even, edge_odd, mine, pay = call(
        functools.partial(first_pass, theta_step),
        "first_pass",
        0,
        out_shape=(padded, edge, edge, row, tile),
        in_specs=[anywhere],
        out_specs=(vmem,) * 5,
        scratch_shapes=[pltpu.SemaphoreType.DMA((planes // GROUP,))],
    )(pltpu.with_memory_space_constraint(velocity, pltpu.HBM))
    z_even, z_odd = across_edges(edge_even, edge_odd, "ax")
    fars = [
        routed(pay, "ax", lambda i, step=step: (i + step) % sizes[1])
        for step in range(2, sizes[1] - 1)
    ]
    inner = exchanged(mine, "az", sizes[0] // 2)
    top, vel = call(
        fold,
        "fold",
        0,
        out_shape=(tile, padded),
        in_specs=[vmem] * (4 + len(fars)),
        out_specs=(vmem,) * 2,
        input_output_aliases={3: 1},
    )(z_even, z_odd, pay, vel, *fars)

    spans = cuts(planes)

    def span(n, token):
        kernel, given = (ahead, (vel, coef)) if n == 0 else (ahead_with_ghosts, (vel, inner, coef))
        first, last = spans[n]
        return call(
            functools.partial(kernel, first, last),
            f"span_{n}",
            velocity.size * 2,
            out_shape=shape(3, last - first, axial, radial),
            in_specs=[vmem] * (len(given) + 1),
            out_specs=vmem,
        )(*given, token)

    parts, token = [], top
    for n in range(sizes[0].bit_length() - 1):
        if n > 0:
            top = token = call(
                merged,
                "merged",
                0,
                out_shape=tile,
                in_specs=[vmem] * 3,
                out_specs=vmem,
            )(top, far, parts[-1])
        far = exchanged(top, "az", 1 << n)
        if n < 3:
            parts.append(span(n, token))
    tile_even, tile_odd, vel = call(
        theta_in,
        "theta_in",
        0,
        out_shape=(tile, tile, padded),
        in_specs=[vmem] * 4,
        out_specs=(vmem,) * 3,
        input_output_aliases={2: 2},
    )(theta_even, theta_odd, vel, parts[-1])
    corner_even, corner_odd = across_edges(tile_even, tile_odd, "ax")
    parts.append(span(3, tile_even))
    increment, time_step, _ = call(
        functools.partial(finish, spans),
        "finish",
        0,
        scratch=8,
        out_shape=(shape(*velocity.shape), shape(1), padded),
        in_specs=[vmem] * (7 + len(parts)),
        out_specs=(anywhere, smem, vmem),
        scratch_shapes=[
            pltpu.VMEM(velocity.shape, f32),
            pltpu.SemaphoreType.DMA(((planes - 2 * HALO) // BLOCK + 2,)),
        ],
        input_output_aliases={0: 2},
    )(vel, inner, coef, top, far, corner_even, corner_odd, *parts)
    return increment, time_step.reshape(())


def solution(mesh):
    return jax.shard_map(
        per_device,
        mesh=mesh,
        in_specs=(P(None, "az", "ax", None),),
        out_specs=(P(None, "az", "ax", None), P()),
        check_vma=False,
    )
```

```python
import functools
import math

import jax
import jax.numpy as jnp
import numpy as np
from jax import lax
from jax.experimental import pallas as pl
from jax.experimental.pallas import tpu as pltpu
from jax.sharding import PartitionSpec as P

AXIAL_STEP = 0.01
VISCOSITY = 0.001
CFL_TARGET = 1.2
GAMMA = 8.0 / 15.0

PAD = 8
HALO = 2
BLOCK = 4
GROUP = 4
UNROLL = 4

(
    WALL,
    RADIAL_C,
    THETA_C,
    CROSS_Z,
    SECOND_C,
    CENTRE_Z,
    CENTRE_T,
    CURVE_T,
    TURN_T,
    RADIAL_F,
    THETA_F,
    SECOND_F,
    CENTRE_R,
    CURVE_R,
    TURN_R,
    COUNT,
) = range(16)


UNIT = VISCOSITY / (12.0 * AXIAL_STEP**2)


def coefficients(radial, theta_step):
    dr = 1.0 / radial
    index = np.arange(radial, dtype=np.float64)
    centre = (index + 0.5) * dr
    face = (index + 1.0) * dr
    wall = np.where(index < radial - 1.5, 1.0, 0.0)
    h = theta_step
    nu = VISCOSITY
    rows = np.zeros((COUNT, radial))
    rows[WALL] = wall
    common = -2.0 * nu / dr**2 - 30.0 * nu / (12.0 * AXIAL_STEP**2)
    rows[RADIAL_C] = nu / (2.0 * dr * centre)
    rows[THETA_C] = -1.0 / (12.0 * h * centre)
    rows[CROSS_Z] = 0.25 * rows[THETA_C]
    rows[SECOND_C] = nu / (12.0 * h * h * centre**2)
    rows[CENTRE_Z] = common - 30.0 * rows[SECOND_C]
    rows[CENTRE_T] = rows[CENTRE_Z] - nu / centre**2
    rows[CURVE_T] = 0.25 / centre
    rows[TURN_T] = nu / (h * centre**2)
    rows[RADIAL_F] = nu / (2.0 * dr * face)
    rows[THETA_F] = -0.25 / (12.0 * h * face)
    rows[SECOND_F] = nu / (12.0 * h * h * face**2)
    rows[CENTRE_R] = common - 30.0 * rows[SECOND_F] - nu / face**2
    rows[CURVE_R] = 1.0 / (16.0 * face)
    rows[TURN_R] = -nu / (h * face**2)
    rows[RADIAL_C:] /= UNIT
    return np.broadcast_to(rows[:, None, :], (COUNT, 8, radial)).astype(np.float32)


class Cells:
    def __init__(self, vel, j, k):
        self.vel, self.j, self.k, self.known = vel, j, k, {}

    def once(self, key, make):
        if key not in self.known:
            self.known[key] = make()
        return self.known[key]

    def at(self, n, dj, dk=0):
        rows = pl.ds(self.k + PAD + dk, 8)
        return self.once((n, dj, dk), lambda: self.vel[n, self.j + HALO + dj, rows, :])

    def turned(self, by, n, dj, dk=0):
        return self.once(
            (by, n, dj, dk), lambda: pltpu.roll(self.at(n, dj, dk), by % self.vel.shape[3], 1)
        )

    def pair(self, by, n, dj, dk=0):
        return self.once(
            ("pair", n, dj, dk), lambda: self.at(n, dj, dk) + self.turned(by, n, dj, dk)
        )

    def beside(self, dj, dk):
        n = 1 if dk >= 0 else 2
        other = (1, dj - 1, dk) if n == 1 else (2, dj, dk)
        here = (1, dj, dk) if n == 1 else (2, dj, dk + 1)
        return self.once(("sum", n, dj, dk), lambda: self.at(*other) + self.at(*here))


def terms(cells, ghost, coef, q, dr):
    at, turned, pair = cells.at, cells.turned, cells.pair
    a, b, c = (at(n, q) for n in range(3))
    lane = lax.broadcasted_iota(jnp.int32, a.shape, 1)
    first_lane = lane == 0
    last_lane = lane == a.shape[1] - 1

    lap = VISCOSITY / dr**2 / UNIT
    adv_z = -1.0 / (12.0 * AXIAL_STEP) / UNIT
    by_dr = 1.0 / dr / UNIT

    def differences(p1, m1, p2, m2):
        return 8.0 * (p1 - m1) - (p2 - m2), 16.0 * (p1 + m1) - (p2 + m2)

    def pieces(n):
        over = differences(*(at(n, q + d) for d in (1, -1, 2, -2)))
        along = differences(*(at(n, q, d) for d in (1, -1, 2, -2)))
        return over, along

    def below(n):
        if ghost is not None and n > 0 and q % 2 == 0:
            x = jnp.where(last_lane, ghost(n, q + 1), at(n, q))
            return pltpu.roll(x, 1, 1)
        x = turned(1, n, q)
        if ghost is not None:
            return jnp.where(first_lane, ghost(n, q), x)
        return x if n == 0 else jnp.where(first_lane, 0.0, x)

    def above(n):
        return jnp.where(last_lane, -at(n, q), turned(-1, n, q))

    pair_a, pair_side, pair_next = pair(1, 0, q), pair(1, 0, q + 1), pair(1, 0, q, 1)
    pair_b, pair_back = pair(-1, 1, q), pair(-1, 1, q - 1)

    theta, axial = pieces(2)
    up, low = above(2), below(2)
    u_r = pair_a + pair_next
    u_t = cells.beside(q, 0) + cells.beside(q, 1)
    h_z = (up - low) * (coef[RADIAL_C] - u_r * (0.125 * by_dr)) + (up + low) * lap
    h_z = h_z + theta[0] * (u_t * coef[CROSS_Z])
    h_z = h_z + (theta[1] * coef[SECOND_C] + axial[1])
    h_z = h_z + c * (coef[CENTRE_Z] + axial[0] * adv_z)

    theta, axial = pieces(1)
    up, low = above(1), below(1)
    u_r = pair_a + pair_side
    u_z = cells.beside(q, -1) + cells.beside(q + 1, -1)
    h_t = (up - low) * (coef[RADIAL_C] - u_r * (0.125 * by_dr)) + (up + low) * lap
    h_t = h_t + b * (coef[CENTRE_T] + theta[0] * coef[THETA_C] - u_r * coef[CURVE_T])
    h_t = h_t + (theta[1] * coef[SECOND_C] + axial[1])
    h_t = h_t + axial[0] * (u_z * (0.25 * adv_z))
    h_t = h_t + (pair_side - pair_a) * coef[TURN_T]

    theta, axial = pieces(0)
    up, low = turned(-1, 0, q), below(0)
    u_t = pair_b + pair_back
    u_z = pair(-1, 2, q) + pair(-1, 2, q, -1)
    h_r = (up - low) * (coef[RADIAL_F] - a * (0.5 * by_dr)) + (up + low) * lap
    h_r = h_r + u_t * (u_t * coef[CURVE_R] + theta[0] * coef[THETA_F])
    h_r = h_r + (theta[1] * coef[SECOND_F] + axial[1])
    h_r = h_r + (axial[0] * (u_z * (0.25 * adv_z)) + a * coef[CENTRE_R])
    h_r = h_r + (pair_b - pair_back) * coef[TURN_R]
    return h_r, h_t, h_z


def lane_zero_terms(cells, ghost, coef, q, dr):
    lap = VISCOSITY / dr**2 / UNIT
    by_dr = 1.0 / dr / UNIT
    a = cells.at(0, q)
    first_lane = lax.broadcasted_iota(jnp.int32, a.shape, 1) == 0
    add_r = ghost(0, q) * (lap - coef[RADIAL_F] + a * (0.5 * by_dr))
    add_t = ghost(1, q) * (lap - coef[RADIAL_C] + (a + cells.at(0, q + 1)) * (0.125 * by_dr))
    add_z = ghost(2, q) * (lap - coef[RADIAL_C] + (a + cells.at(0, q, 1)) * (0.125 * by_dr))
    return tuple(jnp.where(first_lane, x, 0.0) for x in (add_r, add_t, add_z))


def wall_mask(rows, radial):
    lane = lax.broadcasted_iota(jnp.int32, (rows, radial), 1)
    return jnp.where(lane == radial - 1, 0.0, 1.0).astype(jnp.float32)


def first_pass(theta_step, v_ref, vel_ref, even_ref, odd_ref, inner_ref, pay_ref, sems):
    _, planes, axial, radial = v_ref.shape
    lane = lax.broadcasted_iota(jnp.int32, (8, radial), 1)
    wall = wall_mask(8, radial)
    rate_t = (radial / theta_step) / (lane.astype(jnp.float32) + 0.5)
    odd = lax.rem(lax.axis_index("ax"), 2) == 1

    def fetch(g):
        part = pl.ds(g * GROUP, GROUP)
        target = vel_ref.at[:, pl.ds(g * GROUP + HALO, GROUP), pl.ds(PAD, axial)]
        return pltpu.make_async_copy(v_ref.at[:, part], target, sems.at[g])

    for g in range(planes // GROUP):
        fetch(g).start()

    zero = jnp.zeros((8, radial), jnp.float32)
    largest = [zero] * 4
    for g in range(planes // GROUP):
        fetch(g).wait()
        for i in range(axial // 8):
            k = pl.ds(8 * i, 8)
            padded = pl.ds(8 * i + PAD, 8)
            inner = zero if g == 0 else inner_ref[k, :]
            for q in range(GROUP):
                j = g * GROUP + q
                cells = [vel_ref[n, j + HALO, padded, :] for n in range(3)]
                for n, x in enumerate(cells):
                    place = n * planes + j
                    x = pltpu.roll(x, place, 1) if place else x
                    inner = jnp.where(lane == place, x if n == 2 else -x, inner)
                a, b, c = cells
                a = a * wall
                vel_ref[0, j + HALO, padded, :] = a
                rate = jnp.abs(a) * float(radial) + jnp.abs(b) * rate_t
                rate = rate + jnp.abs(c) * (1.0 / AXIAL_STEP)
                largest[q % 4] = jnp.maximum(largest[q % 4], rate)
            inner_ref[k, :] = inner
        for q in range(GROUP):
            for n in range(3):
                j = g * GROUP + q
                first = vel_ref[n, j + HALO, PAD : PAD + 2, :]
                last = vel_ref[n, j + HALO, PAD + axial - 2 : PAD + axial, :]
                even_ref[n, j] = jnp.where(odd, first, last)
                odd_ref[n, j] = jnp.where(odd, last, first)

    largest = jnp.maximum(
        jnp.maximum(largest[0], largest[1]), jnp.maximum(largest[2], largest[3])
    )
    top = jnp.max(largest, axis=(0, 1), keepdims=True)
    pay_ref[...] = jnp.broadcast_to(top, pay_ref.shape)
    end = lax.broadcasted_iota(jnp.int32, (2, radial), 1) == radial - 1
    for ref in (even_ref, odd_ref):
        ref[0, 0] = jnp.where(end, top, ref[0, 0])


def carried(even_ref, pay_ref, odd_in, odd_ref):
    radial = even_ref.shape[3]
    lane = lax.broadcasted_iota(jnp.int32, (2, radial), 1)
    top = jnp.maximum(even_ref[0, 0], pay_ref[0:2, :])
    odd_ref[0, 0] = jnp.where(lane == radial - 1, top, odd_in[0, 0])


def fold(even_ref, odd_ref, pay_ref, vel_in, _, *refs):
    del vel_in
    top_ref, vel_ref = refs
    planes, radial = even_ref.shape[1], even_ref.shape[3]
    axial = vel_ref.shape[2] - 2 * PAD
    lane = lax.broadcasted_iota(jnp.int32, (1, radial), 1)
    top = jnp.maximum(even_ref[0, 0, 0:1, :], odd_ref[0, 0, 0:1, :])
    top = jnp.max(jnp.where(lane == radial - 1, top, 0.0), axis=(0, 1), keepdims=True)
    top_ref[...] = jnp.maximum(pay_ref[...], top)
    wall = wall_mask(2, radial)
    odd = lax.rem(lax.axis_index("ax"), 2) == 1

    def plane(j, carry):
        for n in range(3):
            mask = wall if n == 0 else 1.0
            even, other = even_ref[n, j] * mask, odd_ref[n, j] * mask
            low, high = jnp.where(odd, even, other), jnp.where(odd, other, even)
            vel_ref[n, j + HALO, PAD - 2 : PAD, :] = low
            vel_ref[n, j + HALO, PAD + axial : PAD + axial + 2, :] = high
        return carry

    lax.fori_loop(0, planes, plane, 0, unroll=4)


def merged(mine_ref, far_ref, *refs):
    refs[-1][...] = jnp.maximum(mine_ref[...], far_ref[...])


def theta_in(even_ref, odd_ref, vel_in, _, even_tile, odd_tile, vel_ref):
    del vel_in
    planes, axial = vel_ref.shape[1] - 2 * HALO, vel_ref.shape[2] - 2 * PAD
    cells = pl.ds(PAD, axial)
    wall = wall_mask(1, vel_ref.shape[3])
    odd = lax.rem(lax.axis_index("az"), 2)
    below, above = 0, HALO + planes
    for ref, place in (
        (even_ref, jnp.where(odd == 1, below, above)),
        (odd_ref, jnp.where(odd == 1, above, below)),
    ):
        for q in range(HALO):
            vel_ref[0, place + q, cells, :] = ref[0, q] * wall
            vel_ref[1, place + q, cells, :] = ref[1, q]
            vel_ref[2, place + q, cells, :] = ref[2, q]
    first = vel_ref[1, below + HALO - 1, PAD : PAD + 1, :]
    last = vel_ref[2, above, PAD + axial - 1 : PAD + axial, :]
    odd = lax.rem(lax.axis_index("ax"), 2) == 1
    shape = even_tile.shape
    even_tile[...] = jnp.broadcast_to(jnp.where(odd, first, last), shape)
    odd_tile[...] = jnp.broadcast_to(jnp.where(odd, last, first), shape)


def ghosts(cells, inner, planes):
    radial = inner.shape[1]

    def ghost(n, q):
        turn = -(n * planes + q + cells.j) % radial
        return cells.once(("ghost", n, q), lambda: pltpu.roll(inner, turn, 1) if turn else inner)

    return ghost


def block_terms(vel_ref, inner_ref, coef_ref, j, size, write, rounds=None):
    planes = vel_ref.shape[1] - 2 * HALO
    axial, radial = vel_ref.shape[2] - 2 * PAD, vel_ref.shape[3]
    groups = 2 * BLOCK // size
    times, places = rounds or (
        axial // (8 * groups),
        lambda i: [(i * groups + u) * 8 for u in range(groups)],
    )

    def rows(i, carry):
        coef = [coef_ref[n] for n in range(COUNT)]
        found = []
        for k in places(i):
            k = pl.multiple_of(k, 8)
            cells = Cells(vel_ref, j, k)
            ghost = None
            if inner_ref is not None:
                ghost = ghosts(cells, inner_ref[pl.ds(k, 8), :], planes)
            for q in range(size):
                found.append((q, k, terms(cells, ghost, coef, q, 1.0 / radial)))
        for q, k, values in found:
            for n, value in enumerate(values):
                write(n, j + q, pl.ds(k, 8), value)
        return carry

    lax.fori_loop(0, times, rows, 0)


def ahead(first, last, rounds, vel_ref, coef_ref, *refs):
    out_ref = refs[-1]

    def write(n, j, k, value):
        out_ref[n, j - first, k, :] = value

    def block(m, carry):
        block_terms(vel_ref, None, coef_ref, first + m * BLOCK, BLOCK, write, rounds)
        return carry

    lax.fori_loop(0, (last - first) // BLOCK, block, 0)


def ahead_with_ghosts(first, last, vel_ref, inner_ref, coef_ref, _, out_ref):
    def write(n, j, k, value):
        out_ref[n, j - first, k, :] = value

    for j in range(first, last, BLOCK):
        block_terms(vel_ref, inner_ref, coef_ref, j, BLOCK, write)


def finish(spans, vel_in, inner_ref, coef_ref, top, far, even, odd, *refs):
    parts, refs = refs[: len(spans)], refs[len(spans) :]
    del vel_in
    out_ref, step_ref, vel_ref, res, sems = refs
    axial, radial = inner_ref.shape
    planes = vel_ref.shape[1] - 2 * HALO
    largest = jnp.maximum(top[0:1, :], far[0:1, :])
    time_step = CFL_TARGET / (jnp.max(largest) + 1e-06)
    step_ref[0] = time_step
    scale = GAMMA * UNIT * time_step
    factors = (scale * coef_ref[WALL], scale, scale)
    pending = []

    def send(j, size):
        part_of = pl.ds(j, size)
        copy = pltpu.make_async_copy(
            res.at[:, part_of], out_ref.at[:, part_of], sems.at[len(pending)]
        )
        copy.start()
        pending.append(copy)

    def write(n, j, k, value):
        res[n, j, k, :] = value * factors[n]

    def complete(part, j, place, add):
        groups = 4

        def rows(i, carry):
            found = []
            for u in range(groups):
                k = pl.multiple_of((i * groups + u) * 8, 8)
                cells = Cells(vel_ref, j, k)
                ghost = ghosts(cells, inner_ref[pl.ds(k, 8), :], planes) if add else None
                for q in range(BLOCK):
                    values = [part[n, place + q, pl.ds(k, 8), :] for n in range(3)]
                    if add:
                        added = lane_zero_terms(cells, ghost, coef_ref, q, 1.0 / radial)
                        values = [x + y for x, y in zip(values, added)]
                    found.append((q, k, values))
            for q, k, values in found:
                for n, value in enumerate(values):
                    write(n, j + q, pl.ds(k, 8), value)
            return carry

        lax.fori_loop(0, axial // (8 * groups), rows, 0)
        send(j, BLOCK)

    for n, (part, (first, last)) in enumerate(zip(parts, spans)):
        for j in range(first, last, BLOCK):
            complete(part, j, j - first, n < 2)

    second = lax.rem(lax.axis_index("ax"), 2) == 1
    even, odd = even[0:1, :], odd[0:1, :]
    following, preceding = jnp.where(second, odd, even), jnp.where(second, even, odd)
    vel_ref[1, HALO - 1, PAD + axial : PAD + axial + 1, :] = following
    vel_ref[2, HALO + planes, PAD - 1 : PAD, :] = preceding
    for j in (0, planes - HALO):
        block_terms(vel_ref, inner_ref, coef_ref, j, HALO, write)
        send(j, HALO)
    for copy in pending:
        copy.wait()


def routed(block, axis, source):
    count = lax.axis_size(axis)
    return lax.ppermute(block, axis, [(source(i), i) for i in range(count)])


def exchanged(block, axis, step):
    return routed(block, axis, lambda i: i ^ step)


def across_even(block, axis):
    return exchanged(block, axis, 1)


def across_odd(block, axis):
    count = lax.axis_size(axis)
    return routed(block, axis, lambda i: (i + (1 if i % 2 else -1)) % count)


def cuts(planes):
    last = planes - HALO
    ends = (HALO, last - 5 * BLOCK, last - 4 * BLOCK, last - 2 * BLOCK, last - BLOCK, last)
    return list(zip(ends[:-1], ends[1:]))


def per_device(velocity):
    _, planes, axial, radial = velocity.shape
    sizes = lax.axis_size("az"), lax.axis_size("ax")
    theta_step = 2.0 * math.pi / (sizes[0] * planes)
    coef = jnp.asarray(coefficients(radial, theta_step))
    f32 = jnp.float32
    anywhere = pl.BlockSpec(memory_space=pl.ANY)
    vmem = pl.BlockSpec(memory_space=pltpu.VMEM)
    smem = pl.BlockSpec(memory_space=pltpu.SMEM)

    def shape(*sizes):
        return jax.ShapeDtypeStruct(sizes, f32)

    def call(kernel, name, work, scratch=0, **kwargs):
        return pl.pallas_call(
            kernel,
            name=name,
            compiler_params=pltpu.CompilerParams(vmem_limit_bytes=(4 + scratch) * 2**20),
            cost_estimate=pl.CostEstimate(flops=work, bytes_accessed=work, transcendentals=0),
            **kwargs,
        )

    odd = lax.axis_index("az") % 2
    ends = (planes - HALO, 0)
    even_end = jnp.where(odd == 1, ends[1], ends[0])
    odd_end = jnp.where(odd == 1, ends[0], ends[1])
    theta_even = across_even(lax.dynamic_slice_in_dim(velocity, even_end, HALO, 1), "az")
    theta_odd = across_odd(lax.dynamic_slice_in_dim(velocity, odd_end, HALO, 1), "az")

    edge = shape(3, planes, 2, radial)
    padded = shape(3, planes + 2 * HALO, axial + 2 * PAD, radial)
    row = shape(axial, radial)
    tile = shape(8, radial)
    vel, edge_even, edge_odd, mine, pay = call(
        functools.partial(first_pass, theta_step),
        "first_pass",
        0,
        out_shape=(padded, edge, edge, row, tile),
        in_specs=[anywhere],
        out_specs=(vmem,) * 5,
        scratch_shapes=[pltpu.SemaphoreType.DMA((planes // GROUP,))],
    )(pltpu.with_memory_space_constraint(velocity, pltpu.HBM))
    inner = exchanged(mine, "az", sizes[0] // 2)
    z_even = across_even(edge_even, "ax")
    edge_odd = call(
        carried,
        "carried",
        0,
        out_shape=edge,
        in_specs=[vmem] * 3,
        out_specs=vmem,
        input_output_aliases={2: 0},
    )(z_even, pay, edge_odd)
    z_odd = across_odd(edge_odd, "ax")

    spans = cuts(planes)

    def part_shape(n):
        return shape(3, spans[n][1] - spans[n][0], axial, radial)

    def without_ghosts(n, name, rounds, vel, *tokens, **kwargs):
        return call(
            functools.partial(ahead, *spans[n], rounds),
            name,
            velocity.size * 2,
            out_shape=part_shape(n),
            in_specs=[vmem] * (2 + len(tokens)),
            out_specs=vmem,
            **kwargs,
        )(vel, coef, *tokens)

    def with_ghosts(n, token):
        return call(
            functools.partial(ahead_with_ghosts, *spans[n]),
            f"span_{n}",
            velocity.size * 2,
            out_shape=part_shape(n),
            in_specs=[vmem] * 4,
            out_specs=vmem,
        )(vel, inner, coef, token)

    middle = (axial - 16) // 16, lambda i: [16 * i + 8, 16 * i + 16]
    outer = 1, lambda i: [i * 8, i * 8 + axial - 8]
    part = without_ghosts(0, "span_0_middle", middle, vel, pay)
    top, vel = call(
        fold,
        "fold",
        0,
        out_shape=(tile, padded),
        in_specs=[vmem] * 5,
        out_specs=(vmem,) * 2,
        input_output_aliases={3: 1},
    )(z_even, z_odd, pay, vel, part)
    for step in (1 << n for n in range(2, sizes[1].bit_length() - 1)):
        top = jnp.maximum(top, routed(top, "ax", lambda i, step=step: (i + step) % sizes[1]))

    bits = [1 << n for n in range(1, sizes[0].bit_length() - 1)] + [1]
    far = exchanged(top, "az", bits[0])
    parts = [
        without_ghosts(0, "span_0_outer", outer, vel, part, input_output_aliases={2: 0}),
        without_ghosts(1, "span_1", None, vel, top),
    ]
    for n, bit in enumerate(bits[1:]):
        top = call(
            merged,
            "merged",
            0,
            out_shape=tile,
            in_specs=[vmem] * 4,
            out_specs=vmem,
        )(top, far, *parts[-2:])
        far = exchanged(top, "az", bit)
        if n < 2:
            parts.append(with_ghosts(n + 2, top))
    tile_even, tile_odd, vel = call(
        theta_in,
        "theta_in",
        0,
        out_shape=(tile, tile, padded),
        in_specs=[vmem] * 4,
        out_specs=(vmem,) * 3,
        input_output_aliases={2: 2},
    )(theta_even, theta_odd, vel, parts[-1])
    corner_even, corner_odd = across_even(tile_even, "ax"), across_odd(tile_odd, "ax")
    parts.append(with_ghosts(4, tile_even))
    increment, time_step, _ = call(
        functools.partial(finish, spans),
        "finish",
        0,
        scratch=8,
        out_shape=(shape(*velocity.shape), shape(1), padded),
        in_specs=[vmem] * (7 + len(parts)),
        out_specs=(anywhere, smem, vmem),
        scratch_shapes=[
            pltpu.VMEM(velocity.shape, f32),
            pltpu.SemaphoreType.DMA(((planes - 2 * HALO) // BLOCK + 2,)),
        ],
        input_output_aliases={0: 2},
    )(vel, inner, coef, top, far, corner_even, corner_odd, *parts)
    return increment, time_step.reshape(())


def solution(mesh):
    return jax.shard_map(
        per_device,
        mesh=mesh,
        in_specs=(P(None, "az", "ax", None),),
        out_specs=(P(None, "az", "ax", None), P()),
        check_vma=False,
    )
```

```python
import functools
import math

import jax
import jax.numpy as jnp
import numpy as np
from jax import lax
from jax.experimental import pallas as pl
from jax.experimental.pallas import tpu as pltpu
from jax.sharding import PartitionSpec as P

AXIAL_STEP = 0.01
VISCOSITY = 0.001
CFL_TARGET = 1.2
GAMMA = 8.0 / 15.0

PAD = 8
HALO = 2
BLOCK = 4
GROUP = 4
UNROLL = 4

(
    WALL,
    RADIAL_C,
    THETA_C,
    CROSS_Z,
    SECOND_C,
    CENTRE_Z,
    CENTRE_T,
    CURVE_T,
    TURN_T,
    RADIAL_F,
    THETA_F,
    SECOND_F,
    CENTRE_R,
    CURVE_R,
    TURN_R,
    COUNT,
) = range(16)


UNIT = VISCOSITY / (12.0 * AXIAL_STEP**2)


def coefficients(radial, theta_step):
    dr = 1.0 / radial
    index = np.arange(radial, dtype=np.float64)
    centre = (index + 0.5) * dr
    face = (index + 1.0) * dr
    wall = np.where(index < radial - 1.5, 1.0, 0.0)
    h = theta_step
    nu = VISCOSITY
    rows = np.zeros((COUNT, radial))
    rows[WALL] = wall
    common = -2.0 * nu / dr**2 - 30.0 * nu / (12.0 * AXIAL_STEP**2)
    rows[RADIAL_C] = nu / (2.0 * dr * centre)
    rows[THETA_C] = -1.0 / (12.0 * h * centre)
    rows[CROSS_Z] = 0.25 * rows[THETA_C]
    rows[SECOND_C] = nu / (12.0 * h * h * centre**2)
    rows[CENTRE_Z] = common - 30.0 * rows[SECOND_C]
    rows[CENTRE_T] = rows[CENTRE_Z] - nu / centre**2
    rows[CURVE_T] = 0.25 / centre
    rows[TURN_T] = nu / (h * centre**2)
    rows[RADIAL_F] = nu / (2.0 * dr * face)
    rows[THETA_F] = -0.25 / (12.0 * h * face)
    rows[SECOND_F] = nu / (12.0 * h * h * face**2)
    rows[CENTRE_R] = common - 30.0 * rows[SECOND_F] - nu / face**2
    rows[CURVE_R] = 1.0 / (16.0 * face)
    rows[TURN_R] = -nu / (h * face**2)
    rows[RADIAL_C:] /= UNIT
    return np.broadcast_to(rows[:, None, :], (COUNT, 8, radial)).astype(np.float32)


class Cells:
    def __init__(self, vel, j, k):
        self.vel, self.j, self.k, self.known = vel, j, k, {}

    def once(self, key, make):
        if key not in self.known:
            self.known[key] = make()
        return self.known[key]

    def at(self, n, dj, dk=0):
        rows = pl.ds(self.k + PAD + dk, 8)
        return self.once((n, dj, dk), lambda: self.vel[n, self.j + HALO + dj, rows, :])

    def turned(self, by, n, dj, dk=0):
        return self.once(
            (by, n, dj, dk), lambda: pltpu.roll(self.at(n, dj, dk), by % self.vel.shape[3], 1)
        )

    def pair(self, by, n, dj, dk=0):
        return self.once(
            ("pair", n, dj, dk), lambda: self.at(n, dj, dk) + self.turned(by, n, dj, dk)
        )

    def beside(self, dj, dk):
        n = 1 if dk >= 0 else 2
        other = (1, dj - 1, dk) if n == 1 else (2, dj, dk)
        here = (1, dj, dk) if n == 1 else (2, dj, dk + 1)
        return self.once(("sum", n, dj, dk), lambda: self.at(*other) + self.at(*here))


def terms(cells, ghost, coef, q, dr):
    at, turned, pair = cells.at, cells.turned, cells.pair
    a, b, c = (at(n, q) for n in range(3))
    lane = lax.broadcasted_iota(jnp.int32, a.shape, 1)
    first_lane = lane == 0
    last_lane = lane == a.shape[1] - 1

    lap = VISCOSITY / dr**2 / UNIT
    adv_z = -1.0 / (12.0 * AXIAL_STEP) / UNIT
    by_dr = 1.0 / dr / UNIT

    def differences(p1, m1, p2, m2):
        return 8.0 * (p1 - m1) - (p2 - m2), 16.0 * (p1 + m1) - (p2 + m2)

    def pieces(n):
        over = differences(*(at(n, q + d) for d in (1, -1, 2, -2)))
        along = differences(*(at(n, q, d) for d in (1, -1, 2, -2)))
        return over, along

    def below(n):
        if ghost is not None and n > 0 and q % 2 == 0:
            x = jnp.where(last_lane, ghost(n, q + 1), at(n, q))
            return pltpu.roll(x, 1, 1)
        x = turned(1, n, q)
        if ghost is not None:
            return jnp.where(first_lane, ghost(n, q), x)
        return x if n == 0 else jnp.where(first_lane, 0.0, x)

    def above(n):
        return jnp.where(last_lane, -at(n, q), turned(-1, n, q))

    pair_a, pair_side, pair_next = pair(1, 0, q), pair(1, 0, q + 1), pair(1, 0, q, 1)
    pair_b, pair_back = pair(-1, 1, q), pair(-1, 1, q - 1)

    theta, axial = pieces(2)
    up, low = above(2), below(2)
    u_r = pair_a + pair_next
    u_t = cells.beside(q, 0) + cells.beside(q, 1)
    h_z = (up - low) * (coef[RADIAL_C] - u_r * (0.125 * by_dr)) + (up + low) * lap
    h_z = h_z + theta[0] * (u_t * coef[CROSS_Z])
    h_z = h_z + (theta[1] * coef[SECOND_C] + axial[1])
    h_z = h_z + c * (coef[CENTRE_Z] + axial[0] * adv_z)

    theta, axial = pieces(1)
    up, low = above(1), below(1)
    u_r = pair_a + pair_side
    u_z = cells.beside(q, -1) + cells.beside(q + 1, -1)
    h_t = (up - low) * (coef[RADIAL_C] - u_r * (0.125 * by_dr)) + (up + low) * lap
    h_t = h_t + b * (coef[CENTRE_T] + theta[0] * coef[THETA_C] - u_r * coef[CURVE_T])
    h_t = h_t + (theta[1] * coef[SECOND_C] + axial[1])
    h_t = h_t + axial[0] * (u_z * (0.25 * adv_z))
    h_t = h_t + (pair_side - pair_a) * coef[TURN_T]

    theta, axial = pieces(0)
    up, low = turned(-1, 0, q), below(0)
    u_t = pair_b + pair_back
    u_z = pair(-1, 2, q) + pair(-1, 2, q, -1)
    h_r = (up - low) * (coef[RADIAL_F] - a * (0.5 * by_dr)) + (up + low) * lap
    h_r = h_r + u_t * (u_t * coef[CURVE_R] + theta[0] * coef[THETA_F])
    h_r = h_r + (theta[1] * coef[SECOND_F] + axial[1])
    h_r = h_r + (axial[0] * (u_z * (0.25 * adv_z)) + a * coef[CENTRE_R])
    h_r = h_r + (pair_b - pair_back) * coef[TURN_R]
    return h_r, h_t, h_z


def lane_zero_terms(cells, ghost, coef, q, dr):
    lap = VISCOSITY / dr**2 / UNIT
    by_dr = 1.0 / dr / UNIT
    a = cells.at(0, q)
    first_lane = lax.broadcasted_iota(jnp.int32, a.shape, 1) == 0
    add_r = ghost(0, q) * (lap - coef[RADIAL_F] + a * (0.5 * by_dr))
    add_t = ghost(1, q) * (lap - coef[RADIAL_C] + (a + cells.at(0, q + 1)) * (0.125 * by_dr))
    add_z = ghost(2, q) * (lap - coef[RADIAL_C] + (a + cells.at(0, q, 1)) * (0.125 * by_dr))
    return tuple(jnp.where(first_lane, x, 0.0) for x in (add_r, add_t, add_z))


def wall_mask(rows, radial):
    lane = lax.broadcasted_iota(jnp.int32, (rows, radial), 1)
    return jnp.where(lane == radial - 1, 0.0, 1.0).astype(jnp.float32)


def first_pass(theta_step, v_ref, vel_ref, even_ref, odd_ref, inner_ref, pay_ref, sems):
    _, planes, axial, radial = v_ref.shape
    lane = lax.broadcasted_iota(jnp.int32, (8, radial), 1)
    wall = wall_mask(8, radial)
    rate_t = (radial / theta_step) / (lane.astype(jnp.float32) + 0.5)
    odd = lax.rem(lax.axis_index("ax"), 2) == 1

    def fetch(g):
        part = pl.ds(g * GROUP, GROUP)
        target = vel_ref.at[:, pl.ds(g * GROUP + HALO, GROUP), pl.ds(PAD, axial)]
        return pltpu.make_async_copy(v_ref.at[:, part], target, sems.at[g])

    for g in range(planes // GROUP):
        fetch(g).start()

    zero = jnp.zeros((8, radial), jnp.float32)
    largest = [zero] * 4
    for g in range(planes // GROUP):
        fetch(g).wait()
        for i in range(axial // 8):
            k = pl.ds(8 * i, 8)
            padded = pl.ds(8 * i + PAD, 8)
            inner = zero if g == 0 else inner_ref[k, :]
            for q in range(GROUP):
                j = g * GROUP + q
                cells = [vel_ref[n, j + HALO, padded, :] for n in range(3)]
                for n, x in enumerate(cells):
                    place = n * planes + j
                    x = pltpu.roll(x, place, 1) if place else x
                    inner = jnp.where(lane == place, x if n == 2 else -x, inner)
                a, b, c = cells
                a = a * wall
                vel_ref[0, j + HALO, padded, :] = a
                rate = jnp.abs(a) * float(radial) + jnp.abs(b) * rate_t
                rate = rate + jnp.abs(c) * (1.0 / AXIAL_STEP)
                largest[q % 4] = jnp.maximum(largest[q % 4], rate)
            inner_ref[k, :] = inner
        for q in range(GROUP):
            for n in range(3):
                j = g * GROUP + q
                first = vel_ref[n, j + HALO, PAD : PAD + 2, :]
                last = vel_ref[n, j + HALO, PAD + axial - 2 : PAD + axial, :]
                even_ref[n, j] = jnp.where(odd, first, last)
                odd_ref[n, j] = jnp.where(odd, last, first)

    largest = jnp.maximum(
        jnp.maximum(largest[0], largest[1]), jnp.maximum(largest[2], largest[3])
    )
    top = jnp.max(largest, axis=(0, 1), keepdims=True)
    pay_ref[...] = jnp.broadcast_to(top, pay_ref.shape)
    end = lax.broadcasted_iota(jnp.int32, (2, radial), 1) == radial - 1
    for ref in (even_ref, odd_ref):
        ref[0, 0] = jnp.where(end, top, ref[0, 0])


def carried(even_ref, pay_ref, odd_in, odd_ref):
    radial = even_ref.shape[3]
    lane = lax.broadcasted_iota(jnp.int32, (2, radial), 1)
    top = jnp.maximum(even_ref[0, 0], pay_ref[0:2, :])
    odd_ref[0, 0] = jnp.where(lane == radial - 1, top, odd_in[0, 0])


def fold(even_ref, odd_ref, pay_ref, vel_in, _, *refs):
    del vel_in
    top_ref, vel_ref = refs
    planes, radial = even_ref.shape[1], even_ref.shape[3]
    axial = vel_ref.shape[2] - 2 * PAD
    lane = lax.broadcasted_iota(jnp.int32, (1, radial), 1)
    top = jnp.maximum(even_ref[0, 0, 0:1, :], odd_ref[0, 0, 0:1, :])
    top = jnp.max(jnp.where(lane == radial - 1, top, 0.0), axis=(0, 1), keepdims=True)
    top_ref[...] = jnp.maximum(pay_ref[...], top)
    wall = wall_mask(2, radial)
    odd = lax.rem(lax.axis_index("ax"), 2) == 1

    def plane(j, carry):
        for n in range(3):
            mask = wall if n == 0 else 1.0
            even, other = even_ref[n, j] * mask, odd_ref[n, j] * mask
            low, high = jnp.where(odd, even, other), jnp.where(odd, other, even)
            vel_ref[n, j + HALO, PAD - 2 : PAD, :] = low
            vel_ref[n, j + HALO, PAD + axial : PAD + axial + 2, :] = high
        return carry

    lax.fori_loop(0, planes, plane, 0, unroll=4)


def merged(mine_ref, far_ref, *refs):
    refs[-1][...] = jnp.maximum(mine_ref[...], far_ref[...])


def theta_in(even_ref, odd_ref, vel_in, _, even_tile, odd_tile, vel_ref):
    del vel_in
    planes, axial = vel_ref.shape[1] - 2 * HALO, vel_ref.shape[2] - 2 * PAD
    cells = pl.ds(PAD, axial)
    wall = wall_mask(1, vel_ref.shape[3])
    odd = lax.rem(lax.axis_index("az"), 2)
    below, above = 0, HALO + planes
    for ref, place in (
        (even_ref, jnp.where(odd == 1, below, above)),
        (odd_ref, jnp.where(odd == 1, above, below)),
    ):
        for q in range(HALO):
            vel_ref[0, place + q, cells, :] = ref[0, q] * wall
            vel_ref[1, place + q, cells, :] = ref[1, q]
            vel_ref[2, place + q, cells, :] = ref[2, q]
    first = vel_ref[1, below + HALO - 1, PAD : PAD + 1, :]
    last = vel_ref[2, above, PAD + axial - 1 : PAD + axial, :]
    odd = lax.rem(lax.axis_index("ax"), 2) == 1
    shape = even_tile.shape
    even_tile[...] = jnp.broadcast_to(jnp.where(odd, first, last), shape)
    odd_tile[...] = jnp.broadcast_to(jnp.where(odd, last, first), shape)


def ghosts(cells, inner, planes):
    radial = inner.shape[1]

    def ghost(n, q):
        turn = -(n * planes + q + cells.j) % radial
        return cells.once(("ghost", n, q), lambda: pltpu.roll(inner, turn, 1) if turn else inner)

    return ghost


def block_terms(vel_ref, inner_ref, coef_ref, j, size, write, rounds=None):
    planes = vel_ref.shape[1] - 2 * HALO
    axial, radial = vel_ref.shape[2] - 2 * PAD, vel_ref.shape[3]
    groups = 2 * BLOCK // size
    times, places = rounds or (
        axial // (8 * groups),
        lambda i: [(i * groups + u) * 8 for u in range(groups)],
    )

    def rows(i, carry):
        coef = [coef_ref[n] for n in range(COUNT)]
        found = []
        for k in places(i):
            k = pl.multiple_of(k, 8)
            cells = Cells(vel_ref, j, k)
            ghost = None
            if inner_ref is not None:
                ghost = ghosts(cells, inner_ref[pl.ds(k, 8), :], planes)
            for q in range(size):
                found.append((q, k, terms(cells, ghost, coef, q, 1.0 / radial)))
        for q, k, values in found:
            for n, value in enumerate(values):
                write(n, j + q, pl.ds(k, 8), value)
        return carry

    lax.fori_loop(0, times, rows, 0)


def ahead(first, last, rounds, vel_ref, coef_ref, *refs):
    out_ref = refs[-1]

    def write(n, j, k, value):
        out_ref[n, j - first, k, :] = value

    def block(m, carry):
        block_terms(vel_ref, None, coef_ref, first + m * BLOCK, BLOCK, write, rounds)
        return carry

    lax.fori_loop(0, (last - first) // BLOCK, block, 0)


def ahead_with_ghosts(first, last, vel_ref, inner_ref, coef_ref, _, out_ref):
    def write(n, j, k, value):
        out_ref[n, j - first, k, :] = value

    for j in range(first, last, BLOCK):
        block_terms(vel_ref, inner_ref, coef_ref, j, BLOCK, write)


def finish(spans, vel_in, inner_ref, coef_ref, top, far, even, odd, *refs):
    parts, refs = refs[: len(spans)], refs[len(spans) :]
    del vel_in
    out_ref, step_ref, vel_ref, res, sems = refs
    axial, radial = inner_ref.shape
    planes = vel_ref.shape[1] - 2 * HALO
    largest = jnp.maximum(top[0:1, :], far[0:1, :])
    time_step = CFL_TARGET / (jnp.max(largest) + 1e-06)
    step_ref[0] = time_step
    scale = GAMMA * UNIT * time_step
    factors = (scale * coef_ref[WALL], scale, scale)
    pending = []

    def send(j, size):
        part_of = pl.ds(j, size)
        copy = pltpu.make_async_copy(
            res.at[:, part_of], out_ref.at[:, part_of], sems.at[len(pending)]
        )
        copy.start()
        pending.append(copy)

    def write(n, j, k, value):
        res[n, j, k, :] = value * factors[n]

    def complete(part, j, place, add):
        groups = 4

        def rows(i, carry):
            found = []
            for u in range(groups):
                k = pl.multiple_of((i * groups + u) * 8, 8)
                cells = Cells(vel_ref, j, k)
                ghost = ghosts(cells, inner_ref[pl.ds(k, 8), :], planes) if add else None
                for q in range(BLOCK):
                    values = [part[n, place + q, pl.ds(k, 8), :] for n in range(3)]
                    if add:
                        added = lane_zero_terms(cells, ghost, coef_ref, q, 1.0 / radial)
                        values = [x + y for x, y in zip(values, added)]
                    found.append((q, k, values))
            for q, k, values in found:
                for n, value in enumerate(values):
                    write(n, j + q, pl.ds(k, 8), value)
            return carry

        lax.fori_loop(0, axial // (8 * groups), rows, 0)
        send(j, BLOCK)

    for n, (part, (first, last)) in enumerate(zip(parts, spans)):
        for j in range(first, last, BLOCK):
            complete(part, j, j - first, n < 2)

    second = lax.rem(lax.axis_index("ax"), 2) == 1
    even, odd = even[0:1, :], odd[0:1, :]
    following, preceding = jnp.where(second, odd, even), jnp.where(second, even, odd)
    vel_ref[1, HALO - 1, PAD + axial : PAD + axial + 1, :] = following
    vel_ref[2, HALO + planes, PAD - 1 : PAD, :] = preceding
    for j in (0, planes - HALO):
        block_terms(vel_ref, inner_ref, coef_ref, j, HALO, write)
        send(j, HALO)
    for copy in pending:
        copy.wait()


def routed(block, axis, source):
    count = lax.axis_size(axis)
    return lax.ppermute(block, axis, [(source(i), i) for i in range(count)])


def exchanged(block, axis, step):
    return routed(block, axis, lambda i: i ^ step)


def across_even(block, axis):
    return exchanged(block, axis, 1)


def across_odd(block, axis):
    count = lax.axis_size(axis)
    return routed(block, axis, lambda i: (i + (1 if i % 2 else -1)) % count)


def cuts(planes):
    last = planes - HALO
    ends = (HALO, last - 5 * BLOCK, last - 3 * BLOCK, last - BLOCK, last)
    return list(zip(ends[:-1], ends[1:]))


def per_device(velocity):
    _, planes, axial, radial = velocity.shape
    sizes = lax.axis_size("az"), lax.axis_size("ax")
    theta_step = 2.0 * math.pi / (sizes[0] * planes)
    coef = jnp.asarray(coefficients(radial, theta_step))
    f32 = jnp.float32
    anywhere = pl.BlockSpec(memory_space=pl.ANY)
    vmem = pl.BlockSpec(memory_space=pltpu.VMEM)
    smem = pl.BlockSpec(memory_space=pltpu.SMEM)

    def shape(*sizes):
        return jax.ShapeDtypeStruct(sizes, f32)

    def call(kernel, name, work, scratch=0, **kwargs):
        return pl.pallas_call(
            kernel,
            name=name,
            compiler_params=pltpu.CompilerParams(vmem_limit_bytes=(4 + scratch) * 2**20),
            cost_estimate=pl.CostEstimate(flops=work, bytes_accessed=work, transcendentals=0),
            **kwargs,
        )

    odd = lax.axis_index("az") % 2
    ends = (planes - HALO, 0)
    even_end = jnp.where(odd == 1, ends[1], ends[0])
    odd_end = jnp.where(odd == 1, ends[0], ends[1])
    theta_even = across_even(lax.dynamic_slice_in_dim(velocity, even_end, HALO, 1), "az")
    theta_odd = across_odd(lax.dynamic_slice_in_dim(velocity, odd_end, HALO, 1), "az")

    edge = shape(3, planes, 2, radial)
    padded = shape(3, planes + 2 * HALO, axial + 2 * PAD, radial)
    row = shape(axial, radial)
    tile = shape(8, radial)
    vel, edge_even, edge_odd, mine, pay = call(
        functools.partial(first_pass, theta_step),
        "first_pass",
        0,
        out_shape=(padded, edge, edge, row, tile),
        in_specs=[anywhere],
        out_specs=(vmem,) * 5,
        scratch_shapes=[pltpu.SemaphoreType.DMA((planes // GROUP,))],
    )(pltpu.with_memory_space_constraint(velocity, pltpu.HBM))
    inner = exchanged(mine, "az", sizes[0] // 2)
    z_even = across_even(edge_even, "ax")
    edge_odd = call(
        carried,
        "carried",
        0,
        out_shape=edge,
        in_specs=[vmem] * 3,
        out_specs=vmem,
        input_output_aliases={2: 0},
    )(z_even, pay, edge_odd)
    z_odd = across_odd(edge_odd, "ax")

    spans = cuts(planes)

    def part_shape(n):
        return shape(3, spans[n][1] - spans[n][0], axial, radial)

    def without_ghosts(n, name, rounds, vel, *tokens, **kwargs):
        return call(
            functools.partial(ahead, *spans[n], rounds),
            name,
            velocity.size * 2,
            out_shape=part_shape(n),
            in_specs=[vmem] * (2 + len(tokens)),
            out_specs=vmem,
            **kwargs,
        )(vel, coef, *tokens)

    def with_ghosts(n, token):
        return call(
            functools.partial(ahead_with_ghosts, *spans[n]),
            f"span_{n}",
            velocity.size * 2,
            out_shape=part_shape(n),
            in_specs=[vmem] * 4,
            out_specs=vmem,
        )(vel, inner, coef, token)

    middle = (axial - 16) // 16, lambda i: [16 * i + 8, 16 * i + 16]
    outer = 1, lambda i: [i * 8, i * 8 + axial - 8]
    part = without_ghosts(0, "span_0_middle", middle, vel, pay)
    top, vel = call(
        fold,
        "fold",
        0,
        out_shape=(tile, padded),
        in_specs=[vmem] * 5,
        out_specs=(vmem,) * 2,
        input_output_aliases={3: 1},
    )(z_even, z_odd, pay, vel, part)
    for step in (1 << n for n in range(2, sizes[1].bit_length() - 1)):
        top = jnp.maximum(top, routed(top, "ax", lambda i, step=step: (i + step) % sizes[1]))

    bits = [1 << n for n in range(1, sizes[0].bit_length() - 1)] + [1]
    far = exchanged(top, "az", bits[0])
    parts = [
        without_ghosts(0, "span_0_outer", outer, vel, part, input_output_aliases={2: 0}),
        without_ghosts(1, "span_1", None, vel, top),
    ]
    for n, bit in enumerate(bits[1:]):
        top = call(
            merged,
            "merged",
            0,
            out_shape=tile,
            in_specs=[vmem] * 4,
            out_specs=vmem,
        )(top, far, *parts[-2:])
        far = exchanged(top, "az", bit)
        if n == 0:
            parts.append(with_ghosts(2, top))
    tile_even, tile_odd, vel = call(
        theta_in,
        "theta_in",
        0,
        out_shape=(tile, tile, padded),
        in_specs=[vmem] * 4,
        out_specs=(vmem,) * 3,
        input_output_aliases={2: 2},
    )(theta_even, theta_odd, vel, parts[-1])
    corner_even, corner_odd = across_even(tile_even, "ax"), across_odd(tile_odd, "ax")
    parts.append(with_ghosts(3, tile_even))
    increment, time_step, _ = call(
        functools.partial(finish, spans),
        "finish",
        0,
        scratch=8,
        out_shape=(shape(*velocity.shape), shape(1), padded),
        in_specs=[vmem] * (7 + len(parts)),
        out_specs=(anywhere, smem, vmem),
        scratch_shapes=[
            pltpu.VMEM(velocity.shape, f32),
            pltpu.SemaphoreType.DMA(((planes - 2 * HALO) // BLOCK + 2,)),
        ],
        input_output_aliases={0: 2},
    )(vel, inner, coef, top, far, corner_even, corner_odd, *parts)
    return increment, time_step.reshape(())


def solution(mesh):
    return jax.shard_map(
        per_device,
        mesh=mesh,
        in_specs=(P(None, "az", "ax", None),),
        out_specs=(P(None, "az", "ax", None), P()),
        check_vma=False,
    )
```

```python
import functools
import math

import jax
import jax.numpy as jnp
import numpy as np
from jax import lax
from jax.experimental import pallas as pl
from jax.experimental.pallas import tpu as pltpu
from jax.sharding import PartitionSpec as P

AXIAL_STEP = 0.01
VISCOSITY = 0.001
CFL_TARGET = 1.2
GAMMA = 8.0 / 15.0

PAD = 8
HALO = 2
BLOCK = 4
GROUP = 4
UNROLL = 4

(
    WALL,
    RADIAL_C,
    THETA_C,
    CROSS_Z,
    SECOND_C,
    CENTRE_Z,
    CENTRE_T,
    CURVE_T,
    TURN_T,
    RADIAL_F,
    THETA_F,
    SECOND_F,
    CENTRE_R,
    CURVE_R,
    TURN_R,
    COUNT,
) = range(16)


UNIT = VISCOSITY / (12.0 * AXIAL_STEP**2)


def coefficients(radial, theta_step):
    dr = 1.0 / radial
    index = np.arange(radial, dtype=np.float64)
    centre = (index + 0.5) * dr
    face = (index + 1.0) * dr
    wall = np.where(index < radial - 1.5, 1.0, 0.0)
    h = theta_step
    nu = VISCOSITY
    rows = np.zeros((COUNT, radial))
    rows[WALL] = wall
    common = -2.0 * nu / dr**2 - 30.0 * nu / (12.0 * AXIAL_STEP**2)
    rows[RADIAL_C] = nu / (2.0 * dr * centre)
    rows[THETA_C] = -1.0 / (12.0 * h * centre)
    rows[CROSS_Z] = 0.25 * rows[THETA_C]
    rows[SECOND_C] = nu / (12.0 * h * h * centre**2)
    rows[CENTRE_Z] = common - 30.0 * rows[SECOND_C]
    rows[CENTRE_T] = rows[CENTRE_Z] - nu / centre**2
    rows[CURVE_T] = 0.25 / centre
    rows[TURN_T] = nu / (h * centre**2)
    rows[RADIAL_F] = nu / (2.0 * dr * face)
    rows[THETA_F] = -0.25 / (12.0 * h * face)
    rows[SECOND_F] = nu / (12.0 * h * h * face**2)
    rows[CENTRE_R] = common - 30.0 * rows[SECOND_F] - nu / face**2
    rows[CURVE_R] = 1.0 / (16.0 * face)
    rows[TURN_R] = -nu / (h * face**2)
    rows[RADIAL_C:] /= UNIT
    return np.broadcast_to(rows[:, None, :], (COUNT, 8, radial)).astype(np.float32)


class Cells:
    def __init__(self, vel, j, k):
        self.vel, self.j, self.k, self.known = vel, j, k, {}

    def once(self, key, make):
        if key not in self.known:
            self.known[key] = make()
        return self.known[key]

    def at(self, n, dj, dk=0):
        rows = pl.ds(self.k + PAD + dk, 8)
        return self.once((n, dj, dk), lambda: self.vel[n, self.j + HALO + dj, rows, :])

    def turned(self, by, n, dj, dk=0):
        return self.once(
            (by, n, dj, dk), lambda: pltpu.roll(self.at(n, dj, dk), by % self.vel.shape[3], 1)
        )

    def pair(self, by, n, dj, dk=0):
        return self.once(
            ("pair", n, dj, dk), lambda: self.at(n, dj, dk) + self.turned(by, n, dj, dk)
        )

    def beside(self, dj, dk):
        n = 1 if dk >= 0 else 2
        other = (1, dj - 1, dk) if n == 1 else (2, dj, dk)
        here = (1, dj, dk) if n == 1 else (2, dj, dk + 1)
        return self.once(("sum", n, dj, dk), lambda: self.at(*other) + self.at(*here))


def terms(cells, ghost, coef, q, dr):
    at, turned, pair = cells.at, cells.turned, cells.pair
    a, b, c = (at(n, q) for n in range(3))
    lane = lax.broadcasted_iota(jnp.int32, a.shape, 1)
    first_lane = lane == 0
    last_lane = lane == a.shape[1] - 1

    lap = VISCOSITY / dr**2 / UNIT
    adv_z = -1.0 / (12.0 * AXIAL_STEP) / UNIT
    by_dr = 1.0 / dr / UNIT

    def differences(p1, m1, p2, m2):
        return 8.0 * (p1 - m1) - (p2 - m2), 16.0 * (p1 + m1) - (p2 + m2)

    def pieces(n):
        over = differences(*(at(n, q + d) for d in (1, -1, 2, -2)))
        along = differences(*(at(n, q, d) for d in (1, -1, 2, -2)))
        return over, along

    def below(n):
        if ghost is not None and n > 0 and q % 2 == 0:
            x = jnp.where(last_lane, ghost(n, q + 1), at(n, q))
            return pltpu.roll(x, 1, 1)
        x = turned(1, n, q)
        if ghost is not None:
            return jnp.where(first_lane, ghost(n, q), x)
        return x if n == 0 else jnp.where(first_lane, 0.0, x)

    def above(n):
        return jnp.where(last_lane, -at(n, q), turned(-1, n, q))

    pair_a, pair_side, pair_next = pair(1, 0, q), pair(1, 0, q + 1), pair(1, 0, q, 1)
    pair_b, pair_back = pair(-1, 1, q), pair(-1, 1, q - 1)

    theta, axial = pieces(2)
    up, low = above(2), below(2)
    u_r = pair_a + pair_next
    u_t = cells.beside(q, 0) + cells.beside(q, 1)
    h_z = (up - low) * (coef[RADIAL_C] - u_r * (0.125 * by_dr)) + (up + low) * lap
    h_z = h_z + theta[0] * (u_t * coef[CROSS_Z])
    h_z = h_z + (theta[1] * coef[SECOND_C] + axial[1])
    h_z = h_z + c * (coef[CENTRE_Z] + axial[0] * adv_z)

    theta, axial = pieces(1)
    up, low = above(1), below(1)
    u_r = pair_a + pair_side
    u_z = cells.beside(q, -1) + cells.beside(q + 1, -1)
    h_t = (up - low) * (coef[RADIAL_C] - u_r * (0.125 * by_dr)) + (up + low) * lap
    h_t = h_t + b * (coef[CENTRE_T] + theta[0] * coef[THETA_C] - u_r * coef[CURVE_T])
    h_t = h_t + (theta[1] * coef[SECOND_C] + axial[1])
    h_t = h_t + axial[0] * (u_z * (0.25 * adv_z))
    h_t = h_t + (pair_side - pair_a) * coef[TURN_T]

    theta, axial = pieces(0)
    up, low = turned(-1, 0, q), below(0)
    u_t = pair_b + pair_back
    u_z = pair(-1, 2, q) + pair(-1, 2, q, -1)
    h_r = (up - low) * (coef[RADIAL_F] - a * (0.5 * by_dr)) + (up + low) * lap
    h_r = h_r + u_t * (u_t * coef[CURVE_R] + theta[0] * coef[THETA_F])
    h_r = h_r + (theta[1] * coef[SECOND_F] + axial[1])
    h_r = h_r + (axial[0] * (u_z * (0.25 * adv_z)) + a * coef[CENTRE_R])
    h_r = h_r + (pair_b - pair_back) * coef[TURN_R]
    return h_r, h_t, h_z


def lane_zero_terms(cells, ghost, coef, q, dr):
    lap = VISCOSITY / dr**2 / UNIT
    by_dr = 1.0 / dr / UNIT
    a = cells.at(0, q)
    first_lane = lax.broadcasted_iota(jnp.int32, a.shape, 1) == 0
    add_r = ghost(0, q) * (lap - coef[RADIAL_F] + a * (0.5 * by_dr))
    add_t = ghost(1, q) * (lap - coef[RADIAL_C] + (a + cells.at(0, q + 1)) * (0.125 * by_dr))
    add_z = ghost(2, q) * (lap - coef[RADIAL_C] + (a + cells.at(0, q, 1)) * (0.125 * by_dr))
    return tuple(jnp.where(first_lane, x, 0.0) for x in (add_r, add_t, add_z))


def wall_mask(rows, radial):
    lane = lax.broadcasted_iota(jnp.int32, (rows, radial), 1)
    return jnp.where(lane == radial - 1, 0.0, 1.0).astype(jnp.float32)


def first_pass(theta_step, v_ref, vel_ref, even_ref, odd_ref, inner_ref, pay_ref, sems):
    _, planes, axial, radial = v_ref.shape
    lane = lax.broadcasted_iota(jnp.int32, (8, radial), 1)
    wall = wall_mask(8, radial)
    rate_t = (radial / theta_step) / (lane.astype(jnp.float32) + 0.5)
    odd = lax.rem(lax.axis_index("ax"), 2) == 1

    def fetch(g):
        part = pl.ds(g * GROUP, GROUP)
        target = vel_ref.at[:, pl.ds(g * GROUP + HALO, GROUP), pl.ds(PAD, axial)]
        return pltpu.make_async_copy(v_ref.at[:, part], target, sems.at[g])

    for g in range(planes // GROUP):
        fetch(g).start()

    zero = jnp.zeros((8, radial), jnp.float32)
    largest = [zero] * 4
    for g in range(planes // GROUP):
        fetch(g).wait()
        for i in range(axial // 8):
            k = pl.ds(8 * i, 8)
            padded = pl.ds(8 * i + PAD, 8)
            inner = zero if g == 0 else inner_ref[k, :]
            for q in range(GROUP):
                j = g * GROUP + q
                cells = [vel_ref[n, j + HALO, padded, :] for n in range(3)]
                for n, x in enumerate(cells):
                    place = n * planes + j
                    x = pltpu.roll(x, place, 1) if place else x
                    inner = jnp.where(lane == place, x if n == 2 else -x, inner)
                a, b, c = cells
                a = a * wall
                vel_ref[0, j + HALO, padded, :] = a
                rate = jnp.abs(a) * float(radial) + jnp.abs(b) * rate_t
                rate = rate + jnp.abs(c) * (1.0 / AXIAL_STEP)
                largest[q % 4] = jnp.maximum(largest[q % 4], rate)
            inner_ref[k, :] = inner
        for q in range(GROUP):
            for n in range(3):
                j = g * GROUP + q
                first = vel_ref[n, j + HALO, PAD : PAD + 2, :]
                last = vel_ref[n, j + HALO, PAD + axial - 2 : PAD + axial, :]
                even_ref[n, j] = jnp.where(odd, first, last)
                odd_ref[n, j] = jnp.where(odd, last, first)

    largest = jnp.maximum(
        jnp.maximum(largest[0], largest[1]), jnp.maximum(largest[2], largest[3])
    )
    top = jnp.max(largest, axis=(0, 1), keepdims=True)
    pay_ref[...] = jnp.broadcast_to(top, pay_ref.shape)
    end = lax.broadcasted_iota(jnp.int32, (2, radial), 1) == radial - 1
    for ref in (even_ref, odd_ref):
        ref[0, 0] = jnp.where(end, top, ref[0, 0])


def carried(even_ref, pay_ref, odd_in, odd_ref):
    radial = even_ref.shape[3]
    lane = lax.broadcasted_iota(jnp.int32, (2, radial), 1)
    top = jnp.maximum(even_ref[0, 0], pay_ref[0:2, :])
    odd_ref[0, 0] = jnp.where(lane == radial - 1, top, odd_in[0, 0])


def fold(even_ref, odd_ref, pay_ref, vel_in, _, *refs):
    del vel_in
    top_ref, vel_ref = refs
    planes, radial = even_ref.shape[1], even_ref.shape[3]
    axial = vel_ref.shape[2] - 2 * PAD
    lane = lax.broadcasted_iota(jnp.int32, (1, radial), 1)
    top = jnp.maximum(even_ref[0, 0, 0:1, :], odd_ref[0, 0, 0:1, :])
    top = jnp.max(jnp.where(lane == radial - 1, top, 0.0), axis=(0, 1), keepdims=True)
    top_ref[...] = jnp.maximum(pay_ref[...], top)
    wall = wall_mask(2, radial)
    odd = lax.rem(lax.axis_index("ax"), 2) == 1

    def plane(j, carry):
        for n in range(3):
            mask = wall if n == 0 else 1.0
            even, other = even_ref[n, j] * mask, odd_ref[n, j] * mask
            low, high = jnp.where(odd, even, other), jnp.where(odd, other, even)
            vel_ref[n, j + HALO, PAD - 2 : PAD, :] = low
            vel_ref[n, j + HALO, PAD + axial : PAD + axial + 2, :] = high
        return carry

    lax.fori_loop(0, planes, plane, 0, unroll=4)


def merged(mine_ref, far_ref, *refs):
    refs[-1][...] = jnp.maximum(mine_ref[...], far_ref[...])


def theta_in(even_ref, odd_ref, vel_in, _, even_tile, odd_tile, vel_ref):
    del vel_in
    planes, axial = vel_ref.shape[1] - 2 * HALO, vel_ref.shape[2] - 2 * PAD
    cells = pl.ds(PAD, axial)
    wall = wall_mask(1, vel_ref.shape[3])
    odd = lax.rem(lax.axis_index("az"), 2)
    below, above = 0, HALO + planes
    for ref, place in (
        (even_ref, jnp.where(odd == 1, below, above)),
        (odd_ref, jnp.where(odd == 1, above, below)),
    ):
        for q in range(HALO):
            vel_ref[0, place + q, cells, :] = ref[0, q] * wall
            vel_ref[1, place + q, cells, :] = ref[1, q]
            vel_ref[2, place + q, cells, :] = ref[2, q]
    first = vel_ref[1, below + HALO - 1, PAD : PAD + 1, :]
    last = vel_ref[2, above, PAD + axial - 1 : PAD + axial, :]
    odd = lax.rem(lax.axis_index("ax"), 2) == 1
    shape = even_tile.shape
    even_tile[...] = jnp.broadcast_to(jnp.where(odd, first, last), shape)
    odd_tile[...] = jnp.broadcast_to(jnp.where(odd, last, first), shape)


def ghosts(cells, inner, planes):
    radial = inner.shape[1]

    def ghost(n, q):
        turn = -(n * planes + q + cells.j) % radial
        return cells.once(("ghost", n, q), lambda: pltpu.roll(inner, turn, 1) if turn else inner)

    return ghost


def block_terms(vel_ref, inner_ref, coef_ref, j, size, write, rounds=None):
    planes = vel_ref.shape[1] - 2 * HALO
    axial, radial = vel_ref.shape[2] - 2 * PAD, vel_ref.shape[3]
    groups = 4 * BLOCK // size
    times, places = rounds or (
        axial // (8 * groups),
        lambda i: [(i * groups + u) * 8 for u in range(groups)],
    )

    def rows(i, carry):
        coef = [coef_ref[n] for n in range(COUNT)]
        found = []
        for k in places(i):
            k = pl.multiple_of(k, 8)
            cells = Cells(vel_ref, j, k)
            ghost = None
            if inner_ref is not None:
                ghost = ghosts(cells, inner_ref[pl.ds(k, 8), :], planes)
            for q in range(size):
                found.append((q, k, terms(cells, ghost, coef, q, 1.0 / radial)))
        for q, k, values in found:
            for n, value in enumerate(values):
                write(n, j + q, pl.ds(k, 8), value)
        return carry

    lax.fori_loop(0, times, rows, 0)


def ahead(first, last, rounds, vel_ref, coef_ref, *refs):
    out_ref = refs[-1]

    def write(n, j, k, value):
        out_ref[n, j - first, k, :] = value

    def block(m, carry):
        block_terms(vel_ref, None, coef_ref, first + m * BLOCK, BLOCK, write, rounds)
        return carry

    lax.fori_loop(0, (last - first) // BLOCK, block, 0)


def ahead_with_ghosts(first, last, vel_ref, inner_ref, coef_ref, _, out_ref):
    def write(n, j, k, value):
        out_ref[n, j - first, k, :] = value

    for j in range(first, last, BLOCK):
        block_terms(vel_ref, inner_ref, coef_ref, j, BLOCK, write)


def finish(spans, vel_in, inner_ref, coef_ref, top, far, even, odd, *refs):
    parts, refs = refs[: len(spans)], refs[len(spans) :]
    del vel_in
    out_ref, step_ref, vel_ref, res, sems = refs
    axial, radial = inner_ref.shape
    planes = vel_ref.shape[1] - 2 * HALO
    largest = jnp.maximum(top[0:1, :], far[0:1, :])
    time_step = CFL_TARGET / (jnp.max(largest) + 1e-06)
    step_ref[0] = time_step
    scale = GAMMA * UNIT * time_step
    factors = (scale * coef_ref[WALL], scale, scale)
    pending = []

    def send(j, size):
        part_of = pl.ds(j, size)
        copy = pltpu.make_async_copy(
            res.at[:, part_of], out_ref.at[:, part_of], sems.at[len(pending)]
        )
        copy.start()
        pending.append(copy)

    def write(n, j, k, value):
        res[n, j, k, :] = value * factors[n]

    def complete(part, j, place, add):
        groups = 4

        def rows(i, carry):
            found = []
            for u in range(groups):
                k = pl.multiple_of((i * groups + u) * 8, 8)
                cells = Cells(vel_ref, j, k)
                ghost = ghosts(cells, inner_ref[pl.ds(k, 8), :], planes) if add else None
                for q in range(BLOCK):
                    values = [part[n, place + q, pl.ds(k, 8), :] for n in range(3)]
                    if add:
                        added = lane_zero_terms(cells, ghost, coef_ref, q, 1.0 / radial)
                        values = [x + y for x, y in zip(values, added)]
                    found.append((q, k, values))
            for q, k, values in found:
                for n, value in enumerate(values):
                    write(n, j + q, pl.ds(k, 8), value)
            return carry

        lax.fori_loop(0, axial // (8 * groups), rows, 0)
        send(j, BLOCK)

    for n, (part, (first, last)) in enumerate(zip(parts, spans)):
        for j in range(first, last, BLOCK):
            complete(part, j, j - first, n < 2)

    second = lax.rem(lax.axis_index("ax"), 2) == 1
    even, odd = even[0:1, :], odd[0:1, :]
    following, preceding = jnp.where(second, odd, even), jnp.where(second, even, odd)
    vel_ref[1, HALO - 1, PAD + axial : PAD + axial + 1, :] = following
    vel_ref[2, HALO + planes, PAD - 1 : PAD, :] = preceding
    for j in (0, planes - HALO):
        block_terms(vel_ref, inner_ref, coef_ref, j, HALO, write)
        send(j, HALO)
    for copy in pending:
        copy.wait()


def routed(block, axis, source):
    count = lax.axis_size(axis)
    return lax.ppermute(block, axis, [(source(i), i) for i in range(count)])


def exchanged(block, axis, step):
    return routed(block, axis, lambda i: i ^ step)


def across_even(block, axis):
    return exchanged(block, axis, 1)


def across_odd(block, axis):
    count = lax.axis_size(axis)
    return routed(block, axis, lambda i: (i + (1 if i % 2 else -1)) % count)


def cuts(planes):
    last = planes - HALO
    ends = (HALO, last - 5 * BLOCK, last - 3 * BLOCK, last - BLOCK, last)
    return list(zip(ends[:-1], ends[1:]))


def per_device(velocity):
    _, planes, axial, radial = velocity.shape
    sizes = lax.axis_size("az"), lax.axis_size("ax")
    theta_step = 2.0 * math.pi / (sizes[0] * planes)
    coef = jnp.asarray(coefficients(radial, theta_step))
    f32 = jnp.float32
    anywhere = pl.BlockSpec(memory_space=pl.ANY)
    vmem = pl.BlockSpec(memory_space=pltpu.VMEM)
    smem = pl.BlockSpec(memory_space=pltpu.SMEM)

    def shape(*sizes):
        return jax.ShapeDtypeStruct(sizes, f32)

    def call(kernel, name, work, scratch=0, **kwargs):
        return pl.pallas_call(
            kernel,
            name=name,
            compiler_params=pltpu.CompilerParams(vmem_limit_bytes=(4 + scratch) * 2**20),
            cost_estimate=pl.CostEstimate(flops=work, bytes_accessed=work, transcendentals=0),
            **kwargs,
        )

    odd = lax.axis_index("az") % 2
    ends = (planes - HALO, 0)
    even_end = jnp.where(odd == 1, ends[1], ends[0])
    odd_end = jnp.where(odd == 1, ends[0], ends[1])
    theta_even = across_even(lax.dynamic_slice_in_dim(velocity, even_end, HALO, 1), "az")
    theta_odd = across_odd(lax.dynamic_slice_in_dim(velocity, odd_end, HALO, 1), "az")

    edge = shape(3, planes, 2, radial)
    padded = shape(3, planes + 2 * HALO, axial + 2 * PAD, radial)
    row = shape(axial, radial)
    tile = shape(8, radial)
    vel, edge_even, edge_odd, mine, pay = call(
        functools.partial(first_pass, theta_step),
        "first_pass",
        0,
        out_shape=(padded, edge, edge, row, tile),
        in_specs=[anywhere],
        out_specs=(vmem,) * 5,
        scratch_shapes=[pltpu.SemaphoreType.DMA((planes // GROUP,))],
    )(pltpu.with_memory_space_constraint(velocity, pltpu.HBM))
    inner = exchanged(mine, "az", sizes[0] // 2)
    z_even = across_even(edge_even, "ax")
    edge_odd = call(
        carried,
        "carried",
        0,
        out_shape=edge,
        in_specs=[vmem] * 3,
        out_specs=vmem,
        input_output_aliases={2: 0},
    )(z_even, pay, edge_odd)
    z_odd = across_odd(edge_odd, "ax")

    spans = cuts(planes)

    def part_shape(n):
        return shape(3, spans[n][1] - spans[n][0], axial, radial)

    def without_ghosts(n, name, rounds, vel, *tokens, **kwargs):
        return call(
            functools.partial(ahead, *spans[n], rounds),
            name,
            velocity.size * 2,
            out_shape=part_shape(n),
            in_specs=[vmem] * (2 + len(tokens)),
            out_specs=vmem,
            **kwargs,
        )(vel, coef, *tokens)

    def with_ghosts(n, token):
        return call(
            functools.partial(ahead_with_ghosts, *spans[n]),
            f"span_{n}",
            velocity.size * 2,
            out_shape=part_shape(n),
            in_specs=[vmem] * 4,
            out_specs=vmem,
        )(vel, inner, coef, token)

    middle = (axial - 16) // 16, lambda i: [16 * i + 8, 16 * i + 16]
    outer = 1, lambda i: [i * 8, i * 8 + axial - 8]
    part = without_ghosts(0, "span_0_middle", middle, vel, pay)
    top, vel = call(
        fold,
        "fold",
        0,
        out_shape=(tile, padded),
        in_specs=[vmem] * 5,
        out_specs=(vmem,) * 2,
        input_output_aliases={3: 1},
    )(z_even, z_odd, pay, vel, part)
    for step in (1 << n for n in range(2, sizes[1].bit_length() - 1)):
        top = jnp.maximum(top, routed(top, "ax", lambda i, step=step: (i + step) % sizes[1]))

    bits = [1 << n for n in range(1, sizes[0].bit_length() - 1)] + [1]
    far = exchanged(top, "az", bits[0])
    parts = [
        without_ghosts(0, "span_0_outer", outer, vel, part, input_output_aliases={2: 0}),
        without_ghosts(1, "span_1", None, vel, top),
    ]
    for n, bit in enumerate(bits[1:]):
        top = call(
            merged,
            "merged",
            0,
            out_shape=tile,
            in_specs=[vmem] * 4,
            out_specs=vmem,
        )(top, far, *parts[-2:])
        far = exchanged(top, "az", bit)
        if n == 0:
            parts.append(with_ghosts(2, top))
    tile_even, tile_odd, vel = call(
        theta_in,
        "theta_in",
        0,
        out_shape=(tile, tile, padded),
        in_specs=[vmem] * 4,
        out_specs=(vmem,) * 3,
        input_output_aliases={2: 2},
    )(theta_even, theta_odd, vel, parts[-1])
    corner_even, corner_odd = across_even(tile_even, "ax"), across_odd(tile_odd, "ax")
    parts.append(with_ghosts(3, tile_even))
    increment, time_step, _ = call(
        functools.partial(finish, spans),
        "finish",
        0,
        scratch=8,
        out_shape=(shape(*velocity.shape), shape(1), padded),
        in_specs=[vmem] * (7 + len(parts)),
        out_specs=(anywhere, smem, vmem),
        scratch_shapes=[
            pltpu.VMEM(velocity.shape, f32),
            pltpu.SemaphoreType.DMA(((planes - 2 * HALO) // BLOCK + 2,)),
        ],
        input_output_aliases={0: 2},
    )(vel, inner, coef, top, far, corner_even, corner_odd, *parts)
    return increment, time_step.reshape(())


def solution(mesh):
    return jax.shard_map(
        per_device,
        mesh=mesh,
        in_specs=(P(None, "az", "ax", None),),
        out_specs=(P(None, "az", "ax", None), P()),
        check_vma=False,
    )
```

```python
import functools
import math

import jax
import jax.numpy as jnp
import numpy as np
from jax import lax
from jax.experimental import pallas as pl
from jax.experimental.pallas import tpu as pltpu
from jax.sharding import PartitionSpec as P

AXIAL_STEP = 0.01
VISCOSITY = 0.001
CFL_TARGET = 1.2
GAMMA = 8.0 / 15.0

PAD = 8
HALO = 2
BLOCK = 4
GROUP = 4
UNROLL = 4

(
    WALL,
    RADIAL_C,
    THETA_C,
    CROSS_Z,
    SECOND_C,
    CENTRE_Z,
    CENTRE_T,
    CURVE_T,
    TURN_T,
    RADIAL_F,
    THETA_F,
    SECOND_F,
    CENTRE_R,
    CURVE_R,
    TURN_R,
    COUNT,
) = range(16)


UNIT = VISCOSITY / (12.0 * AXIAL_STEP**2)


def coefficients(radial, theta_step):
    dr = 1.0 / radial
    index = np.arange(radial, dtype=np.float64)
    centre = (index + 0.5) * dr
    face = (index + 1.0) * dr
    wall = np.where(index < radial - 1.5, 1.0, 0.0)
    h = theta_step
    nu = VISCOSITY
    rows = np.zeros((COUNT, radial))
    rows[WALL] = wall
    common = -2.0 * nu / dr**2 - 30.0 * nu / (12.0 * AXIAL_STEP**2)
    rows[RADIAL_C] = nu / (2.0 * dr * centre)
    rows[THETA_C] = -1.0 / (12.0 * h * centre)
    rows[CROSS_Z] = 0.25 * rows[THETA_C]
    rows[SECOND_C] = nu / (12.0 * h * h * centre**2)
    rows[CENTRE_Z] = common - 30.0 * rows[SECOND_C]
    rows[CENTRE_T] = rows[CENTRE_Z] - nu / centre**2
    rows[CURVE_T] = 0.25 / centre
    rows[TURN_T] = nu / (h * centre**2)
    rows[RADIAL_F] = nu / (2.0 * dr * face)
    rows[THETA_F] = -0.25 / (12.0 * h * face)
    rows[SECOND_F] = nu / (12.0 * h * h * face**2)
    rows[CENTRE_R] = common - 30.0 * rows[SECOND_F] - nu / face**2
    rows[CURVE_R] = 1.0 / (16.0 * face)
    rows[TURN_R] = -nu / (h * face**2)
    rows[RADIAL_C:] /= UNIT
    return np.broadcast_to(rows[:, None, :], (COUNT, 8, radial)).astype(np.float32)


class Cells:
    def __init__(self, vel, j, k):
        self.vel, self.j, self.k, self.known = vel, j, k, {}

    def once(self, key, make):
        if key not in self.known:
            self.known[key] = make()
        return self.known[key]

    def at(self, n, dj, dk=0):
        rows = pl.ds(self.k + PAD + dk, 8)
        return self.once((n, dj, dk), lambda: self.vel[n, self.j + HALO + dj, rows, :])

    def turned(self, by, n, dj, dk=0):
        return self.once(
            (by, n, dj, dk), lambda: pltpu.roll(self.at(n, dj, dk), by % self.vel.shape[3], 1)
        )

    def pair(self, by, n, dj, dk=0):
        return self.once(
            ("pair", n, dj, dk), lambda: self.at(n, dj, dk) + self.turned(by, n, dj, dk)
        )

    def beside(self, dj, dk):
        n = 1 if dk >= 0 else 2
        other = (1, dj - 1, dk) if n == 1 else (2, dj, dk)
        here = (1, dj, dk) if n == 1 else (2, dj, dk + 1)
        return self.once(("sum", n, dj, dk), lambda: self.at(*other) + self.at(*here))


def terms(cells, ghost, coef, q, dr):
    at, turned, pair = cells.at, cells.turned, cells.pair
    a, b, c = (at(n, q) for n in range(3))
    lane = lax.broadcasted_iota(jnp.int32, a.shape, 1)
    first_lane = lane == 0
    last_lane = lane == a.shape[1] - 1

    lap = VISCOSITY / dr**2 / UNIT
    adv_z = -1.0 / (12.0 * AXIAL_STEP) / UNIT
    by_dr = 1.0 / dr / UNIT

    def differences(p1, m1, p2, m2):
        return 8.0 * (p1 - m1) - (p2 - m2), 16.0 * (p1 + m1) - (p2 + m2)

    def pieces(n):
        over = differences(*(at(n, q + d) for d in (1, -1, 2, -2)))
        along = differences(*(at(n, q, d) for d in (1, -1, 2, -2)))
        return over, along

    def below(n):
        if ghost is not None and n > 0 and q % 2 == 0:
            x = jnp.where(last_lane, ghost(n, q + 1), at(n, q))
            return pltpu.roll(x, 1, 1)
        x = turned(1, n, q)
        if ghost is not None:
            return jnp.where(first_lane, ghost(n, q), x)
        return x if n == 0 else jnp.where(first_lane, 0.0, x)

    def above(n):
        return jnp.where(last_lane, -at(n, q), turned(-1, n, q))

    pair_a, pair_side, pair_next = pair(1, 0, q), pair(1, 0, q + 1), pair(1, 0, q, 1)
    pair_b, pair_back = pair(-1, 1, q), pair(-1, 1, q - 1)

    theta, axial = pieces(2)
    up, low = above(2), below(2)
    u_r = pair_a + pair_next
    u_t = cells.beside(q, 0) + cells.beside(q, 1)
    h_z = (up - low) * (coef[RADIAL_C] - u_r * (0.125 * by_dr)) + (up + low) * lap
    h_z = h_z + theta[0] * (u_t * coef[CROSS_Z])
    h_z = h_z + (theta[1] * coef[SECOND_C] + axial[1])
    h_z = h_z + c * (coef[CENTRE_Z] + axial[0] * adv_z)

    theta, axial = pieces(1)
    up, low = above(1), below(1)
    u_r = pair_a + pair_side
    u_z = cells.beside(q, -1) + cells.beside(q + 1, -1)
    h_t = (up - low) * (coef[RADIAL_C] - u_r * (0.125 * by_dr)) + (up + low) * lap
    h_t = h_t + b * (coef[CENTRE_T] + theta[0] * coef[THETA_C] - u_r * coef[CURVE_T])
    h_t = h_t + (theta[1] * coef[SECOND_C] + axial[1])
    h_t = h_t + axial[0] * (u_z * (0.25 * adv_z))
    h_t = h_t + (pair_side - pair_a) * coef[TURN_T]

    theta, axial = pieces(0)
    up, low = turned(-1, 0, q), below(0)
    u_t = pair_b + pair_back
    u_z = pair(-1, 2, q) + pair(-1, 2, q, -1)
    h_r = (up - low) * (coef[RADIAL_F] - a * (0.5 * by_dr)) + (up + low) * lap
    h_r = h_r + u_t * (u_t * coef[CURVE_R] + theta[0] * coef[THETA_F])
    h_r = h_r + (theta[1] * coef[SECOND_F] + axial[1])
    h_r = h_r + (axial[0] * (u_z * (0.25 * adv_z)) + a * coef[CENTRE_R])
    h_r = h_r + (pair_b - pair_back) * coef[TURN_R]
    return h_r, h_t, h_z


def lane_zero_terms(cells, ghost, coef, q, dr):
    lap = VISCOSITY / dr**2 / UNIT
    by_dr = 1.0 / dr / UNIT
    a = cells.at(0, q)
    first_lane = lax.broadcasted_iota(jnp.int32, a.shape, 1) == 0
    add_r = ghost(0, q) * (lap - coef[RADIAL_F] + a * (0.5 * by_dr))
    add_t = ghost(1, q) * (lap - coef[RADIAL_C] + (a + cells.at(0, q + 1)) * (0.125 * by_dr))
    add_z = ghost(2, q) * (lap - coef[RADIAL_C] + (a + cells.at(0, q, 1)) * (0.125 * by_dr))
    return tuple(jnp.where(first_lane, x, 0.0) for x in (add_r, add_t, add_z))


def wall_mask(rows, radial):
    lane = lax.broadcasted_iota(jnp.int32, (rows, radial), 1)
    return jnp.where(lane == radial - 1, 0.0, 1.0).astype(jnp.float32)


def first_pass(theta_step, v_ref, vel_ref, even_ref, odd_ref, inner_ref, pay_ref, sems):
    _, planes, axial, radial = v_ref.shape
    lane = lax.broadcasted_iota(jnp.int32, (8, radial), 1)
    wall = wall_mask(8, radial)
    rate_t = (radial / theta_step) / (lane.astype(jnp.float32) + 0.5)
    odd = lax.rem(lax.axis_index("ax"), 2) == 1

    def fetch(g):
        part = pl.ds(g * GROUP, GROUP)
        target = vel_ref.at[:, pl.ds(g * GROUP + HALO, GROUP), pl.ds(PAD, axial)]
        return pltpu.make_async_copy(v_ref.at[:, part], target, sems.at[g])

    for g in range(planes // GROUP):
        fetch(g).start()

    zero = jnp.zeros((8, radial), jnp.float32)
    largest = [zero] * 4
    for g in range(planes // GROUP):
        fetch(g).wait()
        for i in range(axial // 8):
            k = pl.ds(8 * i, 8)
            padded = pl.ds(8 * i + PAD, 8)
            inner = zero if g == 0 else inner_ref[k, :]
            for q in range(GROUP):
                j = g * GROUP + q
                cells = [vel_ref[n, j + HALO, padded, :] for n in range(3)]
                for n, x in enumerate(cells):
                    place = n * planes + j
                    x = pltpu.roll(x, place, 1) if place else x
                    inner = jnp.where(lane == place, x if n == 2 else -x, inner)
                a, b, c = cells
                a = a * wall
                vel_ref[0, j + HALO, padded, :] = a
                rate = jnp.abs(a) * float(radial) + jnp.abs(b) * rate_t
                rate = rate + jnp.abs(c) * (1.0 / AXIAL_STEP)
                largest[q % 4] = jnp.maximum(largest[q % 4], rate)
            inner_ref[k, :] = inner
        for q in range(GROUP):
            for n in range(3):
                j = g * GROUP + q
                first = vel_ref[n, j + HALO, PAD : PAD + 2, :]
                last = vel_ref[n, j + HALO, PAD + axial - 2 : PAD + axial, :]
                even_ref[n, j] = jnp.where(odd, first, last)
                odd_ref[n, j] = jnp.where(odd, last, first)

    largest = jnp.maximum(
        jnp.maximum(largest[0], largest[1]), jnp.maximum(largest[2], largest[3])
    )
    top = jnp.max(largest, axis=(0, 1), keepdims=True)
    pay_ref[...] = jnp.broadcast_to(top, pay_ref.shape)
    end = lax.broadcasted_iota(jnp.int32, (2, radial), 1) == radial - 1
    for ref in (even_ref, odd_ref):
        ref[0, 0] = jnp.where(end, top, ref[0, 0])


def carried(even_ref, pay_ref, odd_in, odd_ref):
    radial = even_ref.shape[3]
    lane = lax.broadcasted_iota(jnp.int32, (2, radial), 1)
    top = jnp.maximum(even_ref[0, 0], pay_ref[0:2, :])
    odd_ref[0, 0] = jnp.where(lane == radial - 1, top, odd_in[0, 0])


def fold(even_ref, odd_ref, pay_ref, vel_in, _, *refs):
    del vel_in
    top_ref, vel_ref = refs
    planes, radial = even_ref.shape[1], even_ref.shape[3]
    axial = vel_ref.shape[2] - 2 * PAD
    lane = lax.broadcasted_iota(jnp.int32, (1, radial), 1)
    top = jnp.maximum(even_ref[0, 0, 0:1, :], odd_ref[0, 0, 0:1, :])
    top = jnp.max(jnp.where(lane == radial - 1, top, 0.0), axis=(0, 1), keepdims=True)
    top_ref[...] = jnp.maximum(pay_ref[...], top)
    wall = wall_mask(2, radial)
    odd = lax.rem(lax.axis_index("ax"), 2) == 1

    def plane(j, carry):
        for n in range(3):
            mask = wall if n == 0 else 1.0
            even, other = even_ref[n, j] * mask, odd_ref[n, j] * mask
            low, high = jnp.where(odd, even, other), jnp.where(odd, other, even)
            vel_ref[n, j + HALO, PAD - 2 : PAD, :] = low
            vel_ref[n, j + HALO, PAD + axial : PAD + axial + 2, :] = high
        return carry

    lax.fori_loop(0, planes, plane, 0, unroll=4)


def merged(mine_ref, far_ref, *refs):
    refs[-1][...] = jnp.maximum(mine_ref[...], far_ref[...])


def theta_in(even_ref, odd_ref, vel_in, _, even_tile, odd_tile, vel_ref):
    del vel_in
    planes, axial = vel_ref.shape[1] - 2 * HALO, vel_ref.shape[2] - 2 * PAD
    cells = pl.ds(PAD, axial)
    wall = wall_mask(1, vel_ref.shape[3])
    odd = lax.rem(lax.axis_index("az"), 2)
    below, above = 0, HALO + planes
    for ref, place in (
        (even_ref, jnp.where(odd == 1, below, above)),
        (odd_ref, jnp.where(odd == 1, above, below)),
    ):
        for q in range(HALO):
            vel_ref[0, place + q, cells, :] = ref[0, q] * wall
            vel_ref[1, place + q, cells, :] = ref[1, q]
            vel_ref[2, place + q, cells, :] = ref[2, q]
    first = vel_ref[1, below + HALO - 1, PAD : PAD + 1, :]
    last = vel_ref[2, above, PAD + axial - 1 : PAD + axial, :]
    odd = lax.rem(lax.axis_index("ax"), 2) == 1
    shape = even_tile.shape
    even_tile[...] = jnp.broadcast_to(jnp.where(odd, first, last), shape)
    odd_tile[...] = jnp.broadcast_to(jnp.where(odd, last, first), shape)


def ghosts(cells, inner, planes):
    radial = inner.shape[1]

    def ghost(n, q):
        turn = -(n * planes + q + cells.j) % radial
        return cells.once(("ghost", n, q), lambda: pltpu.roll(inner, turn, 1) if turn else inner)

    return ghost


def block_terms(vel_ref, inner_ref, coef_ref, kept, j, size, write, rounds=None):
    planes = vel_ref.shape[1] - 2 * HALO
    axial, radial = vel_ref.shape[2] - 2 * PAD, vel_ref.shape[3]
    a_kept, c_kept = kept
    groups = 4 * BLOCK // size
    start, times, places = rounds or (
        0,
        axial // (8 * groups),
        lambda i: [(i * groups + u) * 8 for u in range(groups)],
    )

    def keep_c(cells, q):
        value = cells.pair(-1, 2, q)
        c_kept[q, pl.ds(cells.k + PAD, 8), :] = value

    if start is not None:
        before = Cells(vel_ref, j, start - 8)
        for q in range(size):
            keep_c(before, q)

    def rows(i, carry):
        coef = [coef_ref[n] for n in range(COUNT)]
        ks = [pl.multiple_of(k, 8) for k in places(i)]
        all_cells = [Cells(vel_ref, j, k) for k in ks]
        if start is not None:
            for cells in all_cells + [Cells(vel_ref, j, ks[-1] + 8)]:
                for q in range(size):
                    a_kept[q, pl.ds(cells.k + PAD, 8), :] = cells.pair(1, 0, q)
            for cells in all_cells:
                for q in range(size):
                    keep_c(cells, q)
            for cells in all_cells:
                for q in range(size):
                    ahead_row = pl.ds(cells.k + PAD + 1, 8)
                    cells.known["pair", 0, q, 1] = a_kept[q, ahead_row, :]
                    back_row = pl.ds(cells.k + PAD - 1, 8)
                    cells.known["pair", 2, q, -1] = c_kept[q, back_row, :]
        found = []
        for k, cells in zip(ks, all_cells):
            ghost = None
            if inner_ref is not None:
                ghost = ghosts(cells, inner_ref[pl.ds(k, 8), :], planes)
            for q in range(size):
                found.append((q, k, terms(cells, ghost, coef, q, 1.0 / radial)))
        for q, k, values in found:
            for n, value in enumerate(values):
                write(n, j + q, pl.ds(k, 8), value)
        return carry

    lax.fori_loop(0, times, rows, 0)


def ahead(first, last, rounds, vel_ref, coef_ref, *refs):
    out_ref, *kept = refs[-3:]

    def write(n, j, k, value):
        out_ref[n, j - first, k, :] = value

    def block(m, carry):
        block_terms(vel_ref, None, coef_ref, kept, first + m * BLOCK, BLOCK, write, rounds)
        return carry

    lax.fori_loop(0, (last - first) // BLOCK, block, 0)


def ahead_with_ghosts(first, last, vel_ref, inner_ref, coef_ref, _, out_ref, *kept):
    def write(n, j, k, value):
        out_ref[n, j - first, k, :] = value

    for j in range(first, last, BLOCK):
        block_terms(vel_ref, inner_ref, coef_ref, kept, j, BLOCK, write)


def finish(spans, vel_in, inner_ref, coef_ref, top, far, even, odd, *refs):
    parts, refs = refs[: len(spans)], refs[len(spans) :]
    del vel_in
    out_ref, step_ref, vel_ref, res, sems, *kept = refs
    axial, radial = inner_ref.shape
    planes = vel_ref.shape[1] - 2 * HALO
    largest = jnp.maximum(top[0:1, :], far[0:1, :])
    time_step = CFL_TARGET / (jnp.max(largest) + 1e-06)
    step_ref[0] = time_step
    scale = GAMMA * UNIT * time_step
    factors = (scale * coef_ref[WALL], scale, scale)
    pending = []

    def send(j, size):
        part_of = pl.ds(j, size)
        copy = pltpu.make_async_copy(
            res.at[:, part_of], out_ref.at[:, part_of], sems.at[len(pending)]
        )
        copy.start()
        pending.append(copy)

    def write(n, j, k, value):
        res[n, j, k, :] = value * factors[n]

    def complete(part, j, place, add):
        groups = 4

        def rows(i, carry):
            found = []
            for u in range(groups):
                k = pl.multiple_of((i * groups + u) * 8, 8)
                cells = Cells(vel_ref, j, k)
                ghost = ghosts(cells, inner_ref[pl.ds(k, 8), :], planes) if add else None
                for q in range(BLOCK):
                    values = [part[n, place + q, pl.ds(k, 8), :] for n in range(3)]
                    if add:
                        added = lane_zero_terms(cells, ghost, coef_ref, q, 1.0 / radial)
                        values = [x + y for x, y in zip(values, added)]
                    found.append((q, k, values))
            for q, k, values in found:
                for n, value in enumerate(values):
                    write(n, j + q, pl.ds(k, 8), value)
            return carry

        lax.fori_loop(0, axial // (8 * groups), rows, 0)
        send(j, BLOCK)

    for n, (part, (first, last)) in enumerate(zip(parts, spans)):
        for j in range(first, last, BLOCK):
            complete(part, j, j - first, n < 2)

    second = lax.rem(lax.axis_index("ax"), 2) == 1
    even, odd = even[0:1, :], odd[0:1, :]
    following, preceding = jnp.where(second, odd, even), jnp.where(second, even, odd)
    vel_ref[1, HALO - 1, PAD + axial : PAD + axial + 1, :] = following
    vel_ref[2, HALO + planes, PAD - 1 : PAD, :] = preceding
    for j in (0, planes - HALO):
        block_terms(vel_ref, inner_ref, coef_ref, kept, j, HALO, write)
        send(j, HALO)
    for copy in pending:
        copy.wait()


def routed(block, axis, source):
    count = lax.axis_size(axis)
    return lax.ppermute(block, axis, [(source(i), i) for i in range(count)])


def exchanged(block, axis, step):
    return routed(block, axis, lambda i: i ^ step)


def across_even(block, axis):
    return exchanged(block, axis, 1)


def across_odd(block, axis):
    count = lax.axis_size(axis)
    return routed(block, axis, lambda i: (i + (1 if i % 2 else -1)) % count)


def cuts(planes):
    last = planes - HALO
    ends = (HALO, last - 5 * BLOCK, last - 3 * BLOCK, last - BLOCK, last)
    return list(zip(ends[:-1], ends[1:]))


def per_device(velocity):
    _, planes, axial, radial = velocity.shape
    sizes = lax.axis_size("az"), lax.axis_size("ax")
    theta_step = 2.0 * math.pi / (sizes[0] * planes)
    coef = jnp.asarray(coefficients(radial, theta_step))
    f32 = jnp.float32
    anywhere = pl.BlockSpec(memory_space=pl.ANY)
    vmem = pl.BlockSpec(memory_space=pltpu.VMEM)
    smem = pl.BlockSpec(memory_space=pltpu.SMEM)

    def shape(*sizes):
        return jax.ShapeDtypeStruct(sizes, f32)

    def call(kernel, name, work, scratch=0, **kwargs):
        return pl.pallas_call(
            kernel,
            name=name,
            compiler_params=pltpu.CompilerParams(vmem_limit_bytes=(4 + scratch) * 2**20),
            cost_estimate=pl.CostEstimate(flops=work, bytes_accessed=work, transcendentals=0),
            **kwargs,
        )

    odd = lax.axis_index("az") % 2
    ends = (planes - HALO, 0)
    even_end = jnp.where(odd == 1, ends[1], ends[0])
    odd_end = jnp.where(odd == 1, ends[0], ends[1])
    theta_even = across_even(lax.dynamic_slice_in_dim(velocity, even_end, HALO, 1), "az")
    theta_odd = across_odd(lax.dynamic_slice_in_dim(velocity, odd_end, HALO, 1), "az")

    edge = shape(3, planes, 2, radial)
    padded = shape(3, planes + 2 * HALO, axial + 2 * PAD, radial)
    row = shape(axial, radial)
    tile = shape(8, radial)
    vel, edge_even, edge_odd, mine, pay = call(
        functools.partial(first_pass, theta_step),
        "first_pass",
        0,
        out_shape=(padded, edge, edge, row, tile),
        in_specs=[anywhere],
        out_specs=(vmem,) * 5,
        scratch_shapes=[pltpu.SemaphoreType.DMA((planes // GROUP,))],
    )(pltpu.with_memory_space_constraint(velocity, pltpu.HBM))
    inner = exchanged(mine, "az", sizes[0] // 2)
    z_even = across_even(edge_even, "ax")
    edge_odd = call(
        carried,
        "carried",
        0,
        out_shape=edge,
        in_specs=[vmem] * 3,
        out_specs=vmem,
        input_output_aliases={2: 0},
    )(z_even, pay, edge_odd)
    z_odd = across_odd(edge_odd, "ax")

    spans = cuts(planes)

    def part_shape(n):
        return shape(3, spans[n][1] - spans[n][0], axial, radial)

    kept = [pltpu.VMEM((BLOCK, axial + 2 * PAD, radial), f32)] * 2

    def without_ghosts(n, name, rounds, vel, *tokens, **kwargs):
        return call(
            functools.partial(ahead, *spans[n], rounds),
            name,
            velocity.size * 2,
            out_shape=part_shape(n),
            in_specs=[vmem] * (2 + len(tokens)),
            out_specs=vmem,
            scratch_shapes=kept,
            **kwargs,
        )(vel, coef, *tokens)

    def with_ghosts(n, token):
        return call(
            functools.partial(ahead_with_ghosts, *spans[n]),
            f"span_{n}",
            velocity.size * 2,
            out_shape=part_shape(n),
            in_specs=[vmem] * 4,
            out_specs=vmem,
            scratch_shapes=kept,
        )(vel, inner, coef, token)

    middle = 8, (axial - 16) // 16, lambda i: [16 * i + 8, 16 * i + 16]
    outer = None, 1, lambda i: [i * 8, i * 8 + axial - 8]
    part = without_ghosts(0, "span_0_middle", middle, vel, pay)
    top, vel = call(
        fold,
        "fold",
        0,
        out_shape=(tile, padded),
        in_specs=[vmem] * 5,
        out_specs=(vmem,) * 2,
        input_output_aliases={3: 1},
    )(z_even, z_odd, pay, vel, part)
    for step in (1 << n for n in range(2, sizes[1].bit_length() - 1)):
        top = jnp.maximum(top, routed(top, "ax", lambda i, step=step: (i + step) % sizes[1]))

    bits = [1 << n for n in range(1, sizes[0].bit_length() - 1)] + [1]
    far = exchanged(top, "az", bits[0])
    parts = [
        without_ghosts(0, "span_0_outer", outer, vel, part, input_output_aliases={2: 0}),
        without_ghosts(1, "span_1", None, vel, top),
    ]
    for n, bit in enumerate(bits[1:]):
        top = call(
            merged,
            "merged",
            0,
            out_shape=tile,
            in_specs=[vmem] * 4,
            out_specs=vmem,
        )(top, far, *parts[-2:])
        far = exchanged(top, "az", bit)
        if n == 0:
            parts.append(with_ghosts(2, top))
    tile_even, tile_odd, vel = call(
        theta_in,
        "theta_in",
        0,
        out_shape=(tile, tile, padded),
        in_specs=[vmem] * 4,
        out_specs=(vmem,) * 3,
        input_output_aliases={2: 2},
    )(theta_even, theta_odd, vel, parts[-1])
    corner_even, corner_odd = across_even(tile_even, "ax"), across_odd(tile_odd, "ax")
    parts.append(with_ghosts(3, tile_even))
    increment, time_step, _ = call(
        functools.partial(finish, spans),
        "finish",
        0,
        scratch=8,
        out_shape=(shape(*velocity.shape), shape(1), padded),
        in_specs=[vmem] * (7 + len(parts)),
        out_specs=(anywhere, smem, vmem),
        scratch_shapes=[
            pltpu.VMEM(velocity.shape, f32),
            pltpu.SemaphoreType.DMA(((planes - 2 * HALO) // BLOCK + 2,)),
            *kept,
        ],
        input_output_aliases={0: 2},
    )(vel, inner, coef, top, far, corner_even, corner_odd, *parts)
    return increment, time_step.reshape(())


def solution(mesh):
    return jax.shard_map(
        per_device,
        mesh=mesh,
        in_specs=(P(None, "az", "ax", None),),
        out_specs=(P(None, "az", "ax", None), P()),
        check_vma=False,
    )
```

```python
import functools
import math

import jax
import jax.numpy as jnp
import numpy as np
from jax import lax
from jax.experimental import pallas as pl
from jax.experimental.pallas import tpu as pltpu
from jax.sharding import PartitionSpec as P

AXIAL_STEP = 0.01
VISCOSITY = 0.001
CFL_TARGET = 1.2
GAMMA = 8.0 / 15.0

PAD = 8
HALO = 2
BLOCK = 4
GROUP = 4
UNROLL = 4

(
    WALL,
    RADIAL_C,
    THETA_C,
    CROSS_Z,
    SECOND_C,
    CENTRE_Z,
    CENTRE_T,
    CURVE_T,
    TURN_T,
    RADIAL_F,
    THETA_F,
    SECOND_F,
    CENTRE_R,
    CURVE_R,
    TURN_R,
    COUNT,
) = range(16)


UNIT = VISCOSITY / (12.0 * AXIAL_STEP**2)


def coefficients(radial, theta_step):
    dr = 1.0 / radial
    index = np.arange(radial, dtype=np.float64)
    centre = (index + 0.5) * dr
    face = (index + 1.0) * dr
    wall = np.where(index < radial - 1.5, 1.0, 0.0)
    h = theta_step
    nu = VISCOSITY
    rows = np.zeros((COUNT, radial))
    rows[WALL] = wall
    common = -2.0 * nu / dr**2 - 30.0 * nu / (12.0 * AXIAL_STEP**2)
    rows[RADIAL_C] = nu / (2.0 * dr * centre)
    rows[THETA_C] = -1.0 / (12.0 * h * centre)
    rows[CROSS_Z] = 0.25 * rows[THETA_C]
    rows[SECOND_C] = nu / (12.0 * h * h * centre**2)
    rows[CENTRE_Z] = common - 30.0 * rows[SECOND_C]
    rows[CENTRE_T] = rows[CENTRE_Z] - nu / centre**2
    rows[CURVE_T] = 0.25 / centre
    rows[TURN_T] = nu / (h * centre**2)
    rows[RADIAL_F] = nu / (2.0 * dr * face)
    rows[THETA_F] = -0.25 / (12.0 * h * face)
    rows[SECOND_F] = nu / (12.0 * h * h * face**2)
    rows[CENTRE_R] = common - 30.0 * rows[SECOND_F] - nu / face**2
    rows[CURVE_R] = 1.0 / (16.0 * face)
    rows[TURN_R] = -nu / (h * face**2)
    rows[RADIAL_C:] /= UNIT
    return np.broadcast_to(rows[:, None, :], (COUNT, 8, radial)).astype(np.float32)


class Cells:
    def __init__(self, vel, j, k):
        self.vel, self.j, self.k, self.known = vel, j, k, {}

    def once(self, key, make):
        if key not in self.known:
            self.known[key] = make()
        return self.known[key]

    def at(self, n, dj, dk=0):
        rows = pl.ds(self.k + PAD + dk, 8)
        return self.once((n, dj, dk), lambda: self.vel[n, self.j + HALO + dj, rows, :])

    def turned(self, by, n, dj, dk=0):
        return self.once(
            (by, n, dj, dk), lambda: pltpu.roll(self.at(n, dj, dk), by % self.vel.shape[3], 1)
        )

    def pair(self, by, n, dj, dk=0):
        return self.once(
            ("pair", n, dj, dk), lambda: self.at(n, dj, dk) + self.turned(by, n, dj, dk)
        )

    def beside(self, dj, dk):
        n = 1 if dk >= 0 else 2
        other = (1, dj - 1, dk) if n == 1 else (2, dj, dk)
        here = (1, dj, dk) if n == 1 else (2, dj, dk + 1)
        return self.once(("sum", n, dj, dk), lambda: self.at(*other) + self.at(*here))


def terms(cells, ghost, coef, q, dr):
    at, turned, pair = cells.at, cells.turned, cells.pair
    a, b, c = (at(n, q) for n in range(3))
    lane = lax.broadcasted_iota(jnp.int32, a.shape, 1)
    first_lane = lane == 0
    last_lane = lane == a.shape[1] - 1

    lap = VISCOSITY / dr**2 / UNIT
    adv_z = -1.0 / (12.0 * AXIAL_STEP) / UNIT
    by_dr = 1.0 / dr / UNIT

    def differences(p1, m1, p2, m2):
        return 8.0 * (p1 - m1) - (p2 - m2), 16.0 * (p1 + m1) - (p2 + m2)

    def pieces(n):
        over = differences(*(at(n, q + d) for d in (1, -1, 2, -2)))
        along = differences(*(at(n, q, d) for d in (1, -1, 2, -2)))
        return over, along

    def below(n):
        if ghost is not None and n > 0 and q % 2 == 0:
            x = jnp.where(last_lane, ghost(n, q + 1), at(n, q))
            return pltpu.roll(x, 1, 1)
        x = turned(1, n, q)
        if ghost is not None:
            return jnp.where(first_lane, ghost(n, q), x)
        return x if n == 0 else jnp.where(first_lane, 0.0, x)

    def above(n):
        return jnp.where(last_lane, -at(n, q), turned(-1, n, q))

    pair_a, pair_side, pair_next = pair(1, 0, q), pair(1, 0, q + 1), pair(1, 0, q, 1)
    pair_b, pair_back = pair(-1, 1, q), pair(-1, 1, q - 1)

    theta, axial = pieces(2)
    up, low = above(2), below(2)
    u_r = pair_a + pair_next
    u_t = cells.beside(q, 0) + cells.beside(q, 1)
    h_z = (up - low) * (coef[RADIAL_C] - u_r * (0.125 * by_dr)) + (up + low) * lap
    h_z = h_z + theta[0] * (u_t * coef[CROSS_Z])
    h_z = h_z + (theta[1] * coef[SECOND_C] + axial[1])
    h_z = h_z + c * (coef[CENTRE_Z] + axial[0] * adv_z)

    theta, axial = pieces(1)
    up, low = above(1), below(1)
    u_r = pair_a + pair_side
    u_z = cells.beside(q, -1) + cells.beside(q + 1, -1)
    h_t = (up - low) * (coef[RADIAL_C] - u_r * (0.125 * by_dr)) + (up + low) * lap
    h_t = h_t + b * (coef[CENTRE_T] + theta[0] * coef[THETA_C] - u_r * coef[CURVE_T])
    h_t = h_t + (theta[1] * coef[SECOND_C] + axial[1])
    h_t = h_t + axial[0] * (u_z * (0.25 * adv_z))
    h_t = h_t + (pair_side - pair_a) * coef[TURN_T]

    theta, axial = pieces(0)
    up, low = turned(-1, 0, q), below(0)
    u_t = pair_b + pair_back
    u_z = pair(-1, 2, q) + pair(-1, 2, q, -1)
    h_r = (up - low) * (coef[RADIAL_F] - a * (0.5 * by_dr)) + (up + low) * lap
    h_r = h_r + u_t * (u_t * coef[CURVE_R] + theta[0] * coef[THETA_F])
    h_r = h_r + (theta[1] * coef[SECOND_F] + axial[1])
    h_r = h_r + (axial[0] * (u_z * (0.25 * adv_z)) + a * coef[CENTRE_R])
    h_r = h_r + (pair_b - pair_back) * coef[TURN_R]
    return h_r, h_t, h_z


def lane_zero_terms(cells, ghost, coef, q, dr):
    lap = VISCOSITY / dr**2 / UNIT
    by_dr = 1.0 / dr / UNIT
    a = cells.at(0, q)
    first_lane = lax.broadcasted_iota(jnp.int32, a.shape, 1) == 0
    add_r = ghost(0, q) * (lap - coef[RADIAL_F] + a * (0.5 * by_dr))
    add_t = ghost(1, q) * (lap - coef[RADIAL_C] + (a + cells.at(0, q + 1)) * (0.125 * by_dr))
    add_z = ghost(2, q) * (lap - coef[RADIAL_C] + (a + cells.at(0, q, 1)) * (0.125 * by_dr))
    return tuple(jnp.where(first_lane, x, 0.0) for x in (add_r, add_t, add_z))


def wall_mask(rows, radial):
    lane = lax.broadcasted_iota(jnp.int32, (rows, radial), 1)
    return jnp.where(lane == radial - 1, 0.0, 1.0).astype(jnp.float32)


def first_pass(theta_step, v_ref, vel_ref, even_ref, odd_ref, inner_ref, pay_ref, sems):
    _, planes, axial, radial = v_ref.shape
    lane = lax.broadcasted_iota(jnp.int32, (8, radial), 1)
    wall = wall_mask(8, radial)
    rate_t = (radial / theta_step) / (lane.astype(jnp.float32) + 0.5)
    odd = lax.rem(lax.axis_index("ax"), 2) == 1

    def fetch(g):
        part = pl.ds(g * GROUP, GROUP)
        target = vel_ref.at[:, pl.ds(g * GROUP + HALO, GROUP), pl.ds(PAD, axial)]
        return pltpu.make_async_copy(v_ref.at[:, part], target, sems.at[g])

    for g in range(planes // GROUP):
        fetch(g).start()

    zero = jnp.zeros((8, radial), jnp.float32)
    largest = [zero] * 4
    for g in range(planes // GROUP):
        fetch(g).wait()
        for i in range(axial // 8):
            k = pl.ds(8 * i, 8)
            padded = pl.ds(8 * i + PAD, 8)
            inner = zero if g == 0 else inner_ref[k, :]
            for q in range(GROUP):
                j = g * GROUP + q
                cells = [vel_ref[n, j + HALO, padded, :] for n in range(3)]
                for n, x in enumerate(cells):
                    place = n * planes + j
                    x = pltpu.roll(x, place, 1) if place else x
                    inner = jnp.where(lane == place, x if n == 2 else -x, inner)
                a, b, c = cells
                a = a * wall
                vel_ref[0, j + HALO, padded, :] = a
                rate = jnp.abs(a) * float(radial) + jnp.abs(b) * rate_t
                rate = rate + jnp.abs(c) * (1.0 / AXIAL_STEP)
                largest[q % 4] = jnp.maximum(largest[q % 4], rate)
            inner_ref[k, :] = inner
        for q in range(GROUP):
            for n in range(3):
                j = g * GROUP + q
                first = vel_ref[n, j + HALO, PAD : PAD + 2, :]
                last = vel_ref[n, j + HALO, PAD + axial - 2 : PAD + axial, :]
                even_ref[n, j] = jnp.where(odd, first, last)
                odd_ref[n, j] = jnp.where(odd, last, first)

    largest = jnp.maximum(
        jnp.maximum(largest[0], largest[1]), jnp.maximum(largest[2], largest[3])
    )
    top = jnp.max(largest, axis=(0, 1), keepdims=True)
    pay_ref[...] = jnp.broadcast_to(top, pay_ref.shape)
    end = lax.broadcasted_iota(jnp.int32, (2, radial), 1) == radial - 1
    for ref in (even_ref, odd_ref):
        ref[0, 0] = jnp.where(end, top, ref[0, 0])


def carried(even_ref, pay_ref, odd_in, odd_ref):
    radial = even_ref.shape[3]
    lane = lax.broadcasted_iota(jnp.int32, (2, radial), 1)
    top = jnp.maximum(even_ref[0, 0], pay_ref[0:2, :])
    odd_ref[0, 0] = jnp.where(lane == radial - 1, top, odd_in[0, 0])


def fold(even_ref, odd_ref, pay_ref, vel_in, _, *refs):
    del vel_in
    top_ref, vel_ref = refs
    planes, radial = even_ref.shape[1], even_ref.shape[3]
    axial = vel_ref.shape[2] - 2 * PAD
    lane = lax.broadcasted_iota(jnp.int32, (1, radial), 1)
    top = jnp.maximum(even_ref[0, 0, 0:1, :], odd_ref[0, 0, 0:1, :])
    top = jnp.max(jnp.where(lane == radial - 1, top, 0.0), axis=(0, 1), keepdims=True)
    top_ref[...] = jnp.maximum(pay_ref[...], top)
    wall = wall_mask(2, radial)
    odd = lax.rem(lax.axis_index("ax"), 2) == 1

    def plane(j, carry):
        for n in range(3):
            mask = wall if n == 0 else 1.0
            even, other = even_ref[n, j] * mask, odd_ref[n, j] * mask
            low, high = jnp.where(odd, even, other), jnp.where(odd, other, even)
            vel_ref[n, j + HALO, PAD - 2 : PAD, :] = low
            vel_ref[n, j + HALO, PAD + axial : PAD + axial + 2, :] = high
        return carry

    lax.fori_loop(0, planes, plane, 0, unroll=4)


def merged(mine_ref, far_ref, *refs):
    refs[-1][...] = jnp.maximum(mine_ref[...], far_ref[...])


def theta_in(even_ref, odd_ref, vel_in, _, even_tile, odd_tile, vel_ref):
    del vel_in
    planes, axial = vel_ref.shape[1] - 2 * HALO, vel_ref.shape[2] - 2 * PAD
    cells = pl.ds(PAD, axial)
    wall = wall_mask(1, vel_ref.shape[3])
    odd = lax.rem(lax.axis_index("az"), 2)
    below, above = 0, HALO + planes
    for ref, place in (
        (even_ref, jnp.where(odd == 1, below, above)),
        (odd_ref, jnp.where(odd == 1, above, below)),
    ):
        for q in range(HALO):
            vel_ref[0, place + q, cells, :] = ref[0, q] * wall
            vel_ref[1, place + q, cells, :] = ref[1, q]
            vel_ref[2, place + q, cells, :] = ref[2, q]
    first = vel_ref[1, below + HALO - 1, PAD : PAD + 1, :]
    last = vel_ref[2, above, PAD + axial - 1 : PAD + axial, :]
    odd = lax.rem(lax.axis_index("ax"), 2) == 1
    shape = even_tile.shape
    even_tile[...] = jnp.broadcast_to(jnp.where(odd, first, last), shape)
    odd_tile[...] = jnp.broadcast_to(jnp.where(odd, last, first), shape)


def ghosts(cells, inner, planes):
    radial = inner.shape[1]

    def ghost(n, q):
        turn = -(n * planes + q + cells.j) % radial
        return cells.once(("ghost", n, q), lambda: pltpu.roll(inner, turn, 1) if turn else inner)

    return ghost


def block_terms(vel_ref, inner_ref, coef_ref, j, size, write, rounds=None):
    planes = vel_ref.shape[1] - 2 * HALO
    axial, radial = vel_ref.shape[2] - 2 * PAD, vel_ref.shape[3]
    groups = 4 * BLOCK // size
    times, places = rounds or (
        axial // (8 * groups),
        lambda i: [(i * groups + u) * 8 for u in range(groups)],
    )

    def rows(i, carry):
        coef = [coef_ref[n] for n in range(COUNT)]
        for k in places(i):
            k = pl.multiple_of(k, 8)
            cells = Cells(vel_ref, j, k)
            ghost = None
            if inner_ref is not None:
                ghost = ghosts(cells, inner_ref[pl.ds(k, 8), :], planes)
            for q in range(size):
                for n, value in enumerate(terms(cells, ghost, coef, q, 1.0 / radial)):
                    write(n, j + q, pl.ds(k, 8), value)
        return carry

    lax.fori_loop(0, times, rows, 0)


def ahead(first, last, rounds, vel_ref, coef_ref, *refs):
    out_ref = refs[-1]

    def write(n, j, k, value):
        out_ref[n, j - first, k, :] = value

    def block(m, carry):
        block_terms(vel_ref, None, coef_ref, first + m * BLOCK, BLOCK, write, rounds)
        return carry

    lax.fori_loop(0, (last - first) // BLOCK, block, 0)


def ahead_with_ghosts(first, last, vel_ref, inner_ref, coef_ref, _, out_ref):
    def write(n, j, k, value):
        out_ref[n, j - first, k, :] = value

    for j in range(first, last, BLOCK):
        block_terms(vel_ref, inner_ref, coef_ref, j, BLOCK, write)


def finish(spans, vel_in, inner_ref, coef_ref, top, far, even, odd, *refs):
    parts, refs = refs[: len(spans)], refs[len(spans) :]
    del vel_in
    out_ref, step_ref, vel_ref, res, sems = refs
    axial, radial = inner_ref.shape
    planes = vel_ref.shape[1] - 2 * HALO
    largest = jnp.maximum(top[0:1, :], far[0:1, :])
    time_step = CFL_TARGET / (jnp.max(largest) + 1e-06)
    step_ref[0] = time_step
    scale = GAMMA * UNIT * time_step
    factors = (scale * coef_ref[WALL], scale, scale)
    pending = []

    def send(j, size):
        part_of = pl.ds(j, size)
        copy = pltpu.make_async_copy(
            res.at[:, part_of], out_ref.at[:, part_of], sems.at[len(pending)]
        )
        copy.start()
        pending.append(copy)

    def write(n, j, k, value):
        res[n, j, k, :] = value * factors[n]

    def complete(part, j, place, add):
        groups = 4

        def rows(i, carry):
            found = []
            for u in range(groups):
                k = pl.multiple_of((i * groups + u) * 8, 8)
                cells = Cells(vel_ref, j, k)
                ghost = ghosts(cells, inner_ref[pl.ds(k, 8), :], planes) if add else None
                for q in range(BLOCK):
                    values = [part[n, place + q, pl.ds(k, 8), :] for n in range(3)]
                    if add:
                        added = lane_zero_terms(cells, ghost, coef_ref, q, 1.0 / radial)
                        values = [x + y for x, y in zip(values, added)]
                    found.append((q, k, values))
            for q, k, values in found:
                for n, value in enumerate(values):
                    write(n, j + q, pl.ds(k, 8), value)
            return carry

        lax.fori_loop(0, axial // (8 * groups), rows, 0)
        send(j, BLOCK)

    for n, (part, (first, last)) in enumerate(zip(parts, spans)):
        for j in range(first, last, BLOCK):
            complete(part, j, j - first, n < 2)

    second = lax.rem(lax.axis_index("ax"), 2) == 1
    even, odd = even[0:1, :], odd[0:1, :]
    following, preceding = jnp.where(second, odd, even), jnp.where(second, even, odd)
    vel_ref[1, HALO - 1, PAD + axial : PAD + axial + 1, :] = following
    vel_ref[2, HALO + planes, PAD - 1 : PAD, :] = preceding
    for j in (0, planes - HALO):
        block_terms(vel_ref, inner_ref, coef_ref, j, HALO, write)
        send(j, HALO)
    for copy in pending:
        copy.wait()


def routed(block, axis, source):
    count = lax.axis_size(axis)
    return lax.ppermute(block, axis, [(source(i), i) for i in range(count)])


def exchanged(block, axis, step):
    return routed(block, axis, lambda i: i ^ step)


def across_even(block, axis):
    return exchanged(block, axis, 1)


def across_odd(block, axis):
    count = lax.axis_size(axis)
    return routed(block, axis, lambda i: (i + (1 if i % 2 else -1)) % count)


def cuts(planes):
    last = planes - HALO
    ends = (HALO, last - 5 * BLOCK, last - 3 * BLOCK, last - BLOCK, last)
    return list(zip(ends[:-1], ends[1:]))


def per_device(velocity):
    _, planes, axial, radial = velocity.shape
    sizes = lax.axis_size("az"), lax.axis_size("ax")
    theta_step = 2.0 * math.pi / (sizes[0] * planes)
    coef = jnp.asarray(coefficients(radial, theta_step))
    f32 = jnp.float32
    anywhere = pl.BlockSpec(memory_space=pl.ANY)
    vmem = pl.BlockSpec(memory_space=pltpu.VMEM)
    smem = pl.BlockSpec(memory_space=pltpu.SMEM)

    def shape(*sizes):
        return jax.ShapeDtypeStruct(sizes, f32)

    def call(kernel, name, work, scratch=0, **kwargs):
        return pl.pallas_call(
            kernel,
            name=name,
            compiler_params=pltpu.CompilerParams(vmem_limit_bytes=(4 + scratch) * 2**20),
            cost_estimate=pl.CostEstimate(flops=work, bytes_accessed=work, transcendentals=0),
            **kwargs,
        )

    odd = lax.axis_index("az") % 2
    ends = (planes - HALO, 0)
    even_end = jnp.where(odd == 1, ends[1], ends[0])
    odd_end = jnp.where(odd == 1, ends[0], ends[1])
    theta_even = across_even(lax.dynamic_slice_in_dim(velocity, even_end, HALO, 1), "az")
    theta_odd = across_odd(lax.dynamic_slice_in_dim(velocity, odd_end, HALO, 1), "az")

    edge = shape(3, planes, 2, radial)
    padded = shape(3, planes + 2 * HALO, axial + 2 * PAD, radial)
    row = shape(axial, radial)
    tile = shape(8, radial)
    vel, edge_even, edge_odd, mine, pay = call(
        functools.partial(first_pass, theta_step),
        "first_pass",
        0,
        out_shape=(padded, edge, edge, row, tile),
        in_specs=[anywhere],
        out_specs=(vmem,) * 5,
        scratch_shapes=[pltpu.SemaphoreType.DMA((planes // GROUP,))],
    )(pltpu.with_memory_space_constraint(velocity, pltpu.HBM))
    inner = exchanged(mine, "az", sizes[0] // 2)
    z_even = across_even(edge_even, "ax")
    edge_odd = call(
        carried,
        "carried",
        0,
        out_shape=edge,
        in_specs=[vmem] * 3,
        out_specs=vmem,
        input_output_aliases={2: 0},
    )(z_even, pay, edge_odd)
    z_odd = across_odd(edge_odd, "ax")

    spans = cuts(planes)

    def part_shape(n):
        return shape(3, spans[n][1] - spans[n][0], axial, radial)

    def without_ghosts(n, name, rounds, vel, *tokens, **kwargs):
        return call(
            functools.partial(ahead, *spans[n], rounds),
            name,
            velocity.size * 2,
            out_shape=part_shape(n),
            in_specs=[vmem] * (2 + len(tokens)),
            out_specs=vmem,
            **kwargs,
        )(vel, coef, *tokens)

    def with_ghosts(n, token):
        return call(
            functools.partial(ahead_with_ghosts, *spans[n]),
            f"span_{n}",
            velocity.size * 2,
            out_shape=part_shape(n),
            in_specs=[vmem] * 4,
            out_specs=vmem,
        )(vel, inner, coef, token)

    middle = (axial - 16) // 16, lambda i: [16 * i + 8, 16 * i + 16]
    outer = 1, lambda i: [i * 8, i * 8 + axial - 8]
    part = without_ghosts(0, "span_0_middle", middle, vel, pay)
    top, vel = call(
        fold,
        "fold",
        0,
        out_shape=(tile, padded),
        in_specs=[vmem] * 5,
        out_specs=(vmem,) * 2,
        input_output_aliases={3: 1},
    )(z_even, z_odd, pay, vel, part)
    for step in (1 << n for n in range(2, sizes[1].bit_length() - 1)):
        top = jnp.maximum(top, routed(top, "ax", lambda i, step=step: (i + step) % sizes[1]))

    bits = [1 << n for n in range(1, sizes[0].bit_length() - 1)] + [1]
    far = exchanged(top, "az", bits[0])
    parts = [
        without_ghosts(0, "span_0_outer", outer, vel, part, input_output_aliases={2: 0}),
        without_ghosts(1, "span_1", None, vel, top),
    ]
    for n, bit in enumerate(bits[1:]):
        top = call(
            merged,
            "merged",
            0,
            out_shape=tile,
            in_specs=[vmem] * 4,
            out_specs=vmem,
        )(top, far, *parts[-2:])
        far = exchanged(top, "az", bit)
        if n == 0:
            parts.append(with_ghosts(2, top))
    tile_even, tile_odd, vel = call(
        theta_in,
        "theta_in",
        0,
        out_shape=(tile, tile, padded),
        in_specs=[vmem] * 4,
        out_specs=(vmem,) * 3,
        input_output_aliases={2: 2},
    )(theta_even, theta_odd, vel, parts[-1])
    corner_even, corner_odd = across_even(tile_even, "ax"), across_odd(tile_odd, "ax")
    parts.append(with_ghosts(3, tile_even))
    increment, time_step, _ = call(
        functools.partial(finish, spans),
        "finish",
        0,
        scratch=8,
        out_shape=(shape(*velocity.shape), shape(1), padded),
        in_specs=[vmem] * (7 + len(parts)),
        out_specs=(anywhere, smem, vmem),
        scratch_shapes=[
            pltpu.VMEM(velocity.shape, f32),
            pltpu.SemaphoreType.DMA(((planes - 2 * HALO) // BLOCK + 2,)),
        ],
        input_output_aliases={0: 2},
    )(vel, inner, coef, top, far, corner_even, corner_odd, *parts)
    return increment, time_step.reshape(())


def solution(mesh):
    return jax.shard_map(
        per_device,
        mesh=mesh,
        in_specs=(P(None, "az", "ax", None),),
        out_specs=(P(None, "az", "ax", None), P()),
        check_vma=False,
    )
```

```python
import functools
import math

import jax
import jax.numpy as jnp
import numpy as np
from jax import lax
from jax.experimental import pallas as pl
from jax.experimental.pallas import tpu as pltpu
from jax.sharding import PartitionSpec as P

AXIAL_STEP = 0.01
VISCOSITY = 0.001
CFL_TARGET = 1.2
GAMMA = 8.0 / 15.0

PAD = 8
HALO = 2
BLOCK = 4
GROUP = 4
UNROLL = 4

(
    WALL,
    RADIAL_C,
    THETA_C,
    CROSS_Z,
    SECOND_C,
    CENTRE_Z,
    CENTRE_T,
    CURVE_T,
    TURN_T,
    RADIAL_F,
    THETA_F,
    SECOND_F,
    CENTRE_R,
    CURVE_R,
    TURN_R,
    COUNT,
) = range(16)


UNIT = VISCOSITY / (12.0 * AXIAL_STEP**2)


def coefficients(radial, theta_step):
    dr = 1.0 / radial
    index = np.arange(radial, dtype=np.float64)
    centre = (index + 0.5) * dr
    face = (index + 1.0) * dr
    wall = np.where(index < radial - 1.5, 1.0, 0.0)
    h = theta_step
    nu = VISCOSITY
    rows = np.zeros((COUNT, radial))
    rows[WALL] = wall
    common = -2.0 * nu / dr**2 - 30.0 * nu / (12.0 * AXIAL_STEP**2)
    rows[RADIAL_C] = nu / (2.0 * dr * centre)
    rows[THETA_C] = -1.0 / (12.0 * h * centre)
    rows[CROSS_Z] = 0.25 * rows[THETA_C]
    rows[SECOND_C] = nu / (12.0 * h * h * centre**2)
    rows[CENTRE_Z] = common - 30.0 * rows[SECOND_C]
    rows[CENTRE_T] = rows[CENTRE_Z] - nu / centre**2
    rows[CURVE_T] = 0.25 / centre
    rows[TURN_T] = nu / (h * centre**2)
    rows[RADIAL_F] = nu / (2.0 * dr * face)
    rows[THETA_F] = -0.25 / (12.0 * h * face)
    rows[SECOND_F] = nu / (12.0 * h * h * face**2)
    rows[CENTRE_R] = common - 30.0 * rows[SECOND_F] - nu / face**2
    rows[CURVE_R] = 1.0 / (16.0 * face)
    rows[TURN_R] = -nu / (h * face**2)
    rows[RADIAL_C:] /= UNIT
    return np.broadcast_to(rows[:, None, :], (COUNT, 8, radial)).astype(np.float32)


class Cells:
    def __init__(self, vel, j, k):
        self.vel, self.j, self.k, self.known = vel, j, k, {}

    def once(self, key, make):
        if key not in self.known:
            self.known[key] = make()
        return self.known[key]

    def at(self, n, dj, dk=0):
        rows = pl.ds(self.k + PAD + dk, 8)
        return self.once((n, dj, dk), lambda: self.vel[n, self.j + HALO + dj, rows, :])

    def turned(self, by, n, dj, dk=0):
        return self.once(
            (by, n, dj, dk), lambda: pltpu.roll(self.at(n, dj, dk), by % self.vel.shape[3], 1)
        )

    def pair(self, by, n, dj, dk=0):
        return self.once(
            ("pair", n, dj, dk), lambda: self.at(n, dj, dk) + self.turned(by, n, dj, dk)
        )

    def beside(self, dj, dk):
        n = 1 if dk >= 0 else 2
        other = (1, dj - 1, dk) if n == 1 else (2, dj, dk)
        here = (1, dj, dk) if n == 1 else (2, dj, dk + 1)
        return self.once(("sum", n, dj, dk), lambda: self.at(*other) + self.at(*here))


def terms(cells, ghost, coef, q, dr):
    at, turned, pair = cells.at, cells.turned, cells.pair
    a, b, c = (at(n, q) for n in range(3))
    lane = lax.broadcasted_iota(jnp.int32, a.shape, 1)
    first_lane = lane == 0
    last_lane = lane == a.shape[1] - 1

    lap = VISCOSITY / dr**2 / UNIT
    adv_z = -1.0 / (12.0 * AXIAL_STEP) / UNIT
    by_dr = 1.0 / dr / UNIT

    def differences(p1, m1, p2, m2):
        return 8.0 * (p1 - m1) - (p2 - m2), 16.0 * (p1 + m1) - (p2 + m2)

    def pieces(n):
        over = differences(*(at(n, q + d) for d in (1, -1, 2, -2)))
        along = differences(*(at(n, q, d) for d in (1, -1, 2, -2)))
        return over, along

    def below(n):
        if ghost is not None and n > 0 and q % 2 == 0:
            x = jnp.where(last_lane, ghost(n, q + 1), at(n, q))
            return pltpu.roll(x, 1, 1)
        x = turned(1, n, q)
        if ghost is not None:
            return jnp.where(first_lane, ghost(n, q), x)
        return x if n == 0 else jnp.where(first_lane, 0.0, x)

    def above(n):
        return jnp.where(last_lane, -at(n, q), turned(-1, n, q))

    pair_a, pair_side, pair_next = pair(1, 0, q), pair(1, 0, q + 1), pair(1, 0, q, 1)
    pair_b, pair_back = pair(-1, 1, q), pair(-1, 1, q - 1)

    theta, axial = pieces(2)
    up, low = above(2), below(2)
    u_r = pair_a + pair_next
    u_t = cells.beside(q, 0) + cells.beside(q, 1)
    h_z = (up - low) * (coef[RADIAL_C] - u_r * (0.125 * by_dr)) + (up + low) * lap
    h_z = h_z + theta[0] * (u_t * coef[CROSS_Z])
    h_z = h_z + (theta[1] * coef[SECOND_C] + axial[1])
    h_z = h_z + c * (coef[CENTRE_Z] + axial[0] * adv_z)

    theta, axial = pieces(1)
    up, low = above(1), below(1)
    u_r = pair_a + pair_side
    u_z = cells.beside(q, -1) + cells.beside(q + 1, -1)
    h_t = (up - low) * (coef[RADIAL_C] - u_r * (0.125 * by_dr)) + (up + low) * lap
    h_t = h_t + b * (coef[CENTRE_T] + theta[0] * coef[THETA_C] - u_r * coef[CURVE_T])
    h_t = h_t + (theta[1] * coef[SECOND_C] + axial[1])
    h_t = h_t + axial[0] * (u_z * (0.25 * adv_z))
    h_t = h_t + (pair_side - pair_a) * coef[TURN_T]

    theta, axial = pieces(0)
    up, low = turned(-1, 0, q), below(0)
    u_t = pair_b + pair_back
    u_z = pair(-1, 2, q) + pair(-1, 2, q, -1)
    h_r = (up - low) * (coef[RADIAL_F] - a * (0.5 * by_dr)) + (up + low) * lap
    h_r = h_r + u_t * (u_t * coef[CURVE_R] + theta[0] * coef[THETA_F])
    h_r = h_r + (theta[1] * coef[SECOND_F] + axial[1])
    h_r = h_r + (axial[0] * (u_z * (0.25 * adv_z)) + a * coef[CENTRE_R])
    h_r = h_r + (pair_b - pair_back) * coef[TURN_R]
    return h_r, h_t, h_z


def lane_zero_terms(cells, ghost, coef, q, dr):
    lap = VISCOSITY / dr**2 / UNIT
    by_dr = 1.0 / dr / UNIT
    a = cells.at(0, q)
    first_lane = lax.broadcasted_iota(jnp.int32, a.shape, 1) == 0
    add_r = ghost(0, q) * (lap - coef[RADIAL_F] + a * (0.5 * by_dr))
    add_t = ghost(1, q) * (lap - coef[RADIAL_C] + (a + cells.at(0, q + 1)) * (0.125 * by_dr))
    add_z = ghost(2, q) * (lap - coef[RADIAL_C] + (a + cells.at(0, q, 1)) * (0.125 * by_dr))
    return tuple(jnp.where(first_lane, x, 0.0) for x in (add_r, add_t, add_z))


def wall_mask(rows, radial):
    lane = lax.broadcasted_iota(jnp.int32, (rows, radial), 1)
    return jnp.where(lane == radial - 1, 0.0, 1.0).astype(jnp.float32)


def first_pass(theta_step, v_ref, vel_ref, even_ref, odd_ref, inner_ref, pay_ref, sems):
    _, planes, axial, radial = v_ref.shape
    lane = lax.broadcasted_iota(jnp.int32, (8, radial), 1)
    wall = wall_mask(8, radial)
    rate_t = (radial / theta_step) / (lane.astype(jnp.float32) + 0.5)
    odd = lax.rem(lax.axis_index("ax"), 2) == 1

    def fetch(g):
        part = pl.ds(g * GROUP, GROUP)
        target = vel_ref.at[:, pl.ds(g * GROUP + HALO, GROUP), pl.ds(PAD, axial)]
        return pltpu.make_async_copy(v_ref.at[:, part], target, sems.at[g])

    for g in range(planes // GROUP):
        fetch(g).start()

    zero = jnp.zeros((8, radial), jnp.float32)
    largest = [zero] * 4
    for g in range(planes // GROUP):
        fetch(g).wait()
        for i in range(axial // 8):
            k = pl.ds(8 * i, 8)
            padded = pl.ds(8 * i + PAD, 8)
            inner = zero if g == 0 else inner_ref[k, :]
            for q in range(GROUP):
                j = g * GROUP + q
                cells = [vel_ref[n, j + HALO, padded, :] for n in range(3)]
                for n, x in enumerate(cells):
                    place = n * planes + j
                    x = pltpu.roll(x, place, 1) if place else x
                    inner = jnp.where(lane == place, x if n == 2 else -x, inner)
                a, b, c = cells
                a = a * wall
                vel_ref[0, j + HALO, padded, :] = a
                rate = jnp.abs(a) * float(radial) + jnp.abs(b) * rate_t
                rate = rate + jnp.abs(c) * (1.0 / AXIAL_STEP)
                largest[q % 4] = jnp.maximum(largest[q % 4], rate)
            inner_ref[k, :] = inner
        for q in range(GROUP):
            for n in range(3):
                j = g * GROUP + q
                first = vel_ref[n, j + HALO, PAD : PAD + 2, :]
                last = vel_ref[n, j + HALO, PAD + axial - 2 : PAD + axial, :]
                even_ref[n, j] = jnp.where(odd, first, last)
                odd_ref[n, j] = jnp.where(odd, last, first)

    largest = jnp.maximum(
        jnp.maximum(largest[0], largest[1]), jnp.maximum(largest[2], largest[3])
    )
    top = jnp.max(largest, axis=(0, 1), keepdims=True)
    pay_ref[...] = jnp.broadcast_to(top, pay_ref.shape)
    end = lax.broadcasted_iota(jnp.int32, (2, radial), 1) == radial - 1
    for ref in (even_ref, odd_ref):
        ref[0, 0] = jnp.where(end, top, ref[0, 0])


def carried(even_ref, pay_ref, odd_in, _, odd_ref):
    radial = even_ref.shape[3]
    lane = lax.broadcasted_iota(jnp.int32, (2, radial), 1)
    top = jnp.maximum(even_ref[0, 0], pay_ref[0:2, :])
    odd_ref[0, 0] = jnp.where(lane == radial - 1, top, odd_in[0, 0])


def fold(even_ref, odd_ref, pay_ref, vel_in, _, *refs):
    del vel_in
    top_ref, vel_ref = refs
    planes, radial = even_ref.shape[1], even_ref.shape[3]
    axial = vel_ref.shape[2] - 2 * PAD
    lane = lax.broadcasted_iota(jnp.int32, (1, radial), 1)
    top = jnp.maximum(even_ref[0, 0, 0:1, :], odd_ref[0, 0, 0:1, :])
    top = jnp.max(jnp.where(lane == radial - 1, top, 0.0), axis=(0, 1), keepdims=True)
    top_ref[...] = jnp.maximum(pay_ref[...], top)
    wall = wall_mask(2, radial)
    odd = lax.rem(lax.axis_index("ax"), 2) == 1

    def plane(j, carry):
        for n in range(3):
            mask = wall if n == 0 else 1.0
            even, other = even_ref[n, j] * mask, odd_ref[n, j] * mask
            low, high = jnp.where(odd, even, other), jnp.where(odd, other, even)
            vel_ref[n, j + HALO, PAD - 2 : PAD, :] = low
            vel_ref[n, j + HALO, PAD + axial : PAD + axial + 2, :] = high
        return carry

    lax.fori_loop(0, planes, plane, 0, unroll=4)


def merged(mine_ref, far_ref, *refs):
    refs[-1][...] = jnp.maximum(mine_ref[...], far_ref[...])


def theta_in(even_ref, odd_ref, vel_in, _, even_tile, odd_tile, vel_ref):
    del vel_in
    planes, axial = vel_ref.shape[1] - 2 * HALO, vel_ref.shape[2] - 2 * PAD
    cells = pl.ds(PAD, axial)
    wall = wall_mask(1, vel_ref.shape[3])
    odd = lax.rem(lax.axis_index("az"), 2)
    below, above = 0, HALO + planes
    for ref, place in (
        (even_ref, jnp.where(odd == 1, below, above)),
        (odd_ref, jnp.where(odd == 1, above, below)),
    ):
        for q in range(HALO):
            vel_ref[0, place + q, cells, :] = ref[0, q] * wall
            vel_ref[1, place + q, cells, :] = ref[1, q]
            vel_ref[2, place + q, cells, :] = ref[2, q]
    first = vel_ref[1, below + HALO - 1, PAD : PAD + 1, :]
    last = vel_ref[2, above, PAD + axial - 1 : PAD + axial, :]
    odd = lax.rem(lax.axis_index("ax"), 2) == 1
    shape = even_tile.shape
    even_tile[...] = jnp.broadcast_to(jnp.where(odd, first, last), shape)
    odd_tile[...] = jnp.broadcast_to(jnp.where(odd, last, first), shape)


def ghosts(cells, inner, planes):
    radial = inner.shape[1]

    def ghost(n, q):
        turn = -(n * planes + q + cells.j) % radial
        return cells.once(("ghost", n, q), lambda: pltpu.roll(inner, turn, 1) if turn else inner)

    return ghost


def block_terms(vel_ref, inner_ref, coef_ref, j, size, write, rounds=None):
    planes = vel_ref.shape[1] - 2 * HALO
    axial, radial = vel_ref.shape[2] - 2 * PAD, vel_ref.shape[3]
    groups = 4 * BLOCK // size
    times, places = rounds or (
        axial // (8 * groups),
        lambda i: [(i * groups + u) * 8 for u in range(groups)],
    )

    def rows(i, carry):
        coef = [coef_ref[n] for n in range(COUNT)]
        found = []
        for k in places(i):
            k = pl.multiple_of(k, 8)
            cells = Cells(vel_ref, j, k)
            ghost = None
            if inner_ref is not None:
                ghost = ghosts(cells, inner_ref[pl.ds(k, 8), :], planes)
            for q in range(size):
                found.append((q, k, terms(cells, ghost, coef, q, 1.0 / radial)))
        for q, k, values in found:
            for n, value in enumerate(values):
                write(n, j + q, pl.ds(k, 8), value)
        return carry

    lax.fori_loop(0, times, rows, 0)


def ahead(first, last, rounds, vel_ref, coef_ref, *refs):
    out_ref = refs[-1]

    def write(n, j, k, value):
        out_ref[n, j - first, k, :] = value

    def block(m, carry):
        block_terms(vel_ref, None, coef_ref, first + m * BLOCK, BLOCK, write, rounds)
        return carry

    lax.fori_loop(0, (last - first) // BLOCK, block, 0)


def ahead_with_ghosts(first, last, vel_ref, inner_ref, coef_ref, _, out_ref):
    def write(n, j, k, value):
        out_ref[n, j - first, k, :] = value

    for j in range(first, last, BLOCK):
        block_terms(vel_ref, inner_ref, coef_ref, j, BLOCK, write)


def finish(spans, vel_in, inner_ref, coef_ref, top, far, even, odd, *refs):
    parts, refs = refs[: len(spans)], refs[len(spans) :]
    del vel_in
    out_ref, step_ref, vel_ref, res, sems = refs
    axial, radial = inner_ref.shape
    planes = vel_ref.shape[1] - 2 * HALO
    largest = jnp.maximum(top[0:1, :], far[0:1, :])
    time_step = CFL_TARGET / (jnp.max(largest) + 1e-06)
    step_ref[0] = time_step
    scale = GAMMA * UNIT * time_step
    factors = (scale * coef_ref[WALL], scale, scale)
    pending = []

    def send(j, size):
        part_of = pl.ds(j, size)
        copy = pltpu.make_async_copy(
            res.at[:, part_of], out_ref.at[:, part_of], sems.at[len(pending)]
        )
        copy.start()
        pending.append(copy)

    def write(n, j, k, value):
        res[n, j, k, :] = value * factors[n]

    def complete(part, j, place, add):
        groups = 4

        def rows(i, carry):
            found = []
            for u in range(groups):
                k = pl.multiple_of((i * groups + u) * 8, 8)
                cells = Cells(vel_ref, j, k)
                ghost = ghosts(cells, inner_ref[pl.ds(k, 8), :], planes) if add else None
                for q in range(BLOCK):
                    values = [part[n, place + q, pl.ds(k, 8), :] for n in range(3)]
                    if add:
                        added = lane_zero_terms(cells, ghost, coef_ref, q, 1.0 / radial)
                        values = [x + y for x, y in zip(values, added)]
                    found.append((q, k, values))
            for q, k, values in found:
                for n, value in enumerate(values):
                    write(n, j + q, pl.ds(k, 8), value)
            return carry

        lax.fori_loop(0, axial // (8 * groups), rows, 0)
        send(j, BLOCK)

    for n, (part, (first, last)) in enumerate(zip(parts, spans)):
        for j in range(first, last, BLOCK):
            complete(part, j, j - first, n < 3)

    second = lax.rem(lax.axis_index("ax"), 2) == 1
    even, odd = even[0:1, :], odd[0:1, :]
    following, preceding = jnp.where(second, odd, even), jnp.where(second, even, odd)
    vel_ref[1, HALO - 1, PAD + axial : PAD + axial + 1, :] = following
    vel_ref[2, HALO + planes, PAD - 1 : PAD, :] = preceding
    for j in (0, planes - HALO):
        block_terms(vel_ref, inner_ref, coef_ref, j, HALO, write)
        send(j, HALO)
    for copy in pending:
        copy.wait()


def routed(block, axis, source):
    count = lax.axis_size(axis)
    return lax.ppermute(block, axis, [(source(i), i) for i in range(count)])


def exchanged(block, axis, step):
    return routed(block, axis, lambda i: i ^ step)


def across_even(block, axis):
    return exchanged(block, axis, 1)


def across_odd(block, axis):
    count = lax.axis_size(axis)
    return routed(block, axis, lambda i: (i + (1 if i % 2 else -1)) % count)


def cuts(planes):
    last = planes - HALO
    ends = (HALO, HALO + BLOCK, last - 5 * BLOCK, last - 3 * BLOCK, last - BLOCK, last)
    return list(zip(ends[:-1], ends[1:]))


def per_device(velocity):
    _, planes, axial, radial = velocity.shape
    sizes = lax.axis_size("az"), lax.axis_size("ax")
    theta_step = 2.0 * math.pi / (sizes[0] * planes)
    coef = jnp.asarray(coefficients(radial, theta_step))
    f32 = jnp.float32
    anywhere = pl.BlockSpec(memory_space=pl.ANY)
    vmem = pl.BlockSpec(memory_space=pltpu.VMEM)
    smem = pl.BlockSpec(memory_space=pltpu.SMEM)

    def shape(*sizes):
        return jax.ShapeDtypeStruct(sizes, f32)

    def call(kernel, name, work, scratch=0, **kwargs):
        return pl.pallas_call(
            kernel,
            name=name,
            compiler_params=pltpu.CompilerParams(vmem_limit_bytes=(4 + scratch) * 2**20),
            cost_estimate=pl.CostEstimate(flops=work, bytes_accessed=work, transcendentals=0),
            **kwargs,
        )

    odd = lax.axis_index("az") % 2
    ends = (planes - HALO, 0)
    even_end = jnp.where(odd == 1, ends[1], ends[0])
    odd_end = jnp.where(odd == 1, ends[0], ends[1])
    theta_even = across_even(lax.dynamic_slice_in_dim(velocity, even_end, HALO, 1), "az")
    theta_odd = across_odd(lax.dynamic_slice_in_dim(velocity, odd_end, HALO, 1), "az")

    edge = shape(3, planes, 2, radial)
    padded = shape(3, planes + 2 * HALO, axial + 2 * PAD, radial)
    row = shape(axial, radial)
    tile = shape(8, radial)
    vel, edge_even, edge_odd, mine, pay = call(
        functools.partial(first_pass, theta_step),
        "first_pass",
        0,
        out_shape=(padded, edge, edge, row, tile),
        in_specs=[anywhere],
        out_specs=(vmem,) * 5,
        scratch_shapes=[pltpu.SemaphoreType.DMA((planes // GROUP,))],
    )(pltpu.with_memory_space_constraint(velocity, pltpu.HBM))
    inner = exchanged(mine, "az", sizes[0] // 2)
    z_even = across_even(edge_even, "ax")
    spans = cuts(planes)

    def part_shape(n):
        return shape(3, spans[n][1] - spans[n][0], axial, radial)

    def without_ghosts(n, name, rounds, vel, *tokens, **kwargs):
        return call(
            functools.partial(ahead, *spans[n], rounds),
            name,
            velocity.size * 2,
            out_shape=part_shape(n),
            in_specs=[vmem] * (2 + len(tokens)),
            out_specs=vmem,
            **kwargs,
        )(vel, coef, *tokens)

    def with_ghosts(n, token):
        return call(
            functools.partial(ahead_with_ghosts, *spans[n]),
            f"span_{n}",
            velocity.size * 2,
            out_shape=part_shape(n),
            in_specs=[vmem] * 4,
            out_specs=vmem,
        )(vel, inner, coef, token)

    middle = (axial - 16) // 16, lambda i: [16 * i + 8, 16 * i + 16]
    outer = 1, lambda i: [i * 8, i * 8 + axial - 8]
    part_0 = without_ghosts(0, "span_0_middle", middle, vel, pay)
    edge_odd = call(
        carried,
        "carried",
        0,
        out_shape=edge,
        in_specs=[vmem] * 4,
        out_specs=vmem,
        input_output_aliases={2: 0},
    )(z_even, pay, edge_odd, part_0)
    z_odd = across_odd(edge_odd, "ax")

    part_1 = without_ghosts(1, "span_1_middle", middle, vel, edge_odd)
    top, vel = call(
        fold,
        "fold",
        0,
        out_shape=(tile, padded),
        in_specs=[vmem] * 5,
        out_specs=(vmem,) * 2,
        input_output_aliases={3: 1},
    )(z_even, z_odd, pay, vel, part_1)
    for step in (1 << n for n in range(2, sizes[1].bit_length() - 1)):
        top = jnp.maximum(top, routed(top, "ax", lambda i, step=step: (i + step) % sizes[1]))

    bits = [1 << n for n in range(1, sizes[0].bit_length() - 1)] + [1]
    far = exchanged(top, "az", bits[0])
    parts = [
        without_ghosts(0, "span_0_outer", outer, vel, part_0, input_output_aliases={2: 0}),
        without_ghosts(1, "span_1_outer", outer, vel, part_1, input_output_aliases={2: 0}),
        without_ghosts(2, "span_2", None, vel, top),
    ]
    for n, bit in enumerate(bits[1:]):
        top = call(
            merged,
            "merged",
            0,
            out_shape=tile,
            in_specs=[vmem] * 5,
            out_specs=vmem,
        )(top, far, *parts[-3:])
        far = exchanged(top, "az", bit)
        if n == 0:
            parts.append(with_ghosts(3, top))
    tile_even, tile_odd, vel = call(
        theta_in,
        "theta_in",
        0,
        out_shape=(tile, tile, padded),
        in_specs=[vmem] * 4,
        out_specs=(vmem,) * 3,
        input_output_aliases={2: 2},
    )(theta_even, theta_odd, vel, parts[-1])
    corner_even, corner_odd = across_even(tile_even, "ax"), across_odd(tile_odd, "ax")
    parts.append(with_ghosts(4, tile_even))
    increment, time_step, _ = call(
        functools.partial(finish, spans),
        "finish",
        0,
        scratch=8,
        out_shape=(shape(*velocity.shape), shape(1), padded),
        in_specs=[vmem] * (7 + len(parts)),
        out_specs=(anywhere, smem, vmem),
        scratch_shapes=[
            pltpu.VMEM(velocity.shape, f32),
            pltpu.SemaphoreType.DMA(((planes - 2 * HALO) // BLOCK + 2,)),
        ],
        input_output_aliases={0: 2},
    )(vel, inner, coef, top, far, corner_even, corner_odd, *parts)
    return increment, time_step.reshape(())


def solution(mesh):
    return jax.shard_map(
        per_device,
        mesh=mesh,
        in_specs=(P(None, "az", "ax", None),),
        out_specs=(P(None, "az", "ax", None), P()),
        check_vma=False,
    )
```

```python
import functools
import math

import jax
import jax.numpy as jnp
import numpy as np
from jax import lax
from jax.experimental import pallas as pl
from jax.experimental.pallas import tpu as pltpu
from jax.sharding import PartitionSpec as P

AXIAL_STEP = 0.01
VISCOSITY = 0.001
CFL_TARGET = 1.2
GAMMA = 8.0 / 15.0

PAD = 8
HALO = 2
BLOCK = 4
GROUP = 4
UNROLL = 4

(
    WALL,
    RADIAL_C,
    THETA_C,
    CROSS_Z,
    SECOND_C,
    CENTRE_Z,
    CENTRE_T,
    CURVE_T,
    TURN_T,
    RADIAL_F,
    THETA_F,
    SECOND_F,
    CENTRE_R,
    CURVE_R,
    TURN_R,
    COUNT,
) = range(16)


UNIT = VISCOSITY / (12.0 * AXIAL_STEP**2)


def coefficients(radial, theta_step):
    dr = 1.0 / radial
    index = np.arange(radial, dtype=np.float64)
    centre = (index + 0.5) * dr
    face = (index + 1.0) * dr
    wall = np.where(index < radial - 1.5, 1.0, 0.0)
    h = theta_step
    nu = VISCOSITY
    rows = np.zeros((COUNT, radial))
    rows[WALL] = wall
    common = -2.0 * nu / dr**2 - 30.0 * nu / (12.0 * AXIAL_STEP**2)
    rows[RADIAL_C] = nu / (2.0 * dr * centre)
    rows[THETA_C] = -1.0 / (12.0 * h * centre)
    rows[CROSS_Z] = 0.25 * rows[THETA_C]
    rows[SECOND_C] = nu / (12.0 * h * h * centre**2)
    rows[CENTRE_Z] = common - 30.0 * rows[SECOND_C]
    rows[CENTRE_T] = rows[CENTRE_Z] - nu / centre**2
    rows[CURVE_T] = 0.25 / centre
    rows[TURN_T] = nu / (h * centre**2)
    rows[RADIAL_F] = nu / (2.0 * dr * face)
    rows[THETA_F] = -0.25 / (12.0 * h * face)
    rows[SECOND_F] = nu / (12.0 * h * h * face**2)
    rows[CENTRE_R] = common - 30.0 * rows[SECOND_F] - nu / face**2
    rows[CURVE_R] = 1.0 / (16.0 * face)
    rows[TURN_R] = -nu / (h * face**2)
    rows[RADIAL_C:] /= UNIT
    return np.broadcast_to(rows[:, None, :], (COUNT, 8, radial)).astype(np.float32)


class Cells:
    def __init__(self, vel, j, k):
        self.vel, self.j, self.k, self.known = vel, j, k, {}

    def once(self, key, make):
        if key not in self.known:
            self.known[key] = make()
        return self.known[key]

    def at(self, n, dj, dk=0):
        rows = pl.ds(self.k + PAD + dk, 8)
        return self.once((n, dj, dk), lambda: self.vel[n, self.j + HALO + dj, rows, :])

    def turned(self, by, n, dj, dk=0):
        return self.once(
            (by, n, dj, dk), lambda: pltpu.roll(self.at(n, dj, dk), by % self.vel.shape[3], 1)
        )

    def pair(self, by, n, dj, dk=0):
        return self.once(
            ("pair", n, dj, dk), lambda: self.at(n, dj, dk) + self.turned(by, n, dj, dk)
        )

    def beside(self, dj, dk):
        n = 1 if dk >= 0 else 2
        other = (1, dj - 1, dk) if n == 1 else (2, dj, dk)
        here = (1, dj, dk) if n == 1 else (2, dj, dk + 1)
        return self.once(("sum", n, dj, dk), lambda: self.at(*other) + self.at(*here))


def terms(cells, ghost, coef, q, dr):
    at, turned, pair = cells.at, cells.turned, cells.pair
    a, b, c = (at(n, q) for n in range(3))
    lane = lax.broadcasted_iota(jnp.int32, a.shape, 1)
    first_lane = lane == 0
    last_lane = lane == a.shape[1] - 1

    lap = VISCOSITY / dr**2 / UNIT
    adv_z = -1.0 / (12.0 * AXIAL_STEP) / UNIT
    by_dr = 1.0 / dr / UNIT

    def differences(p1, m1, p2, m2):
        return 8.0 * (p1 - m1) - (p2 - m2), 16.0 * (p1 + m1) - (p2 + m2)

    def pieces(n):
        over = differences(*(at(n, q + d) for d in (1, -1, 2, -2)))
        along = differences(*(at(n, q, d) for d in (1, -1, 2, -2)))
        return over, along

    def below(n):
        if ghost is not None and n > 0 and q % 2 == 0:
            x = jnp.where(last_lane, ghost(n, q + 1), at(n, q))
            return pltpu.roll(x, 1, 1)
        x = turned(1, n, q)
        if ghost is not None:
            return jnp.where(first_lane, ghost(n, q), x)
        return x if n == 0 else jnp.where(first_lane, 0.0, x)

    def above(n):
        return jnp.where(last_lane, -at(n, q), turned(-1, n, q))

    pair_a, pair_side, pair_next = pair(1, 0, q), pair(1, 0, q + 1), pair(1, 0, q, 1)
    pair_b, pair_back = pair(-1, 1, q), pair(-1, 1, q - 1)

    theta, axial = pieces(2)
    up, low = above(2), below(2)
    u_r = pair_a + pair_next
    u_t = cells.beside(q, 0) + cells.beside(q, 1)
    h_z = (up - low) * (coef[RADIAL_C] - u_r * (0.125 * by_dr)) + (up + low) * lap
    h_z = h_z + theta[0] * (u_t * coef[CROSS_Z])
    h_z = h_z + (theta[1] * coef[SECOND_C] + axial[1])
    h_z = h_z + c * (coef[CENTRE_Z] + axial[0] * adv_z)

    theta, axial = pieces(1)
    up, low = above(1), below(1)
    u_r = pair_a + pair_side
    u_z = cells.beside(q, -1) + cells.beside(q + 1, -1)
    h_t = (up - low) * (coef[RADIAL_C] - u_r * (0.125 * by_dr)) + (up + low) * lap
    h_t = h_t + b * (coef[CENTRE_T] + theta[0] * coef[THETA_C] - u_r * coef[CURVE_T])
    h_t = h_t + (theta[1] * coef[SECOND_C] + axial[1])
    h_t = h_t + axial[0] * (u_z * (0.25 * adv_z))
    h_t = h_t + (pair_side - pair_a) * coef[TURN_T]

    theta, axial = pieces(0)
    up, low = turned(-1, 0, q), below(0)
    u_t = pair_b + pair_back
    u_z = pair(-1, 2, q) + pair(-1, 2, q, -1)
    h_r = (up - low) * (coef[RADIAL_F] - a * (0.5 * by_dr)) + (up + low) * lap
    h_r = h_r + u_t * (u_t * coef[CURVE_R] + theta[0] * coef[THETA_F])
    h_r = h_r + (theta[1] * coef[SECOND_F] + axial[1])
    h_r = h_r + (axial[0] * (u_z * (0.25 * adv_z)) + a * coef[CENTRE_R])
    h_r = h_r + (pair_b - pair_back) * coef[TURN_R]
    return h_r, h_t, h_z


def lane_zero_terms(cells, ghost, coef, q, dr):
    lap = VISCOSITY / dr**2 / UNIT
    by_dr = 1.0 / dr / UNIT
    a = cells.at(0, q)
    first_lane = lax.broadcasted_iota(jnp.int32, a.shape, 1) == 0
    add_r = ghost(0, q) * (lap - coef[RADIAL_F] + a * (0.5 * by_dr))
    add_t = ghost(1, q) * (lap - coef[RADIAL_C] + (a + cells.at(0, q + 1)) * (0.125 * by_dr))
    add_z = ghost(2, q) * (lap - coef[RADIAL_C] + (a + cells.at(0, q, 1)) * (0.125 * by_dr))
    return tuple(jnp.where(first_lane, x, 0.0) for x in (add_r, add_t, add_z))


def wall_mask(rows, radial):
    lane = lax.broadcasted_iota(jnp.int32, (rows, radial), 1)
    return jnp.where(lane == radial - 1, 0.0, 1.0).astype(jnp.float32)


def first_pass(theta_step, v_ref, vel_ref, even_ref, odd_ref, inner_ref, pay_ref, sems):
    _, planes, axial, radial = v_ref.shape
    lane = lax.broadcasted_iota(jnp.int32, (8, radial), 1)
    wall = wall_mask(8, radial)
    rate_t = (radial / theta_step) / (lane.astype(jnp.float32) + 0.5)
    odd = lax.rem(lax.axis_index("ax"), 2) == 1

    def fetch(g):
        part = pl.ds(g * GROUP, GROUP)
        target = vel_ref.at[:, pl.ds(g * GROUP + HALO, GROUP), pl.ds(PAD, axial)]
        return pltpu.make_async_copy(v_ref.at[:, part], target, sems.at[g])

    for g in range(planes // GROUP):
        fetch(g).start()

    zero = jnp.zeros((8, radial), jnp.float32)
    largest = [zero] * 4
    for g in range(planes // GROUP):
        fetch(g).wait()
        for i in range(axial // 8):
            k = pl.ds(8 * i, 8)
            padded = pl.ds(8 * i + PAD, 8)
            inner = zero if g == 0 else inner_ref[k, :]
            for q in range(GROUP):
                j = g * GROUP + q
                cells = [vel_ref[n, j + HALO, padded, :] for n in range(3)]
                for n, x in enumerate(cells):
                    place = n * planes + j
                    x = pltpu.roll(x, place, 1) if place else x
                    inner = jnp.where(lane == place, x if n == 2 else -x, inner)
                a, b, c = cells
                a = a * wall
                vel_ref[0, j + HALO, padded, :] = a
                rate = jnp.abs(a) * float(radial) + jnp.abs(b) * rate_t
                rate = rate + jnp.abs(c) * (1.0 / AXIAL_STEP)
                largest[q % 4] = jnp.maximum(largest[q % 4], rate)
            inner_ref[k, :] = inner
        for q in range(GROUP):
            for n in range(3):
                j = g * GROUP + q
                first = vel_ref[n, j + HALO, PAD : PAD + 2, :]
                last = vel_ref[n, j + HALO, PAD + axial - 2 : PAD + axial, :]
                even_ref[n, j] = jnp.where(odd, first, last)
                odd_ref[n, j] = jnp.where(odd, last, first)

    largest = jnp.maximum(
        jnp.maximum(largest[0], largest[1]), jnp.maximum(largest[2], largest[3])
    )
    top = jnp.max(largest, axis=(0, 1), keepdims=True)
    pay_ref[...] = jnp.broadcast_to(top, pay_ref.shape)
    end = lax.broadcasted_iota(jnp.int32, (2, radial), 1) == radial - 1
    for ref in (even_ref, odd_ref):
        ref[0, 0] = jnp.where(end, top, ref[0, 0])


def carried(even_ref, pay_ref, odd_in, _, odd_ref):
    radial = even_ref.shape[3]
    lane = lax.broadcasted_iota(jnp.int32, (2, radial), 1)
    top = jnp.maximum(even_ref[0, 0], pay_ref[0:2, :])
    odd_ref[0, 0] = jnp.where(lane == radial - 1, top, odd_in[0, 0])


def fold(even_ref, odd_ref, pay_ref, vel_in, _, *refs):
    del vel_in
    top_ref, vel_ref = refs
    planes, radial = even_ref.shape[1], even_ref.shape[3]
    axial = vel_ref.shape[2] - 2 * PAD
    lane = lax.broadcasted_iota(jnp.int32, (1, radial), 1)
    top = jnp.maximum(even_ref[0, 0, 0:1, :], odd_ref[0, 0, 0:1, :])
    top = jnp.max(jnp.where(lane == radial - 1, top, 0.0), axis=(0, 1), keepdims=True)
    top_ref[...] = jnp.maximum(pay_ref[...], top)
    wall = wall_mask(2, radial)
    odd = lax.rem(lax.axis_index("ax"), 2) == 1

    def plane(j, carry):
        for n in range(3):
            mask = wall if n == 0 else 1.0
            even, other = even_ref[n, j] * mask, odd_ref[n, j] * mask
            low, high = jnp.where(odd, even, other), jnp.where(odd, other, even)
            vel_ref[n, j + HALO, PAD - 2 : PAD, :] = low
            vel_ref[n, j + HALO, PAD + axial : PAD + axial + 2, :] = high
        return carry

    lax.fori_loop(0, planes, plane, 0, unroll=4)


def merged(mine_ref, far_ref, *refs):
    refs[-1][...] = jnp.maximum(mine_ref[...], far_ref[...])


def theta_in(even_ref, odd_ref, vel_in, _, even_tile, odd_tile, vel_ref):
    del vel_in
    planes, axial = vel_ref.shape[1] - 2 * HALO, vel_ref.shape[2] - 2 * PAD
    cells = pl.ds(PAD, axial)
    wall = wall_mask(1, vel_ref.shape[3])
    odd = lax.rem(lax.axis_index("az"), 2)
    below, above = 0, HALO + planes
    for ref, place in (
        (even_ref, jnp.where(odd == 1, below, above)),
        (odd_ref, jnp.where(odd == 1, above, below)),
    ):
        for q in range(HALO):
            vel_ref[0, place + q, cells, :] = ref[0, q] * wall
            vel_ref[1, place + q, cells, :] = ref[1, q]
            vel_ref[2, place + q, cells, :] = ref[2, q]
    first = vel_ref[1, below + HALO - 1, PAD : PAD + 1, :]
    last = vel_ref[2, above, PAD + axial - 1 : PAD + axial, :]
    odd = lax.rem(lax.axis_index("ax"), 2) == 1
    shape = even_tile.shape
    even_tile[...] = jnp.broadcast_to(jnp.where(odd, first, last), shape)
    odd_tile[...] = jnp.broadcast_to(jnp.where(odd, last, first), shape)


def ghosts(cells, inner, planes):
    radial = inner.shape[1]

    def ghost(n, q):
        turn = -(n * planes + q + cells.j) % radial
        return cells.once(("ghost", n, q), lambda: pltpu.roll(inner, turn, 1) if turn else inner)

    return ghost


def block_terms(vel_ref, inner_ref, coef_ref, j, size, write, rounds=None):
    planes = vel_ref.shape[1] - 2 * HALO
    axial, radial = vel_ref.shape[2] - 2 * PAD, vel_ref.shape[3]
    groups = (4 if inner_ref is None else 2) * BLOCK // size
    times, places = rounds or (
        axial // (8 * groups),
        lambda i: [(i * groups + u) * 8 for u in range(groups)],
    )

    def rows(i, carry):
        coef = [coef_ref[n] for n in range(COUNT)]
        found = []
        for k in places(i):
            k = pl.multiple_of(k, 8)
            cells = Cells(vel_ref, j, k)
            ghost = None
            if inner_ref is not None:
                ghost = ghosts(cells, inner_ref[pl.ds(k, 8), :], planes)
            for q in range(size):
                found.append((q, k, terms(cells, ghost, coef, q, 1.0 / radial)))
        for q, k, values in found:
            for n, value in enumerate(values):
                write(n, j + q, pl.ds(k, 8), value)
        return carry

    lax.fori_loop(0, times, rows, 0)


def ahead(first, last, rounds, vel_ref, coef_ref, *refs):
    out_ref = refs[-1]

    def write(n, j, k, value):
        out_ref[n, j - first, k, :] = value

    def block(m, carry):
        block_terms(vel_ref, None, coef_ref, first + m * BLOCK, BLOCK, write, rounds)
        return carry

    lax.fori_loop(0, (last - first) // BLOCK, block, 0)


def ahead_with_ghosts(first, last, vel_ref, inner_ref, coef_ref, _, out_ref):
    def write(n, j, k, value):
        out_ref[n, j - first, k, :] = value

    for j in range(first, last, BLOCK):
        block_terms(vel_ref, inner_ref, coef_ref, j, BLOCK, write)


def finish(spans, vel_in, inner_ref, coef_ref, top, far, even, odd, *refs):
    parts, refs = refs[: len(spans)], refs[len(spans) :]
    del vel_in
    out_ref, step_ref, vel_ref, res, sems = refs
    axial, radial = inner_ref.shape
    planes = vel_ref.shape[1] - 2 * HALO
    largest = jnp.maximum(top[0:1, :], far[0:1, :])
    time_step = CFL_TARGET / (jnp.max(largest) + 1e-06)
    step_ref[0] = time_step
    scale = GAMMA * UNIT * time_step
    factors = (scale * coef_ref[WALL], scale, scale)
    pending = []

    def send(j, size):
        part_of = pl.ds(j, size)
        copy = pltpu.make_async_copy(
            res.at[:, part_of], out_ref.at[:, part_of], sems.at[len(pending)]
        )
        copy.start()
        pending.append(copy)

    def write(n, j, k, value):
        res[n, j, k, :] = value * factors[n]

    def complete(part, j, place, add):
        groups = 4

        def rows(i, carry):
            found = []
            for u in range(groups):
                k = pl.multiple_of((i * groups + u) * 8, 8)
                cells = Cells(vel_ref, j, k)
                ghost = ghosts(cells, inner_ref[pl.ds(k, 8), :], planes) if add else None
                for q in range(BLOCK):
                    values = [part[n, place + q, pl.ds(k, 8), :] for n in range(3)]
                    if add:
                        added = lane_zero_terms(cells, ghost, coef_ref, q, 1.0 / radial)
                        values = [x + y for x, y in zip(values, added)]
                    found.append((q, k, values))
            for q, k, values in found:
                for n, value in enumerate(values):
                    write(n, j + q, pl.ds(k, 8), value)
            return carry

        lax.fori_loop(0, axial // (8 * groups), rows, 0)
        send(j, BLOCK)

    for n, (part, (first, last)) in enumerate(zip(parts, spans)):
        for j in range(first, last, BLOCK):
            complete(part, j, j - first, n < 3)

    second = lax.rem(lax.axis_index("ax"), 2) == 1
    even, odd = even[0:1, :], odd[0:1, :]
    following, preceding = jnp.where(second, odd, even), jnp.where(second, even, odd)
    vel_ref[1, HALO - 1, PAD + axial : PAD + axial + 1, :] = following
    vel_ref[2, HALO + planes, PAD - 1 : PAD, :] = preceding
    for j in (0, planes - HALO):
        block_terms(vel_ref, inner_ref, coef_ref, j, HALO, write)
        send(j, HALO)
    for copy in pending:
        copy.wait()


def routed(block, axis, source):
    count = lax.axis_size(axis)
    return lax.ppermute(block, axis, [(source(i), i) for i in range(count)])


def exchanged(block, axis, step):
    return routed(block, axis, lambda i: i ^ step)


def across_even(block, axis):
    return exchanged(block, axis, 1)


def across_odd(block, axis):
    count = lax.axis_size(axis)
    return routed(block, axis, lambda i: (i + (1 if i % 2 else -1)) % count)


def cuts(planes):
    last = planes - HALO
    ends = (HALO, HALO + BLOCK, last - 5 * BLOCK, last - 3 * BLOCK, last - BLOCK, last)
    return list(zip(ends[:-1], ends[1:]))


def per_device(velocity):
    _, planes, axial, radial = velocity.shape
    sizes = lax.axis_size("az"), lax.axis_size("ax")
    theta_step = 2.0 * math.pi / (sizes[0] * planes)
    coef = jnp.asarray(coefficients(radial, theta_step))
    f32 = jnp.float32
    anywhere = pl.BlockSpec(memory_space=pl.ANY)
    vmem = pl.BlockSpec(memory_space=pltpu.VMEM)
    smem = pl.BlockSpec(memory_space=pltpu.SMEM)

    def shape(*sizes):
        return jax.ShapeDtypeStruct(sizes, f32)

    def call(kernel, name, work, scratch=0, **kwargs):
        return pl.pallas_call(
            kernel,
            name=name,
            compiler_params=pltpu.CompilerParams(vmem_limit_bytes=(4 + scratch) * 2**20),
            cost_estimate=pl.CostEstimate(flops=work, bytes_accessed=work, transcendentals=0),
            **kwargs,
        )

    odd = lax.axis_index("az") % 2
    ends = (planes - HALO, 0)
    even_end = jnp.where(odd == 1, ends[1], ends[0])
    odd_end = jnp.where(odd == 1, ends[0], ends[1])
    theta_odd = across_odd(lax.dynamic_slice_in_dim(velocity, odd_end, HALO, 1), "az")
    theta_even = across_even(lax.dynamic_slice_in_dim(velocity, even_end, HALO, 1), "az")

    edge = shape(3, planes, 2, radial)
    padded = shape(3, planes + 2 * HALO, axial + 2 * PAD, radial)
    row = shape(axial, radial)
    tile = shape(8, radial)
    vel, edge_even, edge_odd, mine, pay = call(
        functools.partial(first_pass, theta_step),
        "first_pass",
        0,
        out_shape=(padded, edge, edge, row, tile),
        in_specs=[anywhere],
        out_specs=(vmem,) * 5,
        scratch_shapes=[pltpu.SemaphoreType.DMA((planes // GROUP,))],
    )(pltpu.with_memory_space_constraint(velocity, pltpu.HBM))
    inner = exchanged(mine, "az", sizes[0] // 2)
    z_even = across_even(edge_even, "ax")
    spans = cuts(planes)

    def part_shape(n):
        return shape(3, spans[n][1] - spans[n][0], axial, radial)

    def without_ghosts(n, name, rounds, vel, *tokens, **kwargs):
        return call(
            functools.partial(ahead, *spans[n], rounds),
            name,
            velocity.size * 2,
            out_shape=part_shape(n),
            in_specs=[vmem] * (2 + len(tokens)),
            out_specs=vmem,
            **kwargs,
        )(vel, coef, *tokens)

    def with_ghosts(n, token):
        return call(
            functools.partial(ahead_with_ghosts, *spans[n]),
            f"span_{n}",
            velocity.size * 2,
            out_shape=part_shape(n),
            in_specs=[vmem] * 4,
            out_specs=vmem,
        )(vel, inner, coef, token)

    middle = (axial - 16) // 16, lambda i: [16 * i + 8, 16 * i + 16]
    outer = 1, lambda i: [i * 8, i * 8 + axial - 8]
    part_0 = without_ghosts(0, "span_0_middle", middle, vel, pay)
    edge_odd = call(
        carried,
        "carried",
        0,
        out_shape=edge,
        in_specs=[vmem] * 4,
        out_specs=vmem,
        input_output_aliases={2: 0},
    )(z_even, pay, edge_odd, part_0)
    z_odd = across_odd(edge_odd, "ax")

    part_1 = without_ghosts(1, "span_1_middle", middle, vel, edge_odd)
    top, vel = call(
        fold,
        "fold",
        0,
        out_shape=(tile, padded),
        in_specs=[vmem] * 5,
        out_specs=(vmem,) * 2,
        input_output_aliases={3: 1},
    )(z_even, z_odd, pay, vel, part_1)
    for step in (1 << n for n in range(2, sizes[1].bit_length() - 1)):
        top = jnp.maximum(top, routed(top, "ax", lambda i, step=step: (i + step) % sizes[1]))

    bits = [1 << n for n in range(1, sizes[0].bit_length() - 1)] + [1]
    far = exchanged(top, "az", bits[0])
    parts = [
        without_ghosts(0, "span_0_outer", outer, vel, part_0, input_output_aliases={2: 0}),
        without_ghosts(1, "span_1_outer", outer, vel, part_1, input_output_aliases={2: 0}),
        without_ghosts(2, "span_2", None, vel, top),
    ]
    for n, bit in enumerate(bits[1:]):
        top = call(
            merged,
            "merged",
            0,
            out_shape=tile,
            in_specs=[vmem] * 5,
            out_specs=vmem,
        )(top, far, *parts[-3:])
        far = exchanged(top, "az", bit)
        if n == 0:
            parts.append(with_ghosts(3, top))
    tile_even, tile_odd, vel = call(
        theta_in,
        "theta_in",
        0,
        out_shape=(tile, tile, padded),
        in_specs=[vmem] * 4,
        out_specs=(vmem,) * 3,
        input_output_aliases={2: 2},
    )(theta_even, theta_odd, vel, parts[-1])
    corner_even, corner_odd = across_even(tile_even, "ax"), across_odd(tile_odd, "ax")
    parts.append(with_ghosts(4, tile_even))
    increment, time_step, _ = call(
        functools.partial(finish, spans),
        "finish",
        0,
        scratch=8,
        out_shape=(shape(*velocity.shape), shape(1), padded),
        in_specs=[vmem] * (7 + len(parts)),
        out_specs=(anywhere, smem, vmem),
        scratch_shapes=[
            pltpu.VMEM(velocity.shape, f32),
            pltpu.SemaphoreType.DMA(((planes - 2 * HALO) // BLOCK + 2,)),
        ],
        input_output_aliases={0: 2},
    )(vel, inner, coef, top, far, corner_even, corner_odd, *parts)
    return increment, time_step.reshape(())


def solution(mesh):
    return jax.shard_map(
        per_device,
        mesh=mesh,
        in_specs=(P(None, "az", "ax", None),),
        out_specs=(P(None, "az", "ax", None), P()),
        check_vma=False,
    )
```

```python
import functools
import math

import jax
import jax.numpy as jnp
import numpy as np
from jax import lax
from jax.experimental import pallas as pl
from jax.experimental.pallas import tpu as pltpu
from jax.sharding import PartitionSpec as P

AXIAL_STEP = 0.01
VISCOSITY = 0.001
CFL_TARGET = 1.2
GAMMA = 8.0 / 15.0

PAD = 8
HALO = 2
BLOCK = 4
GROUP = 4
UNROLL = 4

(
    WALL,
    RADIAL_C,
    THETA_C,
    CROSS_Z,
    SECOND_C,
    CENTRE_Z,
    CENTRE_T,
    CURVE_T,
    TURN_T,
    RADIAL_F,
    THETA_F,
    SECOND_F,
    CENTRE_R,
    CURVE_R,
    TURN_R,
    COUNT,
) = range(16)


UNIT = VISCOSITY / (12.0 * AXIAL_STEP**2)


def coefficients(radial, theta_step):
    dr = 1.0 / radial
    index = np.arange(radial, dtype=np.float64)
    centre = (index + 0.5) * dr
    face = (index + 1.0) * dr
    wall = np.where(index < radial - 1.5, 1.0, 0.0)
    h = theta_step
    nu = VISCOSITY
    rows = np.zeros((COUNT, radial))
    rows[WALL] = wall
    common = -2.0 * nu / dr**2 - 30.0 * nu / (12.0 * AXIAL_STEP**2)
    rows[RADIAL_C] = nu / (2.0 * dr * centre)
    rows[THETA_C] = -1.0 / (12.0 * h * centre)
    rows[CROSS_Z] = 0.25 * rows[THETA_C]
    rows[SECOND_C] = nu / (12.0 * h * h * centre**2)
    rows[CENTRE_Z] = common - 30.0 * rows[SECOND_C]
    rows[CENTRE_T] = rows[CENTRE_Z] - nu / centre**2
    rows[CURVE_T] = 0.25 / centre
    rows[TURN_T] = nu / (h * centre**2)
    rows[RADIAL_F] = nu / (2.0 * dr * face)
    rows[THETA_F] = -0.25 / (12.0 * h * face)
    rows[SECOND_F] = nu / (12.0 * h * h * face**2)
    rows[CENTRE_R] = common - 30.0 * rows[SECOND_F] - nu / face**2
    rows[CURVE_R] = 1.0 / (16.0 * face)
    rows[TURN_R] = -nu / (h * face**2)
    rows[RADIAL_C:] /= UNIT
    return np.broadcast_to(rows[:, None, :], (COUNT, 8, radial)).astype(np.float32)


class Cells:
    def __init__(self, vel, j, k):
        self.vel, self.j, self.k, self.known = vel, j, k, {}

    def once(self, key, make):
        if key not in self.known:
            self.known[key] = make()
        return self.known[key]

    def at(self, n, dj, dk=0):
        rows = pl.ds(self.k + PAD + dk, 8)
        return self.once((n, dj, dk), lambda: self.vel[n, self.j + HALO + dj, rows, :])

    def turned(self, by, n, dj, dk=0):
        return self.once(
            (by, n, dj, dk), lambda: pltpu.roll(self.at(n, dj, dk), by % self.vel.shape[3], 1)
        )

    def pair(self, by, n, dj, dk=0):
        return self.once(
            ("pair", n, dj, dk), lambda: self.at(n, dj, dk) + self.turned(by, n, dj, dk)
        )

    def beside(self, dj, dk):
        n = 1 if dk >= 0 else 2
        other = (1, dj - 1, dk) if n == 1 else (2, dj, dk)
        here = (1, dj, dk) if n == 1 else (2, dj, dk + 1)
        return self.once(("sum", n, dj, dk), lambda: self.at(*other) + self.at(*here))


def terms(cells, ghost, coef, q, dr):
    at, turned, pair = cells.at, cells.turned, cells.pair
    a, b, c = (at(n, q) for n in range(3))
    lane = lax.broadcasted_iota(jnp.int32, a.shape, 1)
    first_lane = lane == 0
    last_lane = lane == a.shape[1] - 1

    lap = VISCOSITY / dr**2 / UNIT
    adv_z = -1.0 / (12.0 * AXIAL_STEP) / UNIT
    by_dr = 1.0 / dr / UNIT

    def differences(p1, m1, p2, m2):
        return 8.0 * (p1 - m1) - (p2 - m2), 16.0 * (p1 + m1) - (p2 + m2)

    def pieces(n):
        over = differences(*(at(n, q + d) for d in (1, -1, 2, -2)))
        along = differences(*(at(n, q, d) for d in (1, -1, 2, -2)))
        return over, along

    def below(n):
        if ghost is not None and n > 0 and q % 2 == 0:
            x = jnp.where(last_lane, ghost(n, q + 1), at(n, q))
            return pltpu.roll(x, 1, 1)
        x = turned(1, n, q)
        if ghost is not None:
            return jnp.where(first_lane, ghost(n, q), x)
        return x if n == 0 else jnp.where(first_lane, 0.0, x)

    def above(n):
        return jnp.where(last_lane, -at(n, q), turned(-1, n, q))

    pair_a, pair_side, pair_next = pair(1, 0, q), pair(1, 0, q + 1), pair(1, 0, q, 1)
    pair_b, pair_back = pair(-1, 1, q), pair(-1, 1, q - 1)

    theta, axial = pieces(2)
    up, low = above(2), below(2)
    u_r = pair_a + pair_next
    u_t = cells.beside(q, 0) + cells.beside(q, 1)
    h_z = (up - low) * (coef[RADIAL_C] - u_r * (0.125 * by_dr)) + (up + low) * lap
    h_z = h_z + theta[0] * (u_t * coef[CROSS_Z])
    h_z = h_z + (theta[1] * coef[SECOND_C] + axial[1])
    h_z = h_z + c * (coef[CENTRE_Z] + axial[0] * adv_z)

    theta, axial = pieces(1)
    up, low = above(1), below(1)
    u_r = pair_a + pair_side
    u_z = cells.beside(q, -1) + cells.beside(q + 1, -1)
    h_t = (up - low) * (coef[RADIAL_C] - u_r * (0.125 * by_dr)) + (up + low) * lap
    h_t = h_t + b * (coef[CENTRE_T] + theta[0] * coef[THETA_C] - u_r * coef[CURVE_T])
    h_t = h_t + (theta[1] * coef[SECOND_C] + axial[1])
    h_t = h_t + axial[0] * (u_z * (0.25 * adv_z))
    h_t = h_t + (pair_side - pair_a) * coef[TURN_T]

    theta, axial = pieces(0)
    up, low = turned(-1, 0, q), below(0)
    u_t = pair_b + pair_back
    u_z = pair(-1, 2, q) + pair(-1, 2, q, -1)
    h_r = (up - low) * (coef[RADIAL_F] - a * (0.5 * by_dr)) + (up + low) * lap
    h_r = h_r + u_t * (u_t * coef[CURVE_R] + theta[0] * coef[THETA_F])
    h_r = h_r + (theta[1] * coef[SECOND_F] + axial[1])
    h_r = h_r + (axial[0] * (u_z * (0.25 * adv_z)) + a * coef[CENTRE_R])
    h_r = h_r + (pair_b - pair_back) * coef[TURN_R]
    return h_r, h_t, h_z


def lane_zero_terms(cells, ghost, coef, q, dr):
    lap = VISCOSITY / dr**2 / UNIT
    by_dr = 1.0 / dr / UNIT
    a = cells.at(0, q)
    first_lane = lax.broadcasted_iota(jnp.int32, a.shape, 1) == 0
    add_r = ghost(0, q) * (lap - coef[RADIAL_F] + a * (0.5 * by_dr))
    add_t = ghost(1, q) * (lap - coef[RADIAL_C] + (a + cells.at(0, q + 1)) * (0.125 * by_dr))
    add_z = ghost(2, q) * (lap - coef[RADIAL_C] + (a + cells.at(0, q, 1)) * (0.125 * by_dr))
    return tuple(jnp.where(first_lane, x, 0.0) for x in (add_r, add_t, add_z))


def wall_mask(rows, radial):
    lane = lax.broadcasted_iota(jnp.int32, (rows, radial), 1)
    return jnp.where(lane == radial - 1, 0.0, 1.0).astype(jnp.float32)


def first_pass(theta_step, v_ref, vel_ref, even_ref, odd_ref, inner_ref, pay_ref, sems):
    _, planes, axial, radial = v_ref.shape
    lane = lax.broadcasted_iota(jnp.int32, (8, radial), 1)
    wall = wall_mask(8, radial)
    rate_t = (radial / theta_step) / (lane.astype(jnp.float32) + 0.5)
    odd = lax.rem(lax.axis_index("ax"), 2) == 1

    def fetch(g):
        part = pl.ds(g * GROUP, GROUP)
        target = vel_ref.at[:, pl.ds(g * GROUP + HALO, GROUP), pl.ds(PAD, axial)]
        return pltpu.make_async_copy(v_ref.at[:, part], target, sems.at[g])

    for g in range(planes // GROUP):
        fetch(g).start()

    zero = jnp.zeros((8, radial), jnp.float32)
    largest = [zero] * 4
    for g in range(planes // GROUP):
        fetch(g).wait()
        for i in range(axial // 8):
            k = pl.ds(8 * i, 8)
            padded = pl.ds(8 * i + PAD, 8)
            inner = zero if g == 0 else inner_ref[k, :]
            for q in range(GROUP):
                j = g * GROUP + q
                cells = [vel_ref[n, j + HALO, padded, :] for n in range(3)]
                for n, x in enumerate(cells):
                    place = n * planes + j
                    x = pltpu.roll(x, place, 1) if place else x
                    inner = jnp.where(lane == place, x if n == 2 else -x, inner)
                a, b, c = cells
                a = a * wall
                vel_ref[0, j + HALO, padded, :] = a
                rate = jnp.abs(a) * float(radial) + jnp.abs(b) * rate_t
                rate = rate + jnp.abs(c) * (1.0 / AXIAL_STEP)
                largest[q % 4] = jnp.maximum(largest[q % 4], rate)
            inner_ref[k, :] = inner
        for q in range(GROUP):
            for n in range(3):
                j = g * GROUP + q
                first = vel_ref[n, j + HALO, PAD : PAD + 2, :]
                last = vel_ref[n, j + HALO, PAD + axial - 2 : PAD + axial, :]
                even_ref[n, j] = jnp.where(odd, first, last)
                odd_ref[n, j] = jnp.where(odd, last, first)

    largest = jnp.maximum(
        jnp.maximum(largest[0], largest[1]), jnp.maximum(largest[2], largest[3])
    )
    top = jnp.max(largest, axis=(0, 1), keepdims=True)
    pay_ref[...] = jnp.broadcast_to(top, pay_ref.shape)
    end = lax.broadcasted_iota(jnp.int32, (2, radial), 1) == radial - 1
    for ref in (even_ref, odd_ref):
        ref[0, 0] = jnp.where(end, top, ref[0, 0])


def carried(even_ref, pay_ref, odd_in, _, odd_ref):
    radial = even_ref.shape[3]
    lane = lax.broadcasted_iota(jnp.int32, (2, radial), 1)
    top = jnp.maximum(even_ref[0, 0], pay_ref[0:2, :])
    odd_ref[0, 0] = jnp.where(lane == radial - 1, top, odd_in[0, 0])


def fold(even_ref, odd_ref, pay_ref, vel_in, _, *refs):
    del vel_in
    top_ref, vel_ref = refs
    planes, radial = even_ref.shape[1], even_ref.shape[3]
    axial = vel_ref.shape[2] - 2 * PAD
    lane = lax.broadcasted_iota(jnp.int32, (1, radial), 1)
    top = jnp.maximum(even_ref[0, 0, 0:1, :], odd_ref[0, 0, 0:1, :])
    top = jnp.max(jnp.where(lane == radial - 1, top, 0.0), axis=(0, 1), keepdims=True)
    top_ref[...] = jnp.maximum(pay_ref[...], top)
    wall = wall_mask(2, radial)
    odd = lax.rem(lax.axis_index("ax"), 2) == 1

    def plane(j, carry):
        for n in range(3):
            mask = wall if n == 0 else 1.0
            even, other = even_ref[n, j] * mask, odd_ref[n, j] * mask
            low, high = jnp.where(odd, even, other), jnp.where(odd, other, even)
            vel_ref[n, j + HALO, PAD - 2 : PAD, :] = low
            vel_ref[n, j + HALO, PAD + axial : PAD + axial + 2, :] = high
        return carry

    lax.fori_loop(0, planes, plane, 0, unroll=4)


def merged(mine_ref, far_ref, *refs):
    refs[-1][...] = jnp.maximum(mine_ref[...], far_ref[...])


def theta_in(odd_ref, even_ref, vel_in, _, even_tile, odd_tile, vel_ref):
    del vel_in
    planes, axial = vel_ref.shape[1] - 2 * HALO, vel_ref.shape[2] - 2 * PAD
    cells = pl.ds(PAD, axial)
    wall = wall_mask(1, vel_ref.shape[3])
    odd = lax.rem(lax.axis_index("az"), 2)
    below, above = 0, HALO + planes
    for ref, place in (
        (even_ref, jnp.where(odd == 1, below, above)),
        (odd_ref, jnp.where(odd == 1, above, below)),
    ):
        for q in range(HALO):
            vel_ref[0, place + q, cells, :] = ref[0, q] * wall
            vel_ref[1, place + q, cells, :] = ref[1, q]
            vel_ref[2, place + q, cells, :] = ref[2, q]
    first = vel_ref[1, below + HALO - 1, PAD : PAD + 1, :]
    last = vel_ref[2, above, PAD + axial - 1 : PAD + axial, :]
    odd = lax.rem(lax.axis_index("ax"), 2) == 1
    shape = even_tile.shape
    even_tile[...] = jnp.broadcast_to(jnp.where(odd, first, last), shape)
    odd_tile[...] = jnp.broadcast_to(jnp.where(odd, last, first), shape)


def ghosts(cells, inner, planes):
    radial = inner.shape[1]

    def ghost(n, q):
        turn = -(n * planes + q + cells.j) % radial
        return cells.once(("ghost", n, q), lambda: pltpu.roll(inner, turn, 1) if turn else inner)

    return ghost


def block_terms(vel_ref, inner_ref, coef_ref, j, size, write, rounds=None):
    planes = vel_ref.shape[1] - 2 * HALO
    axial, radial = vel_ref.shape[2] - 2 * PAD, vel_ref.shape[3]
    groups = (4 if inner_ref is None else 2) * BLOCK // size
    times, places = rounds or (
        axial // (8 * groups),
        lambda i: [(i * groups + u) * 8 for u in range(groups)],
    )

    def rows(i, carry):
        coef = [coef_ref[n] for n in range(COUNT)]
        found = []
        for k in places(i):
            k = pl.multiple_of(k, 8)
            cells = Cells(vel_ref, j, k)
            ghost = None
            if inner_ref is not None:
                ghost = ghosts(cells, inner_ref[pl.ds(k, 8), :], planes)
            for q in range(size):
                found.append((q, k, terms(cells, ghost, coef, q, 1.0 / radial)))
        for q, k, values in found:
            for n, value in enumerate(values):
                write(n, j + q, pl.ds(k, 8), value)
        return carry

    lax.fori_loop(0, times, rows, 0)


def ahead(first, last, rounds, vel_ref, coef_ref, *refs):
    out_ref = refs[-1]

    def write(n, j, k, value):
        out_ref[n, j - first, k, :] = value

    def block(m, carry):
        block_terms(vel_ref, None, coef_ref, first + m * BLOCK, BLOCK, write, rounds)
        return carry

    lax.fori_loop(0, (last - first) // BLOCK, block, 0)


def ahead_with_ghosts(first, last, vel_ref, inner_ref, coef_ref, _, out_ref):
    def write(n, j, k, value):
        out_ref[n, j - first, k, :] = value

    for j in range(first, last, BLOCK):
        block_terms(vel_ref, inner_ref, coef_ref, j, BLOCK, write)


def finish(spans, vel_in, inner_ref, coef_ref, top, far, even, odd, *refs):
    parts, refs = refs[: len(spans)], refs[len(spans) :]
    del vel_in
    out_ref, step_ref, vel_ref, res, sems = refs
    axial, radial = inner_ref.shape
    planes = vel_ref.shape[1] - 2 * HALO
    largest = jnp.maximum(top[0:1, :], far[0:1, :])
    time_step = CFL_TARGET / (jnp.max(largest) + 1e-06)
    step_ref[0] = time_step
    scale = GAMMA * UNIT * time_step
    factors = (scale * coef_ref[WALL], scale, scale)
    pending = []

    def send(j, size):
        part_of = pl.ds(j, size)
        copy = pltpu.make_async_copy(
            res.at[:, part_of], out_ref.at[:, part_of], sems.at[len(pending)]
        )
        copy.start()
        pending.append(copy)

    def write(n, j, k, value):
        res[n, j, k, :] = value * factors[n]

    def complete(part, j, place, add):
        groups = 4

        def rows(i, carry):
            found = []
            for u in range(groups):
                k = pl.multiple_of((i * groups + u) * 8, 8)
                cells = Cells(vel_ref, j, k)
                ghost = ghosts(cells, inner_ref[pl.ds(k, 8), :], planes) if add else None
                for q in range(BLOCK):
                    values = [part[n, place + q, pl.ds(k, 8), :] for n in range(3)]
                    if add:
                        added = lane_zero_terms(cells, ghost, coef_ref, q, 1.0 / radial)
                        values = [x + y for x, y in zip(values, added)]
                    found.append((q, k, values))
            for q, k, values in found:
                for n, value in enumerate(values):
                    write(n, j + q, pl.ds(k, 8), value)
            return carry

        lax.fori_loop(0, axial // (8 * groups), rows, 0)
        send(j, BLOCK)

    for n, (part, (first, last)) in enumerate(zip(parts, spans)):
        for j in range(first, last, BLOCK):
            complete(part, j, j - first, n < 3)

    second = lax.rem(lax.axis_index("ax"), 2) == 1
    even, odd = even[0:1, :], odd[0:1, :]
    following, preceding = jnp.where(second, odd, even), jnp.where(second, even, odd)
    vel_ref[1, HALO - 1, PAD + axial : PAD + axial + 1, :] = following
    vel_ref[2, HALO + planes, PAD - 1 : PAD, :] = preceding
    for j in (0, planes - HALO):
        block_terms(vel_ref, inner_ref, coef_ref, j, HALO, write)
        send(j, HALO)
    for copy in pending:
        copy.wait()


def routed(block, axis, source):
    count = lax.axis_size(axis)
    return lax.ppermute(block, axis, [(source(i), i) for i in range(count)])


def exchanged(block, axis, step):
    return routed(block, axis, lambda i: i ^ step)


def across_even(block, axis):
    return exchanged(block, axis, 1)


def across_odd(block, axis):
    count = lax.axis_size(axis)
    return routed(block, axis, lambda i: (i + (1 if i % 2 else -1)) % count)


def cuts(planes):
    last = planes - HALO
    ends = (HALO, HALO + BLOCK, last - 5 * BLOCK, last - 3 * BLOCK, last - BLOCK, last)
    return list(zip(ends[:-1], ends[1:]))


def per_device(velocity):
    _, planes, axial, radial = velocity.shape
    sizes = lax.axis_size("az"), lax.axis_size("ax")
    theta_step = 2.0 * math.pi / (sizes[0] * planes)
    coef = jnp.asarray(coefficients(radial, theta_step))
    f32 = jnp.float32
    anywhere = pl.BlockSpec(memory_space=pl.ANY)
    vmem = pl.BlockSpec(memory_space=pltpu.VMEM)
    smem = pl.BlockSpec(memory_space=pltpu.SMEM)

    def shape(*sizes):
        return jax.ShapeDtypeStruct(sizes, f32)

    def call(kernel, name, work, scratch=0, **kwargs):
        return pl.pallas_call(
            kernel,
            name=name,
            compiler_params=pltpu.CompilerParams(vmem_limit_bytes=(4 + scratch) * 2**20),
            cost_estimate=pl.CostEstimate(flops=work, bytes_accessed=work, transcendentals=0),
            **kwargs,
        )

    odd = lax.axis_index("az") % 2
    ends = (planes - HALO, 0)
    even_end = jnp.where(odd == 1, ends[1], ends[0])
    odd_end = jnp.where(odd == 1, ends[0], ends[1])
    theta_odd = across_odd(lax.dynamic_slice_in_dim(velocity, odd_end, HALO, 1), "az")
    theta_even = across_even(lax.dynamic_slice_in_dim(velocity, even_end, HALO, 1), "az")

    edge = shape(3, planes, 2, radial)
    padded = shape(3, planes + 2 * HALO, axial + 2 * PAD, radial)
    row = shape(axial, radial)
    tile = shape(8, radial)
    vel, edge_even, edge_odd, mine, pay = call(
        functools.partial(first_pass, theta_step),
        "first_pass",
        0,
        out_shape=(padded, edge, edge, row, tile),
        in_specs=[anywhere],
        out_specs=(vmem,) * 5,
        scratch_shapes=[pltpu.SemaphoreType.DMA((planes // GROUP,))],
    )(pltpu.with_memory_space_constraint(velocity, pltpu.HBM))
    inner = exchanged(mine, "az", sizes[0] // 2)
    z_even = across_even(edge_even, "ax")
    spans = cuts(planes)

    def part_shape(n):
        return shape(3, spans[n][1] - spans[n][0], axial, radial)

    def without_ghosts(n, name, rounds, vel, *tokens, **kwargs):
        return call(
            functools.partial(ahead, *spans[n], rounds),
            name,
            velocity.size * 2,
            out_shape=part_shape(n),
            in_specs=[vmem] * (2 + len(tokens)),
            out_specs=vmem,
            **kwargs,
        )(vel, coef, *tokens)

    def with_ghosts(n, token):
        return call(
            functools.partial(ahead_with_ghosts, *spans[n]),
            f"span_{n}",
            velocity.size * 2,
            out_shape=part_shape(n),
            in_specs=[vmem] * 4,
            out_specs=vmem,
        )(vel, inner, coef, token)

    middle = (axial - 16) // 16, lambda i: [16 * i + 8, 16 * i + 16]
    outer = 1, lambda i: [i * 8, i * 8 + axial - 8]
    part_0 = without_ghosts(0, "span_0_middle", middle, vel, pay)
    edge_odd = call(
        carried,
        "carried",
        0,
        out_shape=edge,
        in_specs=[vmem] * 4,
        out_specs=vmem,
        input_output_aliases={2: 0},
    )(z_even, pay, edge_odd, part_0)
    z_odd = across_odd(edge_odd, "ax")

    part_1 = without_ghosts(1, "span_1_middle", middle, vel, edge_odd)
    top, vel = call(
        fold,
        "fold",
        0,
        out_shape=(tile, padded),
        in_specs=[vmem] * 5,
        out_specs=(vmem,) * 2,
        input_output_aliases={3: 1},
    )(z_even, z_odd, pay, vel, part_1)
    for step in (1 << n for n in range(2, sizes[1].bit_length() - 1)):
        top = jnp.maximum(top, routed(top, "ax", lambda i, step=step: (i + step) % sizes[1]))

    bits = [1 << n for n in range(1, sizes[0].bit_length() - 1)] + [1]
    far = exchanged(top, "az", bits[0])
    parts = [
        without_ghosts(0, "span_0_outer", outer, vel, part_0, input_output_aliases={2: 0}),
        without_ghosts(1, "span_1_outer", outer, vel, part_1, input_output_aliases={2: 0}),
        without_ghosts(2, "span_2", None, vel, top),
    ]
    for n, bit in enumerate(bits[1:]):
        top = call(
            merged,
            "merged",
            0,
            out_shape=tile,
            in_specs=[vmem] * 5,
            out_specs=vmem,
        )(top, far, *parts[-3:])
        far = exchanged(top, "az", bit)
        if n == 0:
            parts.append(with_ghosts(3, top))
    tile_even, tile_odd, vel = call(
        theta_in,
        "theta_in",
        0,
        out_shape=(tile, tile, padded),
        in_specs=[vmem] * 4,
        out_specs=(vmem,) * 3,
        input_output_aliases={2: 2},
    )(theta_odd, theta_even, vel, parts[-1])
    corner_even, corner_odd = across_even(tile_even, "ax"), across_odd(tile_odd, "ax")
    parts.append(with_ghosts(4, tile_even))
    increment, time_step, _ = call(
        functools.partial(finish, spans),
        "finish",
        0,
        scratch=8,
        out_shape=(shape(*velocity.shape), shape(1), padded),
        in_specs=[vmem] * (7 + len(parts)),
        out_specs=(anywhere, smem, vmem),
        scratch_shapes=[
            pltpu.VMEM(velocity.shape, f32),
            pltpu.SemaphoreType.DMA(((planes - 2 * HALO) // BLOCK + 2,)),
        ],
        input_output_aliases={0: 2},
    )(vel, inner, coef, top, far, corner_even, corner_odd, *parts)
    return increment, time_step.reshape(())


def solution(mesh):
    return jax.shard_map(
        per_device,
        mesh=mesh,
        in_specs=(P(None, "az", "ax", None),),
        out_specs=(P(None, "az", "ax", None), P()),
        check_vma=False,
    )
```

```python
import functools
import math

import jax
import jax.numpy as jnp
import numpy as np
from jax import lax
from jax.experimental import pallas as pl
from jax.experimental.pallas import tpu as pltpu
from jax.sharding import PartitionSpec as P

AXIAL_STEP = 0.01
VISCOSITY = 0.001
CFL_TARGET = 1.2
GAMMA = 8.0 / 15.0

PAD = 8
HALO = 2
BLOCK = 4
GROUP = 2
UNROLL = 4

(
    WALL,
    RADIAL_C,
    THETA_C,
    CROSS_Z,
    SECOND_C,
    CENTRE_Z,
    CENTRE_T,
    CURVE_T,
    TURN_T,
    RADIAL_F,
    THETA_F,
    SECOND_F,
    CENTRE_R,
    CURVE_R,
    TURN_R,
    COUNT,
) = range(16)


UNIT = VISCOSITY / (12.0 * AXIAL_STEP**2)


def coefficients(radial, theta_step):
    dr = 1.0 / radial
    index = np.arange(radial, dtype=np.float64)
    centre = (index + 0.5) * dr
    face = (index + 1.0) * dr
    wall = np.where(index < radial - 1.5, 1.0, 0.0)
    h = theta_step
    nu = VISCOSITY
    rows = np.zeros((COUNT, radial))
    rows[WALL] = wall
    common = -2.0 * nu / dr**2 - 30.0 * nu / (12.0 * AXIAL_STEP**2)
    rows[RADIAL_C] = nu / (2.0 * dr * centre)
    rows[THETA_C] = -1.0 / (12.0 * h * centre)
    rows[CROSS_Z] = 0.25 * rows[THETA_C]
    rows[SECOND_C] = nu / (12.0 * h * h * centre**2)
    rows[CENTRE_Z] = common - 30.0 * rows[SECOND_C]
    rows[CENTRE_T] = rows[CENTRE_Z] - nu / centre**2
    rows[CURVE_T] = 0.25 / centre
    rows[TURN_T] = nu / (h * centre**2)
    rows[RADIAL_F] = nu / (2.0 * dr * face)
    rows[THETA_F] = -0.25 / (12.0 * h * face)
    rows[SECOND_F] = nu / (12.0 * h * h * face**2)
    rows[CENTRE_R] = common - 30.0 * rows[SECOND_F] - nu / face**2
    rows[CURVE_R] = 1.0 / (16.0 * face)
    rows[TURN_R] = -nu / (h * face**2)
    rows[RADIAL_C:] /= UNIT
    return np.broadcast_to(rows[:, None, :], (COUNT, 8, radial)).astype(np.float32)


class Cells:
    def __init__(self, vel, j, k):
        self.vel, self.j, self.k, self.known = vel, j, k, {}

    def once(self, key, make):
        if key not in self.known:
            self.known[key] = make()
        return self.known[key]

    def at(self, n, dj, dk=0):
        rows = pl.ds(self.k + PAD + dk, 8)
        return self.once((n, dj, dk), lambda: self.vel[n, self.j + HALO + dj, rows, :])

    def turned(self, by, n, dj, dk=0):
        return self.once(
            (by, n, dj, dk), lambda: pltpu.roll(self.at(n, dj, dk), by % self.vel.shape[3], 1)
        )

    def pair(self, by, n, dj, dk=0):
        return self.once(
            ("pair", n, dj, dk), lambda: self.at(n, dj, dk) + self.turned(by, n, dj, dk)
        )

    def beside(self, dj, dk):
        n = 1 if dk >= 0 else 2
        other = (1, dj - 1, dk) if n == 1 else (2, dj, dk)
        here = (1, dj, dk) if n == 1 else (2, dj, dk + 1)
        return self.once(("sum", n, dj, dk), lambda: self.at(*other) + self.at(*here))


def terms(cells, ghost, coef, q, dr):
    at, turned, pair = cells.at, cells.turned, cells.pair
    a, b, c = (at(n, q) for n in range(3))
    lane = lax.broadcasted_iota(jnp.int32, a.shape, 1)
    first_lane = lane == 0
    last_lane = lane == a.shape[1] - 1

    lap = VISCOSITY / dr**2 / UNIT
    adv_z = -1.0 / (12.0 * AXIAL_STEP) / UNIT
    by_dr = 1.0 / dr / UNIT

    def differences(p1, m1, p2, m2):
        return 8.0 * (p1 - m1) - (p2 - m2), 16.0 * (p1 + m1) - (p2 + m2)

    def pieces(n):
        over = differences(*(at(n, q + d) for d in (1, -1, 2, -2)))
        along = differences(*(at(n, q, d) for d in (1, -1, 2, -2)))
        return over, along

    def below(n):
        if ghost is not None and n > 0 and q % 2 == 0:
            x = jnp.where(last_lane, ghost(n, q + 1), at(n, q))
            return pltpu.roll(x, 1, 1)
        x = turned(1, n, q)
        if ghost is not None:
            return jnp.where(first_lane, ghost(n, q), x)
        return x if n == 0 else jnp.where(first_lane, 0.0, x)

    def above(n):
        return jnp.where(last_lane, -at(n, q), turned(-1, n, q))

    pair_a, pair_side, pair_next = pair(1, 0, q), pair(1, 0, q + 1), pair(1, 0, q, 1)
    pair_b, pair_back = pair(-1, 1, q), pair(-1, 1, q - 1)

    theta, axial = pieces(2)
    up, low = above(2), below(2)
    u_r = pair_a + pair_next
    u_t = cells.beside(q, 0) + cells.beside(q, 1)
    h_z = (up - low) * (coef[RADIAL_C] - u_r * (0.125 * by_dr)) + (up + low) * lap
    h_z = h_z + theta[0] * (u_t * coef[CROSS_Z])
    h_z = h_z + (theta[1] * coef[SECOND_C] + axial[1])
    h_z = h_z + c * (coef[CENTRE_Z] + axial[0] * adv_z)

    theta, axial = pieces(1)
    up, low = above(1), below(1)
    u_r = pair_a + pair_side
    u_z = cells.beside(q, -1) + cells.beside(q + 1, -1)
    h_t = (up - low) * (coef[RADIAL_C] - u_r * (0.125 * by_dr)) + (up + low) * lap
    h_t = h_t + b * (coef[CENTRE_T] + theta[0] * coef[THETA_C] - u_r * coef[CURVE_T])
    h_t = h_t + (theta[1] * coef[SECOND_C] + axial[1])
    h_t = h_t + axial[0] * (u_z * (0.25 * adv_z))
    h_t = h_t + (pair_side - pair_a) * coef[TURN_T]

    theta, axial = pieces(0)
    up, low = turned(-1, 0, q), below(0)
    u_t = pair_b + pair_back
    u_z = pair(-1, 2, q) + pair(-1, 2, q, -1)
    h_r = (up - low) * (coef[RADIAL_F] - a * (0.5 * by_dr)) + (up + low) * lap
    h_r = h_r + u_t * (u_t * coef[CURVE_R] + theta[0] * coef[THETA_F])
    h_r = h_r + (theta[1] * coef[SECOND_F] + axial[1])
    h_r = h_r + (axial[0] * (u_z * (0.25 * adv_z)) + a * coef[CENTRE_R])
    h_r = h_r + (pair_b - pair_back) * coef[TURN_R]
    return h_r, h_t, h_z


def lane_zero_terms(cells, ghost, coef, q, dr):
    lap = VISCOSITY / dr**2 / UNIT
    by_dr = 1.0 / dr / UNIT
    a = cells.at(0, q)
    first_lane = lax.broadcasted_iota(jnp.int32, a.shape, 1) == 0
    add_r = ghost(0, q) * (lap - coef[RADIAL_F] + a * (0.5 * by_dr))
    add_t = ghost(1, q) * (lap - coef[RADIAL_C] + (a + cells.at(0, q + 1)) * (0.125 * by_dr))
    add_z = ghost(2, q) * (lap - coef[RADIAL_C] + (a + cells.at(0, q, 1)) * (0.125 * by_dr))
    return tuple(jnp.where(first_lane, x, 0.0) for x in (add_r, add_t, add_z))


def wall_mask(rows, radial):
    lane = lax.broadcasted_iota(jnp.int32, (rows, radial), 1)
    return jnp.where(lane == radial - 1, 0.0, 1.0).astype(jnp.float32)


def first_pass(theta_step, v_ref, vel_ref, even_ref, odd_ref, inner_ref, pay_ref, sems):
    _, planes, axial, radial = v_ref.shape
    lane = lax.broadcasted_iota(jnp.int32, (8, radial), 1)
    wall = wall_mask(8, radial)
    rate_t = (radial / theta_step) / (lane.astype(jnp.float32) + 0.5)
    odd = lax.rem(lax.axis_index("ax"), 2) == 1

    def fetch(g):
        part = pl.ds(g * GROUP, GROUP)
        target = vel_ref.at[:, pl.ds(g * GROUP + HALO, GROUP), pl.ds(PAD, axial)]
        return pltpu.make_async_copy(v_ref.at[:, part], target, sems.at[g])

    for g in range(planes // GROUP):
        fetch(g).start()

    zero = jnp.zeros((8, radial), jnp.float32)
    largest = [zero] * 4
    for g in range(planes // GROUP):
        fetch(g).wait()
        for i in range(axial // 8):
            k = pl.ds(8 * i, 8)
            padded = pl.ds(8 * i + PAD, 8)
            inner = zero if g == 0 else inner_ref[k, :]
            for q in range(GROUP):
                j = g * GROUP + q
                cells = [vel_ref[n, j + HALO, padded, :] for n in range(3)]
                for n, x in enumerate(cells):
                    place = n * planes + j
                    x = pltpu.roll(x, place, 1) if place else x
                    inner = jnp.where(lane == place, x if n == 2 else -x, inner)
                a, b, c = cells
                a = a * wall
                vel_ref[0, j + HALO, padded, :] = a
                rate = jnp.abs(a) * float(radial) + jnp.abs(b) * rate_t
                rate = rate + jnp.abs(c) * (1.0 / AXIAL_STEP)
                largest[q % 4] = jnp.maximum(largest[q % 4], rate)
            inner_ref[k, :] = inner
        for q in range(GROUP):
            for n in range(3):
                j = g * GROUP + q
                first = vel_ref[n, j + HALO, PAD : PAD + 2, :]
                last = vel_ref[n, j + HALO, PAD + axial - 2 : PAD + axial, :]
                even_ref[n, j] = jnp.where(odd, first, last)
                odd_ref[n, j] = jnp.where(odd, last, first)

    largest = jnp.maximum(
        jnp.maximum(largest[0], largest[1]), jnp.maximum(largest[2], largest[3])
    )
    top = jnp.max(largest, axis=(0, 1), keepdims=True)
    pay_ref[...] = jnp.broadcast_to(top, pay_ref.shape)
    end = lax.broadcasted_iota(jnp.int32, (2, radial), 1) == radial - 1
    for ref in (even_ref, odd_ref):
        ref[0, 0] = jnp.where(end, top, ref[0, 0])


def carried(even_ref, pay_ref, odd_in, _, odd_ref):
    radial = even_ref.shape[3]
    lane = lax.broadcasted_iota(jnp.int32, (2, radial), 1)
    top = jnp.maximum(even_ref[0, 0], pay_ref[0:2, :])
    odd_ref[0, 0] = jnp.where(lane == radial - 1, top, odd_in[0, 0])


def fold(even_ref, odd_ref, pay_ref, vel_in, _, *refs):
    del vel_in
    top_ref, vel_ref = refs
    planes, radial = even_ref.shape[1], even_ref.shape[3]
    axial = vel_ref.shape[2] - 2 * PAD
    lane = lax.broadcasted_iota(jnp.int32, (1, radial), 1)
    top = jnp.maximum(even_ref[0, 0, 0:1, :], odd_ref[0, 0, 0:1, :])
    top = jnp.max(jnp.where(lane == radial - 1, top, 0.0), axis=(0, 1), keepdims=True)
    top_ref[...] = jnp.maximum(pay_ref[...], top)
    wall = wall_mask(2, radial)
    odd = lax.rem(lax.axis_index("ax"), 2) == 1

    def plane(j, carry):
        for n in range(3):
            mask = wall if n == 0 else 1.0
            even, other = even_ref[n, j] * mask, odd_ref[n, j] * mask
            low, high = jnp.where(odd, even, other), jnp.where(odd, other, even)
            vel_ref[n, j + HALO, PAD - 2 : PAD, :] = low
            vel_ref[n, j + HALO, PAD + axial : PAD + axial + 2, :] = high
        return carry

    lax.fori_loop(0, planes, plane, 0, unroll=4)


def merged(mine_ref, far_ref, *refs):
    refs[-1][...] = jnp.maximum(mine_ref[...], far_ref[...])


def theta_in(odd_ref, even_ref, vel_in, _, even_tile, odd_tile, vel_ref):
    del vel_in
    planes, axial = vel_ref.shape[1] - 2 * HALO, vel_ref.shape[2] - 2 * PAD
    cells = pl.ds(PAD, axial)
    wall = wall_mask(1, vel_ref.shape[3])
    odd = lax.rem(lax.axis_index("az"), 2)
    below, above = 0, HALO + planes
    for ref, place in (
        (even_ref, jnp.where(odd == 1, below, above)),
        (odd_ref, jnp.where(odd == 1, above, below)),
    ):
        for q in range(HALO):
            vel_ref[0, place + q, cells, :] = ref[0, q] * wall
            vel_ref[1, place + q, cells, :] = ref[1, q]
            vel_ref[2, place + q, cells, :] = ref[2, q]
    first = vel_ref[1, below + HALO - 1, PAD : PAD + 1, :]
    last = vel_ref[2, above, PAD + axial - 1 : PAD + axial, :]
    odd = lax.rem(lax.axis_index("ax"), 2) == 1
    shape = even_tile.shape
    even_tile[...] = jnp.broadcast_to(jnp.where(odd, first, last), shape)
    odd_tile[...] = jnp.broadcast_to(jnp.where(odd, last, first), shape)


def ghosts(cells, inner, planes):
    radial = inner.shape[1]

    def ghost(n, q):
        turn = -(n * planes + q + cells.j) % radial
        return cells.once(("ghost", n, q), lambda: pltpu.roll(inner, turn, 1) if turn else inner)

    return ghost


def block_terms(vel_ref, inner_ref, coef_ref, j, size, write, rounds=None):
    planes = vel_ref.shape[1] - 2 * HALO
    axial, radial = vel_ref.shape[2] - 2 * PAD, vel_ref.shape[3]
    groups = (4 if inner_ref is None else 2) * BLOCK // size
    times, places = rounds or (
        axial // (8 * groups),
        lambda i: [(i * groups + u) * 8 for u in range(groups)],
    )

    def rows(i, carry):
        coef = [coef_ref[n] for n in range(COUNT)]
        found = []
        for k in places(i):
            k = pl.multiple_of(k, 8)
            cells = Cells(vel_ref, j, k)
            ghost = None
            if inner_ref is not None:
                ghost = ghosts(cells, inner_ref[pl.ds(k, 8), :], planes)
            for q in range(size):
                found.append((q, k, terms(cells, ghost, coef, q, 1.0 / radial)))
        for q, k, values in found:
            for n, value in enumerate(values):
                write(n, j + q, pl.ds(k, 8), value)
        return carry

    lax.fori_loop(0, times, rows, 0)


def ahead(first, last, rounds, vel_ref, coef_ref, *refs):
    out_ref = refs[-1]

    def write(n, j, k, value):
        out_ref[n, j - first, k, :] = value

    def block(m, carry):
        block_terms(vel_ref, None, coef_ref, first + m * BLOCK, BLOCK, write, rounds)
        return carry

    lax.fori_loop(0, (last - first) // BLOCK, block, 0)


def ahead_with_ghosts(first, last, vel_ref, inner_ref, coef_ref, _, out_ref):
    def write(n, j, k, value):
        out_ref[n, j - first, k, :] = value

    for j in range(first, last, BLOCK):
        block_terms(vel_ref, inner_ref, coef_ref, j, BLOCK, write)


def finish(spans, vel_in, inner_ref, coef_ref, top, far, even, odd, *refs):
    parts, refs = refs[: len(spans)], refs[len(spans) :]
    del vel_in
    out_ref, step_ref, vel_ref, res, sems = refs
    axial, radial = inner_ref.shape
    planes = vel_ref.shape[1] - 2 * HALO
    largest = jnp.maximum(top[0:1, :], far[0:1, :])
    time_step = CFL_TARGET / (jnp.max(largest) + 1e-06)
    step_ref[0] = time_step
    scale = GAMMA * UNIT * time_step
    factors = (scale * coef_ref[WALL], scale, scale)
    pending = []

    def send(j, size):
        part_of = pl.ds(j, size)
        copy = pltpu.make_async_copy(
            res.at[:, part_of], out_ref.at[:, part_of], sems.at[len(pending)]
        )
        copy.start()
        pending.append(copy)

    def write(n, j, k, value):
        res[n, j, k, :] = value * factors[n]

    def complete(part, j, place, add):
        groups = 4

        def rows(i, carry):
            found = []
            for u in range(groups):
                k = pl.multiple_of((i * groups + u) * 8, 8)
                cells = Cells(vel_ref, j, k)
                ghost = ghosts(cells, inner_ref[pl.ds(k, 8), :], planes) if add else None
                for q in range(BLOCK):
                    values = [part[n, place + q, pl.ds(k, 8), :] for n in range(3)]
                    if add:
                        added = lane_zero_terms(cells, ghost, coef_ref, q, 1.0 / radial)
                        values = [x + y for x, y in zip(values, added)]
                    found.append((q, k, values))
            for q, k, values in found:
                for n, value in enumerate(values):
                    write(n, j + q, pl.ds(k, 8), value)
            return carry

        lax.fori_loop(0, axial // (8 * groups), rows, 0)
        send(j, BLOCK)

    for n, (part, (first, last)) in enumerate(zip(parts, spans)):
        for j in range(first, last, BLOCK):
            complete(part, j, j - first, n < 3)

    second = lax.rem(lax.axis_index("ax"), 2) == 1
    even, odd = even[0:1, :], odd[0:1, :]
    following, preceding = jnp.where(second, odd, even), jnp.where(second, even, odd)
    vel_ref[1, HALO - 1, PAD + axial : PAD + axial + 1, :] = following
    vel_ref[2, HALO + planes, PAD - 1 : PAD, :] = preceding
    for j in (0, planes - HALO):
        block_terms(vel_ref, inner_ref, coef_ref, j, HALO, write)
        send(j, HALO)
    for copy in pending:
        copy.wait()


def routed(block, axis, source):
    count = lax.axis_size(axis)
    return lax.ppermute(block, axis, [(source(i), i) for i in range(count)])


def exchanged(block, axis, step):
    return routed(block, axis, lambda i: i ^ step)


def across_even(block, axis):
    return exchanged(block, axis, 1)


def across_odd(block, axis):
    count = lax.axis_size(axis)
    return routed(block, axis, lambda i: (i + (1 if i % 2 else -1)) % count)


def cuts(planes):
    last = planes - HALO
    ends = (HALO, HALO + BLOCK, last - 5 * BLOCK, last - 3 * BLOCK, last - BLOCK, last)
    return list(zip(ends[:-1], ends[1:]))


def per_device(velocity):
    _, planes, axial, radial = velocity.shape
    sizes = lax.axis_size("az"), lax.axis_size("ax")
    theta_step = 2.0 * math.pi / (sizes[0] * planes)
    coef = jnp.asarray(coefficients(radial, theta_step))
    f32 = jnp.float32
    anywhere = pl.BlockSpec(memory_space=pl.ANY)
    vmem = pl.BlockSpec(memory_space=pltpu.VMEM)
    smem = pl.BlockSpec(memory_space=pltpu.SMEM)

    def shape(*sizes):
        return jax.ShapeDtypeStruct(sizes, f32)

    def call(kernel, name, work, scratch=0, **kwargs):
        return pl.pallas_call(
            kernel,
            name=name,
            compiler_params=pltpu.CompilerParams(vmem_limit_bytes=(4 + scratch) * 2**20),
            cost_estimate=pl.CostEstimate(flops=work, bytes_accessed=work, transcendentals=0),
            **kwargs,
        )

    odd = lax.axis_index("az") % 2
    ends = (planes - HALO, 0)
    even_end = jnp.where(odd == 1, ends[1], ends[0])
    odd_end = jnp.where(odd == 1, ends[0], ends[1])
    theta_odd = across_odd(lax.dynamic_slice_in_dim(velocity, odd_end, HALO, 1), "az")
    theta_even = across_even(lax.dynamic_slice_in_dim(velocity, even_end, HALO, 1), "az")

    edge = shape(3, planes, 2, radial)
    padded = shape(3, planes + 2 * HALO, axial + 2 * PAD, radial)
    row = shape(axial, radial)
    tile = shape(8, radial)
    vel, edge_even, edge_odd, mine, pay = call(
        functools.partial(first_pass, theta_step),
        "first_pass",
        0,
        out_shape=(padded, edge, edge, row, tile),
        in_specs=[anywhere],
        out_specs=(vmem,) * 5,
        scratch_shapes=[pltpu.SemaphoreType.DMA((planes // GROUP,))],
    )(pltpu.with_memory_space_constraint(velocity, pltpu.HBM))
    inner = exchanged(mine, "az", sizes[0] // 2)
    z_even = across_even(edge_even, "ax")
    spans = cuts(planes)

    def part_shape(n):
        return shape(3, spans[n][1] - spans[n][0], axial, radial)

    def without_ghosts(n, name, rounds, vel, *tokens, **kwargs):
        return call(
            functools.partial(ahead, *spans[n], rounds),
            name,
            velocity.size * 2,
            out_shape=part_shape(n),
            in_specs=[vmem] * (2 + len(tokens)),
            out_specs=vmem,
            **kwargs,
        )(vel, coef, *tokens)

    def with_ghosts(n, token):
        return call(
            functools.partial(ahead_with_ghosts, *spans[n]),
            f"span_{n}",
            velocity.size * 2,
            out_shape=part_shape(n),
            in_specs=[vmem] * 4,
            out_specs=vmem,
        )(vel, inner, coef, token)

    middle = (axial - 16) // 16, lambda i: [16 * i + 8, 16 * i + 16]
    outer = 1, lambda i: [i * 8, i * 8 + axial - 8]
    part_0 = without_ghosts(0, "span_0_middle", middle, vel, pay)
    edge_odd = call(
        carried,
        "carried",
        0,
        out_shape=edge,
        in_specs=[vmem] * 4,
        out_specs=vmem,
        input_output_aliases={2: 0},
    )(z_even, pay, edge_odd, part_0)
    z_odd = across_odd(edge_odd, "ax")

    part_1 = without_ghosts(1, "span_1_middle", middle, vel, edge_odd)
    top, vel = call(
        fold,
        "fold",
        0,
        out_shape=(tile, padded),
        in_specs=[vmem] * 5,
        out_specs=(vmem,) * 2,
        input_output_aliases={3: 1},
    )(z_even, z_odd, pay, vel, part_1)
    for step in (1 << n for n in range(2, sizes[1].bit_length() - 1)):
        top = jnp.maximum(top, routed(top, "ax", lambda i, step=step: (i + step) % sizes[1]))

    bits = [1 << n for n in range(1, sizes[0].bit_length() - 1)] + [1]
    far = exchanged(top, "az", bits[0])
    parts = [
        without_ghosts(0, "span_0_outer", outer, vel, part_0, input_output_aliases={2: 0}),
        without_ghosts(1, "span_1_outer", outer, vel, part_1, input_output_aliases={2: 0}),
        without_ghosts(2, "span_2", None, vel, top),
    ]
    for n, bit in enumerate(bits[1:]):
        top = call(
            merged,
            "merged",
            0,
            out_shape=tile,
            in_specs=[vmem] * 5,
            out_specs=vmem,
        )(top, far, *parts[-3:])
        far = exchanged(top, "az", bit)
        if n == 0:
            parts.append(with_ghosts(3, top))
    tile_even, tile_odd, vel = call(
        theta_in,
        "theta_in",
        0,
        out_shape=(tile, tile, padded),
        in_specs=[vmem] * 4,
        out_specs=(vmem,) * 3,
        input_output_aliases={2: 2},
    )(theta_odd, theta_even, vel, parts[-1])
    corner_even, corner_odd = across_even(tile_even, "ax"), across_odd(tile_odd, "ax")
    parts.append(with_ghosts(4, tile_even))
    increment, time_step, _ = call(
        functools.partial(finish, spans),
        "finish",
        0,
        scratch=8,
        out_shape=(shape(*velocity.shape), shape(1), padded),
        in_specs=[vmem] * (7 + len(parts)),
        out_specs=(anywhere, smem, vmem),
        scratch_shapes=[
            pltpu.VMEM(velocity.shape, f32),
            pltpu.SemaphoreType.DMA(((planes - 2 * HALO) // BLOCK + 2,)),
        ],
        input_output_aliases={0: 2},
    )(vel, inner, coef, top, far, corner_even, corner_odd, *parts)
    return increment, time_step.reshape(())


def solution(mesh):
    return jax.shard_map(
        per_device,
        mesh=mesh,
        in_specs=(P(None, "az", "ax", None),),
        out_specs=(P(None, "az", "ax", None), P()),
        check_vma=False,
    )
```
